32 devices in a mesh: seq: 8 (over z, core), tok: 4 (over y, x).
Axes of the slice: x: 2, y: 2, z: 4, core: 2. Of those that a mesh axis runs over, the one named last changes fastest.
Arguments:
- x_in: bfloat16 [2, 16, 1024, 768], P(None, 'seq', 'tok'), may hold values from -6 to 6
- cotangent: bfloat16 [2, 16, 1024, 768], P(None, 'seq', 'tok'), may hold values from -6 to 6
- counts: int32 [2, 8], P(None, 'seq'), may hold values from 1 to 2, as said below
- ln1_gain: bfloat16 [2, 768], replicated, may hold values from 0.5 to 1.5
- ln1_bias: bfloat16 [2, 768], replicated, may hold values from -3 to 3
- w_in: bfloat16 [2, 768, 2304], replicated, may hold values from -0.21875 to 0.21875
- short_w: bfloat16 [2, 3, 2304], replicated, may hold values from -5 to 5
- filt_w1: bfloat16 [2, 33, 64], replicated, may hold values from -1 to 1
- filt_freq: bfloat16 [2, 2, 64], replicated, may hold values from 0.5 to 4
- filt_w2: bfloat16 [2, 64, 64], replicated, may hold values from -0.75 to 0.75
- filt_w3: bfloat16 [2, 64, 768], replicated, may hold values from -0.09375 to 0.09375
- long_bias: bfloat16 [2, 768], replicated, may hold values from -5 to 5
- w_out: bfloat16 [2, 768, 768], replicated, may hold values from -0.21875 to 0.21875
- ln2_gain: bfloat16 [2, 768], replicated, may hold values from 0.5 to 1.5
- ln2_bias: bfloat16 [2, 768], replicated, may hold values from -3 to 3
- w_up: bfloat16 [2, 768, 3072], replicated, may hold values from -0.21875 to 0.21875
- w_down: bfloat16 [2, 3072, 768], replicated, may hold values from -0.109375 to 0.109375
Outputs:
- out_act: float32 [2, 16, 1024, 768], P(None, 'seq', 'tok')
- grad_in: float32 [2, 16, 1024, 768], P(None, 'seq', 'tok')
- grad_ln1_gain: float32 [2, 768], replicated
- grad_ln1_bias: float32 [2, 768], replicated
- grad_w_in: float32 [2, 768, 2304], P(None, 'seq', 'tok')
- grad_short_w: float32 [2, 3, 2304], replicated
- grad_filt_w1: float32 [2, 33, 64], replicated
- grad_filt_freq: float32 [2, 2, 64], replicated
- grad_filt_w2: float32 [2, 64, 64], replicated
- grad_filt_w3: float32 [2, 64, 768], replicated
- grad_long_bias: float32 [2, 768], replicated
- grad_w_out: float32 [2, 768, 768], P(None, 'seq', 'tok')
- grad_ln2_gain: float32 [2, 768], replicated
- grad_ln2_bias: float32 [2, 768], replicated
- grad_w_up: float32 [2, 768, 3072], P(None, 'seq', 'tok')
- grad_w_down: float32 [2, 3072, 768], P(None, 'tok', 'seq')
The draws below stay inside these ranges and needn't reach their ends.
Inputs may be any that keep to these rules, and one draw needn't show every extreme that they name: Live sequences of group g in micro-batch m are its slots 0 to counts[m, g] - 1 of 2; in every micro-batch one group has all 2 slots live and another group has one.
All inputs are finite; a program needn't handle non-finite values.
Results may differ from the reference program's by a relative error of at most 0.019.
Values may be sent and summed in bfloat16 or wider, within the bound.
A program may use at most 512 MiB of HBM per device.

```python
import math
from functools import partial
import jax
import jax.numpy as jnp
from jax import lax

D = 768
FF = 3072
FDIM = 64
EMB = 33
LAYERS = 2
MICRO = 2
CAP = 2
GROUPS = 8
SEQS = 16
LENGTH = 1024


def draw_counts(key, part):
    key = jax.random.fold_in(key, 7)
    key_base, key_full, key_single = jax.random.split(key, 3)
    drawn = jax.random.randint(key_base, (MICRO, GROUPS), 1, CAP + 1)
    full_group = jax.random.randint(key_full, (MICRO,), 0, GROUPS)
    offset = jax.random.randint(key_single, (MICRO,), 1, GROUPS)
    single_group = (full_group + offset) % GROUPS
    group_ids = jnp.arange(GROUPS, dtype=jnp.int32)
    drawn = jnp.where(group_ids[None, :] == full_group[:, None], CAP, drawn)
    drawn = jnp.where(group_ids[None, :] == single_group[:, None], 1, drawn)
    return drawn.astype(jnp.int32)


def strengthened(values, own_key, source, target, blocks, factor):
    def block_of(axis_at):
        return (jnp.arange(values.shape[axis_at]) // (values.shape[axis_at] // blocks)).reshape((-1,) + (1,) * (values.ndim - 1 - axis_at))

    one_side = jax.random.permutation(own_key, blocks)[block_of(target)]
    other_side = (block_of(target) + blocks // 2) % blocks
    return jnp.where((block_of(source) == one_side) | (block_of(source) == other_side), factor * values, values)


def block_scale(own_key, extent, cuts, least, high):
    loudness = 1.0
    for axis_at, parts in cuts:
        heights = jax.random.uniform(jax.random.fold_in(jax.random.fold_in(own_key, 6), axis_at), (parts,), jnp.float32, least / len(cuts), high / len(cuts))
        loudness = loudness * jnp.repeat(jnp.exp(heights), extent[axis_at] // parts).reshape((-1,) + (1,) * (len(extent) - 1 - axis_at))
    return loudness


def normal_values(key, shape, deviation, limit, cuts=(), held_as=jnp.bfloat16):
    entries = deviation * jax.random.normal(key, shape, jnp.float32)
    if cuts:
        entries = entries * block_scale(key, shape, cuts, -0.22, 0.18)
    return jnp.clip(entries, -limit, limit).astype(held_as)


def heavy_noise(key, dims, deviation, reach, cuts, heavy, kind=jnp.bfloat16):
    entries = deviation * jax.random.normal(key, dims, jnp.float32)
    if cuts:
        entries = entries * block_scale(key, dims, cuts, -0.22, 0.18)
    return jnp.clip(strengthened(entries, jax.random.fold_in(key, 3), *heavy), -reach, reach).astype(kind)


def setup_inputs(seed: int = 0) -> dict:
    key_list = jax.random.split(jax.random.key(seed), 18)
    return {
        "x_in": normal_values(key_list[0], (MICRO, SEQS, LENGTH, D), 1.0, 6.0, ((1, 8), (2, 4))),
        "cotangent": heavy_noise(key_list[1], (MICRO, SEQS, LENGTH, D), 1.0, 6.0, ((1, 8), (2, 4)), (1, 3, 8, 2.0)),
        "counts": draw_counts(jax.random.fold_in(key_list[17], 71), 0),
        "ln1_gain": jnp.clip(1.0 + 0.1 * jax.random.normal(key_list[3], (LAYERS, D), jnp.float32), 0.5, 1.5).astype(jnp.bfloat16),
        "ln1_bias": normal_values(key_list[4], (LAYERS, D), 0.2, 3.0),
        "w_in": normal_values(key_list[5], (LAYERS, D, 3 * D), D ** -0.5, 0.21875),
        "short_w": normal_values(key_list[6], (LAYERS, 3, 3 * D), 0.5, 5.0),
        "filt_w1": normal_values(key_list[7], (LAYERS, EMB, FDIM), EMB ** -0.5, 1.0),
        "filt_freq": jnp.clip(jnp.exp(jax.random.uniform(key_list[8], (LAYERS, 2, FDIM), jnp.float32, math.log(0.5), math.log(4.0))), 0.5, 4.0).astype(jnp.bfloat16),
        "filt_w2": normal_values(key_list[9], (LAYERS, FDIM, FDIM), FDIM ** -0.5, 0.75),
        "filt_w3": normal_values(key_list[10], (LAYERS, FDIM, D), (FDIM * FDIM) ** -0.5, 0.09375),
        "long_bias": normal_values(key_list[11], (LAYERS, D), 1.0, 5.0),
        "w_out": normal_values(key_list[12], (LAYERS, D, D), D ** -0.5, 0.21875),
        "ln2_gain": jnp.clip(1.0 + 0.1 * jax.random.normal(key_list[13], (LAYERS, D), jnp.float32), 0.5, 1.5).astype(jnp.bfloat16),
        "ln2_bias": normal_values(key_list[14], (LAYERS, D), 0.2, 3.0),
        "w_up": normal_values(key_list[15], (LAYERS, D, FF), D ** -0.5, 0.21875),
        "w_down": normal_values(key_list[16], (LAYERS, FF, D), FF ** -0.5, 0.109375),
    }


HIGHEST = lax.Precision.HIGHEST
NORM_EPS = 1e-05
MOD_SHIFT = 0.05

@jax.custom_vjp
def low(v):
    return lax.optimization_barrier(v.astype(jnp.bfloat16)).astype(jnp.float32)

@jax.custom_vjp
def low_back(v):
    return v

def low_keep(v):
    return (low(v), None)

def low_pass(kept, grad):
    return (grad,)

def back_keep(v):
    return (v, None)

def back_low(kept, grad):
    return (low(grad),)
low.defvjp(low_keep, low_pass)
low_back.defvjp(back_keep, back_low)

def matmul(left_side, right_side):
    return jnp.dot(left_side, right_side, precision=HIGHEST, preferred_element_type=jnp.float32)

def position_features(length):
    band_count = (EMB - 1) // 2
    step_index = jnp.arange(length, dtype=jnp.int32).astype(jnp.float32)
    time_grid = step_index / (length - 1)
    base_angle = step_index * (2.0 * math.pi / length)
    band_freq = jnp.linspace(0.0001, band_count - 1, band_count, dtype=jnp.float32)
    phases = base_angle[:, None] * band_freq[None, :]
    return jnp.concatenate([time_grid[:, None], jnp.cos(phases), -jnp.sin(phases)], axis=1)

def decay_table(time_grid, first_chan, channels, model_width):
    fast_rate = math.log(0.01) / 0.3
    slow_rate = math.log(0.01) / 1.5
    chan_index = first_chan + jnp.arange(channels, dtype=jnp.int32).astype(jnp.float32)
    deltas = jnp.abs(fast_rate + (slow_rate - fast_rate) * chan_index / (model_width - 1))
    return jnp.exp(-time_grid * deltas[None, :]) + MOD_SHIFT

def filter_taps(features, weight_one, sine_freq, weight_two, weight_three, envelope):
    first_sine = jnp.sin(sine_freq[0] * matmul(features, weight_one))
    second_sine = jnp.sin(sine_freq[1] * matmul(first_sine, weight_two))
    return matmul(second_sine, weight_three) * envelope

def layer_norm(values_in, gain_vec, bias_vec):
    mean_row = lax.optimization_barrier(jnp.mean(values_in, axis=-1, keepdims=True))
    centred = values_in - mean_row
    variance = lax.optimization_barrier(jnp.mean(centred * centred, axis=-1, keepdims=True))
    return centred * lax.rsqrt(variance + NORM_EPS) * gain_vec + bias_vec

def gelu_tanh(values_in):
    return jax.nn.gelu(values_in, approximate=True)

def causal_conv(series, filter_rows):
    length = series.shape[0]
    spectrum = jnp.fft.rfft(series, n=2 * length, axis=0) * jnp.fft.rfft(filter_rows, n=2 * length, axis=0)
    return jnp.fft.irfft(spectrum, n=2 * length, axis=0)[:length]

def hyena_layer(residual, params, features, envelope):
    gain_one, bias_one, proj_in, kernel, weight_one, sine_freq, weight_two, weight_three, skip_scale, proj_out, gain_two, bias_two, proj_up, proj_down = params
    model_width = residual.shape[1]
    normed = low(layer_norm(residual, gain_one, bias_one))
    projected = low_back(matmul(normed, proj_in))
    padded = jnp.concatenate([jnp.zeros((2, 3 * model_width), jnp.float32), projected], axis=0)
    short_out = kernel[0] * padded[:-2] + kernel[1] * padded[1:-1] + kernel[2] * padded[2:]
    gate_out = short_out[:, :model_width]
    gate_in = short_out[:, model_width:2 * model_width]
    values = short_out[:, 2 * model_width:]
    carried = values * gate_in
    filter_rows = filter_taps(features, weight_one, sine_freq, weight_two, weight_three, envelope)
    long_out = causal_conv(carried, filter_rows) + skip_scale * carried
    gated_rows = low(long_out * gate_out)
    hidden = residual + low_back(matmul(gated_rows, proj_out))
    normed_two = low(layer_norm(hidden, gain_two, bias_two))
    raised = low_back(matmul(normed_two, proj_up))
    active = low(gelu_tanh(raised))
    return hidden + low_back(matmul(active, proj_down))

def network(live_flag, features, envelope, seq_in, *params):
    residual = seq_in
    for layer_index in range(LAYERS):
        residual = hyena_layer(residual, tuple((stored[layer_index] for stored in params)), features, envelope)
    return residual * live_flag

def reference(x_in, cotangent, counts, ln1_gain, ln1_bias, w_in, short_w, filt_w1, filt_freq, filt_w2, filt_w3, long_bias, w_out, ln2_gain, ln2_bias, w_up, w_down):
    weights = tuple((stored.astype(jnp.float32) for stored in (ln1_gain, ln1_bias, w_in, short_w, filt_w1, filt_freq, filt_w2, filt_w3, long_bias, w_out, ln2_gain, ln2_bias, w_up, w_down)))
    micro_count, seq_count, length, model_width = x_in.shape
    features = position_features(length)
    envelope = decay_table(features[:, :1], 0.0, model_width, model_width)
    slot_index = jnp.arange(seq_count, dtype=jnp.int32) % CAP
    group_index = jnp.arange(seq_count, dtype=jnp.int32) // CAP
    live_mask = (slot_index[None, :] < counts[:, group_index]).astype(jnp.float32)
    flat_x = x_in.astype(jnp.float32).reshape(micro_count * seq_count, length, model_width)
    flat_cot = cotangent.astype(jnp.float32).reshape(micro_count * seq_count, length, model_width)
    flat_live = live_mask.reshape(micro_count * seq_count)

    def one_sequence(totals, inputs):
        seq_in, seq_cot, live_flag = inputs
        result, pullback = jax.vjp(partial(network, live_flag, features, envelope), seq_in, *weights)
        gradients = pullback(seq_cot)
        totals = tuple((running + update for running, update in zip(totals, gradients[1:])))
        return (totals, (result, gradients[0]))
    initial = tuple((jnp.zeros_like(stored) for stored in weights))
    totals, (outputs, input_grads) = lax.scan(one_sequence, initial, (flat_x, flat_cot, flat_live))
    return (outputs.reshape(x_in.shape), input_grads.reshape(x_in.shape), totals[0], totals[1], totals[2], totals[3], totals[4], totals[5], totals[6], totals[7], totals[8], totals[9], totals[10], totals[11], totals[12], totals[13])
```

```python
import math

import jax
import jax.numpy as jnp
import numpy as np
from jax import lax
from jax.sharding import PartitionSpec as P

EMB = 33
INNER = 64


HIGHEST = lax.Precision.HIGHEST
NORM_EPS = 1e-05
MOD_SHIFT = 0.05


def passed_along(block, axis, distance):
    devices = range(lax.axis_size(axis))
    route = [(i - distance, i) for i in devices if i - distance in devices]
    return lax.ppermute(block, axis, route)


def for_sending(value):

    def short(part):
        return part.astype(jnp.bfloat16) if part.dtype == jnp.float32 else part

    return jax.tree.map(short, value)


def position_features(length):
    band_count = (EMB - 1) // 2
    step_index = jnp.arange(length, dtype=jnp.int32).astype(jnp.float32)
    time_grid = step_index / (length - 1)
    base_angle = step_index * (2.0 * math.pi / length)
    band_freq = jnp.linspace(0.0001, band_count - 1, band_count, dtype=jnp.float32)
    phases = base_angle[:, None] * band_freq[None, :]
    return jnp.concatenate([time_grid[:, None], jnp.cos(phases), -jnp.sin(phases)], axis=1)


def decay_table(time_grid, first_chan, channels, model_width):
    fast_rate = math.log(0.01) / 0.3
    slow_rate = math.log(0.01) / 1.5
    chan_index = first_chan + jnp.arange(channels, dtype=jnp.int32).astype(jnp.float32)
    deltas = jnp.abs(fast_rate + (slow_rate - fast_rate) * chan_index / (model_width - 1))
    return jnp.exp(-time_grid * deltas[None, :]) + MOD_SHIFT


def filter_taps(features, weight_one, sine_freq, weight_two, weight_three, envelope):
    first_sine = jnp.sin(sine_freq[0] * jnp.dot(features, weight_one, precision=HIGHEST))
    second_sine = jnp.sin(sine_freq[1] * jnp.dot(first_sine, weight_two, precision=HIGHEST))
    return jnp.dot(second_sine, weight_three, precision=HIGHEST) * envelope


def layer_norm(values_in, gain_vec, bias_vec):
    mean_row = jnp.mean(values_in, axis=-1, keepdims=True)
    centred = values_in - mean_row
    variance = jnp.mean(centred * centred, axis=-1, keepdims=True)
    return centred * lax.rsqrt(variance + NORM_EPS) * gain_vec + bias_vec


def gelu_tanh(values_in):
    return jax.nn.gelu(values_in, approximate=True)


def dft_tables(outer_size, inner_size):
    padded_len = outer_size * inner_size
    outer_index = jnp.arange(outer_size, dtype=jnp.int32)
    half_index = jnp.arange(outer_size // 2, dtype=jnp.int32)
    inner_index = jnp.arange(inner_size, dtype=jnp.int32)
    angle_outer = (outer_index[:, None] * half_index[None, :] % outer_size).astype(jnp.float32) * (
        2.0 * math.pi / outer_size
    )
    angle_twist = (outer_index[:, None] * inner_index[None, :] % padded_len).astype(jnp.float32) * (
        2.0 * math.pi / padded_len
    )
    angle_inner = (inner_index[:, None] * inner_index[None, :] % inner_size).astype(jnp.float32) * (
        2.0 * math.pi / inner_size
    )
    return (
        jnp.cos(angle_outer),
        jnp.sin(angle_outer),
        jnp.cos(angle_twist)[None, :, :, None],
        jnp.sin(angle_twist)[None, :, :, None],
        jnp.cos(angle_inner),
        jnp.sin(angle_inner),
    )


def forward_dft(series, tables):
    cos_outer, sin_outer, cos_twist, sin_twist, cos_inner, sin_inner = tables
    outer_size = cos_outer.shape[0]
    inner_size = cos_inner.shape[0]
    seq_count = series.shape[0]
    channels = series.shape[2]
    token_grid = series.reshape(seq_count, outer_size // 2, inner_size, channels)
    first_re = jnp.einsum("ka,sabc->skbc", cos_outer, token_grid, precision=HIGHEST)
    first_im = -jnp.einsum("ka,sabc->skbc", sin_outer, token_grid, precision=HIGHEST)
    twist_re = first_re * cos_twist + first_im * sin_twist
    twist_im = first_im * cos_twist - first_re * sin_twist
    out_re = jnp.einsum("skbc,bj->skjc", twist_re, cos_inner, precision=HIGHEST) + jnp.einsum(
        "skbc,bj->skjc", twist_im, sin_inner, precision=HIGHEST
    )
    out_im = jnp.einsum("skbc,bj->skjc", twist_im, cos_inner, precision=HIGHEST) - jnp.einsum(
        "skbc,bj->skjc", twist_re, sin_inner, precision=HIGHEST
    )
    return (out_re, out_im)


def inverse_dft(spec_re, spec_im, tables):
    cos_outer, sin_outer, cos_twist, sin_twist, cos_inner, sin_inner = tables
    outer_size = cos_outer.shape[0]
    inner_size = cos_inner.shape[0]
    seq_count = spec_re.shape[0]
    channels = spec_re.shape[3]
    back_re = jnp.einsum("skjc,bj->skbc", spec_re, cos_inner, precision=HIGHEST) - jnp.einsum(
        "skjc,bj->skbc", spec_im, sin_inner, precision=HIGHEST
    )
    back_im = jnp.einsum("skjc,bj->skbc", spec_im, cos_inner, precision=HIGHEST) + jnp.einsum(
        "skjc,bj->skbc", spec_re, sin_inner, precision=HIGHEST
    )
    turn_re = back_re * cos_twist - back_im * sin_twist
    turn_im = back_im * cos_twist + back_re * sin_twist
    token_grid = (
        jnp.einsum("skbc,ka->sabc", turn_re, cos_outer, precision=HIGHEST)
        - jnp.einsum("skbc,ka->sabc", turn_im, sin_outer, precision=HIGHEST)
    ) / (outer_size * inner_size)
    return token_grid.reshape(seq_count, outer_size // 2 * inner_size, channels)


def complex_product(left_re, left_im, right_re, right_im):
    return (left_re * right_re - left_im * right_im, left_re * right_im + left_im * right_re)


def add_tree(running, update):
    if running is None:
        return update
    return jax.tree.map(jnp.add, running, update)


def split_positions(
    x_in,
    cotangent,
    counts,
    ln1_gain,
    ln1_bias,
    w_in,
    short_w,
    filt_w1,
    filt_freq,
    filt_w2,
    filt_w3,
    long_bias,
    w_out,
    ln2_gain,
    ln2_bias,
    w_up,
    w_down,
):
    tok_count = lax.axis_size("tok")
    micro_count, cap_size, tok_rows, model_width = x_in.shape
    channels = model_width // tok_count
    first_chan = lax.axis_index("tok") * channels
    layer_count = w_in.shape[0]
    length = tok_rows * tok_count
    tables = dft_tables(2 * length // INNER, INNER)
    features = position_features(length)
    envelope = decay_table(features[:, :1], first_chan.astype(jnp.float32), channels, model_width)
    gain_one = ln1_gain.astype(jnp.float32)
    bias_one = ln1_bias.astype(jnp.float32)
    gain_two = ln2_gain.astype(jnp.float32)
    bias_two = ln2_bias.astype(jnp.float32)
    short_taps = short_w.astype(jnp.float32)
    skip_scale = long_bias.astype(jnp.float32)
    filt_one = filt_w1.astype(jnp.float32)
    filt_sine = filt_freq.astype(jnp.float32)
    filt_two = filt_w2.astype(jnp.float32)
    filt_three = filt_w3.astype(jnp.float32)

    def taps_of(layer_index):

        def taps_fn(weight_one, sine_freq, weight_two, three_slice):
            return filter_taps(features, weight_one, sine_freq, weight_two, three_slice, envelope)

        three_slice = lax.dynamic_slice_in_dim(filt_three[layer_index], first_chan, channels, 1)
        return jax.vjp(
            taps_fn,
            filt_one[layer_index],
            filt_sine[layer_index],
            filt_two[layer_index],
            three_slice,
        )

    taps_spectra = []
    for layer_index in range(layer_count):
        filter_rows, _ = taps_of(layer_index)
        taps_spectra.append(forward_dft(filter_rows[None], tables))

    def backward_layer(grad_rows, kept, layer_index):
        (
            residual,
            normed,
            padded,
            short_out,
            carried,
            long_out,
            gated_rows,
            hidden,
            normed_two,
            raised,
            active,
            kept_signal,
        ) = kept
        down_grad = grad_rows.astype(jnp.bfloat16)
        active_grad = jnp.einsum(
            "std,fd->stf", down_grad, w_down[layer_index], preferred_element_type=jnp.float32
        )
        _, gelu_pull = jax.vjp(gelu_tanh, raised)
        raised_grad = gelu_pull(active_grad)[0].astype(jnp.bfloat16)
        normed_two_grad = jnp.einsum(
            "stf,df->std", raised_grad, w_up[layer_index], preferred_element_type=jnp.float32
        )
        _, second_pull = jax.vjp(layer_norm, hidden, gain_two[layer_index], bias_two[layer_index])
        hidden_part, grad_gain_two, grad_bias_two = second_pull(normed_two_grad)
        hidden_grad = grad_rows + hidden_part
        out_grad = hidden_grad.astype(jnp.bfloat16)
        gated_grad = jnp.einsum(
            "ste,de->std", out_grad, w_out[layer_index], preferred_element_type=jnp.float32
        )
        gate_out = short_out[:, :, :model_width]
        gate_in = short_out[:, :, model_width : 2 * model_width]
        values = short_out[:, :, 2 * model_width :]
        long_grad = gated_grad * gate_out
        gate_out_grad = gated_grad * long_out
        grad_skip = jnp.sum(carried * long_grad, axis=(0, 1))
        spec_re, spec_im = taps_spectra[layer_index]
        upstream_re, upstream_im = forward_dft(
            lax.all_to_all(
                long_grad.astype(jnp.bfloat16), "tok", split_axis=2, concat_axis=1, tiled=True
            ).astype(long_grad.dtype),
            tables,
        )
        back_re, back_im = complex_product(upstream_re, upstream_im, spec_re, -spec_im)
        back_rows = lax.all_to_all(
            for_sending(inverse_dft(back_re, back_im, tables)),
            "tok",
            split_axis=1,
            concat_axis=2,
            tiled=True,
        )
        back_rows, upstream_re, upstream_im = (back_rows, upstream_re, upstream_im)
        signal_re, signal_im = kept_signal
        cross_re = jnp.sum(signal_re * upstream_re + signal_im * upstream_im, axis=0)
        cross_im = jnp.sum(signal_re * upstream_im - signal_im * upstream_re, axis=0)
        carried_grad = back_rows + skip_scale[layer_index] * long_grad
        short_grad = jnp.concatenate(
            [gate_out_grad, carried_grad * values, carried_grad * gate_in], axis=2
        )
        next_rows = passed_along(for_sending(short_grad[:, :2, :]), "tok", -1)
        extended = jnp.concatenate([short_grad, next_rows], axis=1)
        kernel = short_taps[layer_index]
        projected_grad = (
            kernel[2] * short_grad + kernel[1] * extended[:, 1:-1] + kernel[0] * extended[:, 2:]
        ).astype(jnp.bfloat16)
        grad_short = jnp.stack(
            [
                jnp.sum(short_grad * padded[:, tap_index : tap_index + tok_rows], axis=(0, 1))
                for tap_index in range(3)
            ]
        )
        normed_grad = jnp.einsum(
            "ste,de->std", projected_grad, w_in[layer_index], preferred_element_type=jnp.float32
        )
        _, first_pull = jax.vjp(layer_norm, residual, gain_one[layer_index], bias_one[layer_index])
        residual_part, grad_gain_one, grad_bias_one = first_pull(normed_grad)
        left_all = (
            lax.all_gather(down_grad, "tok", axis=1, tiled=True),
            lax.all_gather(gated_rows, "tok", axis=1, tiled=True),
            lax.all_gather(normed_two, "tok", axis=1, tiled=True),
            lax.all_gather(normed, "tok", axis=1, tiled=True),
        )
        right_cols = (
            lax.all_to_all(active, "tok", split_axis=2, concat_axis=1, tiled=True),
            lax.all_to_all(out_grad, "tok", split_axis=2, concat_axis=1, tiled=True),
            lax.all_to_all(raised_grad, "tok", split_axis=2, concat_axis=1, tiled=True),
            lax.all_to_all(projected_grad, "tok", split_axis=2, concat_axis=1, tiled=True),
        )
        grad_down = jnp.einsum(
            "stf,std->fd", right_cols[0], left_all[0], preferred_element_type=jnp.float32
        )
        grad_out = jnp.einsum(
            "std,ste->de", left_all[1], right_cols[1], preferred_element_type=jnp.float32
        )
        grad_up = jnp.einsum(
            "std,stf->df", left_all[2], right_cols[2], preferred_element_type=jnp.float32
        )
        grad_in_proj = jnp.einsum(
            "std,ste->de", left_all[3], right_cols[3], preferred_element_type=jnp.float32
        )
        bundle = (
            (grad_in_proj, grad_out, grad_up, grad_down),
            (grad_gain_one, grad_bias_one, grad_short, grad_skip, grad_gain_two, grad_bias_two),
            (cross_re, cross_im),
        )
        return (hidden_grad + residual_part, bundle)

    def filter_grads(cross_re, cross_im, layer_index):
        taps_grad = inverse_dft(cross_re[None], cross_im[None], tables)[0]
        _, taps_pull = taps_of(layer_index)
        grad_one, grad_sine, grad_two, grad_three = taps_pull(taps_grad)
        grad_three_full = lax.dynamic_update_slice_in_dim(
            jnp.zeros_like(filt_three[layer_index]), grad_three, first_chan, 1
        )
        return (grad_one, grad_sine, grad_two, grad_three_full)

    outputs = []
    input_grads = []
    running = None
    reduced = None
    for micro_index in range(micro_count):
        live_mask = (jnp.arange(cap_size, dtype=jnp.int32) < counts[micro_index, 0]).astype(
            jnp.float32
        )[:, None, None]
        residual = x_in[micro_index].astype(jnp.float32)
        saved = []
        for layer_index in range(layer_count):
            forward_normed = layer_norm(
                residual, gain_one[layer_index], bias_one[layer_index]
            ).astype(jnp.bfloat16)
            projected = jnp.einsum(
                "std,de->ste", forward_normed, w_in[layer_index], preferred_element_type=jnp.float32
            )
            prev_rows = passed_along(projected[:, -2:, :], "tok", 1)
            forward_padded = jnp.concatenate([prev_rows, projected], axis=1)
            forward_kernel = short_taps[layer_index]
            forward_short_out = (
                forward_kernel[0] * forward_padded[:, :-2]
                + forward_kernel[1] * forward_padded[:, 1:-1]
                + forward_kernel[2] * forward_padded[:, 2:]
            )
            forward_gate_out = forward_short_out[:, :, :model_width]
            forward_gate_in = forward_short_out[:, :, model_width : 2 * model_width]
            forward_values = forward_short_out[:, :, 2 * model_width :]
            forward_carried = forward_values * forward_gate_in
            forward_spec_re, forward_spec_im = taps_spectra[layer_index]
            convolve_signal_re, convolve_signal_im = forward_dft(
                lax.all_to_all(forward_carried, "tok", split_axis=2, concat_axis=1, tiled=True),
                tables,
            )
            prod_re, prod_im = complex_product(
                convolve_signal_re, convolve_signal_im, forward_spec_re, forward_spec_im
            )
            convolve_back_rows = lax.all_to_all(
                inverse_dft(prod_re, prod_im, tables),
                "tok",
                split_axis=1,
                concat_axis=2,
                tiled=True,
            )
            results = (convolve_back_rows, convolve_signal_re, convolve_signal_im)
            forward_long_out = results[0] + skip_scale[layer_index] * forward_carried
            forward_gated_rows = (forward_long_out * forward_gate_out).astype(jnp.bfloat16)
            forward_hidden = residual + jnp.einsum(
                "std,de->ste",
                forward_gated_rows,
                w_out[layer_index],
                preferred_element_type=jnp.float32,
            )
            forward_normed_two = layer_norm(
                forward_hidden, gain_two[layer_index], bias_two[layer_index]
            ).astype(jnp.bfloat16)
            forward_raised = jnp.einsum(
                "std,df->stf",
                forward_normed_two,
                w_up[layer_index],
                preferred_element_type=jnp.float32,
            )
            forward_active = gelu_tanh(forward_raised).astype(jnp.bfloat16)
            result = forward_hidden + jnp.einsum(
                "stf,fd->std",
                forward_active,
                w_down[layer_index],
                preferred_element_type=jnp.float32,
            )
            forward_kept = (
                residual,
                forward_normed,
                forward_padded,
                forward_short_out,
                forward_carried,
                forward_long_out,
                forward_gated_rows,
                forward_hidden,
                forward_normed_two,
                forward_raised,
                forward_active,
                results[1:],
            )
            residual = result
            kept = forward_kept
            saved.append(kept)
        outputs.append(residual * live_mask)
        grad_rows = cotangent[micro_index].astype(jnp.float32) * live_mask
        layer_bundles = [None] * layer_count
        for layer_index in reversed(range(layer_count)):
            grad_rows, bundle = backward_layer(grad_rows, saved[layer_index], layer_index)
            layer_bundles[layer_index] = bundle
        input_grads.append(grad_rows)
        running = add_tree(running, layer_bundles)
    mats = [
        jnp.stack([running[layer_index][0][member] for layer_index in range(layer_count)])
        for member in range(4)
    ]
    vecs = [
        jnp.stack([running[layer_index][1][member] for layer_index in range(layer_count)])
        for member in range(6)
    ]
    filter_parts = [
        filter_grads(running[layer_index][2][0], running[layer_index][2][1], layer_index)
        for layer_index in range(layer_count)
    ]
    filt_parts = [
        jnp.stack([filter_parts[layer_index][member] for layer_index in range(layer_count)])
        for member in range(4)
    ]
    mat_done = (
        lax.psum_scatter(
            mats[0].astype(jnp.bfloat16), "seq", scatter_dimension=1, tiled=True
        ).astype(jnp.float32),
        lax.psum_scatter(
            mats[1].astype(jnp.bfloat16), "seq", scatter_dimension=1, tiled=True
        ).astype(jnp.float32),
        lax.psum_scatter(
            mats[2].astype(jnp.bfloat16), "seq", scatter_dimension=1, tiled=True
        ).astype(jnp.float32),
        lax.psum_scatter(
            mats[3].astype(jnp.bfloat16), "seq", scatter_dimension=2, tiled=True
        ).astype(jnp.float32),
    )
    small_done = lax.psum(
        (
            vecs[0],
            vecs[1],
            vecs[2],
            vecs[3],
            vecs[4],
            vecs[5],
            filt_parts[0],
            filt_parts[1],
            filt_parts[2],
            filt_parts[3],
        ),
        ("seq", "tok"),
    )
    reduced = (tuple(mat_done), tuple(small_done))
    mat_done, small_done = reduced
    return (
        jnp.stack(outputs),
        jnp.stack(input_grads),
        small_done[0],
        small_done[1],
        mat_done[0],
        small_done[2],
        small_done[6],
        small_done[7],
        small_done[8],
        small_done[9],
        small_done[3],
        mat_done[1],
        small_done[4],
        small_done[5],
        mat_done[2],
        mat_done[3],
    )


def spectral_table(length):
    k = np.arange(length, dtype=np.int64)[:, None]
    t = np.arange(length, dtype=np.int64)[None, :]
    angle = ((2 * k + 1) * t % (4 * length)).astype(np.float64) * (2.0 * math.pi / (4 * length))
    return np.concatenate([np.cos(angle), -np.sin(angle)], axis=0).astype(jnp.bfloat16)


def mm(left, right):
    return jnp.dot(left, right, preferred_element_type=jnp.float32)


def mm_nt(left, right):
    return lax.dot_general(left, right, (((1,), (1,)), ((), ())), preferred_element_type=jnp.float32)


def mm_tn(left, right):
    return lax.dot_general(left, right, (((0,), (0,)), ((), ())), preferred_element_type=jnp.float32)


def shifted(values, distance):
    rows = values.shape[0]
    zeros = jnp.zeros((abs(distance), values.shape[1]), values.dtype)
    if distance > 0:
        return jnp.concatenate([zeros, values[: rows - distance]], axis=0)
    return jnp.concatenate([values[-distance:], zeros], axis=0)


def whole_sequences(
    x_in, cotangent, counts, ln1_gain, ln1_bias, w_in, short_w, filt_w1, filt_freq, filt_w2, filt_w3, long_bias,
    w_out, ln2_gain, ln2_bias, w_up, w_down,
):
    micro_count, cap_size, tok_rows, width = x_in.shape
    slots = micro_count * cap_size
    layers = w_in.shape[0]
    length = tok_rows * lax.axis_size("tok")
    me = lax.axis_index("tok")

    def gather_mine(block):
        return lax.all_to_all(block.reshape(slots, tok_rows, width), "tok", split_axis=0, concat_axis=1, tiled=True)[0]

    def scatter_back(rows):
        blocks = rows.reshape(slots, tok_rows, width)
        back = lax.all_to_all(blocks, "tok", split_axis=0, concat_axis=0, tiled=True)
        return back.reshape(micro_count, cap_size, tok_rows, width)

    live = (me % cap_size < counts[me // cap_size, 0]).astype(jnp.float32)
    f32 = lambda v: v.astype(jnp.float32)
    bf = lambda v: v.astype(jnp.bfloat16)
    table = jnp.asarray(spectral_table(length))
    table_back = jnp.asarray(spectral_table(length).T.copy())
    features = position_features(length)
    envelope = decay_table(features[:, :1], 0.0, width, width)

    def spectrum(rows):
        both = mm(table, rows)
        return both[:length], both[length:]

    def from_spectrum(re, im):
        return mm(table_back, jnp.concatenate([bf(re), bf(im)], axis=0)) * (1.0 / length)

    def taps_fn(layer):
        def fn(one, sine, two, three):
            return filter_taps(features, one, sine, two, three, envelope)

        return jax.vjp(fn, f32(filt_w1[layer]), f32(filt_freq[layer]), f32(filt_w2[layer]), f32(filt_w3[layer]))

    residual = f32(gather_mine(x_in))
    filters = [taps_fn(layer) for layer in range(layers)]
    spectra = [spectrum(bf(filters[layer][0])) for layer in range(layers)]
    kept = []
    for layer in range(layers):
        g1, b1, g2, b2 = f32(ln1_gain[layer]), f32(ln1_bias[layer]), f32(ln2_gain[layer]), f32(ln2_bias[layer])
        kernel, skip = f32(short_w[layer]), f32(long_bias[layer])
        normed = bf(layer_norm(residual, g1, b1))
        projected = mm(normed, w_in[layer])
        mixed = kernel[0] * shifted(projected, 2) + kernel[1] * shifted(projected, 1) + kernel[2] * projected
        gate_out, gate_in, vals = mixed[:, :width], mixed[:, width : 2 * width], mixed[:, 2 * width :]
        carried = vals * gate_in
        sig_re, sig_im = spectrum(bf(carried))
        tap_re, tap_im = spectra[layer]
        long_out = from_spectrum(*complex_product(sig_re, sig_im, tap_re, tap_im)) + skip * carried
        gated = bf(long_out * gate_out)
        hidden = residual + mm(gated, w_out[layer])
        normed_two = bf(layer_norm(hidden, g2, b2))
        raised = mm(normed_two, w_up[layer])
        active = bf(gelu_tanh(raised))
        result = hidden + mm(active, w_down[layer])
        kept.append((residual, normed, projected, mixed, carried, long_out, gated, hidden, normed_two, raised, active,
                     bf(sig_re), bf(sig_im)))
        residual = result
    out_act = scatter_back(bf(residual * live)).astype(jnp.float32)

    grad = f32(gather_mine(cotangent)) * live
    mats = [None] * layers
    vecs = [None] * layers
    for layer in reversed(range(layers)):
        (residual, normed, projected, mixed, carried, long_out, gated, hidden, normed_two, raised, active, sig_re,
         sig_im) = kept[layer]
        g1, b1, g2, b2 = f32(ln1_gain[layer]), f32(ln1_bias[layer]), f32(ln2_gain[layer]), f32(ln2_bias[layer])
        kernel, skip = f32(short_w[layer]), f32(long_bias[layer])
        gate_out, gate_in, vals = mixed[:, :width], mixed[:, width : 2 * width], mixed[:, 2 * width :]
        down_grad = bf(grad)
        grad_down = mm_tn(active, down_grad)
        _, gelu_pull = jax.vjp(gelu_tanh, raised)
        raised_grad = bf(gelu_pull(mm_nt(down_grad, w_down[layer]))[0])
        grad_up = mm_tn(normed_two, raised_grad)
        _, second_pull = jax.vjp(layer_norm, hidden, g2, b2)
        hidden_part, grad_g2, grad_b2 = second_pull(mm_nt(raised_grad, w_up[layer]))
        hidden_grad = grad + hidden_part
        out_grad = bf(hidden_grad)
        grad_out = mm_tn(gated, out_grad)
        gated_grad = mm_nt(out_grad, w_out[layer])
        long_grad = gated_grad * gate_out
        gate_out_grad = gated_grad * long_out
        grad_skip = jnp.sum(carried * long_grad, axis=0)
        up_re, up_im = spectrum(bf(long_grad))
        tap_re, tap_im = spectra[layer]
        carried_grad = from_spectrum(*complex_product(up_re, up_im, tap_re, -tap_im)) + skip * long_grad
        cross = complex_product(up_re, up_im, f32(sig_re), -f32(sig_im))
        taps_grad = from_spectrum(*cross)
        mixed_grad = jnp.concatenate([gate_out_grad, carried_grad * vals, carried_grad * gate_in], axis=1)
        projected_grad = bf(
            kernel[2] * mixed_grad + kernel[1] * shifted(mixed_grad, -1) + kernel[0] * shifted(mixed_grad, -2)
        )
        grad_short = jnp.stack(
            [jnp.sum(mixed_grad * (shifted(projected, 2 - k) if k < 2 else projected), axis=0) for k in range(3)]
        )
        grad_proj = mm_tn(normed, projected_grad)
        _, first_pull = jax.vjp(layer_norm, residual, g1, b1)
        first_part, grad_g1, grad_b1 = first_pull(mm_nt(projected_grad, w_in[layer]))
        grad = hidden_grad + first_part
        filter_grads = filters[layer][1](taps_grad)
        mats[layer] = (grad_proj, grad_out, grad_up, grad_down)
        vecs[layer] = (grad_g1, grad_b1, grad_short, grad_skip, grad_g2, grad_b2) + tuple(filter_grads)
    grad_in = scatter_back(bf(grad)).astype(jnp.float32)

    def pair_sum(block, dim):
        count = lax.axis_size("seq")
        core = lax.axis_index("seq") % 2
        shape = block.shape
        piece = shape[dim] // count
        split = block.reshape(shape[:dim] + (count // 2, 2, piece) + shape[dim + 1 :])
        mine = lax.dynamic_index_in_dim(split, core, dim + 1, keepdims=False)
        other = lax.dynamic_index_in_dim(split, 1 - core, dim + 1, keepdims=False)
        got = lax.ppermute(other, "seq", [(i, i ^ 1) for i in range(count)])
        return mine + got

    def reduced(block, seq_dim, tok_dim):
        block = bf(block)
        return lax.psum_scatter(
            lax.psum_scatter(block, "tok", scatter_dimension=tok_dim, tiled=True),
            "seq", scatter_dimension=seq_dim, tiled=True,
        ).astype(jnp.float32)

    dims = ((0, 1), (0, 1), (0, 1), (1, 0))
    mat_done = [
        jnp.stack([reduced(mats[layer][m], *dims[m]) for layer in range(layers)]) for m in range(4)
    ]
    small = lax.psum(
        tuple(jnp.stack([vecs[layer][m] for layer in range(layers)]) for m in range(10)), ("seq", "tok")
    )
    return (
        out_act, grad_in, small[0], small[1], mat_done[0], small[2], small[6], small[7], small[8], small[9], small[3],
        mat_done[1], small[4], small[5], mat_done[2], mat_done[3],
    )


def shards(*args):
    micro_count, cap_size = args[0].shape[:2]
    if lax.axis_size("tok") == micro_count * cap_size:
        return whole_sequences(*args)
    return split_positions(*args)


def solution(mesh):
    return jax.shard_map(
        shards,
        mesh=mesh,
        in_specs=(
            P(None, "seq", "tok", None),
            P(None, "seq", "tok", None),
            P(None, "seq"),
            P(),
            P(),
            P(),
            P(),
            P(),
            P(),
            P(),
            P(),
            P(),
            P(),
            P(),
            P(),
            P(),
            P(),
        ),
        out_specs=(
            P(None, "seq", "tok", None),
            P(None, "seq", "tok", None),
            P(),
            P(),
            P(None, "seq", "tok"),
            P(),
            P(),
            P(),
            P(),
            P(),
            P(),
            P(None, "seq", "tok"),
            P(),
            P(),
            P(None, "seq", "tok"),
            P(None, "tok", "seq"),
        ),
        check_vma=False,
    )
```

```python
import math

import jax
import jax.numpy as jnp
import numpy as np
from jax import lax
from jax.experimental import pallas as pl
from jax.experimental.pallas import tpu as pltpu
from jax.sharding import PartitionSpec as P

EMB = 33
INNER = 64


HIGHEST = lax.Precision.HIGHEST
NORM_EPS = 1e-05
MOD_SHIFT = 0.05


def passed_along(block, axis, distance):
    devices = range(lax.axis_size(axis))
    route = [(i - distance, i) for i in devices if i - distance in devices]
    return lax.ppermute(block, axis, route)


def for_sending(value):

    def short(part):
        return part.astype(jnp.bfloat16) if part.dtype == jnp.float32 else part

    return jax.tree.map(short, value)


def position_features(length):
    band_count = (EMB - 1) // 2
    step_index = jnp.arange(length, dtype=jnp.int32).astype(jnp.float32)
    time_grid = step_index / (length - 1)
    base_angle = step_index * (2.0 * math.pi / length)
    band_freq = jnp.linspace(0.0001, band_count - 1, band_count, dtype=jnp.float32)
    phases = base_angle[:, None] * band_freq[None, :]
    return jnp.concatenate([time_grid[:, None], jnp.cos(phases), -jnp.sin(phases)], axis=1)


def decay_table(time_grid, first_chan, channels, model_width):
    fast_rate = math.log(0.01) / 0.3
    slow_rate = math.log(0.01) / 1.5
    chan_index = first_chan + jnp.arange(channels, dtype=jnp.int32).astype(jnp.float32)
    deltas = jnp.abs(fast_rate + (slow_rate - fast_rate) * chan_index / (model_width - 1))
    return jnp.exp(-time_grid * deltas[None, :]) + MOD_SHIFT


def filter_taps(features, weight_one, sine_freq, weight_two, weight_three, envelope):
    first_sine = jnp.sin(sine_freq[0] * jnp.dot(features, weight_one, precision=HIGHEST))
    second_sine = jnp.sin(sine_freq[1] * jnp.dot(first_sine, weight_two, precision=HIGHEST))
    return jnp.dot(second_sine, weight_three, precision=HIGHEST) * envelope


def layer_norm(values_in, gain_vec, bias_vec):
    mean_row = jnp.mean(values_in, axis=-1, keepdims=True)
    centred = values_in - mean_row
    variance = jnp.mean(centred * centred, axis=-1, keepdims=True)
    return centred * lax.rsqrt(variance + NORM_EPS) * gain_vec + bias_vec


def gelu_tanh(values_in):
    return jax.nn.gelu(values_in, approximate=True)


def dft_tables(outer_size, inner_size):
    padded_len = outer_size * inner_size
    outer_index = jnp.arange(outer_size, dtype=jnp.int32)
    half_index = jnp.arange(outer_size // 2, dtype=jnp.int32)
    inner_index = jnp.arange(inner_size, dtype=jnp.int32)
    angle_outer = (outer_index[:, None] * half_index[None, :] % outer_size).astype(jnp.float32) * (
        2.0 * math.pi / outer_size
    )
    angle_twist = (outer_index[:, None] * inner_index[None, :] % padded_len).astype(jnp.float32) * (
        2.0 * math.pi / padded_len
    )
    angle_inner = (inner_index[:, None] * inner_index[None, :] % inner_size).astype(jnp.float32) * (
        2.0 * math.pi / inner_size
    )
    return (
        jnp.cos(angle_outer),
        jnp.sin(angle_outer),
        jnp.cos(angle_twist)[None, :, :, None],
        jnp.sin(angle_twist)[None, :, :, None],
        jnp.cos(angle_inner),
        jnp.sin(angle_inner),
    )


def forward_dft(series, tables):
    cos_outer, sin_outer, cos_twist, sin_twist, cos_inner, sin_inner = tables
    outer_size = cos_outer.shape[0]
    inner_size = cos_inner.shape[0]
    seq_count = series.shape[0]
    channels = series.shape[2]
    token_grid = series.reshape(seq_count, outer_size // 2, inner_size, channels)
    first_re = jnp.einsum("ka,sabc->skbc", cos_outer, token_grid, precision=HIGHEST)
    first_im = -jnp.einsum("ka,sabc->skbc", sin_outer, token_grid, precision=HIGHEST)
    twist_re = first_re * cos_twist + first_im * sin_twist
    twist_im = first_im * cos_twist - first_re * sin_twist
    out_re = jnp.einsum("skbc,bj->skjc", twist_re, cos_inner, precision=HIGHEST) + jnp.einsum(
        "skbc,bj->skjc", twist_im, sin_inner, precision=HIGHEST
    )
    out_im = jnp.einsum("skbc,bj->skjc", twist_im, cos_inner, precision=HIGHEST) - jnp.einsum(
        "skbc,bj->skjc", twist_re, sin_inner, precision=HIGHEST
    )
    return (out_re, out_im)


def inverse_dft(spec_re, spec_im, tables):
    cos_outer, sin_outer, cos_twist, sin_twist, cos_inner, sin_inner = tables
    outer_size = cos_outer.shape[0]
    inner_size = cos_inner.shape[0]
    seq_count = spec_re.shape[0]
    channels = spec_re.shape[3]
    back_re = jnp.einsum("skjc,bj->skbc", spec_re, cos_inner, precision=HIGHEST) - jnp.einsum(
        "skjc,bj->skbc", spec_im, sin_inner, precision=HIGHEST
    )
    back_im = jnp.einsum("skjc,bj->skbc", spec_im, cos_inner, precision=HIGHEST) + jnp.einsum(
        "skjc,bj->skbc", spec_re, sin_inner, precision=HIGHEST
    )
    turn_re = back_re * cos_twist - back_im * sin_twist
    turn_im = back_im * cos_twist + back_re * sin_twist
    token_grid = (
        jnp.einsum("skbc,ka->sabc", turn_re, cos_outer, precision=HIGHEST)
        - jnp.einsum("skbc,ka->sabc", turn_im, sin_outer, precision=HIGHEST)
    ) / (outer_size * inner_size)
    return token_grid.reshape(seq_count, outer_size // 2 * inner_size, channels)


def complex_product(left_re, left_im, right_re, right_im):
    return (left_re * right_re - left_im * right_im, left_re * right_im + left_im * right_re)


def add_tree(running, update):
    if running is None:
        return update
    return jax.tree.map(jnp.add, running, update)


def split_positions(
    x_in,
    cotangent,
    counts,
    ln1_gain,
    ln1_bias,
    w_in,
    short_w,
    filt_w1,
    filt_freq,
    filt_w2,
    filt_w3,
    long_bias,
    w_out,
    ln2_gain,
    ln2_bias,
    w_up,
    w_down,
):
    tok_count = lax.axis_size("tok")
    micro_count, cap_size, tok_rows, model_width = x_in.shape
    channels = model_width // tok_count
    first_chan = lax.axis_index("tok") * channels
    layer_count = w_in.shape[0]
    length = tok_rows * tok_count
    tables = dft_tables(2 * length // INNER, INNER)
    features = position_features(length)
    envelope = decay_table(features[:, :1], first_chan.astype(jnp.float32), channels, model_width)
    gain_one = ln1_gain.astype(jnp.float32)
    bias_one = ln1_bias.astype(jnp.float32)
    gain_two = ln2_gain.astype(jnp.float32)
    bias_two = ln2_bias.astype(jnp.float32)
    short_taps = short_w.astype(jnp.float32)
    skip_scale = long_bias.astype(jnp.float32)
    filt_one = filt_w1.astype(jnp.float32)
    filt_sine = filt_freq.astype(jnp.float32)
    filt_two = filt_w2.astype(jnp.float32)
    filt_three = filt_w3.astype(jnp.float32)

    def taps_of(layer_index):

        def taps_fn(weight_one, sine_freq, weight_two, three_slice):
            return filter_taps(features, weight_one, sine_freq, weight_two, three_slice, envelope)

        three_slice = lax.dynamic_slice_in_dim(filt_three[layer_index], first_chan, channels, 1)
        return jax.vjp(
            taps_fn,
            filt_one[layer_index],
            filt_sine[layer_index],
            filt_two[layer_index],
            three_slice,
        )

    taps_spectra = []
    for layer_index in range(layer_count):
        filter_rows, _ = taps_of(layer_index)
        taps_spectra.append(forward_dft(filter_rows[None], tables))

    def backward_layer(grad_rows, kept, layer_index):
        (
            residual,
            normed,
            padded,
            short_out,
            carried,
            long_out,
            gated_rows,
            hidden,
            normed_two,
            raised,
            active,
            kept_signal,
        ) = kept
        down_grad = grad_rows.astype(jnp.bfloat16)
        active_grad = jnp.einsum(
            "std,fd->stf", down_grad, w_down[layer_index], preferred_element_type=jnp.float32
        )
        _, gelu_pull = jax.vjp(gelu_tanh, raised)
        raised_grad = gelu_pull(active_grad)[0].astype(jnp.bfloat16)
        normed_two_grad = jnp.einsum(
            "stf,df->std", raised_grad, w_up[layer_index], preferred_element_type=jnp.float32
        )
        _, second_pull = jax.vjp(layer_norm, hidden, gain_two[layer_index], bias_two[layer_index])
        hidden_part, grad_gain_two, grad_bias_two = second_pull(normed_two_grad)
        hidden_grad = grad_rows + hidden_part
        out_grad = hidden_grad.astype(jnp.bfloat16)
        gated_grad = jnp.einsum(
            "ste,de->std", out_grad, w_out[layer_index], preferred_element_type=jnp.float32
        )
        gate_out = short_out[:, :, :model_width]
        gate_in = short_out[:, :, model_width : 2 * model_width]
        values = short_out[:, :, 2 * model_width :]
        long_grad = gated_grad * gate_out
        gate_out_grad = gated_grad * long_out
        grad_skip = jnp.sum(carried * long_grad, axis=(0, 1))
        spec_re, spec_im = taps_spectra[layer_index]
        upstream_re, upstream_im = forward_dft(
            lax.all_to_all(
                long_grad.astype(jnp.bfloat16), "tok", split_axis=2, concat_axis=1, tiled=True
            ).astype(long_grad.dtype),
            tables,
        )
        back_re, back_im = complex_product(upstream_re, upstream_im, spec_re, -spec_im)
        back_rows = lax.all_to_all(
            for_sending(inverse_dft(back_re, back_im, tables)),
            "tok",
            split_axis=1,
            concat_axis=2,
            tiled=True,
        )
        back_rows, upstream_re, upstream_im = (back_rows, upstream_re, upstream_im)
        signal_re, signal_im = kept_signal
        cross_re = jnp.sum(signal_re * upstream_re + signal_im * upstream_im, axis=0)
        cross_im = jnp.sum(signal_re * upstream_im - signal_im * upstream_re, axis=0)
        carried_grad = back_rows + skip_scale[layer_index] * long_grad
        short_grad = jnp.concatenate(
            [gate_out_grad, carried_grad * values, carried_grad * gate_in], axis=2
        )
        next_rows = passed_along(for_sending(short_grad[:, :2, :]), "tok", -1)
        extended = jnp.concatenate([short_grad, next_rows], axis=1)
        kernel = short_taps[layer_index]
        projected_grad = (
            kernel[2] * short_grad + kernel[1] * extended[:, 1:-1] + kernel[0] * extended[:, 2:]
        ).astype(jnp.bfloat16)
        grad_short = jnp.stack(
            [
                jnp.sum(short_grad * padded[:, tap_index : tap_index + tok_rows], axis=(0, 1))
                for tap_index in range(3)
            ]
        )
        normed_grad = jnp.einsum(
            "ste,de->std", projected_grad, w_in[layer_index], preferred_element_type=jnp.float32
        )
        _, first_pull = jax.vjp(layer_norm, residual, gain_one[layer_index], bias_one[layer_index])
        residual_part, grad_gain_one, grad_bias_one = first_pull(normed_grad)
        left_all = (
            lax.all_gather(down_grad, "tok", axis=1, tiled=True),
            lax.all_gather(gated_rows, "tok", axis=1, tiled=True),
            lax.all_gather(normed_two, "tok", axis=1, tiled=True),
            lax.all_gather(normed, "tok", axis=1, tiled=True),
        )
        right_cols = (
            lax.all_to_all(active, "tok", split_axis=2, concat_axis=1, tiled=True),
            lax.all_to_all(out_grad, "tok", split_axis=2, concat_axis=1, tiled=True),
            lax.all_to_all(raised_grad, "tok", split_axis=2, concat_axis=1, tiled=True),
            lax.all_to_all(projected_grad, "tok", split_axis=2, concat_axis=1, tiled=True),
        )
        grad_down = jnp.einsum(
            "stf,std->fd", right_cols[0], left_all[0], preferred_element_type=jnp.float32
        )
        grad_out = jnp.einsum(
            "std,ste->de", left_all[1], right_cols[1], preferred_element_type=jnp.float32
        )
        grad_up = jnp.einsum(
            "std,stf->df", left_all[2], right_cols[2], preferred_element_type=jnp.float32
        )
        grad_in_proj = jnp.einsum(
            "std,ste->de", left_all[3], right_cols[3], preferred_element_type=jnp.float32
        )
        bundle = (
            (grad_in_proj, grad_out, grad_up, grad_down),
            (grad_gain_one, grad_bias_one, grad_short, grad_skip, grad_gain_two, grad_bias_two),
            (cross_re, cross_im),
        )
        return (hidden_grad + residual_part, bundle)

    def filter_grads(cross_re, cross_im, layer_index):
        taps_grad = inverse_dft(cross_re[None], cross_im[None], tables)[0]
        _, taps_pull = taps_of(layer_index)
        grad_one, grad_sine, grad_two, grad_three = taps_pull(taps_grad)
        grad_three_full = lax.dynamic_update_slice_in_dim(
            jnp.zeros_like(filt_three[layer_index]), grad_three, first_chan, 1
        )
        return (grad_one, grad_sine, grad_two, grad_three_full)

    outputs = []
    input_grads = []
    running = None
    reduced = None
    for micro_index in range(micro_count):
        live_mask = (jnp.arange(cap_size, dtype=jnp.int32) < counts[micro_index, 0]).astype(
            jnp.float32
        )[:, None, None]
        residual = x_in[micro_index].astype(jnp.float32)
        saved = []
        for layer_index in range(layer_count):
            forward_normed = layer_norm(
                residual, gain_one[layer_index], bias_one[layer_index]
            ).astype(jnp.bfloat16)
            projected = jnp.einsum(
                "std,de->ste", forward_normed, w_in[layer_index], preferred_element_type=jnp.float32
            )
            prev_rows = passed_along(projected[:, -2:, :], "tok", 1)
            forward_padded = jnp.concatenate([prev_rows, projected], axis=1)
            forward_kernel = short_taps[layer_index]
            forward_short_out = (
                forward_kernel[0] * forward_padded[:, :-2]
                + forward_kernel[1] * forward_padded[:, 1:-1]
                + forward_kernel[2] * forward_padded[:, 2:]
            )
            forward_gate_out = forward_short_out[:, :, :model_width]
            forward_gate_in = forward_short_out[:, :, model_width : 2 * model_width]
            forward_values = forward_short_out[:, :, 2 * model_width :]
            forward_carried = forward_values * forward_gate_in
            forward_spec_re, forward_spec_im = taps_spectra[layer_index]
            convolve_signal_re, convolve_signal_im = forward_dft(
                lax.all_to_all(forward_carried, "tok", split_axis=2, concat_axis=1, tiled=True),
                tables,
            )
            prod_re, prod_im = complex_product(
                convolve_signal_re, convolve_signal_im, forward_spec_re, forward_spec_im
            )
            convolve_back_rows = lax.all_to_all(
                inverse_dft(prod_re, prod_im, tables),
                "tok",
                split_axis=1,
                concat_axis=2,
                tiled=True,
            )
            results = (convolve_back_rows, convolve_signal_re, convolve_signal_im)
            forward_long_out = results[0] + skip_scale[layer_index] * forward_carried
            forward_gated_rows = (forward_long_out * forward_gate_out).astype(jnp.bfloat16)
            forward_hidden = residual + jnp.einsum(
                "std,de->ste",
                forward_gated_rows,
                w_out[layer_index],
                preferred_element_type=jnp.float32,
            )
            forward_normed_two = layer_norm(
                forward_hidden, gain_two[layer_index], bias_two[layer_index]
            ).astype(jnp.bfloat16)
            forward_raised = jnp.einsum(
                "std,df->stf",
                forward_normed_two,
                w_up[layer_index],
                preferred_element_type=jnp.float32,
            )
            forward_active = gelu_tanh(forward_raised).astype(jnp.bfloat16)
            result = forward_hidden + jnp.einsum(
                "stf,fd->std",
                forward_active,
                w_down[layer_index],
                preferred_element_type=jnp.float32,
            )
            forward_kept = (
                residual,
                forward_normed,
                forward_padded,
                forward_short_out,
                forward_carried,
                forward_long_out,
                forward_gated_rows,
                forward_hidden,
                forward_normed_two,
                forward_raised,
                forward_active,
                results[1:],
            )
            residual = result
            kept = forward_kept
            saved.append(kept)
        outputs.append(residual * live_mask)
        grad_rows = cotangent[micro_index].astype(jnp.float32) * live_mask
        layer_bundles = [None] * layer_count
        for layer_index in reversed(range(layer_count)):
            grad_rows, bundle = backward_layer(grad_rows, saved[layer_index], layer_index)
            layer_bundles[layer_index] = bundle
        input_grads.append(grad_rows)
        running = add_tree(running, layer_bundles)
    mats = [
        jnp.stack([running[layer_index][0][member] for layer_index in range(layer_count)])
        for member in range(4)
    ]
    vecs = [
        jnp.stack([running[layer_index][1][member] for layer_index in range(layer_count)])
        for member in range(6)
    ]
    filter_parts = [
        filter_grads(running[layer_index][2][0], running[layer_index][2][1], layer_index)
        for layer_index in range(layer_count)
    ]
    filt_parts = [
        jnp.stack([filter_parts[layer_index][member] for layer_index in range(layer_count)])
        for member in range(4)
    ]
    mat_done = (
        lax.psum_scatter(
            mats[0].astype(jnp.bfloat16), "seq", scatter_dimension=1, tiled=True
        ).astype(jnp.float32),
        lax.psum_scatter(
            mats[1].astype(jnp.bfloat16), "seq", scatter_dimension=1, tiled=True
        ).astype(jnp.float32),
        lax.psum_scatter(
            mats[2].astype(jnp.bfloat16), "seq", scatter_dimension=1, tiled=True
        ).astype(jnp.float32),
        lax.psum_scatter(
            mats[3].astype(jnp.bfloat16), "seq", scatter_dimension=2, tiled=True
        ).astype(jnp.float32),
    )
    small_done = lax.psum(
        (
            vecs[0],
            vecs[1],
            vecs[2],
            vecs[3],
            vecs[4],
            vecs[5],
            filt_parts[0],
            filt_parts[1],
            filt_parts[2],
            filt_parts[3],
        ),
        ("seq", "tok"),
    )
    reduced = (tuple(mat_done), tuple(small_done))
    mat_done, small_done = reduced
    return (
        jnp.stack(outputs),
        jnp.stack(input_grads),
        small_done[0],
        small_done[1],
        mat_done[0],
        small_done[2],
        small_done[6],
        small_done[7],
        small_done[8],
        small_done[9],
        small_done[3],
        mat_done[1],
        small_done[4],
        small_done[5],
        mat_done[2],
        mat_done[3],
    )


MIB = 1 << 20


def mm(left, right):
    return jnp.dot(left, right, preferred_element_type=jnp.float32)


def mm_nt(left, right):
    return lax.dot_general(left, right, (((1,), (1,)), ((), ())), preferred_element_type=jnp.float32)


def f32(values):
    return values.astype(jnp.float32)


def bf(values):
    return values.astype(jnp.bfloat16)


def row_shift(values, distance):
    rows = values.shape[0]
    index = lax.broadcasted_iota(jnp.int32, values.shape, 0)
    rolled = pltpu.roll(values, distance % rows, 0)
    kept = index >= distance if distance > 0 else index < rows + distance
    return jnp.where(kept, rolled, 0.0)


def standardised(values):
    mean = jnp.mean(values, axis=-1, keepdims=True)
    centred = values - mean
    scale = lax.rsqrt(jnp.mean(centred * centred, axis=-1, keepdims=True) + NORM_EPS)
    return centred * scale, scale


def norm_backward(values, gain, upstream):
    xh, scale = standardised(values)
    dxh = upstream * gain
    part = scale * (
        dxh - jnp.mean(dxh, axis=-1, keepdims=True) - xh * jnp.mean(dxh * xh, axis=-1, keepdims=True)
    )
    return part, jnp.sum(upstream * xh, axis=0, keepdims=True), jnp.sum(upstream, axis=0, keepdims=True)


def gelu_parts(values):
    slope = math.sqrt(2.0 / math.pi)
    square = values * values
    bent = jnp.tanh(slope * values * (1.0 + 0.044715 * square))
    half = 0.5 * (1.0 + bent)
    inner = slope * (1.0 + (3.0 * 0.044715) * square)
    return values * half, half + 0.5 * values * (1.0 - bent * bent) * inner


def spectral_table(length):
    k = np.arange(length, dtype=np.int64)[:, None]
    t = np.arange(length, dtype=np.int64)[None, :]
    angle = ((2 * k + 1) * t % (4 * length)).astype(np.float64) * (2.0 * math.pi / (4 * length))
    return np.concatenate([np.cos(angle), -np.sin(angle)], axis=0).astype(jnp.bfloat16)


def whole(shape):
    return pl.BlockSpec(shape, lambda j: (0,) * len(shape), pipeline_mode=pl.Buffered(1))


def of_layer(layer, shape):
    return pl.BlockSpec((None,) + shape, lambda j: (layer,) + (0,) * len(shape), pipeline_mode=pl.Buffered(1))


def mixed_chunk(proj, kernel):
    return [
        kernel[p][0:1] * row_shift(proj[p], 2) + kernel[p][1:2] * row_shift(proj[p], 1) + kernel[p][2:3] * proj[p]
        for p in range(3)
    ]


def mixer_forward_body(
    r_ref, gain_ref, bias_ref, w0_ref, w1_ref, w2_ref, k0_ref, k1_ref, k2_ref, table_ref, back_ref, taps_ref, skip_ref,
    wo_ref, hidden_ref, normed_ref, proj_ref, signal_ref, long_ref,
):
    length = r_ref.shape[0]

    @pl.when(pl.program_id(0) == 0)
    def _():
        r = r_ref[...]
        xh, _ = standardised(r)
        normed_ref[...] = bf(xh * f32(gain_ref[...]) + f32(bias_ref[...]))
        hidden_ref[...] = r

    normed = normed_ref[...]
    proj = [mm(normed, w_ref[...]) for w_ref in (w0_ref, w1_ref, w2_ref)]
    for p in range(3):
        proj_ref[p] = bf(proj[p])
    gate_out, gate_in, vals = mixed_chunk(proj, [f32(k_ref[...]) for k_ref in (k0_ref, k1_ref, k2_ref)])
    carried = vals * gate_in
    both = mm(table_ref[...], bf(carried))
    re, im = both[:length], both[length:]
    signal_ref[...] = bf(both)
    tap_re, tap_im = f32(taps_ref[:length]), f32(taps_ref[length:])
    out = mm(back_ref[:, :length], bf(re * tap_re - im * tap_im))
    out += mm(back_ref[:, length:], bf(re * tap_im + im * tap_re))
    long_out = out + f32(skip_ref[...]) * carried
    long_ref[...] = bf(long_out)
    hidden_ref[...] += mm(bf(long_out * gate_out), wo_ref[...])


def mixer_forward(layer, r, gain, bias, w_in, short_w, table, back, taps, skip, w_out):
    length, width = r.shape
    chunk = 256
    steps = width // chunk
    third = lambda p: pl.BlockSpec((None, width, chunk), lambda j: (layer, 0, p * steps + j))
    short = lambda p: pl.BlockSpec((None, 3, chunk), lambda j: (layer, 0, p * steps + j))
    return pl.pallas_call(
        mixer_forward_body,
        grid=(steps,),
        in_specs=[
            whole((length, width)), of_layer(layer, (1, width)), of_layer(layer, (1, width)),
            third(0), third(1), third(2), short(0), short(1), short(2),
            whole((2 * length, length)), whole((length, 2 * length)),
            pl.BlockSpec((2 * length, chunk), lambda j: (0, j)),
            pl.BlockSpec((None, 1, chunk), lambda j: (layer, 0, j)),
            pl.BlockSpec((None, chunk, width), lambda j: (layer, j, 0)),
        ],
        out_specs=[
            whole((length, width)), whole((length, width)),
            pl.BlockSpec((3, length, chunk), lambda j: (0, 0, j)),
            pl.BlockSpec((2 * length, chunk), lambda j: (0, j)),
            pl.BlockSpec((length, chunk), lambda j: (0, j)),
        ],
        out_shape=[
            jax.ShapeDtypeStruct((length, width), jnp.float32),
            jax.ShapeDtypeStruct((length, width), jnp.bfloat16),
            jax.ShapeDtypeStruct((3, length, width), jnp.bfloat16),
            jax.ShapeDtypeStruct((2 * length, width), jnp.bfloat16),
            jax.ShapeDtypeStruct((length, width), jnp.bfloat16),
        ],
        compiler_params=pltpu.CompilerParams(vmem_limit_bytes=60 * MIB),
        cost_estimate=pl.CostEstimate(
            flops=2 * length * width * (4 * width + 4 * length), bytes_accessed=30 * MIB, transcendentals=0
        ),
        name="mixer_forward",
    )(r, gain, bias, w_in, w_in, w_in, short_w, short_w, short_w, table, back, taps, skip, w_out)


def ffn_forward_body(hidden_ref, gain_ref, bias_ref, up_ref, down_ref, r_ref, normed_ref, raised_ref):
    @pl.when(pl.program_id(0) == 0)
    def _():
        hidden = hidden_ref[...]
        xh, _ = standardised(hidden)
        normed_ref[...] = bf(xh * f32(gain_ref[...]) + f32(bias_ref[...]))
        r_ref[...] = hidden

    raised = mm(normed_ref[...], up_ref[...])
    raised_ref[...] = bf(raised)
    r_ref[...] += mm(bf(gelu_parts(raised)[0]), down_ref[...])


def ffn_forward(layer, hidden, gain, bias, w_up, w_down):
    length, width = hidden.shape
    inner = w_up.shape[2]
    chunk = 768
    return pl.pallas_call(
        ffn_forward_body,
        grid=(inner // chunk,),
        in_specs=[
            whole((length, width)), of_layer(layer, (1, width)), of_layer(layer, (1, width)),
            pl.BlockSpec((None, width, chunk), lambda j: (layer, 0, j)),
            pl.BlockSpec((None, chunk, width), lambda j: (layer, j, 0)),
        ],
        out_specs=[
            whole((length, width)), whole((length, width)),
            pl.BlockSpec((length, chunk), lambda j: (0, j)),
        ],
        out_shape=[
            jax.ShapeDtypeStruct((length, width), jnp.float32),
            jax.ShapeDtypeStruct((length, width), jnp.bfloat16),
            jax.ShapeDtypeStruct((length, inner), jnp.bfloat16),
        ],
        compiler_params=pltpu.CompilerParams(vmem_limit_bytes=60 * MIB),
        cost_estimate=pl.CostEstimate(
            flops=4 * length * width * inner, bytes_accessed=26 * MIB, transcendentals=length * inner
        ),
        name="ffn_forward",
    )(hidden, gain, bias, w_up, w_down)


def ffn_backward_body(
    g_ref, hidden_ref, gain_ref, normed_ref, raised_ref, up_ref, down_ref, out_ref, grads_ref, gain_grad_ref,
    bias_grad_ref, g16_ref, g16t_ref, normed_t_ref, total_ref,
):
    j = pl.program_id(0)
    width = g_ref.shape[1]

    @pl.when(j == 0)
    def _():
        g16 = bf(g_ref[...])
        g16_ref[...] = g16
        g16t_ref[...] = g16.T
        normed_t_ref[...] = normed_ref[...].T
        total_ref[...] = jnp.zeros_like(total_ref)

    active, slope = gelu_parts(f32(raised_ref[...]))
    raised_grad = bf(mm_nt(g16_ref[...], down_ref[...]) * slope)
    grads_ref[:, :width] = bf(mm(normed_t_ref[...], raised_grad))
    grads_ref[:, width:] = bf(mm(g16t_ref[...], bf(active)))
    total_ref[...] += mm_nt(raised_grad, up_ref[...])

    @pl.when(j == pl.num_programs(0) - 1)
    def _():
        part, gain_grad, bias_grad = norm_backward(hidden_ref[...], f32(gain_ref[...]), total_ref[...])
        out_ref[...] = g_ref[...] + part
        gain_grad_ref[...] = gain_grad
        bias_grad_ref[...] = bias_grad


def ffn_backward(layer, g, hidden, gain, normed, raised, w_up, w_down):
    length, width = g.shape
    inner = w_up.shape[2]
    chunk = 768
    steps = inner // chunk
    return pl.pallas_call(
        ffn_backward_body,
        grid=(steps,),
        in_specs=[
            whole((length, width)), whole((length, width)), of_layer(layer, (1, width)), whole((length, width)),
            pl.BlockSpec((length, chunk), lambda j: (0, j)),
            pl.BlockSpec((None, width, chunk), lambda j: (layer, 0, j)),
            pl.BlockSpec((None, chunk, width), lambda j: (layer, j, 0)),
        ],
        out_specs=[
            whole((length, width)),
            pl.BlockSpec((None, width, 2 * chunk), lambda j: (j, 0, 0)),
            whole((1, width)), whole((1, width)),
        ],
        out_shape=[
            jax.ShapeDtypeStruct((length, width), jnp.float32),
            jax.ShapeDtypeStruct((steps, width, 2 * chunk), jnp.bfloat16),
            jax.ShapeDtypeStruct((1, width), jnp.float32),
            jax.ShapeDtypeStruct((1, width), jnp.float32),
        ],
        scratch_shapes=[
            pltpu.VMEM((length, width), jnp.bfloat16), pltpu.VMEM((width, length), jnp.bfloat16),
            pltpu.VMEM((width, length), jnp.bfloat16), pltpu.VMEM((length, width), jnp.float32),
        ],
        compiler_params=pltpu.CompilerParams(vmem_limit_bytes=60 * MIB),
        cost_estimate=pl.CostEstimate(
            flops=8 * length * width * inner, bytes_accessed=40 * MIB, transcendentals=length * inner
        ),
        name="ffn_backward",
    )(g, hidden, gain, normed, raised, w_up, w_down)


def mixer_backward_body(
    hg_ref, r_ref, gain_ref, normed_ref, proj_ref, k0_ref, k1_ref, k2_ref, signal_ref, long_ref, taps_ref, skip_ref,
    table_ref, back_ref, wo_ref, w0_ref, w1_ref, w2_ref,
    g_ref, grad_out_ref, grad_in_ref, taps_grad_ref, short_grad_ref, skip_grad_ref, gain_grad_ref, bias_grad_ref,
    og_ref, normed_t_ref, total_ref,
):
    j = pl.program_id(0)
    length = hg_ref.shape[0]

    @pl.when(j == 0)
    def _():
        og_ref[...] = bf(hg_ref[...])
        normed_t_ref[...] = normed_ref[...].T
        total_ref[...] = jnp.zeros_like(total_ref)

    proj = [f32(proj_ref[p]) for p in range(3)]
    kernel = [f32(k_ref[...]) for k_ref in (k0_ref, k1_ref, k2_ref)]
    gate_out, gate_in, vals = mixed_chunk(proj, kernel)
    carried = vals * gate_in
    long_out = f32(long_ref[...])
    skip = f32(skip_ref[...])
    og = og_ref[...]
    grad_out_ref[...] = bf(mm(bf(long_out * gate_out).T, og))
    gated_grad = mm_nt(og, wo_ref[...])
    long_grad = gated_grad * gate_out
    skip_grad_ref[...] = jnp.sum(carried * long_grad, axis=0, keepdims=True)
    both = mm(table_ref[...], bf(long_grad))
    up_re, up_im = both[:length], both[length:]
    tap_re, tap_im = f32(taps_ref[:length]), f32(taps_ref[length:])
    out = mm(back_ref[:, :length], bf(up_re * tap_re + up_im * tap_im))
    out += mm(back_ref[:, length:], bf(up_im * tap_re - up_re * tap_im))
    carried_grad = out + skip * long_grad
    sig_re, sig_im = f32(signal_ref[:length]), f32(signal_ref[length:])
    cross = mm(back_ref[:, :length], bf(up_re * sig_re + up_im * sig_im))
    cross += mm(back_ref[:, length:], bf(up_im * sig_re - up_re * sig_im))
    taps_grad_ref[...] = cross * (1.0 / length)
    for p, part in enumerate((gated_grad * long_out, carried_grad * vals, carried_grad * gate_in)):
        one, two = row_shift(part, -1), row_shift(part, -2)
        projected_grad = bf(kernel[p][2:3] * part + kernel[p][1:2] * one + kernel[p][0:1] * two)
        for tap, moved in enumerate((two, one, part)):
            short_grad_ref[p, tap : tap + 1, :] = jnp.sum(moved * proj[p], axis=0, keepdims=True)
        grad_in_ref[p] = bf(mm(normed_t_ref[...], projected_grad))
        total_ref[...] += mm_nt(projected_grad, (w0_ref, w1_ref, w2_ref)[p][...])

    @pl.when(j == pl.num_programs(0) - 1)
    def _():
        part, gain_grad, bias_grad = norm_backward(r_ref[...], f32(gain_ref[...]), total_ref[...])
        g_ref[...] = hg_ref[...] + part
        gain_grad_ref[...] = gain_grad
        bias_grad_ref[...] = bias_grad


def mixer_backward(layer, hidden_grad, r, gain, normed, proj, short_w, signal, long_out, taps, skip, table, back, w_out, w_in):
    length, width = r.shape
    chunk = 256
    steps = width // chunk
    third = lambda p: pl.BlockSpec((None, width, chunk), lambda j: (layer, 0, p * steps + j))
    short = lambda p: pl.BlockSpec((None, 3, chunk), lambda j: (layer, 0, p * steps + j))
    return pl.pallas_call(
        mixer_backward_body,
        grid=(steps,),
        in_specs=[
            whole((length, width)), whole((length, width)), of_layer(layer, (1, width)), whole((length, width)),
            pl.BlockSpec((3, length, chunk), lambda j: (0, 0, j)),
            short(0), short(1), short(2),
            pl.BlockSpec((2 * length, chunk), lambda j: (0, j)),
            pl.BlockSpec((length, chunk), lambda j: (0, j)),
            pl.BlockSpec((2 * length, chunk), lambda j: (0, j)),
            pl.BlockSpec((None, 1, chunk), lambda j: (layer, 0, j)),
            whole((2 * length, length)), whole((length, 2 * length)),
            pl.BlockSpec((None, chunk, width), lambda j: (layer, j, 0)),
            third(0), third(1), third(2),
        ],
        out_specs=[
            whole((length, width)),
            pl.BlockSpec((chunk, width), lambda j: (j, 0)),
            pl.BlockSpec((3, width, chunk), lambda j: (0, 0, j)),
            pl.BlockSpec((length, chunk), lambda j: (0, j)),
            pl.BlockSpec((3, 3, chunk), lambda j: (0, 0, j)),
            pl.BlockSpec((1, chunk), lambda j: (0, j)),
            whole((1, width)), whole((1, width)),
        ],
        out_shape=[
            jax.ShapeDtypeStruct((length, width), jnp.float32),
            jax.ShapeDtypeStruct((width, width), jnp.bfloat16),
            jax.ShapeDtypeStruct((3, width, width), jnp.bfloat16),
            jax.ShapeDtypeStruct((length, width), jnp.float32),
            jax.ShapeDtypeStruct((3, 3, width), jnp.float32),
            jax.ShapeDtypeStruct((1, width), jnp.float32),
            jax.ShapeDtypeStruct((1, width), jnp.float32),
            jax.ShapeDtypeStruct((1, width), jnp.float32),
        ],
        scratch_shapes=[
            pltpu.VMEM((length, width), jnp.bfloat16), pltpu.VMEM((width, length), jnp.bfloat16),
            pltpu.VMEM((length, width), jnp.float32),
        ],
        compiler_params=pltpu.CompilerParams(vmem_limit_bytes=62 * MIB),
        cost_estimate=pl.CostEstimate(
            flops=2 * length * width * (8 * width + 6 * length), bytes_accessed=50 * MIB, transcendentals=0
        ),
        name="mixer_backward",
    )(hidden_grad, r, gain, normed, proj, short_w, short_w, short_w, signal, long_out, taps, skip, table, back, w_out,
      w_in, w_in, w_in)


def swapped(block, axis, flip):
    return lax.ppermute(block, axis, [(i, i ^ flip) for i in range(lax.axis_size(axis))])


def pick(block, index, dim):
    return lax.dynamic_index_in_dim(block, index, dim, keepdims=False)


def halved(block, axis, flip, bit, dim):
    return pick(block, bit, dim) + swapped(pick(block, 1 - bit, dim), axis, flip)


def reduce_scatter(block):
    toks, seqs, rows, columns = block.shape
    s, t = lax.axis_index("seq"), lax.axis_index("tok")
    z, core, y, x = s // 2, s % 2, t // 2, t % 2
    block = halved(block.reshape(2, 2, seqs // 2, 2, rows, columns), "seq", 1, core, 3)
    left, right = block[..., : columns // 2], block[..., columns // 2 :]
    left = halved(left, "tok", 1, x, 1)
    right = halved(right, "tok", 2, y, 0)
    left = halved(left, "tok", 2, y, 0)
    right = halved(right, "tok", 1, x, 0)
    block = jnp.concatenate([left, right], axis=-1)
    total = f32(pick(block, z, 0))
    for step in range(1, seqs // 2):
        sent = pick(block, (z + step) % (seqs // 2), 0)
        total += f32(lax.ppermute(sent, "seq", [(i, (i + 2 * step) % seqs) for i in range(seqs)]))
    return total


def whole_sequences(
    x_in, cotangent, counts, ln1_gain, ln1_bias, w_in, short_w, filt_w1, filt_freq, filt_w2, filt_w3, long_bias,
    w_out, ln2_gain, ln2_bias, w_up, w_down,
):
    micro_count, cap_size, tok_rows, width = x_in.shape
    slots = micro_count * cap_size
    layers, _, inner = w_up.shape
    toks, seqs = lax.axis_size("tok"), lax.axis_size("seq")
    length = tok_rows * toks
    me = lax.axis_index("tok")

    def gather_mine(block):
        return lax.all_to_all(block.reshape(slots, tok_rows, width), "tok", split_axis=0, concat_axis=1, tiled=True)[0]

    def scatter_back(rows):
        blocks = rows.reshape(slots, tok_rows, width)
        back = lax.all_to_all(blocks, "tok", split_axis=0, concat_axis=0, tiled=True)
        return back.reshape(micro_count, cap_size, tok_rows, width)

    live = (me % cap_size < counts[me // cap_size, 0]).astype(jnp.float32)
    table = jnp.asarray(spectral_table(length))
    table_back = jnp.asarray(np.ascontiguousarray(spectral_table(length).T))
    features = position_features(length)
    envelope = decay_table(features[:, :1], 0.0, width, width)
    rowed = lambda v: v.reshape(layers, 1, v.shape[1])
    g1, b1, g2, b2, skip = (rowed(v) for v in (ln1_gain, ln1_bias, ln2_gain, ln2_bias, long_bias))

    def taps_fn(layer):
        def fn(one, sine, two, three):
            return filter_taps(features, one, sine, two, three, envelope)

        return jax.vjp(fn, f32(filt_w1[layer]), f32(filt_freq[layer]), f32(filt_w2[layer]), f32(filt_w3[layer]))

    start = gather_mine(x_in)
    upstream = gather_mine(cotangent)
    filters = [taps_fn(layer) for layer in range(layers)]
    spectra = [bf(mm(table, bf(filters[layer][0])) * (1.0 / length)) for layer in range(layers)]
    r = f32(start)
    kept = []
    for layer in range(layers):
        hidden, normed, proj, signal, long_out = mixer_forward(
            layer, r, g1, b1, w_in, short_w, table, table_back, spectra[layer], skip, w_out
        )
        result, normed_two, raised = ffn_forward(layer, hidden, g2, b2, w_up, w_down)
        kept.append((r, hidden, normed, proj, signal, long_out, normed_two, raised))
        r = result
    out_act = f32(scatter_back(bf(r * live)))

    grad = f32(upstream) * live
    mats = [None] * layers
    vecs = [None] * layers
    for layer in reversed(range(layers)):
        r, hidden, normed, proj, signal, long_out, normed_two, raised = kept[layer]
        grad, ffn_grads, grad_g2, grad_b2 = ffn_backward(layer, grad, hidden, g2, normed_two, raised, w_up, w_down)
        ffn_done = reduce_scatter(ffn_grads.reshape(toks, seqs, width // seqs, -1))
        grad, grad_out, grad_in_proj, taps_grad, grad_short, grad_skip, grad_g1, grad_b1 = mixer_backward(
            layer, grad, r, g1, normed, proj, short_w, signal, long_out, spectra[layer], skip, table, table_back,
            w_out, w_in,
        )
        in_cols = jnp.swapaxes(grad_in_proj, 0, 1).reshape(width, toks, -1)
        mixer_grads = jnp.concatenate([in_cols, grad_out.reshape(width, toks, -1)], axis=2)
        mixer_done = reduce_scatter(jnp.swapaxes(mixer_grads, 0, 1).reshape(toks, seqs, width // seqs, -1))
        split = in_cols.shape[2]
        mats[layer] = (
            mixer_done[:, :split], mixer_done[:, split:], ffn_done[:, : inner // toks],
            ffn_done[:, inner // toks :].T,
        )
        filter_grads = filters[layer][1](taps_grad)
        short = jnp.swapaxes(grad_short, 0, 1).reshape(3, 3 * width)
        vecs[layer] = (grad_g1[0], grad_b1[0], short, grad_skip[0], grad_g2[0], grad_b2[0]) + tuple(filter_grads)
    grad_in = f32(scatter_back(bf(grad)))
    mat_done = [jnp.stack([mats[layer][m] for layer in range(layers)]) for m in range(4)]
    small = lax.psum(
        tuple(jnp.stack([vecs[layer][m] for layer in range(layers)]) for m in range(10)), ("seq", "tok")
    )
    return (
        out_act, grad_in, small[0], small[1], mat_done[0], small[2], small[6], small[7], small[8], small[9], small[3],
        mat_done[1], small[4], small[5], mat_done[2], mat_done[3],
    )


def shards(*args):
    micro_count, cap_size = args[0].shape[:2]
    if lax.axis_size("tok") == 4 and micro_count * cap_size == 4:
        return whole_sequences(*args)
    return split_positions(*args)


def solution(mesh):
    return jax.shard_map(
        shards,
        mesh=mesh,
        in_specs=(
            P(None, "seq", "tok", None),
            P(None, "seq", "tok", None),
            P(None, "seq"),
            P(),
            P(),
            P(),
            P(),
            P(),
            P(),
            P(),
            P(),
            P(),
            P(),
            P(),
            P(),
            P(),
            P(),
        ),
        out_specs=(
            P(None, "seq", "tok", None),
            P(None, "seq", "tok", None),
            P(),
            P(),
            P(None, "seq", "tok"),
            P(),
            P(),
            P(),
            P(),
            P(),
            P(),
            P(None, "seq", "tok"),
            P(),
            P(),
            P(None, "seq", "tok"),
            P(None, "tok", "seq"),
        ),
        check_vma=False,
    )
```

```python
import math

import jax
import jax.numpy as jnp
import numpy as np
from jax import lax
from jax.experimental import pallas as pl
from jax.experimental.pallas import tpu as pltpu
from jax.sharding import PartitionSpec as P

EMB = 33
INNER = 64


HIGHEST = lax.Precision.HIGHEST
NORM_EPS = 1e-05
MOD_SHIFT = 0.05


def passed_along(block, axis, distance):
    devices = range(lax.axis_size(axis))
    route = [(i - distance, i) for i in devices if i - distance in devices]
    return lax.ppermute(block, axis, route)


def for_sending(value):

    def short(part):
        return part.astype(jnp.bfloat16) if part.dtype == jnp.float32 else part

    return jax.tree.map(short, value)


def position_features(length):
    band_count = (EMB - 1) // 2
    step_index = jnp.arange(length, dtype=jnp.int32).astype(jnp.float32)
    time_grid = step_index / (length - 1)
    base_angle = step_index * (2.0 * math.pi / length)
    band_freq = jnp.linspace(0.0001, band_count - 1, band_count, dtype=jnp.float32)
    phases = base_angle[:, None] * band_freq[None, :]
    return jnp.concatenate([time_grid[:, None], jnp.cos(phases), -jnp.sin(phases)], axis=1)


def decay_table(time_grid, first_chan, channels, model_width):
    fast_rate = math.log(0.01) / 0.3
    slow_rate = math.log(0.01) / 1.5
    chan_index = first_chan + jnp.arange(channels, dtype=jnp.int32).astype(jnp.float32)
    deltas = jnp.abs(fast_rate + (slow_rate - fast_rate) * chan_index / (model_width - 1))
    return jnp.exp(-time_grid * deltas[None, :]) + MOD_SHIFT


def filter_taps(features, weight_one, sine_freq, weight_two, weight_three, envelope):
    first_sine = jnp.sin(sine_freq[0] * jnp.dot(features, weight_one, precision=HIGHEST))
    second_sine = jnp.sin(sine_freq[1] * jnp.dot(first_sine, weight_two, precision=HIGHEST))
    return jnp.dot(second_sine, weight_three, precision=HIGHEST) * envelope


def layer_norm(values_in, gain_vec, bias_vec):
    mean_row = jnp.mean(values_in, axis=-1, keepdims=True)
    centred = values_in - mean_row
    variance = jnp.mean(centred * centred, axis=-1, keepdims=True)
    return centred * lax.rsqrt(variance + NORM_EPS) * gain_vec + bias_vec


def gelu_tanh(values_in):
    return jax.nn.gelu(values_in, approximate=True)


def dft_tables(outer_size, inner_size):
    padded_len = outer_size * inner_size
    outer_index = jnp.arange(outer_size, dtype=jnp.int32)
    half_index = jnp.arange(outer_size // 2, dtype=jnp.int32)
    inner_index = jnp.arange(inner_size, dtype=jnp.int32)
    angle_outer = (outer_index[:, None] * half_index[None, :] % outer_size).astype(jnp.float32) * (
        2.0 * math.pi / outer_size
    )
    angle_twist = (outer_index[:, None] * inner_index[None, :] % padded_len).astype(jnp.float32) * (
        2.0 * math.pi / padded_len
    )
    angle_inner = (inner_index[:, None] * inner_index[None, :] % inner_size).astype(jnp.float32) * (
        2.0 * math.pi / inner_size
    )
    return (
        jnp.cos(angle_outer),
        jnp.sin(angle_outer),
        jnp.cos(angle_twist)[None, :, :, None],
        jnp.sin(angle_twist)[None, :, :, None],
        jnp.cos(angle_inner),
        jnp.sin(angle_inner),
    )


def forward_dft(series, tables):
    cos_outer, sin_outer, cos_twist, sin_twist, cos_inner, sin_inner = tables
    outer_size = cos_outer.shape[0]
    inner_size = cos_inner.shape[0]
    seq_count = series.shape[0]
    channels = series.shape[2]
    token_grid = series.reshape(seq_count, outer_size // 2, inner_size, channels)
    first_re = jnp.einsum("ka,sabc->skbc", cos_outer, token_grid, precision=HIGHEST)
    first_im = -jnp.einsum("ka,sabc->skbc", sin_outer, token_grid, precision=HIGHEST)
    twist_re = first_re * cos_twist + first_im * sin_twist
    twist_im = first_im * cos_twist - first_re * sin_twist
    out_re = jnp.einsum("skbc,bj->skjc", twist_re, cos_inner, precision=HIGHEST) + jnp.einsum(
        "skbc,bj->skjc", twist_im, sin_inner, precision=HIGHEST
    )
    out_im = jnp.einsum("skbc,bj->skjc", twist_im, cos_inner, precision=HIGHEST) - jnp.einsum(
        "skbc,bj->skjc", twist_re, sin_inner, precision=HIGHEST
    )
    return (out_re, out_im)


def inverse_dft(spec_re, spec_im, tables):
    cos_outer, sin_outer, cos_twist, sin_twist, cos_inner, sin_inner = tables
    outer_size = cos_outer.shape[0]
    inner_size = cos_inner.shape[0]
    seq_count = spec_re.shape[0]
    channels = spec_re.shape[3]
    back_re = jnp.einsum("skjc,bj->skbc", spec_re, cos_inner, precision=HIGHEST) - jnp.einsum(
        "skjc,bj->skbc", spec_im, sin_inner, precision=HIGHEST
    )
    back_im = jnp.einsum("skjc,bj->skbc", spec_im, cos_inner, precision=HIGHEST) + jnp.einsum(
        "skjc,bj->skbc", spec_re, sin_inner, precision=HIGHEST
    )
    turn_re = back_re * cos_twist - back_im * sin_twist
    turn_im = back_im * cos_twist + back_re * sin_twist
    token_grid = (
        jnp.einsum("skbc,ka->sabc", turn_re, cos_outer, precision=HIGHEST)
        - jnp.einsum("skbc,ka->sabc", turn_im, sin_outer, precision=HIGHEST)
    ) / (outer_size * inner_size)
    return token_grid.reshape(seq_count, outer_size // 2 * inner_size, channels)


def complex_product(left_re, left_im, right_re, right_im):
    return (left_re * right_re - left_im * right_im, left_re * right_im + left_im * right_re)


def add_tree(running, update):
    if running is None:
        return update
    return jax.tree.map(jnp.add, running, update)


def split_positions(
    x_in,
    cotangent,
    counts,
    ln1_gain,
    ln1_bias,
    w_in,
    short_w,
    filt_w1,
    filt_freq,
    filt_w2,
    filt_w3,
    long_bias,
    w_out,
    ln2_gain,
    ln2_bias,
    w_up,
    w_down,
):
    tok_count = lax.axis_size("tok")
    micro_count, cap_size, tok_rows, model_width = x_in.shape
    channels = model_width // tok_count
    first_chan = lax.axis_index("tok") * channels
    layer_count = w_in.shape[0]
    length = tok_rows * tok_count
    tables = dft_tables(2 * length // INNER, INNER)
    features = position_features(length)
    envelope = decay_table(features[:, :1], first_chan.astype(jnp.float32), channels, model_width)
    gain_one = ln1_gain.astype(jnp.float32)
    bias_one = ln1_bias.astype(jnp.float32)
    gain_two = ln2_gain.astype(jnp.float32)
    bias_two = ln2_bias.astype(jnp.float32)
    short_taps = short_w.astype(jnp.float32)
    skip_scale = long_bias.astype(jnp.float32)
    filt_one = filt_w1.astype(jnp.float32)
    filt_sine = filt_freq.astype(jnp.float32)
    filt_two = filt_w2.astype(jnp.float32)
    filt_three = filt_w3.astype(jnp.float32)

    def taps_of(layer_index):

        def taps_fn(weight_one, sine_freq, weight_two, three_slice):
            return filter_taps(features, weight_one, sine_freq, weight_two, three_slice, envelope)

        three_slice = lax.dynamic_slice_in_dim(filt_three[layer_index], first_chan, channels, 1)
        return jax.vjp(
            taps_fn,
            filt_one[layer_index],
            filt_sine[layer_index],
            filt_two[layer_index],
            three_slice,
        )

    taps_spectra = []
    for layer_index in range(layer_count):
        filter_rows, _ = taps_of(layer_index)
        taps_spectra.append(forward_dft(filter_rows[None], tables))

    def backward_layer(grad_rows, kept, layer_index):
        (
            residual,
            normed,
            padded,
            short_out,
            carried,
            long_out,
            gated_rows,
            hidden,
            normed_two,
            raised,
            active,
            kept_signal,
        ) = kept
        down_grad = grad_rows.astype(jnp.bfloat16)
        active_grad = jnp.einsum(
            "std,fd->stf", down_grad, w_down[layer_index], preferred_element_type=jnp.float32
        )
        _, gelu_pull = jax.vjp(gelu_tanh, raised)
        raised_grad = gelu_pull(active_grad)[0].astype(jnp.bfloat16)
        normed_two_grad = jnp.einsum(
            "stf,df->std", raised_grad, w_up[layer_index], preferred_element_type=jnp.float32
        )
        _, second_pull = jax.vjp(layer_norm, hidden, gain_two[layer_index], bias_two[layer_index])
        hidden_part, grad_gain_two, grad_bias_two = second_pull(normed_two_grad)
        hidden_grad = grad_rows + hidden_part
        out_grad = hidden_grad.astype(jnp.bfloat16)
        gated_grad = jnp.einsum(
            "ste,de->std", out_grad, w_out[layer_index], preferred_element_type=jnp.float32
        )
        gate_out = short_out[:, :, :model_width]
        gate_in = short_out[:, :, model_width : 2 * model_width]
        values = short_out[:, :, 2 * model_width :]
        long_grad = gated_grad * gate_out
        gate_out_grad = gated_grad * long_out
        grad_skip = jnp.sum(carried * long_grad, axis=(0, 1))
        spec_re, spec_im = taps_spectra[layer_index]
        upstream_re, upstream_im = forward_dft(
            lax.all_to_all(
                long_grad.astype(jnp.bfloat16), "tok", split_axis=2, concat_axis=1, tiled=True
            ).astype(long_grad.dtype),
            tables,
        )
        back_re, back_im = complex_product(upstream_re, upstream_im, spec_re, -spec_im)
        back_rows = lax.all_to_all(
            for_sending(inverse_dft(back_re, back_im, tables)),
            "tok",
            split_axis=1,
            concat_axis=2,
            tiled=True,
        )
        back_rows, upstream_re, upstream_im = (back_rows, upstream_re, upstream_im)
        signal_re, signal_im = kept_signal
        cross_re = jnp.sum(signal_re * upstream_re + signal_im * upstream_im, axis=0)
        cross_im = jnp.sum(signal_re * upstream_im - signal_im * upstream_re, axis=0)
        carried_grad = back_rows + skip_scale[layer_index] * long_grad
        short_grad = jnp.concatenate(
            [gate_out_grad, carried_grad * values, carried_grad * gate_in], axis=2
        )
        next_rows = passed_along(for_sending(short_grad[:, :2, :]), "tok", -1)
        extended = jnp.concatenate([short_grad, next_rows], axis=1)
        kernel = short_taps[layer_index]
        projected_grad = (
            kernel[2] * short_grad + kernel[1] * extended[:, 1:-1] + kernel[0] * extended[:, 2:]
        ).astype(jnp.bfloat16)
        grad_short = jnp.stack(
            [
                jnp.sum(short_grad * padded[:, tap_index : tap_index + tok_rows], axis=(0, 1))
                for tap_index in range(3)
            ]
        )
        normed_grad = jnp.einsum(
            "ste,de->std", projected_grad, w_in[layer_index], preferred_element_type=jnp.float32
        )
        _, first_pull = jax.vjp(layer_norm, residual, gain_one[layer_index], bias_one[layer_index])
        residual_part, grad_gain_one, grad_bias_one = first_pull(normed_grad)
        left_all = (
            lax.all_gather(down_grad, "tok", axis=1, tiled=True),
            lax.all_gather(gated_rows, "tok", axis=1, tiled=True),
            lax.all_gather(normed_two, "tok", axis=1, tiled=True),
            lax.all_gather(normed, "tok", axis=1, tiled=True),
        )
        right_cols = (
            lax.all_to_all(active, "tok", split_axis=2, concat_axis=1, tiled=True),
            lax.all_to_all(out_grad, "tok", split_axis=2, concat_axis=1, tiled=True),
            lax.all_to_all(raised_grad, "tok", split_axis=2, concat_axis=1, tiled=True),
            lax.all_to_all(projected_grad, "tok", split_axis=2, concat_axis=1, tiled=True),
        )
        grad_down = jnp.einsum(
            "stf,std->fd", right_cols[0], left_all[0], preferred_element_type=jnp.float32
        )
        grad_out = jnp.einsum(
            "std,ste->de", left_all[1], right_cols[1], preferred_element_type=jnp.float32
        )
        grad_up = jnp.einsum(
            "std,stf->df", left_all[2], right_cols[2], preferred_element_type=jnp.float32
        )
        grad_in_proj = jnp.einsum(
            "std,ste->de", left_all[3], right_cols[3], preferred_element_type=jnp.float32
        )
        bundle = (
            (grad_in_proj, grad_out, grad_up, grad_down),
            (grad_gain_one, grad_bias_one, grad_short, grad_skip, grad_gain_two, grad_bias_two),
            (cross_re, cross_im),
        )
        return (hidden_grad + residual_part, bundle)

    def filter_grads(cross_re, cross_im, layer_index):
        taps_grad = inverse_dft(cross_re[None], cross_im[None], tables)[0]
        _, taps_pull = taps_of(layer_index)
        grad_one, grad_sine, grad_two, grad_three = taps_pull(taps_grad)
        grad_three_full = lax.dynamic_update_slice_in_dim(
            jnp.zeros_like(filt_three[layer_index]), grad_three, first_chan, 1
        )
        return (grad_one, grad_sine, grad_two, grad_three_full)

    outputs = []
    input_grads = []
    running = None
    reduced = None
    for micro_index in range(micro_count):
        live_mask = (jnp.arange(cap_size, dtype=jnp.int32) < counts[micro_index, 0]).astype(
            jnp.float32
        )[:, None, None]
        residual = x_in[micro_index].astype(jnp.float32)
        saved = []
        for layer_index in range(layer_count):
            forward_normed = layer_norm(
                residual, gain_one[layer_index], bias_one[layer_index]
            ).astype(jnp.bfloat16)
            projected = jnp.einsum(
                "std,de->ste", forward_normed, w_in[layer_index], preferred_element_type=jnp.float32
            )
            prev_rows = passed_along(projected[:, -2:, :], "tok", 1)
            forward_padded = jnp.concatenate([prev_rows, projected], axis=1)
            forward_kernel = short_taps[layer_index]
            forward_short_out = (
                forward_kernel[0] * forward_padded[:, :-2]
                + forward_kernel[1] * forward_padded[:, 1:-1]
                + forward_kernel[2] * forward_padded[:, 2:]
            )
            forward_gate_out = forward_short_out[:, :, :model_width]
            forward_gate_in = forward_short_out[:, :, model_width : 2 * model_width]
            forward_values = forward_short_out[:, :, 2 * model_width :]
            forward_carried = forward_values * forward_gate_in
            forward_spec_re, forward_spec_im = taps_spectra[layer_index]
            convolve_signal_re, convolve_signal_im = forward_dft(
                lax.all_to_all(forward_carried, "tok", split_axis=2, concat_axis=1, tiled=True),
                tables,
            )
            prod_re, prod_im = complex_product(
                convolve_signal_re, convolve_signal_im, forward_spec_re, forward_spec_im
            )
            convolve_back_rows = lax.all_to_all(
                inverse_dft(prod_re, prod_im, tables),
                "tok",
                split_axis=1,
                concat_axis=2,
                tiled=True,
            )
            results = (convolve_back_rows, convolve_signal_re, convolve_signal_im)
            forward_long_out = results[0] + skip_scale[layer_index] * forward_carried
            forward_gated_rows = (forward_long_out * forward_gate_out).astype(jnp.bfloat16)
            forward_hidden = residual + jnp.einsum(
                "std,de->ste",
                forward_gated_rows,
                w_out[layer_index],
                preferred_element_type=jnp.float32,
            )
            forward_normed_two = layer_norm(
                forward_hidden, gain_two[layer_index], bias_two[layer_index]
            ).astype(jnp.bfloat16)
            forward_raised = jnp.einsum(
                "std,df->stf",
                forward_normed_two,
                w_up[layer_index],
                preferred_element_type=jnp.float32,
            )
            forward_active = gelu_tanh(forward_raised).astype(jnp.bfloat16)
            result = forward_hidden + jnp.einsum(
                "stf,fd->std",
                forward_active,
                w_down[layer_index],
                preferred_element_type=jnp.float32,
            )
            forward_kept = (
                residual,
                forward_normed,
                forward_padded,
                forward_short_out,
                forward_carried,
                forward_long_out,
                forward_gated_rows,
                forward_hidden,
                forward_normed_two,
                forward_raised,
                forward_active,
                results[1:],
            )
            residual = result
            kept = forward_kept
            saved.append(kept)
        outputs.append(residual * live_mask)
        grad_rows = cotangent[micro_index].astype(jnp.float32) * live_mask
        layer_bundles = [None] * layer_count
        for layer_index in reversed(range(layer_count)):
            grad_rows, bundle = backward_layer(grad_rows, saved[layer_index], layer_index)
            layer_bundles[layer_index] = bundle
        input_grads.append(grad_rows)
        running = add_tree(running, layer_bundles)
    mats = [
        jnp.stack([running[layer_index][0][member] for layer_index in range(layer_count)])
        for member in range(4)
    ]
    vecs = [
        jnp.stack([running[layer_index][1][member] for layer_index in range(layer_count)])
        for member in range(6)
    ]
    filter_parts = [
        filter_grads(running[layer_index][2][0], running[layer_index][2][1], layer_index)
        for layer_index in range(layer_count)
    ]
    filt_parts = [
        jnp.stack([filter_parts[layer_index][member] for layer_index in range(layer_count)])
        for member in range(4)
    ]
    mat_done = (
        lax.psum_scatter(
            mats[0].astype(jnp.bfloat16), "seq", scatter_dimension=1, tiled=True
        ).astype(jnp.float32),
        lax.psum_scatter(
            mats[1].astype(jnp.bfloat16), "seq", scatter_dimension=1, tiled=True
        ).astype(jnp.float32),
        lax.psum_scatter(
            mats[2].astype(jnp.bfloat16), "seq", scatter_dimension=1, tiled=True
        ).astype(jnp.float32),
        lax.psum_scatter(
            mats[3].astype(jnp.bfloat16), "seq", scatter_dimension=2, tiled=True
        ).astype(jnp.float32),
    )
    small_done = lax.psum(
        (
            vecs[0],
            vecs[1],
            vecs[2],
            vecs[3],
            vecs[4],
            vecs[5],
            filt_parts[0],
            filt_parts[1],
            filt_parts[2],
            filt_parts[3],
        ),
        ("seq", "tok"),
    )
    reduced = (tuple(mat_done), tuple(small_done))
    mat_done, small_done = reduced
    return (
        jnp.stack(outputs),
        jnp.stack(input_grads),
        small_done[0],
        small_done[1],
        mat_done[0],
        small_done[2],
        small_done[6],
        small_done[7],
        small_done[8],
        small_done[9],
        small_done[3],
        mat_done[1],
        small_done[4],
        small_done[5],
        mat_done[2],
        mat_done[3],
    )


MIB = 1 << 20
MESH = pl.DeviceIdType.MESH


def mm(left, right):
    return jnp.dot(left, right, preferred_element_type=jnp.float32)


def mm_nt(left, right):
    return lax.dot_general(left, right, (((1,), (1,)), ((), ())), preferred_element_type=jnp.float32)


def mm_tn(left, right):
    return lax.dot_general(left, right, (((0,), (0,)), ((), ())), preferred_element_type=jnp.float32)


def f32(values):
    return values.astype(jnp.float32)


def bf(values):
    return values.astype(jnp.bfloat16)


def row_shift(values, distance):
    rows = values.shape[0]
    index = lax.broadcasted_iota(jnp.int32, values.shape, 0)
    rolled = pltpu.roll(values, distance % rows, 0)
    kept = index >= distance if distance > 0 else index < rows + distance
    return jnp.where(kept, rolled, 0.0)


def standardised(values):
    mean = jnp.mean(values, axis=-1, keepdims=True)
    centred = values - mean
    scale = lax.rsqrt(jnp.mean(centred * centred, axis=-1, keepdims=True) + NORM_EPS)
    return centred * scale, scale


def norm_backward(values, gain, upstream):
    xh, scale = standardised(values)
    dxh = upstream * gain
    part = scale * (
        dxh - jnp.mean(dxh, axis=-1, keepdims=True) - xh * jnp.mean(dxh * xh, axis=-1, keepdims=True)
    )
    return part, jnp.sum(upstream * xh, axis=0, keepdims=True), jnp.sum(upstream, axis=0, keepdims=True)


def gelu_parts(values):
    slope = math.sqrt(2.0 / math.pi)
    square = values * values
    bent = jnp.tanh(slope * values * (1.0 + 0.044715 * square))
    half = 0.5 * (1.0 + bent)
    inner = slope * (1.0 + (3.0 * 0.044715) * square)
    return values * half, half + 0.5 * values * (1.0 - bent * bent) * inner


def spectral_table(length):
    k = np.arange(length, dtype=np.int64)[:, None]
    t = np.arange(length, dtype=np.int64)[None, :]
    angle = ((2 * k + 1) * t % (4 * length)).astype(np.float64) * (2.0 * math.pi / (4 * length))
    return np.concatenate([np.cos(angle), -np.sin(angle)], axis=0).astype(jnp.bfloat16)


def whole(shape):
    return pl.BlockSpec(shape, lambda j: (0,) * len(shape), pipeline_mode=pl.Buffered(1))


def of_layer(layer, shape):
    return pl.BlockSpec((None,) + shape, lambda j: (layer,) + (0,) * len(shape), pipeline_mode=pl.Buffered(1))


ANY = pl.BlockSpec(memory_space=pl.ANY)


def sds(shape, kind):
    return jax.ShapeDtypeStruct(shape, kind)


class Place:
    def __init__(self):
        s, t = lax.axis_index("seq"), lax.axis_index("tok")
        self.depth = lax.axis_size("seq") // 2
        self.z, self.core, self.y, self.x = s // 2, s % 2, t // 2, t % 2
        self.s, self.t = s, t
        self.over_core = (2 * self.z + 1 - self.core, t)
        self.over_x = (s, 2 * self.y + 1 - self.x)
        self.over_y = (s, 2 * (1 - self.y) + self.x)
        self.over_z = [(2 * ((self.z + d) % self.depth) + self.core, t) for d in range(1, self.depth)]
        self.from_z = [(2 * ((self.z + self.depth - d) % self.depth) + self.core, t) for d in range(1, self.depth)]


def greet(partners):
    barrier = pltpu.get_barrier_semaphore()
    for partner in partners:
        pl.semaphore_signal(barrier, inc=1, device_id=partner, device_id_type=MESH)
    pl.semaphore_wait(barrier, len(partners))


def remote(source, target, sent, landed, device):
    return pltpu.make_async_remote_copy(
        src_ref=source, dst_ref=target, send_sem=sent, recv_sem=landed, device_id=device, device_id_type=MESH
    )


def other_first(place, s, piece):
    half = place.depth * piece
    mine = (s % 2 + place.core + 1) % 2
    return pl.multiple_of(mine * half + (s // 2) * piece, 16)


def store_rows(place, target, values):
    piece = values.shape[0] // (2 * place.depth)
    for s in range(2 * place.depth):
        target[pl.ds(other_first(place, s, piece), piece), :] = values[s * piece : (s + 1) * piece]


def mixed_chunk(proj, kernel):
    return [
        kernel[p][0:1] * row_shift(proj[p], 2) + kernel[p][1:2] * row_shift(proj[p], 1) + kernel[p][2:3] * proj[p]
        for p in range(3)
    ]


def mixer_forward_body(
    r_ref, gain_ref, bias_ref, w0_ref, w1_ref, w2_ref, k0_ref, k1_ref, k2_ref, table_ref, taps_ref, skip_ref,
    wo_ref, hidden_ref, normed_ref, proj_ref, signal_ref, long_ref,
):
    length = r_ref.shape[0]

    @pl.when(pl.program_id(0) == 0)
    def _():
        r = r_ref[...]
        xh, _ = standardised(r)
        normed_ref[...] = bf(xh * f32(gain_ref[...]) + f32(bias_ref[...]))
        hidden_ref[...] = r

    normed = normed_ref[...]
    proj = [mm(normed, w_ref[...]) for w_ref in (w0_ref, w1_ref, w2_ref)]
    for p in range(3):
        proj_ref[p] = bf(proj[p])
    gate_out, gate_in, vals = mixed_chunk(proj, [f32(k_ref[...]) for k_ref in (k0_ref, k1_ref, k2_ref)])
    carried = vals * gate_in
    both = mm(table_ref[...], bf(carried))
    re, im = both[:length], both[length:]
    signal_ref[...] = bf(both)
    tap_re, tap_im = f32(taps_ref[:length]), f32(taps_ref[length:])
    out = mm_tn(table_ref[:length], bf(re * tap_re - im * tap_im))
    out += mm_tn(table_ref[length:], bf(re * tap_im + im * tap_re))
    long_out = out + f32(skip_ref[...]) * carried
    long_ref[...] = bf(long_out)
    hidden_ref[...] += mm(bf(long_out * gate_out), wo_ref[...])


def mixer_forward(layer, r, gain, bias, w_in, short_w, table, taps, skip, w_out):
    length, width = r.shape
    chunk = 256
    steps = width // chunk
    third = lambda p: pl.BlockSpec((None, width, chunk), lambda j: (layer, 0, p * steps + j))
    short = lambda p: pl.BlockSpec((None, 3, chunk), lambda j: (layer, 0, p * steps + j))
    return pl.pallas_call(
        mixer_forward_body,
        grid=(steps,),
        in_specs=[
            whole((length, width)), of_layer(layer, (1, width)), of_layer(layer, (1, width)),
            third(0), third(1), third(2), short(0), short(1), short(2),
            whole((2 * length, length)),
            pl.BlockSpec((2 * length, chunk), lambda j: (0, j)),
            pl.BlockSpec((None, 1, chunk), lambda j: (layer, 0, j)),
            pl.BlockSpec((None, chunk, width), lambda j: (layer, j, 0)),
        ],
        out_specs=[
            whole((length, width)), whole((length, width)),
            pl.BlockSpec((3, length, chunk), lambda j: (0, 0, j)),
            pl.BlockSpec((2 * length, chunk), lambda j: (0, j)),
            pl.BlockSpec((length, chunk), lambda j: (0, j)),
        ],
        out_shape=[
            sds((length, width), jnp.float32), sds((length, width), jnp.bfloat16),
            sds((3, length, width), jnp.bfloat16), sds((2 * length, width), jnp.bfloat16),
            sds((length, width), jnp.bfloat16),
        ],
        compiler_params=pltpu.CompilerParams(vmem_limit_bytes=60 * MIB),
        cost_estimate=pl.CostEstimate(
            flops=2 * length * width * (4 * width + 4 * length), bytes_accessed=30 * MIB, transcendentals=0
        ),
        name="mixer_forward",
    )(r, gain, bias, w_in, w_in, w_in, short_w, short_w, short_w, table, taps, skip, w_out)


def ffn_forward_body(hidden_ref, gain_ref, bias_ref, up_ref, down_ref, r_ref, normed_ref, raised_ref):
    @pl.when(pl.program_id(0) == 0)
    def _():
        hidden = hidden_ref[...]
        xh, _ = standardised(hidden)
        normed_ref[...] = bf(xh * f32(gain_ref[...]) + f32(bias_ref[...]))
        r_ref[...] = hidden

    raised = mm(normed_ref[...], up_ref[...])
    raised_ref[...] = bf(raised)
    r_ref[...] += mm(bf(gelu_parts(raised)[0]), down_ref[...])


def ffn_forward(layer, hidden, gain, bias, w_up, w_down):
    length, width = hidden.shape
    inner = w_up.shape[2]
    chunk = inner // 4
    return pl.pallas_call(
        ffn_forward_body,
        grid=(inner // chunk,),
        in_specs=[
            whole((length, width)), of_layer(layer, (1, width)), of_layer(layer, (1, width)),
            pl.BlockSpec((None, width, chunk), lambda j: (layer, 0, j)),
            pl.BlockSpec((None, chunk, width), lambda j: (layer, j, 0)),
        ],
        out_specs=[
            whole((length, width)), whole((length, width)), pl.BlockSpec((length, chunk), lambda j: (0, j)),
        ],
        out_shape=[
            sds((length, width), jnp.float32), sds((length, width), jnp.bfloat16),
            sds((length, inner), jnp.bfloat16),
        ],
        compiler_params=pltpu.CompilerParams(vmem_limit_bytes=60 * MIB),
        cost_estimate=pl.CostEstimate(
            flops=4 * length * width * inner, bytes_accessed=26 * MIB, transcendentals=length * inner
        ),
        name="ffn_forward",
    )(hidden, gain, bias, w_up, w_down)


def ffn_backward_body(carry, *refs):
    refs = list(refs)
    take = lambda n: [refs.pop(0) for _ in range(n)]
    g_ref, hidden_ref, gain_ref, normed_ref, raised_ref, up_ref, down_ref = take(7)
    zin_ref, min_ref = take(2) if carry else (None, None)
    out_ref, gain_grad_ref, bias_grad_ref, c_out, w_out = take(5)
    zfin_ref, wmix_ref = take(2) if carry else (None, None)
    g16_ref, g16t_ref, normed_t_ref, give, got, c_ref, s1, core_s, core_r, s1_s, s1_r, out_sem = take(12)
    if carry:
        zgot, zown, mgot, mown, z_s, z_r, m_s, m_r, own_sem = take(9)
    j = pl.program_id(0)
    steps = pl.num_programs(0)
    width = g_ref.shape[1]
    place = Place()
    half = c_ref.shape[1]
    mcols = width // 2

    def z_sends():
        piece = [remote(zin_ref.at[:, (place.z + d) % place.depth], zgot.at[d - 1], z_s.at[d - 1], z_r.at[d - 1],
                        place.over_z[d - 1]) for d in range(1, place.depth)]
        return piece

    def m_sends():
        sends = []
        for k in range(2):
            sends.append(remote(min_ref.at[2 * k + 1 - place.x, :, pl.ds(0, mcols)], mgot.at[0, k], m_s.at[0, k],
                                m_r.at[0, k], place.over_x))
            sends.append(remote(min_ref.at[2 * (1 - place.y) + k, :, pl.ds(mcols, mcols)], mgot.at[1, k], m_s.at[1, k],
                                m_r.at[1, k], place.over_y))
        return sends

    def own_copies():
        copies = [pltpu.make_async_copy(zin_ref.at[:, place.z], zown, own_sem.at[4])]
        for k in range(2):
            copies.append(pltpu.make_async_copy(min_ref.at[2 * k + place.x, :, pl.ds(0, mcols)], mown.at[0, k],
                                                own_sem.at[k]))
            copies.append(pltpu.make_async_copy(min_ref.at[2 * place.y + k, :, pl.ds(mcols, mcols)], mown.at[1, k],
                                                own_sem.at[2 + k]))
        return copies

    def core_send(slot):
        return remote(give.at[slot], got.at[slot], core_s.at[slot], core_r.at[slot], place.over_core)

    def s1_send(side, t):
        device = place.over_x if side == 0 else place.over_y
        return remote(c_ref.at[t, :, pl.ds(side * width, width)], s1.at[side], s1_s.at[side], s1_r.at[side], device)

    def c_copy(t):
        return pltpu.make_async_copy(c_ref.at[t], c_out.at[t], out_sem.at[t])

    def finish(t, slot):
        core_send(slot).wait_recv()
        c_ref[t] = bf(f32(c_ref[t]) + f32(got[slot]))
        c_copy(t).start()

    @pl.when(j == 0)
    def _():
        greet([place.over_core, place.over_x, place.over_y] + (place.over_z if carry else []))
        if carry:
            for copy in z_sends() + m_sends() + own_copies():
                copy.start()
        g16 = bf(g_ref[...])
        g16_ref[...] = g16
        store_rows(place, g16t_ref, g16.T)
        store_rows(place, normed_t_ref, normed_ref[...].T)
        out_ref[...] = jnp.zeros_like(out_ref)

    @pl.when(j == 1)
    def _():
        finish(0, 0)

        @pl.when(place.x == 1)
        def _():
            s1_send(0, 0).start()

        @pl.when(place.y == 1)
        def _():
            s1_send(1, 0).start()

    @pl.when(j == 2)
    def _():
        finish(3, 1)

        @pl.when(place.x == 0)
        def _():
            s1_send(0, 3).start()

        @pl.when(place.y == 0)
        def _():
            s1_send(1, 3).start()

    @pl.when(j == 3)
    def _():
        finish(2, 0)

    active, slope = gelu_parts(f32(raised_ref[...]))
    active = bf(active)
    raised_grad = bf(mm_nt(g16_ref[...], down_ref[...]) * slope)
    slot = j % 2

    @pl.when(j >= 2)
    def _():
        core_send(slot).wait_send()

    give[slot, :, :width] = bf(mm(normed_t_ref[:half], raised_grad))
    give[slot, :, width:] = bf(mm(g16t_ref[:half], active))
    core_send(slot).start()
    t = (steps - j) % steps
    c_ref[t, :, :width] = bf(mm(normed_t_ref[half:], raised_grad))
    c_ref[t, :, width:] = bf(mm(g16t_ref[half:], active))
    out_ref[...] += mm_nt(raised_grad, up_ref[...])

    @pl.when(j == steps - 1)
    def _():
        part, gain_grad, bias_grad = norm_backward(hidden_ref[...], f32(gain_ref[...]), out_ref[...])
        out_ref[...] = g_ref[...] + part
        gain_grad_ref[...] = gain_grad
        bias_grad_ref[...] = bias_grad
        finish(1, 1)
        for k in range(2):
            s1_send(k, 0).wait_recv()
        w_out[0] = bf(f32(c_ref[3 * place.x, :, :width]) + f32(s1[0]))
        w_out[1] = bf(f32(c_ref[3 * place.y, :, width:]) + f32(s1[1]))
        if carry:
            for copy in own_copies():
                copy.wait()
            for copy in z_sends() + m_sends():
                copy.wait()
            total = f32(zown[...])
            for d in range(place.depth - 1):
                total += f32(zgot[d])
            zfin_ref[...] = total
            for side in range(2):
                for k in range(2):
                    wmix_ref[side, k] = bf(f32(mown[side, k]) + f32(mgot[side, k]))
        for k in range(2):
            s1_send(k, 0).wait_send()
            core_send(k).wait_send()
        for k in range(steps):
            c_copy(k).wait()


def ffn_backward(layer, carry, collective, g, hidden, gain, normed, raised, w_up, w_down, *carried):
    length, width = g.shape
    inner = w_up.shape[2]
    chunk = inner // 4
    depth = lax.axis_size("seq") // 2
    piece = width // (2 * depth)
    half = depth * piece
    b16, b32, dma = jnp.bfloat16, jnp.float32, pltpu.SemaphoreType.DMA
    order = lambda j: (4 - j) % 4
    return pl.pallas_call(
        lambda *refs: ffn_backward_body(carry, *refs),
        grid=(4,),
        in_specs=[
            whole((length, width)), whole((length, width)), of_layer(layer, (1, width)), whole((length, width)),
            pl.BlockSpec((length, chunk), lambda j: (0, order(j))),
            pl.BlockSpec((None, width, chunk), lambda j: (layer, 0, order(j))),
            pl.BlockSpec((None, chunk, width), lambda j: (layer, order(j), 0)),
        ] + [ANY] * len(carried),
        out_specs=[whole((length, width)), whole((1, width)), whole((1, width)), ANY, whole((2, half, width))]
        + ([whole((2, piece, width)), whole((2, 2, half, width // 2))] if carry else []),
        out_shape=[
            sds((length, width), b32), sds((1, width), b32), sds((1, width), b32), sds((4, half, 2 * chunk), b16),
            sds((2, half, chunk), b16),
        ] + ([sds((2, piece, chunk), b32), sds((2, 2, half, width // 2), b16)] if carry else []),
        scratch_shapes=[
            pltpu.VMEM((length, width), b16), pltpu.VMEM((width, length), b16), pltpu.VMEM((width, length), b16),
            pltpu.VMEM((2, half, 2 * chunk), b16), pltpu.VMEM((2, half, 2 * chunk), b16),
            pltpu.VMEM((4, half, 2 * chunk), b16), pltpu.VMEM((2, half, chunk), b16),
            dma((2,)), dma((2,)), dma((2,)), dma((2,)), dma((4,)),
        ] + ([
            pltpu.VMEM((depth - 1, 2, piece, chunk), b16), pltpu.VMEM((2, piece, chunk), b16),
            pltpu.VMEM((2, 2, half, width // 2), b16), pltpu.VMEM((2, 2, half, width // 2), b16),
            dma((depth - 1,)), dma((depth - 1,)), dma((2, 2)), dma((2, 2)), dma((5,)),
        ] if carry else []),
        compiler_params=pltpu.CompilerParams(
            vmem_limit_bytes=62 * MIB, collective_id=collective, has_side_effects=True
        ),
        cost_estimate=pl.CostEstimate(
            flops=8 * length * width * inner, bytes_accessed=40 * MIB, transcendentals=length * inner
        ),
        name="ffn_backward",
    )(g, hidden, gain, normed, raised, w_up, w_down, *carried)


def mixer_backward_body(carry, *refs):
    refs = list(refs)
    take = lambda n: [refs.pop(0) for _ in range(n)]
    (hg_ref, r_ref, gain_ref, normed_ref, proj_ref, k0_ref, k1_ref, k2_ref, signal_ref, long_ref, taps_ref, skip_ref,
     table_ref, wo_ref, w0_ref, w1_ref, w2_ref, c_in, w1_in) = take(19)
    wmix_ref = take(1)[0] if carry else None
    (g_ref, c_out, zout_ref, taps_grad_ref, short_grad_ref, skip_grad_ref, gain_grad_ref, bias_grad_ref) = take(8)
    mfin_ref = take(1)[0] if carry else None
    (og_ref, left_t, gated_ref, pg_ref, give, got, s1, wkeep, s2, core_s, core_r, s1_s, s1_r, s2_s, s2_r, own_sem,
     out_sem) = take(17)
    if carry:
        mkeep, m2, mz, mzgot, m2_s, m2_r, mz_s, mz_r, m_sem = take(9)
    j = pl.program_id(0)
    steps = pl.num_programs(0)
    length, width = hg_ref.shape
    place = Place()
    half = give.shape[1]
    piece = half // place.depth
    x, y = place.x, place.y

    def s1_sends():
        return [
            remote(c_in.at[1 + x, :, pl.ds(0, width)], s1.at[0], s1_s.at[0], s1_r.at[0], place.over_x),
            remote(c_in.at[2 - y, :, pl.ds(width, width)], s1.at[1], s1_s.at[1], s1_r.at[1], place.over_y),
        ]

    def own_copies():
        return [
            pltpu.make_async_copy(w1_in.at[0], wkeep.at[0, x], own_sem.at[0]),
            pltpu.make_async_copy(w1_in.at[1], wkeep.at[1, y], own_sem.at[1]),
            pltpu.make_async_copy(c_in.at[2 - x, :, pl.ds(0, width)], wkeep.at[0, 1 - x], own_sem.at[2]),
            pltpu.make_async_copy(c_in.at[1 + y, :, pl.ds(width, width)], wkeep.at[1, 1 - y], own_sem.at[3]),
        ]

    def s2_sends():
        return [
            remote(wkeep.at[0, 1 - y], s2.at[0], s2_s.at[0], s2_r.at[0], place.over_y),
            remote(wkeep.at[1, 1 - x], s2.at[1], s2_s.at[1], s2_r.at[1], place.over_x),
        ]

    def m2_sends():
        return [
            remote(wmix_ref.at[0, 1 - y], m2.at[0], m2_s.at[0], m2_r.at[0], place.over_y),
            remote(wmix_ref.at[1, 1 - x], m2.at[1], m2_s.at[1], m2_r.at[1], place.over_x),
        ]

    def m_copies():
        return [
            pltpu.make_async_copy(wmix_ref.at[0, y], mkeep.at[0], m_sem.at[0]),
            pltpu.make_async_copy(wmix_ref.at[1, x], mkeep.at[1], m_sem.at[1]),
        ]

    def mz_sends():
        return [
            remote(mz.at[:, (place.z + d) % place.depth], mzgot.at[d - 1], mz_s.at[d - 1], mz_r.at[d - 1],
                   place.over_z[d - 1])
            for d in range(1, place.depth)
        ]

    def core_send(t):
        return remote(give.at[t], got.at[t], core_s.at[t], core_r.at[t], place.over_core)

    def c_copy(t):
        return pltpu.make_async_copy(got.at[t], c_out.at[t], out_sem.at[t])

    @pl.when(j == 0)
    def _():
        greet([place.over_core, place.over_x, place.over_y] + (place.over_z if carry else []))
        for copy in s1_sends() + own_copies():
            copy.start()
        if carry:
            for copy in m2_sends() + m_copies():
                copy.start()
        og_ref[...] = bf(hg_ref[...])
        g_ref[...] = jnp.zeros_like(g_ref)

    if carry:
        @pl.when(j == 1)
        def _():
            for copy in m2_sends() + m_copies():
                copy.wait()
            for side in range(2):
                total = bf(f32(mkeep[side]) + f32(m2[side]))
                for k in range(place.depth):
                    mz[side, k] = total[k * piece : (k + 1) * piece]
            for copy in mz_sends():
                copy.start()

    @pl.when(j == 2)
    def _():
        for copy in s1_sends() + own_copies():
            copy.wait()
        wkeep[0, 1 - x] = bf(f32(wkeep[0, 1 - x]) + f32(s1[0]))
        wkeep[1, 1 - y] = bf(f32(wkeep[1, 1 - y]) + f32(s1[1]))
        for copy in s2_sends():
            copy.start()

    @pl.when(j < steps - 1)
    def _():
        chunk = long_ref.shape[1]
        proj = [f32(proj_ref[p]) for p in range(3)]
        kernel = [f32(k_ref[...]) for k_ref in (k0_ref, k1_ref, k2_ref)]
        gate_out, gate_in, vals = mixed_chunk(proj, kernel)
        carried = vals * gate_in
        long_out = f32(long_ref[...])
        skip = f32(skip_ref[...])
        gated_ref[:, pl.ds(pl.multiple_of(j * chunk, chunk), chunk)] = bf(long_out * gate_out)
        gated_grad = mm_nt(og_ref[...], wo_ref[...])
        long_grad = gated_grad * gate_out
        skip_grad_ref[...] = jnp.sum(carried * long_grad, axis=0, keepdims=True)
        both = mm(table_ref[...], bf(long_grad))
        up_re, up_im = both[:length], both[length:]
        tap_re, tap_im = f32(taps_ref[:length]), f32(taps_ref[length:])
        out = mm_tn(table_ref[:length], bf(up_re * tap_re + up_im * tap_im))
        out += mm_tn(table_ref[length:], bf(up_im * tap_re - up_re * tap_im))
        carried_grad = out + skip * long_grad
        sig_re, sig_im = f32(signal_ref[:length]), f32(signal_ref[length:])
        cross = mm_tn(table_ref[:length], bf(up_re * sig_re + up_im * sig_im))
        cross += mm_tn(table_ref[length:], bf(up_im * sig_re - up_re * sig_im))
        taps_grad_ref[...] = cross * (1.0 / length)
        upstream = None
        for p, part in enumerate((gated_grad * long_out, carried_grad * vals, carried_grad * gate_in)):
            one, two = row_shift(part, -1), row_shift(part, -2)
            projected_grad = bf(kernel[p][2:3] * part + kernel[p][1:2] * one + kernel[p][0:1] * two)
            for tap, moved in enumerate((two, one, part)):
                short_grad_ref[p, tap : tap + 1, :] = jnp.sum(moved * proj[p], axis=0, keepdims=True)
            pg_ref[:, pl.ds(pl.multiple_of(p * width + j * chunk, chunk), chunk)] = projected_grad
            term = mm_nt(projected_grad, (w0_ref, w1_ref, w2_ref)[p][...])
            upstream = term if upstream is None else upstream + term
        g_ref[...] += upstream

    @pl.when(j == steps - 1)
    def _():
        in_cols, out_cols = 3 * width // 4, width // 4
        store_rows(place, left_t.at[0], normed_ref[...].T)
        store_rows(place, left_t.at[1], gated_ref[...].T)
        for t in range(4):
            rights = pg_ref[:, in_cols * t : in_cols * (t + 1)], og_ref[:, out_cols * t : out_cols * (t + 1)]
            give[t, :, :in_cols] = bf(mm(left_t[0, :half], rights[0]))
            give[t, :, in_cols:] = bf(mm(left_t[1, :half], rights[1]))
            core_send(t).start()
        part, gain_grad, bias_grad = norm_backward(r_ref[...], f32(gain_ref[...]), g_ref[...])
        g_ref[...] = hg_ref[...] + part
        gain_grad_ref[...] = gain_grad
        bias_grad_ref[...] = bias_grad
        for t in range(4):
            rights = pg_ref[:, in_cols * t : in_cols * (t + 1)], og_ref[:, out_cols * t : out_cols * (t + 1)]
            core_send(t).wait()
            got[t, :, :in_cols] = bf(mm(left_t[0, half:], rights[0]) + f32(got[t, :, :in_cols]))
            got[t, :, in_cols:] = bf(mm(left_t[1, half:], rights[1]) + f32(got[t, :, in_cols:]))
            c_copy(t).start()
        if carry:
            for copy in mz_sends():
                copy.wait()
            for side in range(2):
                total = f32(mz[side, place.z])
                for d in range(place.depth - 1):
                    total += f32(mzgot[d, side])
                mfin_ref[side] = total
        for copy in s2_sends():
            copy.wait()
        for side, keep in enumerate((y, x)):
            total = bf(f32(wkeep[side, keep]) + f32(s2[side]))
            for k in range(place.depth):
                zout_ref[side, k] = total[k * piece : (k + 1) * piece]
        for t in range(4):
            c_copy(t).wait()


def mixer_backward(
    layer, carry, collective, hidden_grad, r, gain, normed, proj, short_w, signal, long_out, taps, skip, table, w_out,
    w_in, ffn_c, ffn_w, *carried
):
    length, width = r.shape
    chunk = 256
    steps = width // chunk
    depth = lax.axis_size("seq") // 2
    piece = width // (2 * depth)
    half = depth * piece
    at = lambda j: jnp.minimum(j, steps - 1)
    third = lambda p: pl.BlockSpec((None, width, chunk), lambda j: (layer, 0, p * steps + at(j)))
    short = lambda p: pl.BlockSpec((None, 3, chunk), lambda j: (layer, 0, p * steps + at(j)))
    b16, b32, dma = jnp.bfloat16, jnp.float32, pltpu.SemaphoreType.DMA
    return pl.pallas_call(
        lambda *refs: mixer_backward_body(carry, *refs),
        grid=(steps + 1,),
        in_specs=[
            whole((length, width)), whole((length, width)), of_layer(layer, (1, width)), whole((length, width)),
            pl.BlockSpec((3, length, chunk), lambda j: (0, 0, at(j))),
            short(0), short(1), short(2),
            pl.BlockSpec((2 * length, chunk), lambda j: (0, at(j))),
            pl.BlockSpec((length, chunk), lambda j: (0, at(j))),
            pl.BlockSpec((2 * length, chunk), lambda j: (0, at(j))),
            pl.BlockSpec((None, 1, chunk), lambda j: (layer, 0, at(j))),
            whole((2 * length, length)),
            pl.BlockSpec((None, chunk, width), lambda j: (layer, at(j), 0)),
            third(0), third(1), third(2),
        ] + [ANY] * (2 + len(carried)),
        out_specs=[
            whole((length, width)), ANY, whole((2, depth, piece, width)),
            pl.BlockSpec((length, chunk), lambda j: (0, at(j))),
            pl.BlockSpec((3, 3, chunk), lambda j: (0, 0, at(j))),
            pl.BlockSpec((1, chunk), lambda j: (0, at(j))),
            whole((1, width)), whole((1, width)),
        ] + ([whole((2, piece, width // 2))] if carry else []),
        out_shape=[
            sds((length, width), b32), sds((4, half, width), b16), sds((2, depth, piece, width), b16),
            sds((length, width), b32), sds((3, 3, width), b32), sds((1, width), b32), sds((1, width), b32),
            sds((1, width), b32),
        ] + ([sds((2, piece, width // 2), b32)] if carry else []),
        scratch_shapes=[
            pltpu.VMEM((length, width), b16), pltpu.VMEM((2, width, length), b16), pltpu.VMEM((length, width), b16),
            pltpu.VMEM((length, 3 * width), b16), pltpu.VMEM((4, half, width), b16), pltpu.VMEM((4, half, width), b16),
            pltpu.VMEM((2, half, width), b16), pltpu.VMEM((2, 2, half, width), b16), pltpu.VMEM((2, half, width), b16),
            dma((4,)), dma((4,)), dma((2,)), dma((2,)), dma((2,)), dma((2,)), dma((4,)), dma((4,)),
        ] + ([
            pltpu.VMEM((2, half, width // 2), b16), pltpu.VMEM((2, half, width // 2), b16),
            pltpu.VMEM((2, depth, piece, width // 2), b16), pltpu.VMEM((depth - 1, 2, piece, width // 2), b16),
            dma((2,)), dma((2,)), dma((depth - 1,)), dma((depth - 1,)), dma((2,)),
        ] if carry else []),
        compiler_params=pltpu.CompilerParams(
            vmem_limit_bytes=63 * MIB, collective_id=collective, has_side_effects=True
        ),
        cost_estimate=pl.CostEstimate(
            flops=2 * length * width * (8 * width + 6 * length), bytes_accessed=50 * MIB, transcendentals=0
        ),
        name="mixer_backward",
    )(hidden_grad, r, gain, normed, proj, short_w, short_w, short_w, signal, long_out, taps, skip, table, w_out,
      w_in, w_in, w_in, ffn_c, ffn_w, *carried)


def last_sums_body(z_in, c_in, zfin_ref, mfin_ref, zgot, zown, mgot, w, m2, mz, mzgot, z_s, z_r, m_s, m_r, m2_s, m2_r,
                   mz_s, mz_r, own_sem):
    place = Place()
    x, y = place.x, place.y
    cols = w.shape[3]
    piece = zown.shape[1]
    greet([place.over_x, place.over_y] + place.over_z)
    m_sends = []
    for k in range(2):
        m_sends.append(remote(c_in.at[2 * k + 1 - x, :, pl.ds(0, cols)], mgot.at[0, k], m_s.at[0, k], m_r.at[0, k],
                              place.over_x))
        m_sends.append(remote(c_in.at[2 * (1 - y) + k, :, pl.ds(cols, cols)], mgot.at[1, k], m_s.at[1, k],
                              m_r.at[1, k], place.over_y))
    z_sends = [
        remote(z_in.at[:, (place.z + d) % place.depth], zgot.at[d - 1], z_s.at[d - 1], z_r.at[d - 1],
               place.over_z[d - 1])
        for d in range(1, place.depth)
    ]
    own = [pltpu.make_async_copy(z_in.at[:, place.z], zown, own_sem.at[4])]
    for k in range(2):
        own.append(pltpu.make_async_copy(c_in.at[2 * k + x, :, pl.ds(0, cols)], w.at[0, k], own_sem.at[k]))
        own.append(pltpu.make_async_copy(c_in.at[2 * y + k, :, pl.ds(cols, cols)], w.at[1, k], own_sem.at[2 + k]))
    for copy in m_sends + z_sends + own:
        copy.start()
    for copy in own + m_sends:
        copy.wait()
    for side in range(2):
        for k in range(2):
            w[side, k] = bf(f32(w[side, k]) + f32(mgot[side, k]))
    m2_sends = [
        remote(w.at[0, 1 - y], m2.at[0], m2_s.at[0], m2_r.at[0], place.over_y),
        remote(w.at[1, 1 - x], m2.at[1], m2_s.at[1], m2_r.at[1], place.over_x),
    ]
    for copy in m2_sends:
        copy.start()
    for copy in m2_sends:
        copy.wait()
    for side, keep in enumerate((y, x)):
        total = bf(f32(w[side, keep]) + f32(m2[side]))
        for k in range(place.depth):
            mz[side, k] = total[k * piece : (k + 1) * piece]
    mz_sends = [
        remote(mz.at[:, (place.z + d) % place.depth], mzgot.at[d - 1], mz_s.at[d - 1], mz_r.at[d - 1],
               place.over_z[d - 1])
        for d in range(1, place.depth)
    ]
    for copy in mz_sends:
        copy.start()
    for copy in z_sends:
        copy.wait()
    total = f32(zown[...])
    for d in range(place.depth - 1):
        total += f32(zgot[d])
    zfin_ref[...] = total
    for copy in mz_sends:
        copy.wait()
    for side in range(2):
        total = f32(mz[side, place.z])
        for d in range(place.depth - 1):
            total += f32(mzgot[d, side])
        mfin_ref[side] = total


def last_sums(collective, ffn_z, mixer_c):
    _, depth, piece, width = ffn_z.shape
    half = depth * piece
    b16, dma = jnp.bfloat16, pltpu.SemaphoreType.DMA
    cols = width // 2
    return pl.pallas_call(
        last_sums_body,
        in_specs=[ANY, ANY],
        out_specs=[pl.BlockSpec(memory_space=pltpu.VMEM)] * 2,
        out_shape=[sds((2, piece, width), jnp.float32), sds((2, piece, cols), jnp.float32)],
        scratch_shapes=[
            pltpu.VMEM((depth - 1, 2, piece, width), b16), pltpu.VMEM((2, piece, width), b16),
            pltpu.VMEM((2, 2, half, cols), b16), pltpu.VMEM((2, 2, half, cols), b16), pltpu.VMEM((2, half, cols), b16),
            pltpu.VMEM((2, depth, piece, cols), b16), pltpu.VMEM((depth - 1, 2, piece, cols), b16),
            dma((depth - 1,)), dma((depth - 1,)), dma((2, 2)), dma((2, 2)), dma((2,)), dma((2,)), dma((depth - 1,)),
            dma((depth - 1,)), dma((5,)),
        ],
        compiler_params=pltpu.CompilerParams(
            vmem_limit_bytes=40 * MIB, collective_id=collective, has_side_effects=True
        ),
        name="last_sums",
    )(ffn_z, mixer_c)


def whole_sequences(
    x_in, cotangent, counts, ln1_gain, ln1_bias, w_in, short_w, filt_w1, filt_freq, filt_w2, filt_w3, long_bias,
    w_out, ln2_gain, ln2_bias, w_up, w_down,
):
    micro_count, cap_size, tok_rows, width = x_in.shape
    slots = micro_count * cap_size
    layers, _, inner = w_up.shape
    toks = lax.axis_size("tok")
    length = tok_rows * toks
    me = lax.axis_index("tok")

    def gather_mine(block):
        return lax.all_to_all(block.reshape(slots, tok_rows, width), "tok", split_axis=0, concat_axis=1, tiled=True)[0]

    def scatter_back(rows):
        blocks = rows.reshape(slots, tok_rows, width)
        back = lax.all_to_all(blocks, "tok", split_axis=0, concat_axis=0, tiled=True)
        return back.reshape(micro_count, cap_size, tok_rows, width)

    live = (me % cap_size < counts[me // cap_size, 0]).astype(jnp.float32)
    table = jnp.asarray(spectral_table(length))
    features = position_features(length)
    envelope = decay_table(features[:, :1], 0.0, width, width)
    rowed = lambda v: v.reshape(layers, 1, v.shape[1])
    g1, b1, g2, b2, skip = (rowed(v) for v in (ln1_gain, ln1_bias, ln2_gain, ln2_bias, long_bias))

    def taps_fn(layer):
        def fn(one, sine, two, three):
            return filter_taps(features, one, sine, two, three, envelope)

        return jax.vjp(fn, f32(filt_w1[layer]), f32(filt_freq[layer]), f32(filt_w2[layer]), f32(filt_w3[layer]))

    start = gather_mine(x_in)
    upstream = gather_mine(cotangent)
    filters = [taps_fn(layer) for layer in range(layers)]
    spectra = [bf(mm(table, bf(filters[layer][0])) * (1.0 / length)) for layer in range(layers)]
    r = f32(start)
    kept = []
    for layer in range(layers):
        hidden, normed, proj, signal, long_out = mixer_forward(
            layer, r, g1, b1, w_in, short_w, table, spectra[layer], skip, w_out
        )
        result, normed_two, raised = ffn_forward(layer, hidden, g2, b2, w_up, w_down)
        kept.append((r, hidden, normed, proj, signal, long_out, normed_two, raised))
        r = result
    out_act = f32(scatter_back(bf(r * live)))

    grad = f32(upstream) * live
    vecs = [None] * layers
    carried_ffn, carried_mixer = (), ()
    done = {}
    for layer in reversed(range(layers)):
        r, hidden, normed, proj, signal, long_out, normed_two, raised = kept[layer]
        carry = layer < layers - 1
        grad, grad_g2, grad_b2, ffn_c, ffn_w, *rest = ffn_backward(
            layer, carry, 2 * layer, grad, hidden, g2, normed_two, raised, w_up, w_down, *carried_ffn
        )
        if carry:
            done["ffn", layer + 1] = rest[0]
            carried_mixer = (rest[1],)
        grad, mixer_c, ffn_z, taps_grad, grad_short, grad_skip, grad_g1, grad_b1, *rest = mixer_backward(
            layer, carry, 2 * layer + 1, grad, r, g1, normed, proj, short_w, signal, long_out, spectra[layer], skip,
            table, w_out, w_in, ffn_c, ffn_w, *carried_mixer,
        )
        if carry:
            done["mixer", layer + 1] = rest[0]
        carried_ffn = (ffn_z, mixer_c)
        filter_grads = filters[layer][1](taps_grad)
        short = jnp.swapaxes(grad_short, 0, 1).reshape(3, 3 * width)
        vecs[layer] = (grad_g1[0], grad_b1[0], short, grad_skip[0], grad_g2[0], grad_b2[0]) + tuple(filter_grads)
    grad_in = f32(scatter_back(bf(grad)))
    done["ffn", 0], done["mixer", 0] = last_sums(2 * layers, *carried_ffn)
    split = 3 * width // toks
    both = [jnp.concatenate([done["mixer", layer][0], done["mixer", layer][1]], axis=1) for layer in range(layers)]
    mat_done = (
        jnp.stack([b[:, :split] for b in both]),
        jnp.stack([b[:, split:] for b in both]),
        jnp.stack([done["ffn", layer][0] for layer in range(layers)]),
        jnp.stack([done["ffn", layer][1].T for layer in range(layers)]),
    )
    small = lax.psum(
        tuple(jnp.stack([vecs[layer][m] for layer in range(layers)]) for m in range(10)), ("seq", "tok")
    )
    return (
        out_act, grad_in, small[0], small[1], mat_done[0], small[2], small[6], small[7], small[8], small[9], small[3],
        mat_done[1], small[4], small[5], mat_done[2], mat_done[3],
    )


def shards(*args):
    micro_count, cap_size = args[0].shape[:2]
    if lax.axis_size("tok") == 4 and micro_count * cap_size == 4:
        return whole_sequences(*args)
    return split_positions(*args)


def solution(mesh):
    return jax.shard_map(
        shards,
        mesh=mesh,
        in_specs=(
            P(None, "seq", "tok", None),
            P(None, "seq", "tok", None),
            P(None, "seq"),
            P(),
            P(),
            P(),
            P(),
            P(),
            P(),
            P(),
            P(),
            P(),
            P(),
            P(),
            P(),
            P(),
            P(),
        ),
        out_specs=(
            P(None, "seq", "tok", None),
            P(None, "seq", "tok", None),
            P(),
            P(),
            P(None, "seq", "tok"),
            P(),
            P(),
            P(),
            P(),
            P(),
            P(),
            P(None, "seq", "tok"),
            P(),
            P(),
            P(None, "seq", "tok"),
            P(None, "tok", "seq"),
        ),
        check_vma=False,
    )
```

```python
import math

import jax
import jax.numpy as jnp
import numpy as np
from jax import lax
from jax.experimental import pallas as pl
from jax.experimental.pallas import tpu as pltpu
from jax.sharding import PartitionSpec as P

EMB = 33
INNER = 64


HIGHEST = lax.Precision.HIGHEST
NORM_EPS = 1e-05
MOD_SHIFT = 0.05


def passed_along(block, axis, distance):
    devices = range(lax.axis_size(axis))
    route = [(i - distance, i) for i in devices if i - distance in devices]
    return lax.ppermute(block, axis, route)


def for_sending(value):

    def short(part):
        return part.astype(jnp.bfloat16) if part.dtype == jnp.float32 else part

    return jax.tree.map(short, value)


def position_features(length):
    band_count = (EMB - 1) // 2
    step_index = jnp.arange(length, dtype=jnp.int32).astype(jnp.float32)
    time_grid = step_index / (length - 1)
    base_angle = step_index * (2.0 * math.pi / length)
    band_freq = jnp.linspace(0.0001, band_count - 1, band_count, dtype=jnp.float32)
    phases = base_angle[:, None] * band_freq[None, :]
    return jnp.concatenate([time_grid[:, None], jnp.cos(phases), -jnp.sin(phases)], axis=1)


def decay_table(time_grid, first_chan, channels, model_width):
    fast_rate = math.log(0.01) / 0.3
    slow_rate = math.log(0.01) / 1.5
    chan_index = first_chan + jnp.arange(channels, dtype=jnp.int32).astype(jnp.float32)
    deltas = jnp.abs(fast_rate + (slow_rate - fast_rate) * chan_index / (model_width - 1))
    return jnp.exp(-time_grid * deltas[None, :]) + MOD_SHIFT


def filter_taps(features, weight_one, sine_freq, weight_two, weight_three, envelope):
    first_sine = jnp.sin(sine_freq[0] * jnp.dot(features, weight_one, precision=HIGHEST))
    second_sine = jnp.sin(sine_freq[1] * jnp.dot(first_sine, weight_two, precision=HIGHEST))
    return jnp.dot(second_sine, weight_three, precision=HIGHEST) * envelope


def layer_norm(values_in, gain_vec, bias_vec):
    mean_row = jnp.mean(values_in, axis=-1, keepdims=True)
    centred = values_in - mean_row
    variance = jnp.mean(centred * centred, axis=-1, keepdims=True)
    return centred * lax.rsqrt(variance + NORM_EPS) * gain_vec + bias_vec


def gelu_tanh(values_in):
    return jax.nn.gelu(values_in, approximate=True)


def dft_tables(outer_size, inner_size):
    padded_len = outer_size * inner_size
    outer_index = jnp.arange(outer_size, dtype=jnp.int32)
    half_index = jnp.arange(outer_size // 2, dtype=jnp.int32)
    inner_index = jnp.arange(inner_size, dtype=jnp.int32)
    angle_outer = (outer_index[:, None] * half_index[None, :] % outer_size).astype(jnp.float32) * (
        2.0 * math.pi / outer_size
    )
    angle_twist = (outer_index[:, None] * inner_index[None, :] % padded_len).astype(jnp.float32) * (
        2.0 * math.pi / padded_len
    )
    angle_inner = (inner_index[:, None] * inner_index[None, :] % inner_size).astype(jnp.float32) * (
        2.0 * math.pi / inner_size
    )
    return (
        jnp.cos(angle_outer),
        jnp.sin(angle_outer),
        jnp.cos(angle_twist)[None, :, :, None],
        jnp.sin(angle_twist)[None, :, :, None],
        jnp.cos(angle_inner),
        jnp.sin(angle_inner),
    )


def forward_dft(series, tables):
    cos_outer, sin_outer, cos_twist, sin_twist, cos_inner, sin_inner = tables
    outer_size = cos_outer.shape[0]
    inner_size = cos_inner.shape[0]
    seq_count = series.shape[0]
    channels = series.shape[2]
    token_grid = series.reshape(seq_count, outer_size // 2, inner_size, channels)
    first_re = jnp.einsum("ka,sabc->skbc", cos_outer, token_grid, precision=HIGHEST)
    first_im = -jnp.einsum("ka,sabc->skbc", sin_outer, token_grid, precision=HIGHEST)
    twist_re = first_re * cos_twist + first_im * sin_twist
    twist_im = first_im * cos_twist - first_re * sin_twist
    out_re = jnp.einsum("skbc,bj->skjc", twist_re, cos_inner, precision=HIGHEST) + jnp.einsum(
        "skbc,bj->skjc", twist_im, sin_inner, precision=HIGHEST
    )
    out_im = jnp.einsum("skbc,bj->skjc", twist_im, cos_inner, precision=HIGHEST) - jnp.einsum(
        "skbc,bj->skjc", twist_re, sin_inner, precision=HIGHEST
    )
    return (out_re, out_im)


def inverse_dft(spec_re, spec_im, tables):
    cos_outer, sin_outer, cos_twist, sin_twist, cos_inner, sin_inner = tables
    outer_size = cos_outer.shape[0]
    inner_size = cos_inner.shape[0]
    seq_count = spec_re.shape[0]
    channels = spec_re.shape[3]
    back_re = jnp.einsum("skjc,bj->skbc", spec_re, cos_inner, precision=HIGHEST) - jnp.einsum(
        "skjc,bj->skbc", spec_im, sin_inner, precision=HIGHEST
    )
    back_im = jnp.einsum("skjc,bj->skbc", spec_im, cos_inner, precision=HIGHEST) + jnp.einsum(
        "skjc,bj->skbc", spec_re, sin_inner, precision=HIGHEST
    )
    turn_re = back_re * cos_twist - back_im * sin_twist
    turn_im = back_im * cos_twist + back_re * sin_twist
    token_grid = (
        jnp.einsum("skbc,ka->sabc", turn_re, cos_outer, precision=HIGHEST)
        - jnp.einsum("skbc,ka->sabc", turn_im, sin_outer, precision=HIGHEST)
    ) / (outer_size * inner_size)
    return token_grid.reshape(seq_count, outer_size // 2 * inner_size, channels)


def complex_product(left_re, left_im, right_re, right_im):
    return (left_re * right_re - left_im * right_im, left_re * right_im + left_im * right_re)


def add_tree(running, update):
    if running is None:
        return update
    return jax.tree.map(jnp.add, running, update)


def split_positions(
    x_in,
    cotangent,
    counts,
    ln1_gain,
    ln1_bias,
    w_in,
    short_w,
    filt_w1,
    filt_freq,
    filt_w2,
    filt_w3,
    long_bias,
    w_out,
    ln2_gain,
    ln2_bias,
    w_up,
    w_down,
):
    tok_count = lax.axis_size("tok")
    micro_count, cap_size, tok_rows, model_width = x_in.shape
    channels = model_width // tok_count
    first_chan = lax.axis_index("tok") * channels
    layer_count = w_in.shape[0]
    length = tok_rows * tok_count
    tables = dft_tables(2 * length // INNER, INNER)
    features = position_features(length)
    envelope = decay_table(features[:, :1], first_chan.astype(jnp.float32), channels, model_width)
    gain_one = ln1_gain.astype(jnp.float32)
    bias_one = ln1_bias.astype(jnp.float32)
    gain_two = ln2_gain.astype(jnp.float32)
    bias_two = ln2_bias.astype(jnp.float32)
    short_taps = short_w.astype(jnp.float32)
    skip_scale = long_bias.astype(jnp.float32)
    filt_one = filt_w1.astype(jnp.float32)
    filt_sine = filt_freq.astype(jnp.float32)
    filt_two = filt_w2.astype(jnp.float32)
    filt_three = filt_w3.astype(jnp.float32)

    def taps_of(layer_index):

        def taps_fn(weight_one, sine_freq, weight_two, three_slice):
            return filter_taps(features, weight_one, sine_freq, weight_two, three_slice, envelope)

        three_slice = lax.dynamic_slice_in_dim(filt_three[layer_index], first_chan, channels, 1)
        return jax.vjp(
            taps_fn,
            filt_one[layer_index],
            filt_sine[layer_index],
            filt_two[layer_index],
            three_slice,
        )

    taps_spectra = []
    for layer_index in range(layer_count):
        filter_rows, _ = taps_of(layer_index)
        taps_spectra.append(forward_dft(filter_rows[None], tables))

    def backward_layer(grad_rows, kept, layer_index):
        (
            residual,
            normed,
            padded,
            short_out,
            carried,
            long_out,
            gated_rows,
            hidden,
            normed_two,
            raised,
            active,
            kept_signal,
        ) = kept
        down_grad = grad_rows.astype(jnp.bfloat16)
        active_grad = jnp.einsum(
            "std,fd->stf", down_grad, w_down[layer_index], preferred_element_type=jnp.float32
        )
        _, gelu_pull = jax.vjp(gelu_tanh, raised)
        raised_grad = gelu_pull(active_grad)[0].astype(jnp.bfloat16)
        normed_two_grad = jnp.einsum(
            "stf,df->std", raised_grad, w_up[layer_index], preferred_element_type=jnp.float32
        )
        _, second_pull = jax.vjp(layer_norm, hidden, gain_two[layer_index], bias_two[layer_index])
        hidden_part, grad_gain_two, grad_bias_two = second_pull(normed_two_grad)
        hidden_grad = grad_rows + hidden_part
        out_grad = hidden_grad.astype(jnp.bfloat16)
        gated_grad = jnp.einsum(
            "ste,de->std", out_grad, w_out[layer_index], preferred_element_type=jnp.float32
        )
        gate_out = short_out[:, :, :model_width]
        gate_in = short_out[:, :, model_width : 2 * model_width]
        values = short_out[:, :, 2 * model_width :]
        long_grad = gated_grad * gate_out
        gate_out_grad = gated_grad * long_out
        grad_skip = jnp.sum(carried * long_grad, axis=(0, 1))
        spec_re, spec_im = taps_spectra[layer_index]
        upstream_re, upstream_im = forward_dft(
            lax.all_to_all(
                long_grad.astype(jnp.bfloat16), "tok", split_axis=2, concat_axis=1, tiled=True
            ).astype(long_grad.dtype),
            tables,
        )
        back_re, back_im = complex_product(upstream_re, upstream_im, spec_re, -spec_im)
        back_rows = lax.all_to_all(
            for_sending(inverse_dft(back_re, back_im, tables)),
            "tok",
            split_axis=1,
            concat_axis=2,
            tiled=True,
        )
        back_rows, upstream_re, upstream_im = (back_rows, upstream_re, upstream_im)
        signal_re, signal_im = kept_signal
        cross_re = jnp.sum(signal_re * upstream_re + signal_im * upstream_im, axis=0)
        cross_im = jnp.sum(signal_re * upstream_im - signal_im * upstream_re, axis=0)
        carried_grad = back_rows + skip_scale[layer_index] * long_grad
        short_grad = jnp.concatenate(
            [gate_out_grad, carried_grad * values, carried_grad * gate_in], axis=2
        )
        next_rows = passed_along(for_sending(short_grad[:, :2, :]), "tok", -1)
        extended = jnp.concatenate([short_grad, next_rows], axis=1)
        kernel = short_taps[layer_index]
        projected_grad = (
            kernel[2] * short_grad + kernel[1] * extended[:, 1:-1] + kernel[0] * extended[:, 2:]
        ).astype(jnp.bfloat16)
        grad_short = jnp.stack(
            [
                jnp.sum(short_grad * padded[:, tap_index : tap_index + tok_rows], axis=(0, 1))
                for tap_index in range(3)
            ]
        )
        normed_grad = jnp.einsum(
            "ste,de->std", projected_grad, w_in[layer_index], preferred_element_type=jnp.float32
        )
        _, first_pull = jax.vjp(layer_norm, residual, gain_one[layer_index], bias_one[layer_index])
        residual_part, grad_gain_one, grad_bias_one = first_pull(normed_grad)
        left_all = (
            lax.all_gather(down_grad, "tok", axis=1, tiled=True),
            lax.all_gather(gated_rows, "tok", axis=1, tiled=True),
            lax.all_gather(normed_two, "tok", axis=1, tiled=True),
            lax.all_gather(normed, "tok", axis=1, tiled=True),
        )
        right_cols = (
            lax.all_to_all(active, "tok", split_axis=2, concat_axis=1, tiled=True),
            lax.all_to_all(out_grad, "tok", split_axis=2, concat_axis=1, tiled=True),
            lax.all_to_all(raised_grad, "tok", split_axis=2, concat_axis=1, tiled=True),
            lax.all_to_all(projected_grad, "tok", split_axis=2, concat_axis=1, tiled=True),
        )
        grad_down = jnp.einsum(
            "stf,std->fd", right_cols[0], left_all[0], preferred_element_type=jnp.float32
        )
        grad_out = jnp.einsum(
            "std,ste->de", left_all[1], right_cols[1], preferred_element_type=jnp.float32
        )
        grad_up = jnp.einsum(
            "std,stf->df", left_all[2], right_cols[2], preferred_element_type=jnp.float32
        )
        grad_in_proj = jnp.einsum(
            "std,ste->de", left_all[3], right_cols[3], preferred_element_type=jnp.float32
        )
        bundle = (
            (grad_in_proj, grad_out, grad_up, grad_down),
            (grad_gain_one, grad_bias_one, grad_short, grad_skip, grad_gain_two, grad_bias_two),
            (cross_re, cross_im),
        )
        return (hidden_grad + residual_part, bundle)

    def filter_grads(cross_re, cross_im, layer_index):
        taps_grad = inverse_dft(cross_re[None], cross_im[None], tables)[0]
        _, taps_pull = taps_of(layer_index)
        grad_one, grad_sine, grad_two, grad_three = taps_pull(taps_grad)
        grad_three_full = lax.dynamic_update_slice_in_dim(
            jnp.zeros_like(filt_three[layer_index]), grad_three, first_chan, 1
        )
        return (grad_one, grad_sine, grad_two, grad_three_full)

    outputs = []
    input_grads = []
    running = None
    reduced = None
    for micro_index in range(micro_count):
        live_mask = (jnp.arange(cap_size, dtype=jnp.int32) < counts[micro_index, 0]).astype(
            jnp.float32
        )[:, None, None]
        residual = x_in[micro_index].astype(jnp.float32)
        saved = []
        for layer_index in range(layer_count):
            forward_normed = layer_norm(
                residual, gain_one[layer_index], bias_one[layer_index]
            ).astype(jnp.bfloat16)
            projected = jnp.einsum(
                "std,de->ste", forward_normed, w_in[layer_index], preferred_element_type=jnp.float32
            )
            prev_rows = passed_along(projected[:, -2:, :], "tok", 1)
            forward_padded = jnp.concatenate([prev_rows, projected], axis=1)
            forward_kernel = short_taps[layer_index]
            forward_short_out = (
                forward_kernel[0] * forward_padded[:, :-2]
                + forward_kernel[1] * forward_padded[:, 1:-1]
                + forward_kernel[2] * forward_padded[:, 2:]
            )
            forward_gate_out = forward_short_out[:, :, :model_width]
            forward_gate_in = forward_short_out[:, :, model_width : 2 * model_width]
            forward_values = forward_short_out[:, :, 2 * model_width :]
            forward_carried = forward_values * forward_gate_in
            forward_spec_re, forward_spec_im = taps_spectra[layer_index]
            convolve_signal_re, convolve_signal_im = forward_dft(
                lax.all_to_all(forward_carried, "tok", split_axis=2, concat_axis=1, tiled=True),
                tables,
            )
            prod_re, prod_im = complex_product(
                convolve_signal_re, convolve_signal_im, forward_spec_re, forward_spec_im
            )
            convolve_back_rows = lax.all_to_all(
                inverse_dft(prod_re, prod_im, tables),
                "tok",
                split_axis=1,
                concat_axis=2,
                tiled=True,
            )
            results = (convolve_back_rows, convolve_signal_re, convolve_signal_im)
            forward_long_out = results[0] + skip_scale[layer_index] * forward_carried
            forward_gated_rows = (forward_long_out * forward_gate_out).astype(jnp.bfloat16)
            forward_hidden = residual + jnp.einsum(
                "std,de->ste",
                forward_gated_rows,
                w_out[layer_index],
                preferred_element_type=jnp.float32,
            )
            forward_normed_two = layer_norm(
                forward_hidden, gain_two[layer_index], bias_two[layer_index]
            ).astype(jnp.bfloat16)
            forward_raised = jnp.einsum(
                "std,df->stf",
                forward_normed_two,
                w_up[layer_index],
                preferred_element_type=jnp.float32,
            )
            forward_active = gelu_tanh(forward_raised).astype(jnp.bfloat16)
            result = forward_hidden + jnp.einsum(
                "stf,fd->std",
                forward_active,
                w_down[layer_index],
                preferred_element_type=jnp.float32,
            )
            forward_kept = (
                residual,
                forward_normed,
                forward_padded,
                forward_short_out,
                forward_carried,
                forward_long_out,
                forward_gated_rows,
                forward_hidden,
                forward_normed_two,
                forward_raised,
                forward_active,
                results[1:],
            )
            residual = result
            kept = forward_kept
            saved.append(kept)
        outputs.append(residual * live_mask)
        grad_rows = cotangent[micro_index].astype(jnp.float32) * live_mask
        layer_bundles = [None] * layer_count
        for layer_index in reversed(range(layer_count)):
            grad_rows, bundle = backward_layer(grad_rows, saved[layer_index], layer_index)
            layer_bundles[layer_index] = bundle
        input_grads.append(grad_rows)
        running = add_tree(running, layer_bundles)
    mats = [
        jnp.stack([running[layer_index][0][member] for layer_index in range(layer_count)])
        for member in range(4)
    ]
    vecs = [
        jnp.stack([running[layer_index][1][member] for layer_index in range(layer_count)])
        for member in range(6)
    ]
    filter_parts = [
        filter_grads(running[layer_index][2][0], running[layer_index][2][1], layer_index)
        for layer_index in range(layer_count)
    ]
    filt_parts = [
        jnp.stack([filter_parts[layer_index][member] for layer_index in range(layer_count)])
        for member in range(4)
    ]
    mat_done = (
        lax.psum_scatter(
            mats[0].astype(jnp.bfloat16), "seq", scatter_dimension=1, tiled=True
        ).astype(jnp.float32),
        lax.psum_scatter(
            mats[1].astype(jnp.bfloat16), "seq", scatter_dimension=1, tiled=True
        ).astype(jnp.float32),
        lax.psum_scatter(
            mats[2].astype(jnp.bfloat16), "seq", scatter_dimension=1, tiled=True
        ).astype(jnp.float32),
        lax.psum_scatter(
            mats[3].astype(jnp.bfloat16), "seq", scatter_dimension=2, tiled=True
        ).astype(jnp.float32),
    )
    small_done = lax.psum(
        (
            vecs[0],
            vecs[1],
            vecs[2],
            vecs[3],
            vecs[4],
            vecs[5],
            filt_parts[0],
            filt_parts[1],
            filt_parts[2],
            filt_parts[3],
        ),
        ("seq", "tok"),
    )
    reduced = (tuple(mat_done), tuple(small_done))
    mat_done, small_done = reduced
    return (
        jnp.stack(outputs),
        jnp.stack(input_grads),
        small_done[0],
        small_done[1],
        mat_done[0],
        small_done[2],
        small_done[6],
        small_done[7],
        small_done[8],
        small_done[9],
        small_done[3],
        mat_done[1],
        small_done[4],
        small_done[5],
        mat_done[2],
        mat_done[3],
    )


MIB = 1 << 20
MESH = pl.DeviceIdType.MESH


def mm(left, right):
    return jnp.dot(left, right, preferred_element_type=jnp.float32)


def mm_nt(left, right):
    return lax.dot_general(left, right, (((1,), (1,)), ((), ())), preferred_element_type=jnp.float32)


def mm_tn(left, right):
    return lax.dot_general(left, right, (((0,), (0,)), ((), ())), preferred_element_type=jnp.float32)


def f32(values):
    return values.astype(jnp.float32)


def bf(values):
    return values.astype(jnp.bfloat16)


def row_shift(values, distance):
    rows = values.shape[0]
    index = lax.broadcasted_iota(jnp.int32, values.shape, 0)
    rolled = pltpu.roll(values, distance % rows, 0)
    kept = index >= distance if distance > 0 else index < rows + distance
    return jnp.where(kept, rolled, 0.0)


def standardised(values):
    mean = jnp.mean(values, axis=-1, keepdims=True)
    centred = values - mean
    scale = lax.rsqrt(jnp.mean(centred * centred, axis=-1, keepdims=True) + NORM_EPS)
    return centred * scale, scale


def norm_backward(values, gain, upstream):
    xh, scale = standardised(values)
    dxh = upstream * gain
    part = scale * (
        dxh - jnp.mean(dxh, axis=-1, keepdims=True) - xh * jnp.mean(dxh * xh, axis=-1, keepdims=True)
    )
    return part, jnp.sum(upstream * xh, axis=0, keepdims=True), jnp.sum(upstream, axis=0, keepdims=True)


def gelu_parts(values):
    slope = math.sqrt(2.0 / math.pi)
    square = values * values
    bent = jnp.tanh(slope * values * (1.0 + 0.044715 * square))
    half = 0.5 * (1.0 + bent)
    inner = slope * (1.0 + (3.0 * 0.044715) * square)
    return values * half, half + 0.5 * values * (1.0 - bent * bent) * inner


def spectral_table(length):
    k = np.arange(length, dtype=np.int64)[:, None]
    t = np.arange(length, dtype=np.int64)[None, :]
    angle = ((2 * k + 1) * t % (4 * length)).astype(np.float64) * (2.0 * math.pi / (4 * length))
    return np.concatenate([np.cos(angle), -np.sin(angle)], axis=0).astype(jnp.bfloat16)


def whole(shape):
    return pl.BlockSpec(shape, lambda j: (0,) * len(shape), pipeline_mode=pl.Buffered(1))


VECS = 14


def vector(ref, layer, k):
    return ref[VECS * layer + k : VECS * layer + k + 1, :]


def short_taps(ref, layer):
    return [ref[VECS * layer + 5 + 3 * p : VECS * layer + 8 + 3 * p, :] for p in range(3)]


ANY = pl.BlockSpec(memory_space=pl.ANY)


def sds(shape, kind):
    return jax.ShapeDtypeStruct(shape, kind)


class Place:
    def __init__(self):
        s, t = lax.axis_index("seq"), lax.axis_index("tok")
        self.depth = lax.axis_size("seq") // 2
        self.z, self.core, self.y, self.x = s // 2, s % 2, t // 2, t % 2
        self.s, self.t = s, t
        self.over_core = (2 * self.z + 1 - self.core, t)
        self.over_x = (s, 2 * self.y + 1 - self.x)
        self.over_y = (s, 2 * (1 - self.y) + self.x)
        self.over_z = [(2 * ((self.z + d) % self.depth) + self.core, t) for d in range(1, self.depth)]
        self.from_z = [(2 * ((self.z + self.depth - d) % self.depth) + self.core, t) for d in range(1, self.depth)]


def greet(partners):
    barrier = pltpu.get_barrier_semaphore()
    for partner in partners:
        pl.semaphore_signal(barrier, inc=1, device_id=partner, device_id_type=MESH)
    pl.semaphore_wait(barrier, len(partners))


def remote(source, target, sent, landed, device):
    return pltpu.make_async_remote_copy(
        src_ref=source, dst_ref=target, send_sem=sent, recv_sem=landed, device_id=device, device_id_type=MESH
    )


def other_first(place, s, piece):
    half = place.depth * piece
    mine = (s % 2 + place.core + 1) % 2
    return pl.multiple_of(mine * half + (s // 2) * piece, 16)


def store_rows(place, target, values):
    piece = values.shape[0] // (2 * place.depth)
    for s in range(2 * place.depth):
        target[pl.ds(other_first(place, s, piece), piece), :] = values[s * piece : (s + 1) * piece]


class Transpose:
    def __init__(self, place, source, target, sent, landed, own, gathering):
        self.place, self.source, self.target, self.sent, self.landed, self.own = place, source, target, sent, landed, own
        self.gathering = gathering
        self.partners = [place.over_x, place.over_y, (place.s, 2 * (1 - place.y) + 1 - place.x)]

    def block(self, ref, k, flat):
        if not flat:
            return ref.at[k]
        rows = ref.shape[0] // 4
        return ref.at[pl.ds(pl.multiple_of(k * rows, rows), rows)]

    def copies(self):
        me = self.place.t
        flat_in, flat_out = not self.gathering, self.gathering
        target = self.block(self.target, me, flat_out)
        out = [
            remote(self.block(self.source, device[1], flat_in), target, self.sent.at[k], self.landed.at[k], device)
            for k, device in enumerate(self.partners)
        ]
        return out + [pltpu.make_async_copy(self.block(self.source, me, flat_in), target, self.own)]

    def start(self):
        for copy in self.copies():
            copy.start()

    def wait(self):
        for copy in self.copies():
            copy.wait()


TRANSPOSE_SEMS = [pltpu.SemaphoreType.DMA((3,)), pltpu.SemaphoreType.DMA((3,)), pltpu.SemaphoreType.DMA]


def sine_cosine(angle):
    turns = jnp.floor(angle * (2.0 / math.pi) + 0.5)
    rest = ((angle - turns * 1.5703125) - turns * 4.837512969970703e-4) - turns * 7.549789948768648e-8
    square = rest * rest
    sine = rest + rest * square * (
        -1.6666654611e-1 + square * (8.3321608736e-3 + square * -1.9515295891e-4)
    )
    cosine = 1.0 - 0.5 * square + square * square * (
        4.166664568298827e-2 + square * (-1.388731625493765e-3 + square * 2.443315711809948e-5)
    )
    quarter = turns - 4.0 * jnp.floor(turns * 0.25)
    odd = (quarter == 1.0) | (quarter == 3.0)
    sin_sign = jnp.where(quarter >= 2.0, -1.0, 1.0)
    cos_sign = jnp.where((quarter == 1.0) | (quarter == 2.0), -1.0, 1.0)
    return sin_sign * jnp.where(odd, cosine, sine), cos_sign * jnp.where(odd, sine, cosine)


def decay(delta, length):
    time = lax.broadcasted_iota(jnp.int32, (length, delta.shape[1]), 0).astype(jnp.float32) * (1.0 / (length - 1))
    return jnp.exp(-time * delta) + MOD_SHIFT


def front_body(x_in, features_ref, net_ref, w3_ref, delta_ref, table_ref, x_out, filt_ref, taps_ref, sent, landed, own):
    place = Place()
    layers, units = w3_ref.shape[:2]
    length = table_ref.shape[1]
    move = Transpose(place, x_in, x_out, sent, landed, own, True)
    greet(move.partners)
    move.start()
    def high(a, b):
        top = bf(a)
        return mm(top, bf(b)) + mm(bf(a - f32(top)), bf(b))

    wide = lambda parts: jnp.concatenate(parts, axis=1)
    freq = [wide([net_ref[layer, 40 + k : 41 + k, :] for layer in range(layers)]) for k in range(2)]
    a1 = wide([high(features_ref[...], net_ref[layer, 0:40, :]) for layer in range(layers)])
    s1, c1 = sine_cosine(freq[0] * a1)
    a2 = wide([
        high(s1[:, units * layer : units * (layer + 1)], net_ref[layer, 48:112, :]) for layer in range(layers)
    ])
    s2, c2 = sine_cosine(freq[1] * a2)
    for k, values in enumerate((s1, s2, c1 * freq[0], c1 * a1, c2 * freq[1], c2 * a2)):
        filt_ref[k] = bf(values)
    envelope = decay(delta_ref[...], length)
    for layer in range(layers):
        taps = high(s2[:, units * layer : units * (layer + 1)], w3_ref[layer]) * envelope
        taps_ref[layer] = bf(mm(table_ref[...], bf(taps)) * (1.0 / length))
    move.wait()


def front(collective, x_in, features, net, w3, delta, table):
    slots, rows, width = x_in.shape
    layers, units, _ = w3.shape
    length = slots * rows
    vm = pl.BlockSpec(memory_space=pltpu.VMEM)
    b16 = jnp.bfloat16
    return pl.pallas_call(
        front_body,
        in_specs=[ANY, vm, vm, vm, vm, vm],
        out_specs=[ANY, vm, vm],
        out_shape=[
            sds((length, width), b16), sds((6, length, layers * units), b16), sds((layers, 2 * length, width), b16),
        ],
        scratch_shapes=TRANSPOSE_SEMS,
        compiler_params=pltpu.CompilerParams(
            vmem_limit_bytes=48 * MIB, collective_id=collective, has_side_effects=True
        ),
        name="front",
    )(x_in, features, net, w3, delta, table)


def mixed_chunk(proj, kernel):
    return [
        kernel[p][0:1] * row_shift(proj[p], 2) + kernel[p][1:2] * row_shift(proj[p], 1) + kernel[p][2:3] * proj[p]
        for p in range(3)
    ]


def mixer_forward_body(layer, carry, *refs):
    refs = list(refs)
    take = lambda n: [refs.pop(0) for _ in range(n)]
    r_ref, vec_ref, cut_ref, w0_ref, w1_ref, w2_ref, table_ref, taps_ref, wo_ref = take(9)
    moving_in = take(1)[0] if carry else None
    hidden_ref, normed_ref, proj_ref, signal_ref, long_ref = take(5)
    if carry:
        moved_out, sent, landed, own = take(4)
        move = Transpose(Place(), moving_in, moved_out, sent, landed, own, True)
    length = r_ref.shape[0]
    j = pl.program_id(0)

    @pl.when(j == 0)
    def _():
        if carry:
            greet(move.partners)
            move.start()
        r = f32(r_ref[...])
        xh, _ = standardised(r)
        normed_ref[...] = bf(xh * vector(vec_ref, layer, 0) + vector(vec_ref, layer, 1))
        hidden_ref[...] = r

    normed = normed_ref[...]
    proj = [mm(normed, w_ref[...]) for w_ref in (w0_ref, w1_ref, w2_ref)]
    for p in range(3):
        proj_ref[p] = bf(proj[p])
    gate_out, gate_in, vals = mixed_chunk(proj, short_taps(cut_ref, layer))
    carried = vals * gate_in
    both = mm(table_ref[...], bf(carried))
    re, im = both[:length], both[length:]
    signal_ref[...] = bf(both)
    tap_re, tap_im = f32(taps_ref[:length]), f32(taps_ref[length:])
    out = mm_tn(table_ref[:length], bf(re * tap_re - im * tap_im))
    out += mm_tn(table_ref[length:], bf(re * tap_im + im * tap_re))
    long_out = out + vector(cut_ref, layer, 4) * carried
    long_ref[...] = bf(long_out)
    hidden_ref[...] += mm(bf(long_out * gate_out), wo_ref[...])

    if carry:
        @pl.when(j == pl.num_programs(0) - 1)
        def _():
            move.wait()


def mixer_forward(layer, collective, r, vecs, w_in, table, taps, w_out, *moving):
    length, width = r.shape
    chunk = 256
    steps = width // chunk
    carry = len(moving) > 0
    third = lambda p: pl.BlockSpec((None, width, chunk), lambda j: (layer, 0, p * steps + j))
    return pl.pallas_call(
        lambda *refs: mixer_forward_body(layer, carry, *refs),
        grid=(steps,),
        in_specs=[
            whole((length, width)), whole(vecs.shape), pl.BlockSpec((vecs.shape[0], chunk), lambda j: (0, j)),
            third(0), third(1), third(2),
            whole((2 * length, length)),
            pl.BlockSpec((None, 2 * length, chunk), lambda j: (layer, 0, j)),
            pl.BlockSpec((None, chunk, width), lambda j: (layer, j, 0)),
        ] + [ANY] * len(moving),
        out_specs=[
            whole((length, width)), whole((length, width)),
            pl.BlockSpec((3, length, chunk), lambda j: (0, 0, j)),
            pl.BlockSpec((2 * length, chunk), lambda j: (0, j)),
            pl.BlockSpec((length, chunk), lambda j: (0, j)),
        ] + [ANY] * len(moving),
        out_shape=[
            sds((length, width), jnp.float32), sds((length, width), jnp.bfloat16),
            sds((3, length, width), jnp.bfloat16), sds((2 * length, width), jnp.bfloat16),
            sds((length, width), jnp.bfloat16),
        ] + ([sds((length, width), jnp.bfloat16)] if carry else []),
        scratch_shapes=TRANSPOSE_SEMS if carry else [],
        compiler_params=pltpu.CompilerParams(
            vmem_limit_bytes=60 * MIB, **(dict(collective_id=collective, has_side_effects=True) if carry else {})
        ),
        cost_estimate=pl.CostEstimate(
            flops=2 * length * width * (4 * width + 4 * length), bytes_accessed=30 * MIB, transcendentals=0
        ),
        name="mixer_forward",
    )(r, vecs, vecs, w_in, w_in, w_in, table, taps, w_out, *moving)


def ffn_forward_body(layer, last, *refs):
    hidden_ref, vec_ref, up_ref, down_ref = refs[:4]
    if last:
        live_ref, out_ref, normed_ref, raised_ref, r_ref = refs[4:]
    else:
        r_ref, normed_ref, raised_ref = refs[4:]

    @pl.when(pl.program_id(0) == 0)
    def _():
        hidden = hidden_ref[...]
        xh, _ = standardised(hidden)
        normed_ref[...] = bf(xh * vector(vec_ref, layer, 2) + vector(vec_ref, layer, 3))
        r_ref[...] = hidden

    raised = mm(normed_ref[...], up_ref[...])
    raised_ref[...] = bf(raised)
    r_ref[...] += mm(bf(gelu_parts(raised)[0]), down_ref[...])

    if last:
        @pl.when(pl.program_id(0) == pl.num_programs(0) - 1)
        def _():
            out_ref[...] = bf(r_ref[...] * live_ref[0, 0])


SCALAR = pl.BlockSpec(memory_space=pltpu.SMEM)


def ffn_forward(layer, hidden, vecs, w_up, w_down, *live):
    length, width = hidden.shape
    inner = w_up.shape[2]
    chunk = inner // 4
    last = len(live) > 0
    return pl.pallas_call(
        lambda *refs: ffn_forward_body(layer, last, *refs),
        grid=(inner // chunk,),
        in_specs=[
            whole((length, width)), whole(vecs.shape),
            pl.BlockSpec((None, width, chunk), lambda j: (layer, 0, j)),
            pl.BlockSpec((None, chunk, width), lambda j: (layer, j, 0)),
        ] + [SCALAR] * len(live),
        out_specs=[
            whole((length, width)), whole((length, width)), pl.BlockSpec((length, chunk), lambda j: (0, j)),
        ],
        out_shape=[
            sds((length, width), jnp.bfloat16 if last else jnp.float32), sds((length, width), jnp.bfloat16),
            sds((length, inner), jnp.bfloat16),
        ],
        scratch_shapes=[pltpu.VMEM((length, width), jnp.float32)] if last else [],
        compiler_params=pltpu.CompilerParams(vmem_limit_bytes=60 * MIB),
        cost_estimate=pl.CostEstimate(
            flops=4 * length * width * inner, bytes_accessed=26 * MIB, transcendentals=length * inner
        ),
        name="ffn_forward",
    )(hidden, vecs, w_up, w_down, *live)


def ffn_backward_body(layer, carry, *refs):
    refs = list(refs)
    take = lambda n: [refs.pop(0) for _ in range(n)]
    g_ref, hidden_ref, vec_ref, normed_ref, raised_ref, up_ref, down_ref = take(7)
    zin_ref, min_ref = take(2) if carry else (None, None)
    live_ref = None if carry else take(1)[0]
    upstream = lambda: g_ref[...] if carry else f32(g_ref[...]) * live_ref[0, 0]
    out_ref, gain_grad_ref, bias_grad_ref, c_out, w_out = take(5)
    zfin_ref, wmix_ref = take(2) if carry else (None, None)
    g16_ref, g16t_ref, normed_t_ref, give, got, c_ref, s1, core_s, core_r, s1_s, s1_r, out_sem = take(12)
    if carry:
        zgot, zown, mgot, mown, z_s, z_r, m_s, m_r, own_sem = take(9)
    j = pl.program_id(0)
    steps = pl.num_programs(0)
    width = g_ref.shape[1]
    place = Place()
    half = c_ref.shape[1]
    mcols = width // 2

    def z_sends():
        piece = [remote(zin_ref.at[:, (place.z + d) % place.depth], zgot.at[d - 1], z_s.at[d - 1], z_r.at[d - 1],
                        place.over_z[d - 1]) for d in range(1, place.depth)]
        return piece

    def m_sends():
        sends = []
        for k in range(2):
            sends.append(remote(min_ref.at[2 * k + 1 - place.x, :, pl.ds(0, mcols)], mgot.at[0, k], m_s.at[0, k],
                                m_r.at[0, k], place.over_x))
            sends.append(remote(min_ref.at[2 * (1 - place.y) + k, :, pl.ds(mcols, mcols)], mgot.at[1, k], m_s.at[1, k],
                                m_r.at[1, k], place.over_y))
        return sends

    def own_copies():
        copies = [pltpu.make_async_copy(zin_ref.at[:, place.z], zown, own_sem.at[4])]
        for k in range(2):
            copies.append(pltpu.make_async_copy(min_ref.at[2 * k + place.x, :, pl.ds(0, mcols)], mown.at[0, k],
                                                own_sem.at[k]))
            copies.append(pltpu.make_async_copy(min_ref.at[2 * place.y + k, :, pl.ds(mcols, mcols)], mown.at[1, k],
                                                own_sem.at[2 + k]))
        return copies

    def core_send(slot):
        return remote(give.at[slot], got.at[slot], core_s.at[slot], core_r.at[slot], place.over_core)

    def s1_send(side, t):
        device = place.over_x if side == 0 else place.over_y
        return remote(c_ref.at[t, :, pl.ds(side * width, width)], s1.at[side], s1_s.at[side], s1_r.at[side], device)

    def c_copy(t):
        return pltpu.make_async_copy(c_ref.at[t], c_out.at[t], out_sem.at[t])

    def finish(t, slot):
        core_send(slot).wait_recv()
        c_ref[t] = bf(f32(c_ref[t]) + f32(got[slot]))
        c_copy(t).start()

    @pl.when(j == 0)
    def _():
        greet([place.over_core, place.over_x, place.over_y] + (place.over_z if carry else []))
        if carry:
            for copy in z_sends() + m_sends() + own_copies():
                copy.start()
        g16 = bf(upstream())
        g16_ref[...] = g16
        store_rows(place, g16t_ref, g16.T)
        store_rows(place, normed_t_ref, normed_ref[...].T)
        out_ref[...] = jnp.zeros_like(out_ref)

    @pl.when(j == 1)
    def _():
        finish(0, 0)

        @pl.when(place.x == 1)
        def _():
            s1_send(0, 0).start()

        @pl.when(place.y == 1)
        def _():
            s1_send(1, 0).start()

    @pl.when(j == 2)
    def _():
        finish(3, 1)

        @pl.when(place.x == 0)
        def _():
            s1_send(0, 3).start()

        @pl.when(place.y == 0)
        def _():
            s1_send(1, 3).start()

    @pl.when(j == 3)
    def _():
        finish(2, 0)

    active, slope = gelu_parts(f32(raised_ref[...]))
    active = bf(active)
    raised_grad = bf(mm_nt(g16_ref[...], down_ref[...]) * slope)
    slot = j % 2

    @pl.when(j >= 2)
    def _():
        core_send(slot).wait_send()

    t = (steps - j) % steps
    for side, (left, right) in enumerate(((normed_t_ref, raised_grad), (g16t_ref, active))):
        product = bf(mm(left[...], right))
        give[slot, :, side * width : (side + 1) * width] = product[:half]
        c_ref[t, :, side * width : (side + 1) * width] = product[half:]
    core_send(slot).start()
    out_ref[...] += mm_nt(raised_grad, up_ref[...])

    @pl.when(j == steps - 1)
    def _():
        part, gain_grad, bias_grad = norm_backward(hidden_ref[...], vector(vec_ref, layer, 2), out_ref[...])
        out_ref[...] = upstream() + part
        gain_grad_ref[...] = gain_grad
        bias_grad_ref[...] = bias_grad
        finish(1, 1)
        for k in range(2):
            s1_send(k, 0).wait_recv()
        w_out[0] = bf(f32(c_ref[3 * place.x, :, :width]) + f32(s1[0]))
        w_out[1] = bf(f32(c_ref[3 * place.y, :, width:]) + f32(s1[1]))
        if carry:
            for copy in own_copies():
                copy.wait()
            for copy in z_sends() + m_sends():
                copy.wait()
            total = f32(zown[...])
            for d in range(place.depth - 1):
                total += f32(zgot[d])
            zfin_ref[...] = total
            for side in range(2):
                for k in range(2):
                    wmix_ref[side, k] = bf(f32(mown[side, k]) + f32(mgot[side, k]))
        for k in range(2):
            s1_send(k, 0).wait_send()
            core_send(k).wait_send()
        for k in range(steps):
            c_copy(k).wait()


def ffn_backward(layer, carry, collective, g, hidden, vecs, normed, raised, w_up, w_down, *carried):
    length, width = g.shape
    inner = w_up.shape[2]
    chunk = inner // 4
    depth = lax.axis_size("seq") // 2
    piece = width // (2 * depth)
    half = depth * piece
    b16, b32, dma = jnp.bfloat16, jnp.float32, pltpu.SemaphoreType.DMA
    order = lambda j: (4 - j) % 4
    return pl.pallas_call(
        lambda *refs: ffn_backward_body(layer, carry, *refs),
        grid=(4,),
        in_specs=[
            whole((length, width)), whole((length, width)), whole(vecs.shape), whole((length, width)),
            pl.BlockSpec((length, chunk), lambda j: (0, order(j))),
            pl.BlockSpec((None, width, chunk), lambda j: (layer, 0, order(j))),
            pl.BlockSpec((None, chunk, width), lambda j: (layer, order(j), 0)),
        ] + ([ANY] * len(carried) if carry else [SCALAR]),
        out_specs=[whole((length, width)), whole((1, width)), whole((1, width)), ANY, whole((2, half, width))]
        + ([whole((2, piece, width)), whole((2, 2, half, width // 2))] if carry else []),
        out_shape=[
            sds((length, width), b32), sds((1, width), b32), sds((1, width), b32), sds((4, half, 2 * chunk), b16),
            sds((2, half, chunk), b16),
        ] + ([sds((2, piece, chunk), b32), sds((2, 2, half, width // 2), b16)] if carry else []),
        scratch_shapes=[
            pltpu.VMEM((length, width), b16), pltpu.VMEM((width, length), b16), pltpu.VMEM((width, length), b16),
            pltpu.VMEM((2, half, 2 * chunk), b16), pltpu.VMEM((2, half, 2 * chunk), b16),
            pltpu.VMEM((4, half, 2 * chunk), b16), pltpu.VMEM((2, half, chunk), b16),
            dma((2,)), dma((2,)), dma((2,)), dma((2,)), dma((4,)),
        ] + ([
            pltpu.VMEM((depth - 1, 2, piece, chunk), b16), pltpu.VMEM((2, piece, chunk), b16),
            pltpu.VMEM((2, 2, half, width // 2), b16), pltpu.VMEM((2, 2, half, width // 2), b16),
            dma((depth - 1,)), dma((depth - 1,)), dma((2, 2)), dma((2, 2)), dma((5,)),
        ] if carry else []),
        compiler_params=pltpu.CompilerParams(
            vmem_limit_bytes=62 * MIB, collective_id=collective, has_side_effects=True
        ),
        cost_estimate=pl.CostEstimate(
            flops=8 * length * width * inner, bytes_accessed=40 * MIB, transcendentals=length * inner
        ),
        name="ffn_backward",
    )(g, hidden, vecs, normed, raised, w_up, w_down, *carried)


def mixer_backward_body(layer, carry, last, *refs):
    refs = list(refs)
    take = lambda n: [refs.pop(0) for _ in range(n)]
    (hg_ref, r_ref, vec_ref, cut_ref, normed_ref, proj_ref, signal_ref, long_ref, taps_ref, table_ref, wo_ref, w0_ref,
     w1_ref, w2_ref, c_in, w1_in) = take(16)
    wmix_ref, moving_in = (take(1)[0], None) if carry else (None, take(1)[0])
    g_out, c_out, zout_ref, taps_grad_ref, short_grad_ref, skip_grad_ref, gain_grad_ref, bias_grad_ref = take(8)
    mfin_ref, moved_out = (take(1)[0], None) if carry else (None, take(1)[0])
    (og_ref, gated_ref, pg_ref, both_ref, got, s1, wkeep, s2, core_s, core_r, s1_s, s1_r, s2_s, s2_r, own_sem,
     out_sem) = take(16)
    if carry:
        mkeep, m2, mz, mzgot, m2_s, m2_r, mz_s, mz_r, m_sem = take(9)
    g_ref, g16_ref = (take(1)[0], g_out) if last else (g_out, None)
    move_sems = None if carry else take(3)
    j = pl.program_id(0)
    steps = pl.num_programs(0)
    length, width = hg_ref.shape
    place = Place()
    half = got.shape[1]
    piece = half // place.depth
    x, y = place.x, place.y
    move = None if carry else Transpose(place, moving_in, moved_out, *move_sems, False)
    over_both = (place.s, 2 * (1 - y) + 1 - x)

    def s1_sends():
        return [
            remote(c_in.at[1 + x, :, pl.ds(0, width)], s1.at[0], s1_s.at[0], s1_r.at[0], place.over_x),
            remote(c_in.at[2 - y, :, pl.ds(width, width)], s1.at[1], s1_s.at[1], s1_r.at[1], place.over_y),
        ]

    def own_copies():
        return [
            pltpu.make_async_copy(w1_in.at[0], wkeep.at[0, x], own_sem.at[0]),
            pltpu.make_async_copy(w1_in.at[1], wkeep.at[1, y], own_sem.at[1]),
            pltpu.make_async_copy(c_in.at[2 - x, :, pl.ds(0, width)], wkeep.at[0, 1 - x], own_sem.at[2]),
            pltpu.make_async_copy(c_in.at[1 + y, :, pl.ds(width, width)], wkeep.at[1, 1 - y], own_sem.at[3]),
        ]

    def s2_sends():
        return [
            remote(wkeep.at[0, 1 - y], s2.at[0], s2_s.at[0], s2_r.at[0], place.over_y),
            remote(wkeep.at[1, 1 - x], s2.at[1], s2_s.at[1], s2_r.at[1], place.over_x),
        ]

    def m2_sends():
        return [
            remote(wmix_ref.at[0, 1 - y], m2.at[0], m2_s.at[0], m2_r.at[0], place.over_y),
            remote(wmix_ref.at[1, 1 - x], m2.at[1], m2_s.at[1], m2_r.at[1], place.over_x),
        ]

    def m_copies():
        return [
            pltpu.make_async_copy(wmix_ref.at[0, y], mkeep.at[0], m_sem.at[0]),
            pltpu.make_async_copy(wmix_ref.at[1, x], mkeep.at[1], m_sem.at[1]),
        ]

    def mz_sends():
        return [
            remote(mz.at[:, (place.z + d) % place.depth], mzgot.at[d - 1], mz_s.at[d - 1], mz_r.at[d - 1],
                   place.over_z[d - 1])
            for d in range(1, place.depth)
        ]

    def core_send(t):
        return remote(both_ref.at[t, pl.ds(0, half)], got.at[t], core_s.at[t], core_r.at[t], place.over_core)

    def c_copy(t):
        return pltpu.make_async_copy(both_ref.at[t, pl.ds(half, half)], c_out.at[t], out_sem.at[t])

    @pl.when(j == 0)
    def _():
        greet([place.over_core, place.over_x, place.over_y] + (place.over_z if carry else [over_both]))
        if carry:
            for copy in m2_sends() + m_copies():
                copy.start()
        for copy in s1_sends() + own_copies():
            copy.start()
        if not carry:
            move.start()
        og_ref[...] = bf(hg_ref[...])
        g_ref[...] = jnp.zeros_like(g_ref)

    @pl.when(j == 2)
    def _():
        if carry:
            for copy in m2_sends() + m_copies():
                copy.wait()
            for side in range(2):
                total = bf(f32(mkeep[side]) + f32(m2[side]))
                for k in range(place.depth):
                    mz[side, k] = total[k * piece : (k + 1) * piece]
            for copy in mz_sends():
                copy.start()
        for copy in s1_sends() + own_copies():
            copy.wait()
        wkeep[0, 1 - x] = bf(f32(wkeep[0, 1 - x]) + f32(s1[0]))
        wkeep[1, 1 - y] = bf(f32(wkeep[1, 1 - y]) + f32(s1[1]))
        for copy in s2_sends():
            copy.start()

    @pl.when(j < steps - 1)
    def _():
        chunk = long_ref.shape[1]
        proj = [f32(proj_ref[p]) for p in range(3)]
        kernel = short_taps(cut_ref, layer)
        gate_out, gate_in, vals = mixed_chunk(proj, kernel)
        carried = vals * gate_in
        long_out = f32(long_ref[...])
        skip = vector(cut_ref, layer, 4)
        gated_ref[:, pl.ds(pl.multiple_of(j * chunk, chunk), chunk)] = bf(long_out * gate_out)
        gated_grad = mm_nt(og_ref[...], wo_ref[...])
        long_grad = gated_grad * gate_out
        skip_grad_ref[...] = jnp.sum(carried * long_grad, axis=0, keepdims=True)
        both = mm(table_ref[...], bf(long_grad))
        up_re, up_im = both[:length], both[length:]
        tap_re, tap_im = f32(taps_ref[:length]), f32(taps_ref[length:])
        out = mm_tn(table_ref[:length], bf(up_re * tap_re + up_im * tap_im))
        out += mm_tn(table_ref[length:], bf(up_im * tap_re - up_re * tap_im))
        carried_grad = out + skip * long_grad
        sig_re, sig_im = f32(signal_ref[:length]), f32(signal_ref[length:])
        cross = mm_tn(table_ref[:length], bf(up_re * sig_re + up_im * sig_im))
        cross += mm_tn(table_ref[length:], bf(up_im * sig_re - up_re * sig_im))
        taps_grad_ref[...] = cross * (1.0 / length)
        upstream = None
        for p, part in enumerate((gated_grad * long_out, carried_grad * vals, carried_grad * gate_in)):
            one, two = row_shift(part, -1), row_shift(part, -2)
            projected_grad = bf(kernel[p][2:3] * part + kernel[p][1:2] * one + kernel[p][0:1] * two)
            for tap, moved in enumerate((two, one, part)):
                short_grad_ref[p, tap : tap + 1, :] = jnp.sum(moved * proj[p], axis=0, keepdims=True)
            pg_ref[:, pl.ds(pl.multiple_of(p * width + j * chunk, chunk), chunk)] = projected_grad
            term = mm_nt(projected_grad, (w0_ref, w1_ref, w2_ref)[p][...])
            upstream = term if upstream is None else upstream + term
        g_ref[...] += upstream

    @pl.when(j == steps - 1)
    def _():
        in_cols, out_cols = 3 * width // 4, width // 4
        for t in range(4):
            rights = pg_ref[:, in_cols * t : in_cols * (t + 1)], og_ref[:, out_cols * t : out_cols * (t + 1)]
            products = [bf(mm_tn(left[...], right)) for left, right in zip((normed_ref, gated_ref), rights)]
            store_rows(place, both_ref.at[t], jnp.concatenate(products, axis=1))
            core_send(t).start()
        part, gain_grad, bias_grad = norm_backward(f32(r_ref[...]), vector(vec_ref, layer, 0), g_ref[...])
        total = hg_ref[...] + part
        if last:
            g16_ref[...] = bf(total)
        else:
            g_ref[...] = total
        gain_grad_ref[...] = gain_grad
        bias_grad_ref[...] = bias_grad
        for t in range(4):
            core_send(t).wait()
            both_ref[t, half:] = bf(f32(both_ref[t, half:]) + f32(got[t]))
            c_copy(t).start()
        if carry:
            for copy in mz_sends():
                copy.wait()
            for side in range(2):
                total = f32(mz[side, place.z])
                for d in range(place.depth - 1):
                    total += f32(mzgot[d, side])
                mfin_ref[side] = total
        for copy in s2_sends():
            copy.wait()
        for side, keep in enumerate((y, x)):
            total = bf(f32(wkeep[side, keep]) + f32(s2[side]))
            for k in range(place.depth):
                zout_ref[side, k] = total[k * piece : (k + 1) * piece]
        for t in range(4):
            c_copy(t).wait()
        if not carry:
            move.wait()


def mixer_backward(
    layer, carry, last, collective, hidden_grad, r, vecs, normed, proj, signal, long_out, taps, table, w_out, w_in, ffn_c,
    ffn_w, carried
):
    length, width = r.shape
    chunk = 256
    steps = width // chunk
    depth = lax.axis_size("seq") // 2
    piece = width // (2 * depth)
    half = depth * piece
    at = lambda j: jnp.minimum(j, steps - 1)
    third = lambda p: pl.BlockSpec((None, width, chunk), lambda j: (layer, 0, p * steps + at(j)))
    b16, b32, dma = jnp.bfloat16, jnp.float32, pltpu.SemaphoreType.DMA
    return pl.pallas_call(
        lambda *refs: mixer_backward_body(layer, carry, last, *refs),
        grid=(steps + 1,),
        in_specs=[
            whole((length, width)), whole((length, width)), whole(vecs.shape),
            pl.BlockSpec((vecs.shape[0], chunk), lambda j: (0, at(j))), whole((length, width)),
            pl.BlockSpec((3, length, chunk), lambda j: (0, 0, at(j))),
            pl.BlockSpec((2 * length, chunk), lambda j: (0, at(j))),
            pl.BlockSpec((length, chunk), lambda j: (0, at(j))),
            pl.BlockSpec((None, 2 * length, chunk), lambda j: (layer, 0, at(j))),
            whole((2 * length, length)),
            pl.BlockSpec((None, chunk, width), lambda j: (layer, at(j), 0)),
            third(0), third(1), third(2),
        ] + [ANY] * 3,
        out_specs=[
            whole((length, width)), ANY, whole((2, depth, piece, width)),
            pl.BlockSpec((length, chunk), lambda j: (0, at(j))),
            pl.BlockSpec((3, 3, chunk), lambda j: (0, 0, at(j))),
            pl.BlockSpec((1, chunk), lambda j: (0, at(j))),
            whole((1, width)), whole((1, width)),
        ] + [whole((2, piece, width // 2)) if carry else ANY],
        out_shape=[
            sds((length, width), b16 if last else b32), sds((4, half, width), b16),
            sds((2, depth, piece, width), b16),
            sds((length, width), b32), sds((3, 3, width), b32), sds((1, width), b32), sds((1, width), b32),
            sds((1, width), b32),
        ] + [sds((2, piece, width // 2), b32) if carry else sds((4, length // 4, width), b16)],
        scratch_shapes=[
            pltpu.VMEM((length, width), b16), pltpu.VMEM((length, width), b16), pltpu.VMEM((length, 3 * width), b16),
            pltpu.VMEM((4, width, width), b16), pltpu.VMEM((4, half, width), b16),
            pltpu.VMEM((2, half, width), b16), pltpu.VMEM((2, 2, half, width), b16), pltpu.VMEM((2, half, width), b16),
            dma((4,)), dma((4,)), dma((2,)), dma((2,)), dma((2,)), dma((2,)), dma((4,)), dma((4,)),
        ] + ([
            pltpu.VMEM((2, half, width // 2), b16), pltpu.VMEM((2, half, width // 2), b16),
            pltpu.VMEM((2, depth, piece, width // 2), b16), pltpu.VMEM((depth - 1, 2, piece, width // 2), b16),
            dma((2,)), dma((2,)), dma((depth - 1,)), dma((depth - 1,)), dma((2,)),
        ] if carry else []) + ([pltpu.VMEM((length, width), b32)] if last else []) + ([] if carry else TRANSPOSE_SEMS),
        compiler_params=pltpu.CompilerParams(
            vmem_limit_bytes=63 * MIB, collective_id=collective, has_side_effects=True
        ),
        cost_estimate=pl.CostEstimate(
            flops=2 * length * width * (8 * width + 6 * length), bytes_accessed=50 * MIB, transcendentals=0
        ),
        name="mixer_backward",
    )(hidden_grad, r, vecs, vecs, normed, proj, signal, long_out, taps, table, w_out, w_in, w_in, w_in, ffn_c, ffn_w,
      carried)


SMALL = 128


def closing_body(
    z_in, c_in, g_in, t0_in, t1_in, v0, v1, v2, v3, v4, v5, v6, v7, v8, v9, v10, v11, features_ref, filt_ref, net_ref,
    w3_ref, delta_ref, zfin_ref, mfin_ref, agot, small_ref,
    zgot, zown, mgot, w, m2, mz, mzgot, tgrad, pack, cgot, xgot, xsum, ygot, ysum, zslot, total16, full,
    z_s, z_r, m_s, m_r, m2_s, m2_r, mz_s, mz_r, a_s, a_r, own_sem, sm_s, sm_r, zs_s, zs_r,
):
    place = Place()
    x, y, z, core = place.x, place.y, place.z, place.core
    cols = w.shape[3]
    piece = zown.shape[1]
    rows = agot.shape[1]
    over_both = (place.s, 2 * (1 - y) + 1 - x)
    m_sends = []
    for k in range(2):
        m_sends.append(remote(c_in.at[2 * k + 1 - x, :, pl.ds(0, cols)], mgot.at[0, k], m_s.at[0, k], m_r.at[0, k],
                              place.over_x))
        m_sends.append(remote(c_in.at[2 * (1 - y) + k, :, pl.ds(cols, cols)], mgot.at[1, k], m_s.at[1, k],
                              m_r.at[1, k], place.over_y))
    z_sends = [
        remote(z_in.at[:, (z + d) % place.depth], zgot.at[d - 1], z_s.at[d - 1], z_r.at[d - 1], place.over_z[d - 1])
        for d in range(1, place.depth)
    ]
    own = [pltpu.make_async_copy(z_in.at[:, z], zown, own_sem.at[4])]
    for k in range(2):
        own.append(pltpu.make_async_copy(c_in.at[2 * k + x, :, pl.ds(0, cols)], w.at[0, k], own_sem.at[k]))
        own.append(pltpu.make_async_copy(c_in.at[2 * y + k, :, pl.ds(cols, cols)], w.at[1, k], own_sem.at[2 + k]))
    loads = [
        pltpu.make_async_copy(t0_in, tgrad.at[0], own_sem.at[5]), pltpu.make_async_copy(t1_in, tgrad.at[1], own_sem.at[6]),
    ]
    part = lambda t: g_in.at[pl.ds(pl.multiple_of(t * rows, rows), rows)]
    home = pltpu.make_async_copy(part(place.t), agot.at[place.t], own_sem.at[8])

    def a_sends():
        out = []
        for k, device in enumerate((place.over_x, place.over_y, over_both)):
            out.append(remote(part(device[1]), agot.at[place.t], a_s.at[k], a_r.at[k], device))
        return out

    for copy in loads:
        copy.start()
    greet([place.over_core, place.over_x, place.over_y, over_both] + place.over_z)
    for copy in m_sends + z_sends + own + [home]:
        copy.start()

    units = w3_ref.shape[1]
    envelope = decay(delta_ref[...], tgrad.shape[1])
    pack[...] = jnp.zeros_like(pack)
    s1, s2 = filt_ref[0], filt_ref[1]
    u1, h1, u2, h2 = (f32(filt_ref[k]) for k in range(2, 6))
    wide = lambda parts: jnp.concatenate(parts, axis=1)
    for copy in loads:
        copy.wait()
    upstream = [bf(tgrad[layer] * envelope) for layer in range(2)]
    ds2 = wide([mm_nt(upstream[layer], w3_ref[layer]) for layer in range(2)])
    for layer in range(2):
        pack[layer, :64] = mm_tn(s2[:, units * layer : units * (layer + 1)], upstream[layer])
    da2 = ds2 * u2
    span = lambda v, layer: v[:, units * layer : units * (layer + 1)]
    ds1 = wide([mm_nt(bf(span(da2, layer)), bf(net_ref[layer, 48:112, :])) for layer in range(2)])
    da1 = ds1 * u1
    dw2 = wide([mm_tn(span(s1, layer), bf(span(da2, layer))) for layer in range(2)])
    dw1 = mm_tn(bf(features_ref[...]), bf(da1))
    freq = [jnp.sum(ds1 * h1, axis=0, keepdims=True), jnp.sum(ds2 * h2, axis=0, keepdims=True)]
    for k, block in enumerate((dw1[:24], jnp.concatenate([dw1[24:40], freq[0], freq[1], jnp.zeros((6, 128), jnp.float32)]),
                               dw2[:24], dw2[24:48], jnp.concatenate([dw2[48:64], jnp.zeros((8, 128), jnp.float32)]))):
        pack[0, 80:104, 128 * k : 128 * (k + 1)] = block
    vectors = ((v0, v1, v2, v3, v4, v5), (v6, v7, v8, v9, v10, v11))
    for layer in range(2):
        for k in range(5):
            pack[layer, 64 + k : 65 + k, :] = vectors[layer][k][...]
        for p in range(3):
            pack[layer, 69 + 3 * p : 72 + 3 * p, :] = vectors[layer][5][p]

    total16[0] = bf(pack[0])
    total16[1] = bf(pack[1])
    to_core = remote(total16.at[1 - core], cgot, sm_s.at[0], sm_r.at[0], place.over_core)
    to_core.start()
    to_core.wait()
    xsum[...] = bf(f32(total16[core]) + f32(cgot[...]))
    half, quarter = SMALL // 2, SMALL // 4
    side = lambda k, n: pl.ds(pl.multiple_of(k * n, n), n)
    to_x = remote(xsum.at[side(1 - x, half)], xgot, sm_s.at[1], sm_r.at[1], place.over_x)
    to_x.start()

    for copy in own + m_sends:
        copy.wait()
    for k in range(2):
        for n in range(2):
            w[k, n] = bf(f32(w[k, n]) + f32(mgot[k, n]))
    m2_sends = [
        remote(w.at[0, 1 - y], m2.at[0], m2_s.at[0], m2_r.at[0], place.over_y),
        remote(w.at[1, 1 - x], m2.at[1], m2_s.at[1], m2_r.at[1], place.over_x),
    ]
    for copy in m2_sends:
        copy.start()

    to_x.wait()
    ysum[...] = bf(f32(xsum[side(x, half)]) + f32(xgot[...]))
    to_y = remote(ysum.at[side(1 - y, quarter)], ygot, sm_s.at[2], sm_r.at[2], place.over_y)
    to_y.start()

    for copy in m2_sends:
        copy.wait()
    for copy in a_sends():
        copy.start()
    for k, keep in enumerate((y, x)):
        total = bf(f32(w[k, keep]) + f32(m2[k]))
        for n in range(place.depth):
            mz[k, n] = total[n * piece : (n + 1) * piece]
    mz_sends = [
        remote(mz.at[:, (z + d) % place.depth], mzgot.at[d - 1], mz_s.at[d - 1], mz_r.at[d - 1], place.over_z[d - 1])
        for d in range(1, place.depth)
    ]
    for copy in mz_sends:
        copy.start()

    to_y.wait()
    zslot[z] = bf(f32(ysum[side(y, quarter)]) + f32(ygot[...]))
    zs_sends = [
        remote(zslot.at[z], zslot.at[z], zs_s.at[d - 1], zs_r.at[d - 1], place.over_z[d - 1])
        for d in range(1, place.depth)
    ]
    for copy in zs_sends:
        copy.start()

    for copy in z_sends:
        copy.wait()
    total = f32(zown[...])
    for d in range(place.depth - 1):
        total += f32(zgot[d])
    zfin_ref[...] = total

    for copy in zs_sends:
        copy.wait()
    total = f32(zslot[0])
    for k in range(1, place.depth):
        total += f32(zslot[k])
    mine = pl.multiple_of(x * half + y * quarter, quarter)
    full[core, pl.ds(mine, quarter)] = bf(total)
    back_y = remote(full.at[core, pl.ds(mine, quarter)], full.at[core, pl.ds(mine, quarter)], sm_s.at[3], sm_r.at[3],
                    place.over_y)
    back_y.start()
    back_y.wait()
    back_x = remote(full.at[core, side(x, half)], full.at[core, side(x, half)], sm_s.at[4], sm_r.at[4], place.over_x)
    back_x.start()
    back_x.wait()
    back_core = remote(full.at[core], full.at[core], sm_s.at[5], sm_r.at[5], place.over_core)
    back_core.start()
    back_core.wait()
    small_ref[...] = f32(full[...])
    for copy in mz_sends:
        copy.wait()
    for k in range(2):
        total = f32(mz[k, z])
        for d in range(place.depth - 1):
            total += f32(mzgot[d, k])
        mfin_ref[k] = total
    home.wait()
    for copy in a_sends():
        copy.wait()


def closing(collective, ffn_z, mixer_c, grad, taps_grads, vectors, features, filt, net, w3, delta):
    _, depth, piece, width = ffn_z.shape
    length = grad.shape[0]
    half = depth * piece
    b16, b32, dma = jnp.bfloat16, jnp.float32, pltpu.SemaphoreType.DMA
    cols = width // 2
    vm = pl.BlockSpec(memory_space=pltpu.VMEM)
    return pl.pallas_call(
        closing_body,
        in_specs=[ANY] * 5 + [vm] * (len(vectors) + 5),
        out_specs=[vm, vm, ANY, vm],
        out_shape=[
            sds((2, piece, width), b32), sds((2, piece, cols), b32), sds((4, length // 4, width), b16),
            sds((2, SMALL, width), b32),
        ],
        scratch_shapes=[
            pltpu.VMEM((depth - 1, 2, piece, width), b16), pltpu.VMEM((2, piece, width), b16),
            pltpu.VMEM((2, 2, half, cols), b16), pltpu.VMEM((2, 2, half, cols), b16), pltpu.VMEM((2, half, cols), b16),
            pltpu.VMEM((2, depth, piece, cols), b16), pltpu.VMEM((depth - 1, 2, piece, cols), b16),
            pltpu.VMEM((2, length, width), b32),
            pltpu.VMEM((2, SMALL, width), b32), pltpu.VMEM((SMALL, width), b16), pltpu.VMEM((SMALL // 2, width), b16),
            pltpu.VMEM((SMALL, width), b16), pltpu.VMEM((SMALL // 4, width), b16), pltpu.VMEM((SMALL // 2, width), b16),
            pltpu.VMEM((depth, SMALL // 4, width), b16), pltpu.VMEM((2, SMALL, width), b16),
            pltpu.VMEM((2, SMALL, width), b16),
            dma((depth - 1,)), dma((depth - 1,)), dma((2, 2)), dma((2, 2)), dma((2,)), dma((2,)), dma((depth - 1,)),
            dma((depth - 1,)), dma((3,)), dma((3,)), dma((9,)), dma((6,)), dma((6,)), dma((depth - 1,)),
            dma((depth - 1,)),
        ],
        compiler_params=pltpu.CompilerParams(
            vmem_limit_bytes=56 * MIB, collective_id=collective, has_side_effects=True
        ),
        name="closing",
    )(ffn_z, mixer_c, grad, *taps_grads, *vectors, features, filt, net, w3, delta)


def assemble_body(
    out_in, grad_in, f0, f1, m0, m1, small, out_act, grad_x, g1, b1, w_in, short, w1, freq, w2, w3, skip, w_out, g2, b2,
    w_up, w_down,
):
    out_act[...] = f32(out_in[...])
    grad_x[...] = f32(grad_in[...])

    @pl.when(pl.program_id(0) == 0)
    def _():
        units = w2.shape[1]
        cols = m0.shape[2]
        split = w_in.shape[2]
        for layer, (f, m) in enumerate(((f0, m0), (f1, m1))):
            row = slice(layer, layer + 1)
            for k, ref in enumerate((g1, b1, g2, b2, skip)):
                ref[row, :] = small[layer, 64 + k : 65 + k, :]
            for p in range(3):
                for tap in range(3):
                    at = 69 + 3 * p + tap
                    width = small.shape[2]
                    short[layer, tap : tap + 1, p * width : (p + 1) * width] = small[layer, at : at + 1, :]
            lanes = lambda k: slice(128 * k + units * layer, 128 * k + units * (layer + 1))
            w1[layer] = jnp.concatenate([small[0, 80:104, lanes(0)], small[0, 80 : 80 + EMB - 24, lanes(1)]], axis=0)
            freq[layer] = small[0, 96:98, lanes(1)]
            w2[layer] = jnp.concatenate(
                [small[0, 80:104, lanes(2)], small[0, 80:104, lanes(3)], small[0, 80:96, lanes(4)]], axis=0
            )
            w3[layer] = small[layer, :64, :]
            w_in[layer] = jnp.concatenate([m[0], m[1][:, : split - cols]], axis=1)
            w_out[layer] = m[1][:, split - cols :]
            w_up[layer] = f[0]
            w_down[layer] = f[1].T


def assemble(out_act, grad_in, ffn, mixer, small, units):
    slots, rows, width = out_act.shape
    _, piece, cols = ffn[0].shape
    split = 3 * width // 4
    b32 = jnp.float32
    shapes = [
        (2, width), (2, width), (2, piece, split), (2, 3, 3 * width), (2, EMB, units), (2, 2, units), (2, units, units),
        (2, units, width), (2, width), (2, piece, width - split), (2, width), (2, width), (2, piece, cols),
        (2, cols, piece),
    ]
    block = pl.BlockSpec((None, rows, width), lambda j: (j, 0, 0))
    return pl.pallas_call(
        assemble_body,
        grid=(slots,),
        in_specs=[block, block] + [whole(v.shape) for v in (*ffn, *mixer, small)],
        out_specs=[block, block] + [whole(shape) for shape in shapes],
        out_shape=[sds((slots, rows, width), b32)] * 2 + [sds(shape, b32) for shape in shapes],
        compiler_params=pltpu.CompilerParams(vmem_limit_bytes=40 * MIB),
        name="assemble",
    )(out_act, grad_in, *ffn, *mixer, small)


def feature_table(length):
    bands = (EMB - 1) // 2
    step = np.arange(length, dtype=np.float64)[:, None]
    phases = 2.0 * math.pi / length * step * np.linspace(1e-4, bands - 1, bands)[None]
    parts = [step / (length - 1), np.cos(phases), -np.sin(phases), np.zeros((length, 40 - EMB))]
    return np.concatenate(parts, axis=1).astype(np.float32)


def whole_sequences(
    x_in, cotangent, counts, ln1_gain, ln1_bias, w_in, short_w, filt_w1, filt_freq, filt_w2, filt_w3, long_bias,
    w_out, ln2_gain, ln2_bias, w_up, w_down,
):
    micro_count, cap_size, tok_rows, width = x_in.shape
    slots = micro_count * cap_size
    layers = w_up.shape[0]
    toks = lax.axis_size("tok")
    length = tok_rows * toks
    me = lax.axis_index("tok")
    live = (me % cap_size < counts[me // cap_size, 0]).astype(jnp.float32).reshape(1, 1)
    table = jnp.asarray(spectral_table(length))
    features = jnp.asarray(feature_table(length))
    delta = jnp.asarray(
        np.abs(np.linspace(math.log(0.01) / 0.3, math.log(0.01) / 1.5, width, dtype=np.float64))[None].astype(np.float32)
    )
    stacked = jnp.stack([ln1_gain, ln1_bias, ln2_gain, ln2_bias, long_bias], axis=1)
    taps_rows = jnp.swapaxes(short_w.reshape(layers, 3, 3, width), 1, 2).reshape(layers, 9, width)
    vecs = f32(jnp.concatenate([stacked, taps_rows], axis=1)).reshape(layers * VECS, width)
    vecs = jnp.pad(vecs, ((0, -layers * VECS % 8), (0, 0)))
    rows = lambda v, n: jnp.pad(v, ((0, 0), (0, n - v.shape[1]), (0, 0)))
    net = f32(jnp.concatenate([rows(filt_w1, 40), rows(filt_freq, 8), filt_w2], axis=1))

    blocks = lambda v: v.reshape(slots, tok_rows, width)
    r, filt, spectra = front(2 * layers + 1, blocks(x_in), features, net, filt_w3, delta, table)
    kept = []
    for layer in range(layers):
        moving = (blocks(cotangent),) if layer == 0 else ()
        hidden, normed, proj, signal, long_out, *moved = mixer_forward(
            layer, 2 * layers + 2, r, vecs, w_in, table, spectra, w_out, *moving
        )
        upstream = moved[0] if moved else upstream
        result, normed_two, raised = ffn_forward(
            layer, hidden, vecs, w_up, w_down, *((live,) if layer == layers - 1 else ())
        )
        kept.append((r, hidden, normed, proj, signal, long_out, normed_two, raised))
        r = result

    grad = upstream
    vectors, taps_grads, done = [None] * layers, [None] * layers, {}
    carried_ffn, carried_mixer = (live,), r
    for layer in reversed(range(layers)):
        r, hidden, normed, proj, signal, long_out, normed_two, raised = kept[layer]
        carry = layer < layers - 1
        grad, grad_g2, grad_b2, ffn_c, ffn_w, *rest = ffn_backward(
            layer, carry, 2 * layer, grad, hidden, vecs, normed_two, raised, w_up, w_down, *carried_ffn
        )
        if carry:
            done["ffn", layer + 1], carried_mixer = rest
        grad, mixer_c, ffn_z, taps_grads[layer], grad_short, grad_skip, grad_g1, grad_b1, rest = mixer_backward(
            layer, carry, layer == 0, 2 * layer + 1, grad, r, vecs, normed, proj, signal, long_out, spectra, table, w_out,
            w_in, ffn_c, ffn_w, carried_mixer,
        )
        if carry:
            done["mixer", layer + 1] = rest
        else:
            out_act = rest
        carried_ffn = (ffn_z, mixer_c)
        vectors[layer] = (grad_g1, grad_b1, grad_g2, grad_b2, grad_skip, grad_short)
    done["ffn", 0], done["mixer", 0], grad_in, small = closing(
        2 * layers, *carried_ffn, grad, taps_grads, vectors[0] + vectors[1], features, filt, net, filt_w3, delta
    )
    pair = lambda kind: [done[kind, layer] for layer in range(layers)]
    out_act, grad_in, *grads = assemble(out_act, grad_in, pair("ffn"), pair("mixer"), small, filt_w2.shape[1])
    home = lambda v: v.reshape(micro_count, cap_size, tok_rows, width)
    return (home(out_act), home(grad_in), *grads)


def shards(*args):
    micro_count, cap_size = args[0].shape[:2]
    if lax.axis_size("tok") == 4 and micro_count * cap_size == 4:
        return whole_sequences(*args)
    return split_positions(*args)


def solution(mesh):
    return jax.shard_map(
        shards,
        mesh=mesh,
        in_specs=(
            P(None, "seq", "tok", None),
            P(None, "seq", "tok", None),
            P(None, "seq"),
            P(),
            P(),
            P(),
            P(),
            P(),
            P(),
            P(),
            P(),
            P(),
            P(),
            P(),
            P(),
            P(),
            P(),
        ),
        out_specs=(
            P(None, "seq", "tok", None),
            P(None, "seq", "tok", None),
            P(),
            P(),
            P(None, "seq", "tok"),
            P(),
            P(),
            P(),
            P(),
            P(),
            P(),
            P(None, "seq", "tok"),
            P(),
            P(),
            P(None, "seq", "tok"),
            P(None, "tok", "seq"),
        ),
        check_vma=False,
    )
```

```python
import math

import jax
import jax.numpy as jnp
import numpy as np
from jax import lax
from jax.experimental import pallas as pl
from jax.experimental.pallas import tpu as pltpu
from jax.sharding import PartitionSpec as P

EMB = 33
INNER = 64


HIGHEST = lax.Precision.HIGHEST
NORM_EPS = 1e-05
MOD_SHIFT = 0.05


def passed_along(block, axis, distance):
    devices = range(lax.axis_size(axis))
    route = [(i - distance, i) for i in devices if i - distance in devices]
    return lax.ppermute(block, axis, route)


def for_sending(value):

    def short(part):
        return part.astype(jnp.bfloat16) if part.dtype == jnp.float32 else part

    return jax.tree.map(short, value)


def position_features(length):
    band_count = (EMB - 1) // 2
    step_index = jnp.arange(length, dtype=jnp.int32).astype(jnp.float32)
    time_grid = step_index / (length - 1)
    base_angle = step_index * (2.0 * math.pi / length)
    band_freq = jnp.linspace(0.0001, band_count - 1, band_count, dtype=jnp.float32)
    phases = base_angle[:, None] * band_freq[None, :]
    return jnp.concatenate([time_grid[:, None], jnp.cos(phases), -jnp.sin(phases)], axis=1)


def decay_table(time_grid, first_chan, channels, model_width):
    fast_rate = math.log(0.01) / 0.3
    slow_rate = math.log(0.01) / 1.5
    chan_index = first_chan + jnp.arange(channels, dtype=jnp.int32).astype(jnp.float32)
    deltas = jnp.abs(fast_rate + (slow_rate - fast_rate) * chan_index / (model_width - 1))
    return jnp.exp(-time_grid * deltas[None, :]) + MOD_SHIFT


def filter_taps(features, weight_one, sine_freq, weight_two, weight_three, envelope):
    first_sine = jnp.sin(sine_freq[0] * jnp.dot(features, weight_one, precision=HIGHEST))
    second_sine = jnp.sin(sine_freq[1] * jnp.dot(first_sine, weight_two, precision=HIGHEST))
    return jnp.dot(second_sine, weight_three, precision=HIGHEST) * envelope


def layer_norm(values_in, gain_vec, bias_vec):
    mean_row = jnp.mean(values_in, axis=-1, keepdims=True)
    centred = values_in - mean_row
    variance = jnp.mean(centred * centred, axis=-1, keepdims=True)
    return centred * lax.rsqrt(variance + NORM_EPS) * gain_vec + bias_vec


def gelu_tanh(values_in):
    return jax.nn.gelu(values_in, approximate=True)


def dft_tables(outer_size, inner_size):
    padded_len = outer_size * inner_size
    outer_index = jnp.arange(outer_size, dtype=jnp.int32)
    half_index = jnp.arange(outer_size // 2, dtype=jnp.int32)
    inner_index = jnp.arange(inner_size, dtype=jnp.int32)
    angle_outer = (outer_index[:, None] * half_index[None, :] % outer_size).astype(jnp.float32) * (
        2.0 * math.pi / outer_size
    )
    angle_twist = (outer_index[:, None] * inner_index[None, :] % padded_len).astype(jnp.float32) * (
        2.0 * math.pi / padded_len
    )
    angle_inner = (inner_index[:, None] * inner_index[None, :] % inner_size).astype(jnp.float32) * (
        2.0 * math.pi / inner_size
    )
    return (
        jnp.cos(angle_outer),
        jnp.sin(angle_outer),
        jnp.cos(angle_twist)[None, :, :, None],
        jnp.sin(angle_twist)[None, :, :, None],
        jnp.cos(angle_inner),
        jnp.sin(angle_inner),
    )


def forward_dft(series, tables):
    cos_outer, sin_outer, cos_twist, sin_twist, cos_inner, sin_inner = tables
    outer_size = cos_outer.shape[0]
    inner_size = cos_inner.shape[0]
    seq_count = series.shape[0]
    channels = series.shape[2]
    token_grid = series.reshape(seq_count, outer_size // 2, inner_size, channels)
    first_re = jnp.einsum("ka,sabc->skbc", cos_outer, token_grid, precision=HIGHEST)
    first_im = -jnp.einsum("ka,sabc->skbc", sin_outer, token_grid, precision=HIGHEST)
    twist_re = first_re * cos_twist + first_im * sin_twist
    twist_im = first_im * cos_twist - first_re * sin_twist
    out_re = jnp.einsum("skbc,bj->skjc", twist_re, cos_inner, precision=HIGHEST) + jnp.einsum(
        "skbc,bj->skjc", twist_im, sin_inner, precision=HIGHEST
    )
    out_im = jnp.einsum("skbc,bj->skjc", twist_im, cos_inner, precision=HIGHEST) - jnp.einsum(
        "skbc,bj->skjc", twist_re, sin_inner, precision=HIGHEST
    )
    return (out_re, out_im)


def inverse_dft(spec_re, spec_im, tables):
    cos_outer, sin_outer, cos_twist, sin_twist, cos_inner, sin_inner = tables
    outer_size = cos_outer.shape[0]
    inner_size = cos_inner.shape[0]
    seq_count = spec_re.shape[0]
    channels = spec_re.shape[3]
    back_re = jnp.einsum("skjc,bj->skbc", spec_re, cos_inner, precision=HIGHEST) - jnp.einsum(
        "skjc,bj->skbc", spec_im, sin_inner, precision=HIGHEST
    )
    back_im = jnp.einsum("skjc,bj->skbc", spec_im, cos_inner, precision=HIGHEST) + jnp.einsum(
        "skjc,bj->skbc", spec_re, sin_inner, precision=HIGHEST
    )
    turn_re = back_re * cos_twist - back_im * sin_twist
    turn_im = back_im * cos_twist + back_re * sin_twist
    token_grid = (
        jnp.einsum("skbc,ka->sabc", turn_re, cos_outer, precision=HIGHEST)
        - jnp.einsum("skbc,ka->sabc", turn_im, sin_outer, precision=HIGHEST)
    ) / (outer_size * inner_size)
    return token_grid.reshape(seq_count, outer_size // 2 * inner_size, channels)


def complex_product(left_re, left_im, right_re, right_im):
    return (left_re * right_re - left_im * right_im, left_re * right_im + left_im * right_re)


def add_tree(running, update):
    if running is None:
        return update
    return jax.tree.map(jnp.add, running, update)


def split_positions(
    x_in,
    cotangent,
    counts,
    ln1_gain,
    ln1_bias,
    w_in,
    short_w,
    filt_w1,
    filt_freq,
    filt_w2,
    filt_w3,
    long_bias,
    w_out,
    ln2_gain,
    ln2_bias,
    w_up,
    w_down,
):
    tok_count = lax.axis_size("tok")
    micro_count, cap_size, tok_rows, model_width = x_in.shape
    channels = model_width // tok_count
    first_chan = lax.axis_index("tok") * channels
    layer_count = w_in.shape[0]
    length = tok_rows * tok_count
    tables = dft_tables(2 * length // INNER, INNER)
    features = position_features(length)
    envelope = decay_table(features[:, :1], first_chan.astype(jnp.float32), channels, model_width)
    gain_one = ln1_gain.astype(jnp.float32)
    bias_one = ln1_bias.astype(jnp.float32)
    gain_two = ln2_gain.astype(jnp.float32)
    bias_two = ln2_bias.astype(jnp.float32)
    short_taps = short_w.astype(jnp.float32)
    skip_scale = long_bias.astype(jnp.float32)
    filt_one = filt_w1.astype(jnp.float32)
    filt_sine = filt_freq.astype(jnp.float32)
    filt_two = filt_w2.astype(jnp.float32)
    filt_three = filt_w3.astype(jnp.float32)

    def taps_of(layer_index):

        def taps_fn(weight_one, sine_freq, weight_two, three_slice):
            return filter_taps(features, weight_one, sine_freq, weight_two, three_slice, envelope)

        three_slice = lax.dynamic_slice_in_dim(filt_three[layer_index], first_chan, channels, 1)
        return jax.vjp(
            taps_fn,
            filt_one[layer_index],
            filt_sine[layer_index],
            filt_two[layer_index],
            three_slice,
        )

    taps_spectra = []
    for layer_index in range(layer_count):
        filter_rows, _ = taps_of(layer_index)
        taps_spectra.append(forward_dft(filter_rows[None], tables))

    def backward_layer(grad_rows, kept, layer_index):
        (
            residual,
            normed,
            padded,
            short_out,
            carried,
            long_out,
            gated_rows,
            hidden,
            normed_two,
            raised,
            active,
            kept_signal,
        ) = kept
        down_grad = grad_rows.astype(jnp.bfloat16)
        active_grad = jnp.einsum(
            "std,fd->stf", down_grad, w_down[layer_index], preferred_element_type=jnp.float32
        )
        _, gelu_pull = jax.vjp(gelu_tanh, raised)
        raised_grad = gelu_pull(active_grad)[0].astype(jnp.bfloat16)
        normed_two_grad = jnp.einsum(
            "stf,df->std", raised_grad, w_up[layer_index], preferred_element_type=jnp.float32
        )
        _, second_pull = jax.vjp(layer_norm, hidden, gain_two[layer_index], bias_two[layer_index])
        hidden_part, grad_gain_two, grad_bias_two = second_pull(normed_two_grad)
        hidden_grad = grad_rows + hidden_part
        out_grad = hidden_grad.astype(jnp.bfloat16)
        gated_grad = jnp.einsum(
            "ste,de->std", out_grad, w_out[layer_index], preferred_element_type=jnp.float32
        )
        gate_out = short_out[:, :, :model_width]
        gate_in = short_out[:, :, model_width : 2 * model_width]
        values = short_out[:, :, 2 * model_width :]
        long_grad = gated_grad * gate_out
        gate_out_grad = gated_grad * long_out
        grad_skip = jnp.sum(carried * long_grad, axis=(0, 1))
        spec_re, spec_im = taps_spectra[layer_index]
        upstream_re, upstream_im = forward_dft(
            lax.all_to_all(
                long_grad.astype(jnp.bfloat16), "tok", split_axis=2, concat_axis=1, tiled=True
            ).astype(long_grad.dtype),
            tables,
        )
        back_re, back_im = complex_product(upstream_re, upstream_im, spec_re, -spec_im)
        back_rows = lax.all_to_all(
            for_sending(inverse_dft(back_re, back_im, tables)),
            "tok",
            split_axis=1,
            concat_axis=2,
            tiled=True,
        )
        back_rows, upstream_re, upstream_im = (back_rows, upstream_re, upstream_im)
        signal_re, signal_im = kept_signal
        cross_re = jnp.sum(signal_re * upstream_re + signal_im * upstream_im, axis=0)
        cross_im = jnp.sum(signal_re * upstream_im - signal_im * upstream_re, axis=0)
        carried_grad = back_rows + skip_scale[layer_index] * long_grad
        short_grad = jnp.concatenate(
            [gate_out_grad, carried_grad * values, carried_grad * gate_in], axis=2
        )
        next_rows = passed_along(for_sending(short_grad[:, :2, :]), "tok", -1)
        extended = jnp.concatenate([short_grad, next_rows], axis=1)
        kernel = short_taps[layer_index]
        projected_grad = (
            kernel[2] * short_grad + kernel[1] * extended[:, 1:-1] + kernel[0] * extended[:, 2:]
        ).astype(jnp.bfloat16)
        grad_short = jnp.stack(
            [
                jnp.sum(short_grad * padded[:, tap_index : tap_index + tok_rows], axis=(0, 1))
                for tap_index in range(3)
            ]
        )
        normed_grad = jnp.einsum(
            "ste,de->std", projected_grad, w_in[layer_index], preferred_element_type=jnp.float32
        )
        _, first_pull = jax.vjp(layer_norm, residual, gain_one[layer_index], bias_one[layer_index])
        residual_part, grad_gain_one, grad_bias_one = first_pull(normed_grad)
        left_all = (
            lax.all_gather(down_grad, "tok", axis=1, tiled=True),
            lax.all_gather(gated_rows, "tok", axis=1, tiled=True),
            lax.all_gather(normed_two, "tok", axis=1, tiled=True),
            lax.all_gather(normed, "tok", axis=1, tiled=True),
        )
        right_cols = (
            lax.all_to_all(active, "tok", split_axis=2, concat_axis=1, tiled=True),
            lax.all_to_all(out_grad, "tok", split_axis=2, concat_axis=1, tiled=True),
            lax.all_to_all(raised_grad, "tok", split_axis=2, concat_axis=1, tiled=True),
            lax.all_to_all(projected_grad, "tok", split_axis=2, concat_axis=1, tiled=True),
        )
        grad_down = jnp.einsum(
            "stf,std->fd", right_cols[0], left_all[0], preferred_element_type=jnp.float32
        )
        grad_out = jnp.einsum(
            "std,ste->de", left_all[1], right_cols[1], preferred_element_type=jnp.float32
        )
        grad_up = jnp.einsum(
            "std,stf->df", left_all[2], right_cols[2], preferred_element_type=jnp.float32
        )
        grad_in_proj = jnp.einsum(
            "std,ste->de", left_all[3], right_cols[3], preferred_element_type=jnp.float32
        )
        bundle = (
            (grad_in_proj, grad_out, grad_up, grad_down),
            (grad_gain_one, grad_bias_one, grad_short, grad_skip, grad_gain_two, grad_bias_two),
            (cross_re, cross_im),
        )
        return (hidden_grad + residual_part, bundle)

    def filter_grads(cross_re, cross_im, layer_index):
        taps_grad = inverse_dft(cross_re[None], cross_im[None], tables)[0]
        _, taps_pull = taps_of(layer_index)
        grad_one, grad_sine, grad_two, grad_three = taps_pull(taps_grad)
        grad_three_full = lax.dynamic_update_slice_in_dim(
            jnp.zeros_like(filt_three[layer_index]), grad_three, first_chan, 1
        )
        return (grad_one, grad_sine, grad_two, grad_three_full)

    outputs = []
    input_grads = []
    running = None
    reduced = None
    for micro_index in range(micro_count):
        live_mask = (jnp.arange(cap_size, dtype=jnp.int32) < counts[micro_index, 0]).astype(
            jnp.float32
        )[:, None, None]
        residual = x_in[micro_index].astype(jnp.float32)
        saved = []
        for layer_index in range(layer_count):
            forward_normed = layer_norm(
                residual, gain_one[layer_index], bias_one[layer_index]
            ).astype(jnp.bfloat16)
            projected = jnp.einsum(
                "std,de->ste", forward_normed, w_in[layer_index], preferred_element_type=jnp.float32
            )
            prev_rows = passed_along(projected[:, -2:, :], "tok", 1)
            forward_padded = jnp.concatenate([prev_rows, projected], axis=1)
            forward_kernel = short_taps[layer_index]
            forward_short_out = (
                forward_kernel[0] * forward_padded[:, :-2]
                + forward_kernel[1] * forward_padded[:, 1:-1]
                + forward_kernel[2] * forward_padded[:, 2:]
            )
            forward_gate_out = forward_short_out[:, :, :model_width]
            forward_gate_in = forward_short_out[:, :, model_width : 2 * model_width]
            forward_values = forward_short_out[:, :, 2 * model_width :]
            forward_carried = forward_values * forward_gate_in
            forward_spec_re, forward_spec_im = taps_spectra[layer_index]
            convolve_signal_re, convolve_signal_im = forward_dft(
                lax.all_to_all(forward_carried, "tok", split_axis=2, concat_axis=1, tiled=True),
                tables,
            )
            prod_re, prod_im = complex_product(
                convolve_signal_re, convolve_signal_im, forward_spec_re, forward_spec_im
            )
            convolve_back_rows = lax.all_to_all(
                inverse_dft(prod_re, prod_im, tables),
                "tok",
                split_axis=1,
                concat_axis=2,
                tiled=True,
            )
            results = (convolve_back_rows, convolve_signal_re, convolve_signal_im)
            forward_long_out = results[0] + skip_scale[layer_index] * forward_carried
            forward_gated_rows = (forward_long_out * forward_gate_out).astype(jnp.bfloat16)
            forward_hidden = residual + jnp.einsum(
                "std,de->ste",
                forward_gated_rows,
                w_out[layer_index],
                preferred_element_type=jnp.float32,
            )
            forward_normed_two = layer_norm(
                forward_hidden, gain_two[layer_index], bias_two[layer_index]
            ).astype(jnp.bfloat16)
            forward_raised = jnp.einsum(
                "std,df->stf",
                forward_normed_two,
                w_up[layer_index],
                preferred_element_type=jnp.float32,
            )
            forward_active = gelu_tanh(forward_raised).astype(jnp.bfloat16)
            result = forward_hidden + jnp.einsum(
                "stf,fd->std",
                forward_active,
                w_down[layer_index],
                preferred_element_type=jnp.float32,
            )
            forward_kept = (
                residual,
                forward_normed,
                forward_padded,
                forward_short_out,
                forward_carried,
                forward_long_out,
                forward_gated_rows,
                forward_hidden,
                forward_normed_two,
                forward_raised,
                forward_active,
                results[1:],
            )
            residual = result
            kept = forward_kept
            saved.append(kept)
        outputs.append(residual * live_mask)
        grad_rows = cotangent[micro_index].astype(jnp.float32) * live_mask
        layer_bundles = [None] * layer_count
        for layer_index in reversed(range(layer_count)):
            grad_rows, bundle = backward_layer(grad_rows, saved[layer_index], layer_index)
            layer_bundles[layer_index] = bundle
        input_grads.append(grad_rows)
        running = add_tree(running, layer_bundles)
    mats = [
        jnp.stack([running[layer_index][0][member] for layer_index in range(layer_count)])
        for member in range(4)
    ]
    vecs = [
        jnp.stack([running[layer_index][1][member] for layer_index in range(layer_count)])
        for member in range(6)
    ]
    filter_parts = [
        filter_grads(running[layer_index][2][0], running[layer_index][2][1], layer_index)
        for layer_index in range(layer_count)
    ]
    filt_parts = [
        jnp.stack([filter_parts[layer_index][member] for layer_index in range(layer_count)])
        for member in range(4)
    ]
    mat_done = (
        lax.psum_scatter(
            mats[0].astype(jnp.bfloat16), "seq", scatter_dimension=1, tiled=True
        ).astype(jnp.float32),
        lax.psum_scatter(
            mats[1].astype(jnp.bfloat16), "seq", scatter_dimension=1, tiled=True
        ).astype(jnp.float32),
        lax.psum_scatter(
            mats[2].astype(jnp.bfloat16), "seq", scatter_dimension=1, tiled=True
        ).astype(jnp.float32),
        lax.psum_scatter(
            mats[3].astype(jnp.bfloat16), "seq", scatter_dimension=2, tiled=True
        ).astype(jnp.float32),
    )
    small_done = lax.psum(
        (
            vecs[0],
            vecs[1],
            vecs[2],
            vecs[3],
            vecs[4],
            vecs[5],
            filt_parts[0],
            filt_parts[1],
            filt_parts[2],
            filt_parts[3],
        ),
        ("seq", "tok"),
    )
    reduced = (tuple(mat_done), tuple(small_done))
    mat_done, small_done = reduced
    return (
        jnp.stack(outputs),
        jnp.stack(input_grads),
        small_done[0],
        small_done[1],
        mat_done[0],
        small_done[2],
        small_done[6],
        small_done[7],
        small_done[8],
        small_done[9],
        small_done[3],
        mat_done[1],
        small_done[4],
        small_done[5],
        mat_done[2],
        mat_done[3],
    )


MIB = 1 << 20
MESH = pl.DeviceIdType.MESH


def mm(left, right):
    return jnp.dot(left, right, preferred_element_type=jnp.float32)


def mm_nt(left, right):
    return lax.dot_general(left, right, (((1,), (1,)), ((), ())), preferred_element_type=jnp.float32)


def mm_tn(left, right):
    return lax.dot_general(left, right, (((0,), (0,)), ((), ())), preferred_element_type=jnp.float32)


def f32(values):
    return values.astype(jnp.float32)


def bf(values):
    return values.astype(jnp.bfloat16)


def row_shift(values, distance):
    rows = values.shape[0]
    index = lax.broadcasted_iota(jnp.int32, values.shape, 0)
    rolled = pltpu.roll(values, distance % rows, 0)
    kept = index >= distance if distance > 0 else index < rows + distance
    return jnp.where(kept, rolled, 0.0)


def standardised(values):
    mean = jnp.mean(values, axis=-1, keepdims=True)
    centred = values - mean
    scale = lax.rsqrt(jnp.mean(centred * centred, axis=-1, keepdims=True) + NORM_EPS)
    return centred * scale, scale


def norm_backward(values, gain, upstream):
    xh, scale = standardised(values)
    dxh = upstream * gain
    part = scale * (
        dxh - jnp.mean(dxh, axis=-1, keepdims=True) - xh * jnp.mean(dxh * xh, axis=-1, keepdims=True)
    )
    return part, jnp.sum(upstream * xh, axis=0, keepdims=True), jnp.sum(upstream, axis=0, keepdims=True)


def gelu_parts(values):
    slope = math.sqrt(2.0 / math.pi)
    square = values * values
    bent = jnp.tanh(slope * values * (1.0 + 0.044715 * square))
    half = 0.5 * (1.0 + bent)
    inner = slope * (1.0 + (3.0 * 0.044715) * square)
    return values * half, half + 0.5 * values * (1.0 - bent * bent) * inner


def spectral_table(length):
    k = np.arange(length, dtype=np.int64)[:, None]
    t = np.arange(length, dtype=np.int64)[None, :]
    angle = ((2 * k + 1) * t % (4 * length)).astype(np.float64) * (2.0 * math.pi / (4 * length))
    return np.concatenate([np.cos(angle), -np.sin(angle)], axis=0).astype(jnp.bfloat16)


def whole(shape):
    return pl.BlockSpec(shape, lambda j: (0,) * len(shape), pipeline_mode=pl.Buffered(1))


VECS = 14


def vector(ref, layer, k):
    return ref[VECS * layer + k : VECS * layer + k + 1, :]


def short_taps(ref, layer):
    return [ref[VECS * layer + 5 + 3 * p : VECS * layer + 8 + 3 * p, :] for p in range(3)]


ANY = pl.BlockSpec(memory_space=pl.ANY)


def sds(shape, kind):
    return jax.ShapeDtypeStruct(shape, kind)


class Place:
    def __init__(self):
        s, t = lax.axis_index("seq"), lax.axis_index("tok")
        self.depth = lax.axis_size("seq") // 2
        self.z, self.core, self.y, self.x = s // 2, s % 2, t // 2, t % 2
        self.s, self.t = s, t
        self.over_core = (2 * self.z + 1 - self.core, t)
        self.over_x = (s, 2 * self.y + 1 - self.x)
        self.over_y = (s, 2 * (1 - self.y) + self.x)
        self.over_z = [(2 * ((self.z + d) % self.depth) + self.core, t) for d in range(1, self.depth)]
        self.from_z = [(2 * ((self.z + self.depth - d) % self.depth) + self.core, t) for d in range(1, self.depth)]


def greet(partners):
    barrier = pltpu.get_barrier_semaphore()
    for partner in partners:
        pl.semaphore_signal(barrier, inc=1, device_id=partner, device_id_type=MESH)


def greeted(partners):
    pl.semaphore_wait(pltpu.get_barrier_semaphore(), len(partners))


def remote(source, target, sent, landed, device):
    return pltpu.make_async_remote_copy(
        src_ref=source, dst_ref=target, send_sem=sent, recv_sem=landed, device_id=device, device_id_type=MESH
    )


def other_first(place, s, piece):
    half = place.depth * piece
    mine = (s % 2 + place.core + 1) % 2
    return pl.multiple_of(mine * half + (s // 2) * piece, 16)


def store_rows(place, target, values):
    piece = values.shape[0] // (2 * place.depth)
    for s in range(2 * place.depth):
        target[pl.ds(other_first(place, s, piece), piece), :] = values[s * piece : (s + 1) * piece]


class Transpose:
    def __init__(self, place, source, target, sent, landed, own, gathering):
        self.place, self.source, self.target, self.sent, self.landed, self.own = place, source, target, sent, landed, own
        self.gathering = gathering
        self.partners = [place.over_x, place.over_y, (place.s, 2 * (1 - place.y) + 1 - place.x)]

    def block(self, ref, k, flat):
        if not flat:
            return ref.at[k]
        rows = ref.shape[0] // 4
        return ref.at[pl.ds(pl.multiple_of(k * rows, rows), rows)]

    def copies(self):
        me = self.place.t
        flat_in, flat_out = not self.gathering, self.gathering
        target = self.block(self.target, me, flat_out)
        out = [
            remote(self.block(self.source, device[1], flat_in), target, self.sent.at[k], self.landed.at[k], device)
            for k, device in enumerate(self.partners)
        ]
        return out + [pltpu.make_async_copy(self.block(self.source, me, flat_in), target, self.own)]

    def start(self):
        for copy in self.copies():
            copy.start()

    def wait(self):
        for copy in self.copies():
            copy.wait()


TRANSPOSE_SEMS = [pltpu.SemaphoreType.DMA((3,)), pltpu.SemaphoreType.DMA((3,)), pltpu.SemaphoreType.DMA]


def sine_cosine(angle):
    turns = jnp.floor(angle * (2.0 / math.pi) + 0.5)
    rest = ((angle - turns * 1.5703125) - turns * 4.837512969970703e-4) - turns * 7.549789948768648e-8
    square = rest * rest
    sine = rest + rest * square * (
        -1.6666654611e-1 + square * (8.3321608736e-3 + square * -1.9515295891e-4)
    )
    cosine = 1.0 - 0.5 * square + square * square * (
        4.166664568298827e-2 + square * (-1.388731625493765e-3 + square * 2.443315711809948e-5)
    )
    quarter = turns - 4.0 * jnp.floor(turns * 0.25)
    odd = (quarter == 1.0) | (quarter == 3.0)
    sin_sign = jnp.where(quarter >= 2.0, -1.0, 1.0)
    cos_sign = jnp.where((quarter == 1.0) | (quarter == 2.0), -1.0, 1.0)
    return sin_sign * jnp.where(odd, cosine, sine), cos_sign * jnp.where(odd, sine, cosine)


def decay(delta, length):
    time = lax.broadcasted_iota(jnp.int32, (length, delta.shape[1]), 0).astype(jnp.float32) * (1.0 / (length - 1))
    return jnp.exp(-time * delta) + MOD_SHIFT


def front_body(
    x_in, table_in, features_ref, delta_ref, g1, b1, g2, b2, skip, short, fw1, freqs, fw2, w3_ref,
    x_out, filt_ref, taps_ref, vec_ref, net_ref, table_ref, table_sem, sent, landed, own,
):
    place = Place()
    layers, units, width = w3_ref.shape
    length = table_ref.shape[1]
    table_copy = pltpu.make_async_copy(table_in, table_ref, table_sem)
    table_copy.start()
    move = Transpose(place, x_in, x_out, sent, landed, own, True)
    greet(move.partners)
    vec_ref[...] = jnp.zeros_like(vec_ref)
    net_ref[...] = jnp.zeros_like(net_ref)
    for layer in range(layers):
        for k, ref in enumerate((g1, b1, g2, b2, skip)):
            vec_ref[VECS * layer + k : VECS * layer + k + 1, :] = f32(ref[...])[layer : layer + 1]
        taps = f32(short[layer])
        for p in range(3):
            vec_ref[VECS * layer + 5 + 3 * p : VECS * layer + 8 + 3 * p, :] = taps[:, width * p : width * (p + 1)]
        net_ref[layer, :EMB, :] = f32(fw1[layer])
        net_ref[layer, 40:42, :] = f32(freqs[layer])
        net_ref[layer, 48:112, :] = f32(fw2[layer])
    greeted(move.partners)
    move.start()

    def high(a, b):
        top = bf(a)
        return mm(top, bf(b)) + mm(bf(a - f32(top)), bf(b))

    wide = lambda parts: jnp.concatenate(parts, axis=1)
    freq = [wide([net_ref[layer, 40 + k : 41 + k, :] for layer in range(layers)]) for k in range(2)]
    a1 = wide([high(features_ref[...], net_ref[layer, 0:40, :]) for layer in range(layers)])
    s1, c1 = sine_cosine(freq[0] * a1)
    a2 = wide([
        high(s1[:, units * layer : units * (layer + 1)], net_ref[layer, 48:112, :]) for layer in range(layers)
    ])
    s2, c2 = sine_cosine(freq[1] * a2)
    for k, values in enumerate((s1, s2, c1 * freq[0], c1 * a1, c2 * freq[1], c2 * a2)):
        filt_ref[k] = bf(values)
    envelope = decay(delta_ref[...], length)
    table_copy.wait()
    for layer in range(layers):
        taps = high(s2[:, units * layer : units * (layer + 1)], w3_ref[layer]) * envelope
        taps_ref[layer] = bf(mm(table_ref[...], bf(taps)) * (1.0 / length))
    move.wait()


def front(collective, x_in, table, features, delta, *small):
    slots, rows, width = x_in.shape
    layers, units, _ = small[-1].shape
    length = slots * rows
    vm = pl.BlockSpec(memory_space=pltpu.VMEM)
    b16, b32 = jnp.bfloat16, jnp.float32
    return pl.pallas_call(
        front_body,
        in_specs=[ANY, ANY] + [vm] * (2 + len(small)),
        out_specs=[ANY, vm, vm, vm, vm],
        out_shape=[
            sds((length, width), b16), sds((6, length, layers * units), b16), sds((layers, 2 * length, width), b16),
            sds((-(-VECS * layers // 8) * 8, width), b32), sds((layers, 112, units), b32),
        ],
        scratch_shapes=[pltpu.VMEM((2 * length, length), b16), pltpu.SemaphoreType.DMA] + TRANSPOSE_SEMS,
        compiler_params=pltpu.CompilerParams(
            vmem_limit_bytes=62 * MIB, collective_id=collective, has_side_effects=True
        ),
        name="front",
    )(x_in, table, features, delta, *small)


def mixed_chunk(proj, kernel):
    return [
        kernel[p][0:1] * row_shift(proj[p], 2) + kernel[p][1:2] * row_shift(proj[p], 1) + kernel[p][2:3] * proj[p]
        for p in range(3)
    ]


def mixer_forward_body(layer, carry, *refs):
    refs = list(refs)
    take = lambda n: [refs.pop(0) for _ in range(n)]
    r_ref, vec_ref, cut_ref, w0_ref, w1_ref, w2_ref, table_ref, taps_ref, wo_ref = take(9)
    moving_in = take(1)[0] if carry else None
    hidden_ref, normed_ref, proj_ref, signal_ref, long_ref = take(5)
    if carry:
        moved_out, sent, landed, own = take(4)
        move = Transpose(Place(), moving_in, moved_out, sent, landed, own, True)
    length = r_ref.shape[0]
    j = pl.program_id(0)

    @pl.when(j == 0)
    def _():
        if carry:
            greet(move.partners)
        r = f32(r_ref[...])
        xh, _ = standardised(r)
        normed_ref[...] = bf(xh * vector(vec_ref, layer, 0) + vector(vec_ref, layer, 1))
        hidden_ref[...] = r
        if carry:
            greeted(move.partners)
            move.start()

    normed = normed_ref[...]
    proj = [mm(normed, w_ref[...]) for w_ref in (w0_ref, w1_ref, w2_ref)]
    for p in range(3):
        proj_ref[p] = bf(proj[p])
    gate_out, gate_in, vals = mixed_chunk(proj, short_taps(cut_ref, layer))
    carried = vals * gate_in
    both = mm(table_ref[...], bf(carried))
    re, im = both[:length], both[length:]
    signal_ref[...] = bf(both)
    tap_re, tap_im = f32(taps_ref[:length]), f32(taps_ref[length:])
    out = mm_tn(table_ref[:length], bf(re * tap_re - im * tap_im))
    out += mm_tn(table_ref[length:], bf(re * tap_im + im * tap_re))
    long_out = out + vector(cut_ref, layer, 4) * carried
    long_ref[...] = bf(long_out)
    hidden_ref[...] += mm(bf(long_out * gate_out), wo_ref[...])

    if carry:
        @pl.when(j == pl.num_programs(0) - 1)
        def _():
            move.wait()


def mixer_forward(layer, collective, r, vecs, w_in, table, taps, w_out, *moving):
    length, width = r.shape
    chunk = 256
    steps = width // chunk
    carry = len(moving) > 0
    third = lambda p: pl.BlockSpec((None, width, chunk), lambda j: (layer, 0, p * steps + j))
    return pl.pallas_call(
        lambda *refs: mixer_forward_body(layer, carry, *refs),
        grid=(steps,),
        in_specs=[
            whole((length, width)), whole(vecs.shape), pl.BlockSpec((vecs.shape[0], chunk), lambda j: (0, j)),
            third(0), third(1), third(2),
            whole((2 * length, length)),
            pl.BlockSpec((None, 2 * length, chunk), lambda j: (layer, 0, j)),
            pl.BlockSpec((None, chunk, width), lambda j: (layer, j, 0)),
        ] + [ANY] * len(moving),
        out_specs=[
            whole((length, width)), whole((length, width)),
            pl.BlockSpec((3, length, chunk), lambda j: (0, 0, j)),
            pl.BlockSpec((2 * length, chunk), lambda j: (0, j)),
            pl.BlockSpec((length, chunk), lambda j: (0, j)),
        ] + [ANY] * len(moving),
        out_shape=[
            sds((length, width), jnp.float32), sds((length, width), jnp.bfloat16),
            sds((3, length, width), jnp.bfloat16), sds((2 * length, width), jnp.bfloat16),
            sds((length, width), jnp.bfloat16),
        ] + ([sds((length, width), jnp.bfloat16)] if carry else []),
        scratch_shapes=TRANSPOSE_SEMS if carry else [],
        compiler_params=pltpu.CompilerParams(
            vmem_limit_bytes=60 * MIB, **(dict(collective_id=collective, has_side_effects=True) if carry else {})
        ),
        cost_estimate=pl.CostEstimate(
            flops=2 * length * width * (4 * width + 4 * length), bytes_accessed=30 * MIB, transcendentals=0
        ),
        name="mixer_forward",
    )(r, vecs, vecs, w_in, w_in, w_in, table, taps, w_out, *moving)


def ffn_forward_body(layer, last, *refs):
    hidden_ref, vec_ref, up_ref, down_ref = refs[:4]
    if last:
        live_ref, out_ref, normed_ref, raised_ref, r_ref = refs[4:]
    else:
        r_ref, normed_ref, raised_ref = refs[4:]

    @pl.when(pl.program_id(0) == 0)
    def _():
        hidden = hidden_ref[...]
        xh, _ = standardised(hidden)
        normed_ref[...] = bf(xh * vector(vec_ref, layer, 2) + vector(vec_ref, layer, 3))
        r_ref[...] = hidden

    raised = mm(normed_ref[...], up_ref[...])
    raised_ref[...] = bf(raised)
    r_ref[...] += mm(bf(gelu_parts(raised)[0]), down_ref[...])

    if last:
        @pl.when(pl.program_id(0) == pl.num_programs(0) - 1)
        def _():
            out_ref[...] = bf(r_ref[...] * live_ref[0, 0])


SCALAR = pl.BlockSpec(memory_space=pltpu.SMEM)


def ffn_forward(layer, hidden, vecs, w_up, w_down, *live):
    length, width = hidden.shape
    inner = w_up.shape[2]
    chunk = inner // 4
    last = len(live) > 0
    return pl.pallas_call(
        lambda *refs: ffn_forward_body(layer, last, *refs),
        grid=(inner // chunk,),
        in_specs=[
            whole((length, width)), whole(vecs.shape),
            pl.BlockSpec((None, width, chunk), lambda j: (layer, 0, j)),
            pl.BlockSpec((None, chunk, width), lambda j: (layer, j, 0)),
        ] + [SCALAR] * len(live),
        out_specs=[
            whole((length, width)), whole((length, width)), pl.BlockSpec((length, chunk), lambda j: (0, j)),
        ],
        out_shape=[
            sds((length, width), jnp.bfloat16 if last else jnp.float32), sds((length, width), jnp.bfloat16),
            sds((length, inner), jnp.bfloat16),
        ],
        scratch_shapes=[pltpu.VMEM((length, width), jnp.float32)] if last else [],
        compiler_params=pltpu.CompilerParams(vmem_limit_bytes=60 * MIB),
        cost_estimate=pl.CostEstimate(
            flops=4 * length * width * inner, bytes_accessed=26 * MIB, transcendentals=length * inner
        ),
        name="ffn_forward",
    )(hidden, vecs, w_up, w_down, *live)


def ffn_backward_body(layer, carry, *refs):
    refs = list(refs)
    take = lambda n: [refs.pop(0) for _ in range(n)]
    g_ref, hidden_in, vec_ref, normed_ref, raised_ref, up_ref, down_ref = take(7)
    zin_ref, min_ref = take(2) if carry else (None, None)
    live_ref, moving_in = (None, None) if carry else take(2)
    upstream = lambda: g_ref[...] if carry else f32(g_ref[...]) * live_ref[0, 0]
    out_ref, gain_grad_ref, bias_grad_ref, c_out, w_out = take(5)
    zfin_ref, wmix_ref = take(2) if carry else (None, None)
    moved_out = None if carry else take(1)[0]
    g16_ref, g16t_ref, normed_t_ref, give, got, c_ref, s1, core_s, core_r, s1_s, s1_r, out_sem, hidden_ref, hidden_sem = take(14)
    hidden_copy = pltpu.make_async_copy(hidden_in, hidden_ref, hidden_sem)
    if carry:
        zgot, zown, mgot, mown, z_s, z_r, m_s, m_r, own_sem = take(9)
    move_sems = None if carry else take(3)
    j = pl.program_id(0)
    steps = pl.num_programs(0)
    width = g_ref.shape[1]
    place = Place()
    half = c_ref.shape[1]
    mcols = width // 2
    move = None if carry else Transpose(place, moving_in, moved_out, *move_sems, False)
    partners = [place.over_core, place.over_x, place.over_y]
    partners += place.over_z if carry else [(place.s, 2 * (1 - place.y) + 1 - place.x)]

    def z_sends():
        piece = [remote(zin_ref.at[:, (place.z + d) % place.depth], zgot.at[d - 1], z_s.at[d - 1], z_r.at[d - 1],
                        place.over_z[d - 1]) for d in range(1, place.depth)]
        return piece

    def m_sends():
        sends = []
        for k in range(2):
            sends.append(remote(min_ref.at[2 * k + 1 - place.x, :, pl.ds(0, mcols)], mgot.at[0, k], m_s.at[0, k],
                                m_r.at[0, k], place.over_x))
            sends.append(remote(min_ref.at[2 * (1 - place.y) + k, :, pl.ds(mcols, mcols)], mgot.at[1, k], m_s.at[1, k],
                                m_r.at[1, k], place.over_y))
        return sends

    def own_copies():
        copies = [pltpu.make_async_copy(zin_ref.at[:, place.z], zown, own_sem.at[4])]
        for k in range(2):
            copies.append(pltpu.make_async_copy(min_ref.at[2 * k + place.x, :, pl.ds(0, mcols)], mown.at[0, k],
                                                own_sem.at[k]))
            copies.append(pltpu.make_async_copy(min_ref.at[2 * place.y + k, :, pl.ds(mcols, mcols)], mown.at[1, k],
                                                own_sem.at[2 + k]))
        return copies

    def core_send(slot, side):
        columns = pl.ds(side * width, width)
        return remote(give.at[slot, :, columns], got.at[slot, :, columns], core_s.at[slot, side], core_r.at[slot, side],
                      place.over_core)

    def s1_send(side, t):
        device = place.over_x if side == 0 else place.over_y
        return remote(c_ref.at[t, :, pl.ds(side * width, width)], s1.at[side], s1_s.at[side], s1_r.at[side], device)

    def c_copy(t):
        return pltpu.make_async_copy(c_ref.at[t], c_out.at[t], out_sem.at[t])

    def finish(t, slot):
        for side in range(2):
            core_send(slot, side).wait_recv()
        c_ref[t] = bf(f32(c_ref[t]) + f32(got[slot]))
        c_copy(t).start()

    @pl.when(j == 0)
    def _():
        greet(partners)
        hidden_copy.start()
        g16 = bf(upstream())
        g16_ref[...] = g16
        store_rows(place, g16t_ref, g16.T)
        store_rows(place, normed_t_ref, normed_ref[...].T)
        out_ref[...] = jnp.zeros_like(out_ref)
        greeted(partners)
        if carry:
            for copy in z_sends() + m_sends() + own_copies():
                copy.start()
        else:
            move.start()

    slot = j % 2

    @pl.when(j == 1)
    def _():
        finish(0, 0)

        @pl.when(place.x == 1)
        def _():
            s1_send(0, 0).start()

        @pl.when(place.y == 1)
        def _():
            s1_send(1, 0).start()

    @pl.when(j == 2)
    def _():
        finish(3, 1)

        @pl.when(place.x == 0)
        def _():
            s1_send(0, 3).start()

        @pl.when(place.y == 0)
        def _():
            s1_send(1, 3).start()

    @pl.when(j == 3)
    def _():
        finish(2, 0)

    @pl.when(j >= 2)
    def _():
        for side in range(2):
            core_send(slot, side).wait_send()

    active, slope = gelu_parts(f32(raised_ref[...]))
    active = bf(active)
    raised_grad = bf(mm_nt(g16_ref[...], down_ref[...]) * slope)
    t = (steps - j) % steps
    for side, (left, right) in enumerate(((normed_t_ref, raised_grad), (g16t_ref, active))):
        product = bf(mm(left[...], right))
        give[slot, :, side * width : (side + 1) * width] = product[:half]
        c_ref[t, :, side * width : (side + 1) * width] = product[half:]
        core_send(slot, side).start()
    out_ref[...] += mm_nt(raised_grad, up_ref[...])

    @pl.when(j == steps - 1)
    def _():
        hidden_copy.wait()
        part, gain_grad, bias_grad = norm_backward(hidden_ref[...], vector(vec_ref, layer, 2), out_ref[...])
        out_ref[...] = upstream() + part
        gain_grad_ref[...] = gain_grad
        bias_grad_ref[...] = bias_grad
        finish(1, 1)
        for k in range(2):
            s1_send(k, 0).wait_recv()
        w_out[0] = bf(f32(c_ref[3 * place.x, :, :width]) + f32(s1[0]))
        w_out[1] = bf(f32(c_ref[3 * place.y, :, width:]) + f32(s1[1]))
        if carry:
            for copy in own_copies():
                copy.wait()
            for copy in z_sends() + m_sends():
                copy.wait()
            total = f32(zown[...])
            for d in range(place.depth - 1):
                total += f32(zgot[d])
            zfin_ref[...] = total
            for side in range(2):
                for k in range(2):
                    wmix_ref[side, k] = bf(f32(mown[side, k]) + f32(mgot[side, k]))
        for k in range(2):
            s1_send(k, 0).wait_send()
            for side in range(2):
                core_send(k, side).wait_send()
        for k in range(steps):
            c_copy(k).wait()
        if not carry:
            move.wait()


def ffn_backward(layer, carry, collective, g, hidden, vecs, normed, raised, w_up, w_down, *carried):
    length, width = g.shape
    inner = w_up.shape[2]
    chunk = inner // 4
    depth = lax.axis_size("seq") // 2
    piece = width // (2 * depth)
    half = depth * piece
    b16, b32, dma = jnp.bfloat16, jnp.float32, pltpu.SemaphoreType.DMA
    order = lambda j: (4 - j) % 4
    return pl.pallas_call(
        lambda *refs: ffn_backward_body(layer, carry, *refs),
        grid=(4,),
        in_specs=[
            whole((length, width)), ANY, whole(vecs.shape), whole((length, width)),
            pl.BlockSpec((length, chunk), lambda j: (0, order(j))),
            pl.BlockSpec((None, width, chunk), lambda j: (layer, 0, order(j))),
            pl.BlockSpec((None, chunk, width), lambda j: (layer, order(j), 0)),
        ] + ([ANY] * 2 if carry else [SCALAR, ANY]),
        out_specs=[whole((length, width)), whole((1, width)), whole((1, width)), ANY, whole((2, half, width))]
        + ([whole((2, piece, width)), whole((2, 2, half, width // 2))] if carry else [ANY]),
        out_shape=[
            sds((length, width), b32), sds((1, width), b32), sds((1, width), b32), sds((4, half, 2 * chunk), b16),
            sds((2, half, chunk), b16),
        ] + ([sds((2, piece, chunk), b32), sds((2, 2, half, width // 2), b16)] if carry
             else [sds((4, length // 4, width), b16)]),
        scratch_shapes=[
            pltpu.VMEM((length, width), b16), pltpu.VMEM((width, length), b16), pltpu.VMEM((width, length), b16),
            pltpu.VMEM((2, half, 2 * chunk), b16), pltpu.VMEM((2, half, 2 * chunk), b16),
            pltpu.VMEM((4, half, 2 * chunk), b16), pltpu.VMEM((2, half, chunk), b16),
            dma((2, 2)), dma((2, 2)), dma((2,)), dma((2,)), dma((4,)), pltpu.VMEM((length, width), b32), dma,
        ] + ([
            pltpu.VMEM((depth - 1, 2, piece, chunk), b16), pltpu.VMEM((2, piece, chunk), b16),
            pltpu.VMEM((2, 2, half, width // 2), b16), pltpu.VMEM((2, 2, half, width // 2), b16),
            dma((depth - 1,)), dma((depth - 1,)), dma((2, 2)), dma((2, 2)), dma((5,)),
        ] if carry else TRANSPOSE_SEMS),
        compiler_params=pltpu.CompilerParams(
            vmem_limit_bytes=62 * MIB, collective_id=collective, has_side_effects=True
        ),
        cost_estimate=pl.CostEstimate(
            flops=8 * length * width * inner, bytes_accessed=40 * MIB, transcendentals=length * inner
        ),
        name="ffn_backward",
    )(g, hidden, vecs, normed, raised, w_up, w_down, *carried)


def mixer_backward_body(layer, carry, *refs):
    refs = list(refs)
    take = lambda n: [refs.pop(0) for _ in range(n)]
    (hg_ref, vec_ref, cut_ref, proj_ref, signal_ref, long_ref, taps_ref, wo_ref, r_in, normed_in, table_in, wi_in, c_in,
     w1_in) = take(14)
    wmix_ref = take(1)[0] if carry else None
    g_ref, c_out, zout_ref, taps_grad_ref, short_grad_ref, skip_grad_ref, gain_grad_ref, bias_grad_ref = take(8)
    mfin_ref = take(1)[0] if carry else None
    (og_ref, gated_ref, pg_ref, both_ref, got, s1, wkeep, s2, core_s, core_r, s1_s, s1_r, s2_s, s2_r, own_sem,
     out_sem, r_ref, normed_ref, table_ref, wi_ref, late_sem) = take(21)
    if carry:
        mkeep, m2, mz, mzgot, m2_s, m2_r, mz_s, mz_r, m_sem = take(9)
    j = pl.program_id(0)
    steps = pl.num_programs(0)
    length, width = hg_ref.shape
    place = Place()
    half = got.shape[1]
    piece = half // place.depth
    x, y = place.x, place.y
    partners = [place.over_core, place.over_x, place.over_y] + (place.over_z if carry else [])
    table_copy = pltpu.make_async_copy(table_in, table_ref, late_sem.at[0])
    late_copies = [
        pltpu.make_async_copy(source, target, late_sem.at[1 + k])
        for k, (source, target) in enumerate(((r_in, r_ref), (normed_in, normed_ref), (wi_in.at[layer], wi_ref)))
    ]

    def s1_sends():
        return [
            remote(c_in.at[1 + x, :, pl.ds(0, width)], s1.at[0], s1_s.at[0], s1_r.at[0], place.over_x),
            remote(c_in.at[2 - y, :, pl.ds(width, width)], s1.at[1], s1_s.at[1], s1_r.at[1], place.over_y),
        ]

    def own_copies():
        return [
            pltpu.make_async_copy(w1_in.at[0], wkeep.at[0, x], own_sem.at[0]),
            pltpu.make_async_copy(w1_in.at[1], wkeep.at[1, y], own_sem.at[1]),
            pltpu.make_async_copy(c_in.at[2 - x, :, pl.ds(0, width)], wkeep.at[0, 1 - x], own_sem.at[2]),
            pltpu.make_async_copy(c_in.at[1 + y, :, pl.ds(width, width)], wkeep.at[1, 1 - y], own_sem.at[3]),
        ]

    def s2_sends():
        return [
            remote(wkeep.at[0, 1 - y], s2.at[0], s2_s.at[0], s2_r.at[0], place.over_y),
            remote(wkeep.at[1, 1 - x], s2.at[1], s2_s.at[1], s2_r.at[1], place.over_x),
        ]

    def m2_sends():
        return [
            remote(wmix_ref.at[0, 1 - y], m2.at[0], m2_s.at[0], m2_r.at[0], place.over_y),
            remote(wmix_ref.at[1, 1 - x], m2.at[1], m2_s.at[1], m2_r.at[1], place.over_x),
        ]

    def m_copies():
        return [
            pltpu.make_async_copy(wmix_ref.at[0, y], mkeep.at[0], m_sem.at[0]),
            pltpu.make_async_copy(wmix_ref.at[1, x], mkeep.at[1], m_sem.at[1]),
        ]

    def mz_sends():
        return [
            remote(mz.at[:, (place.z + d) % place.depth], mzgot.at[d - 1], mz_s.at[d - 1], mz_r.at[d - 1],
                   place.over_z[d - 1])
            for d in range(1, place.depth)
        ]

    def core_send(t):
        return remote(both_ref.at[t, pl.ds(0, half)], got.at[t], core_s.at[t], core_r.at[t], place.over_core)

    def c_copy(t):
        return pltpu.make_async_copy(both_ref.at[t, pl.ds(half, half)], c_out.at[t], out_sem.at[t])

    @pl.when(j == 0)
    def _():
        greet(partners)
        table_copy.start()
        og_ref[...] = bf(hg_ref[...])
        greeted(partners)
        if carry:
            for copy in m2_sends() + m_copies():
                copy.start()
        for copy in s1_sends() + own_copies() + late_copies:
            copy.start()
        table_copy.wait()

    @pl.when(j == 2)
    def _():
        if carry:
            for copy in m2_sends() + m_copies():
                copy.wait()
            for side in range(2):
                total = bf(f32(mkeep[side]) + f32(m2[side]))
                for k in range(place.depth):
                    mz[side, k] = total[k * piece : (k + 1) * piece]
            for copy in mz_sends():
                copy.start()
        for copy in s1_sends() + own_copies():
            copy.wait()
        wkeep[0, 1 - x] = bf(f32(wkeep[0, 1 - x]) + f32(s1[0]))
        wkeep[1, 1 - y] = bf(f32(wkeep[1, 1 - y]) + f32(s1[1]))
        for copy in s2_sends():
            copy.start()

    @pl.when(j < steps - 1)
    def _():
        chunk = long_ref.shape[1]
        proj = [f32(proj_ref[p]) for p in range(3)]
        kernel = short_taps(cut_ref, layer)
        gate_out, gate_in, vals = mixed_chunk(proj, kernel)
        carried = vals * gate_in
        long_out = f32(long_ref[...])
        skip = vector(cut_ref, layer, 4)
        gated_ref[:, pl.ds(pl.multiple_of(j * chunk, chunk), chunk)] = bf(long_out * gate_out)
        gated_grad = mm_nt(og_ref[...], wo_ref[...])
        long_grad = gated_grad * gate_out
        skip_grad_ref[...] = jnp.sum(carried * long_grad, axis=0, keepdims=True)
        both = mm(table_ref[...], bf(long_grad))
        up_re, up_im = both[:length], both[length:]
        tap_re, tap_im = f32(taps_ref[:length]), f32(taps_ref[length:])
        sig_re, sig_im = f32(signal_ref[:length]), f32(signal_ref[length:])
        left = jnp.concatenate([bf(up_re * tap_re + up_im * tap_im), bf(up_im * tap_re - up_re * tap_im)], axis=0)
        right = jnp.concatenate([bf(up_re * sig_re + up_im * sig_im), bf(up_im * sig_re - up_re * sig_im)], axis=0)
        back = mm_tn(table_ref[...], jnp.concatenate([left, right], axis=1))
        carried_grad = back[:, :chunk] + skip * long_grad
        taps_grad_ref[...] = back[:, chunk:]
        for p, part in enumerate((gated_grad * long_out, carried_grad * vals, carried_grad * gate_in)):
            one, two = row_shift(part, -1), row_shift(part, -2)
            projected_grad = bf(kernel[p][2:3] * part + kernel[p][1:2] * one + kernel[p][0:1] * two)
            for tap, moved in enumerate((two, one, part)):
                short_grad_ref[p, tap : tap + 1, :] = jnp.sum(moved * proj[p], axis=0, keepdims=True)
            pg_ref[:, pl.ds(pl.multiple_of(p * width + j * chunk, chunk), chunk)] = projected_grad

    @pl.when(j == steps - 1)
    def _():
        in_cols, out_cols = 3 * width // 4, width // 4
        for copy in late_copies:
            copy.wait()
        upstream = mm_nt(pg_ref[...], wi_ref[...])
        for t in range(4):
            rights = pg_ref[:, in_cols * t : in_cols * (t + 1)], og_ref[:, out_cols * t : out_cols * (t + 1)]
            products = [bf(mm_tn(left[...], right)) for left, right in zip((normed_ref, gated_ref), rights)]
            store_rows(place, both_ref.at[t], jnp.concatenate(products, axis=1))
            core_send(t).start()
        part, gain_grad, bias_grad = norm_backward(f32(r_ref[...]), vector(vec_ref, layer, 0), upstream)
        total = hg_ref[...] + part
        g_ref[...] = total.astype(g_ref.dtype)
        gain_grad_ref[...] = gain_grad
        bias_grad_ref[...] = bias_grad
        for t in range(4):
            core_send(t).wait()
            both_ref[t, half:] = bf(f32(both_ref[t, half:]) + f32(got[t]))
            c_copy(t).start()
        if carry:
            for copy in mz_sends():
                copy.wait()
            for side in range(2):
                total = f32(mz[side, place.z])
                for d in range(place.depth - 1):
                    total += f32(mzgot[d, side])
                mfin_ref[side] = total
        for copy in s2_sends():
            copy.wait()
        for side, keep in enumerate((y, x)):
            total = bf(f32(wkeep[side, keep]) + f32(s2[side]))
            for k in range(place.depth):
                zout_ref[side, k] = total[k * piece : (k + 1) * piece]
        for t in range(4):
            c_copy(t).wait()


def mixer_backward(
    layer, carry, last, collective, hidden_grad, r, vecs, normed, proj, signal, long_out, taps, table, w_out, w_in, ffn_c,
    ffn_w, *carried
):
    length, width = r.shape
    chunk = 256
    steps = width // chunk
    depth = lax.axis_size("seq") // 2
    piece = width // (2 * depth)
    half = depth * piece
    at = lambda j: jnp.minimum(j, steps - 1)
    b16, b32, dma = jnp.bfloat16, jnp.float32, pltpu.SemaphoreType.DMA
    return pl.pallas_call(
        lambda *refs: mixer_backward_body(layer, carry, *refs),
        grid=(steps + 1,),
        in_specs=[
            whole((length, width)), whole(vecs.shape), pl.BlockSpec((vecs.shape[0], chunk), lambda j: (0, at(j))),
            pl.BlockSpec((3, length, chunk), lambda j: (0, 0, at(j))),
            pl.BlockSpec((2 * length, chunk), lambda j: (0, at(j))),
            pl.BlockSpec((length, chunk), lambda j: (0, at(j))),
            pl.BlockSpec((None, 2 * length, chunk), lambda j: (layer, 0, at(j))),
            pl.BlockSpec((None, chunk, width), lambda j: (layer, at(j), 0)),
        ] + [ANY] * (6 + len(carried)),
        out_specs=[
            whole((length, width)), ANY, whole((2, depth, piece, width)),
            pl.BlockSpec((length, chunk), lambda j: (0, at(j))),
            pl.BlockSpec((3, 3, chunk), lambda j: (0, 0, at(j))),
            pl.BlockSpec((1, chunk), lambda j: (0, at(j))),
            whole((1, width)), whole((1, width)),
        ] + ([whole((2, piece, width // 2))] if carry else []),
        out_shape=[
            sds((length, width), b16 if last else b32), sds((4, half, width), b16),
            sds((2, depth, piece, width), b16),
            sds((length, width), b32), sds((3, 3, width), b32), sds((1, width), b32), sds((1, width), b32),
            sds((1, width), b32),
        ] + ([sds((2, piece, width // 2), b32)] if carry else []),
        scratch_shapes=[
            pltpu.VMEM((length, width), b16), pltpu.VMEM((length, width), b16), pltpu.VMEM((length, 3 * width), b16),
            pltpu.VMEM((4, width, width), b16), pltpu.VMEM((4, half, width), b16),
            pltpu.VMEM((2, half, width), b16), pltpu.VMEM((2, 2, half, width), b16), pltpu.VMEM((2, half, width), b16),
            dma((4,)), dma((4,)), dma((2,)), dma((2,)), dma((2,)), dma((2,)), dma((4,)), dma((4,)),
            pltpu.VMEM((length, width), r.dtype), pltpu.VMEM((length, width), b16), pltpu.VMEM((2 * length, length), b16),
            pltpu.VMEM((width, 3 * width), b16), dma((4,)),
        ] + ([
            pltpu.VMEM((2, half, width // 2), b16), pltpu.VMEM((2, half, width // 2), b16),
            pltpu.VMEM((2, depth, piece, width // 2), b16), pltpu.VMEM((depth - 1, 2, piece, width // 2), b16),
            dma((2,)), dma((2,)), dma((depth - 1,)), dma((depth - 1,)), dma((2,)),
        ] if carry else []) ,
        compiler_params=pltpu.CompilerParams(
            vmem_limit_bytes=63 * MIB, collective_id=collective, has_side_effects=True
        ),
        cost_estimate=pl.CostEstimate(
            flops=2 * length * width * (8 * width + 6 * length), bytes_accessed=50 * MIB, transcendentals=0
        ),
        name="mixer_backward",
    )(hidden_grad, vecs, vecs, proj, signal, long_out, taps, w_out, r, normed, table, w_in, ffn_c, ffn_w, *carried)


SMALL = 128


def closing_body(
    z_in, c_in, g_in, t0_in, t1_in, v0, v1, v2, v3, v4, v5, v6, v7, v8, v9, v10, v11, features_ref, filt_ref, net_ref,
    w3_ref, delta_ref, zfin_ref, mfin_ref, agot, small_ref,
    zgot, zown, mgot, w, m2, mz, mzgot, tgrad, pack, cgot, xgot, xsum, ygot, ysum, zslot, total16, full,
    z_s, z_r, m_s, m_r, m2_s, m2_r, mz_s, mz_r, a_s, a_r, own_sem, sm_s, sm_r, zs_s, zs_r,
):
    place = Place()
    x, y, z, core = place.x, place.y, place.z, place.core
    cols = w.shape[3]
    piece = zown.shape[1]
    rows = agot.shape[1]
    over_both = (place.s, 2 * (1 - y) + 1 - x)
    m_sends = []
    for k in range(2):
        m_sends.append(remote(c_in.at[2 * k + 1 - x, :, pl.ds(0, cols)], mgot.at[0, k], m_s.at[0, k], m_r.at[0, k],
                              place.over_x))
        m_sends.append(remote(c_in.at[2 * (1 - y) + k, :, pl.ds(cols, cols)], mgot.at[1, k], m_s.at[1, k],
                              m_r.at[1, k], place.over_y))
    z_sends = [
        remote(z_in.at[:, (z + d) % place.depth], zgot.at[d - 1], z_s.at[d - 1], z_r.at[d - 1], place.over_z[d - 1])
        for d in range(1, place.depth)
    ]
    own = [pltpu.make_async_copy(z_in.at[:, z], zown, own_sem.at[4])]
    for k in range(2):
        own.append(pltpu.make_async_copy(c_in.at[2 * k + x, :, pl.ds(0, cols)], w.at[0, k], own_sem.at[k]))
        own.append(pltpu.make_async_copy(c_in.at[2 * y + k, :, pl.ds(cols, cols)], w.at[1, k], own_sem.at[2 + k]))
    loads = [
        pltpu.make_async_copy(t0_in, tgrad.at[0], own_sem.at[5]), pltpu.make_async_copy(t1_in, tgrad.at[1], own_sem.at[6]),
    ]
    part = lambda t: g_in.at[pl.ds(pl.multiple_of(t * rows, rows), rows)]
    home = pltpu.make_async_copy(part(place.t), agot.at[place.t], own_sem.at[8])

    def a_sends():
        out = []
        for k, device in enumerate((place.over_x, place.over_y, over_both)):
            out.append(remote(part(device[1]), agot.at[place.t], a_s.at[k], a_r.at[k], device))
        return out

    for copy in loads:
        copy.start()
    partners = [place.over_core, place.over_x, place.over_y, over_both] + place.over_z
    greet(partners)
    greeted(partners)
    for copy in m_sends + z_sends + own + [home]:
        copy.start()

    units = w3_ref.shape[1]
    envelope = decay(delta_ref[...], tgrad.shape[1]) * (1.0 / tgrad.shape[1])
    pack[...] = jnp.zeros_like(pack)
    s1, s2 = filt_ref[0], filt_ref[1]
    u1, h1, u2, h2 = (f32(filt_ref[k]) for k in range(2, 6))
    wide = lambda parts: jnp.concatenate(parts, axis=1)
    for copy in loads:
        copy.wait()
    upstream = [bf(tgrad[layer] * envelope) for layer in range(2)]
    ds2 = wide([mm_nt(upstream[layer], w3_ref[layer]) for layer in range(2)])
    for layer in range(2):
        pack[layer, :64] = mm_tn(s2[:, units * layer : units * (layer + 1)], upstream[layer])
    da2 = ds2 * u2
    span = lambda v, layer: v[:, units * layer : units * (layer + 1)]
    ds1 = wide([mm_nt(bf(span(da2, layer)), bf(net_ref[layer, 48:112, :])) for layer in range(2)])
    da1 = ds1 * u1
    dw2 = wide([mm_tn(span(s1, layer), bf(span(da2, layer))) for layer in range(2)])
    dw1 = mm_tn(bf(features_ref[...]), bf(da1))
    freq = [jnp.sum(ds1 * h1, axis=0, keepdims=True), jnp.sum(ds2 * h2, axis=0, keepdims=True)]
    for k, block in enumerate((dw1[:24], jnp.concatenate([dw1[24:40], freq[0], freq[1], jnp.zeros((6, 128), jnp.float32)]),
                               dw2[:24], dw2[24:48], jnp.concatenate([dw2[48:64], jnp.zeros((8, 128), jnp.float32)]))):
        pack[0, 80:104, 128 * k : 128 * (k + 1)] = block
    vectors = ((v0, v1, v2, v3, v4, v5), (v6, v7, v8, v9, v10, v11))
    for layer in range(2):
        for k in range(5):
            pack[layer, 64 + k : 65 + k, :] = vectors[layer][k][...]
        for p in range(3):
            pack[layer, 69 + 3 * p : 72 + 3 * p, :] = vectors[layer][5][p]

    total16[0] = bf(pack[0])
    total16[1] = bf(pack[1])
    to_core = remote(total16.at[1 - core], cgot, sm_s.at[0], sm_r.at[0], place.over_core)
    to_core.start()
    to_core.wait()
    xsum[...] = bf(f32(total16[core]) + f32(cgot[...]))
    half, quarter = SMALL // 2, SMALL // 4
    side = lambda k, n: pl.ds(pl.multiple_of(k * n, n), n)
    to_x = remote(xsum.at[side(1 - x, half)], xgot, sm_s.at[1], sm_r.at[1], place.over_x)
    to_x.start()

    for copy in own + m_sends:
        copy.wait()
    for k in range(2):
        for n in range(2):
            w[k, n] = bf(f32(w[k, n]) + f32(mgot[k, n]))
    m2_sends = [
        remote(w.at[0, 1 - y], m2.at[0], m2_s.at[0], m2_r.at[0], place.over_y),
        remote(w.at[1, 1 - x], m2.at[1], m2_s.at[1], m2_r.at[1], place.over_x),
    ]
    for copy in m2_sends:
        copy.start()

    to_x.wait()
    ysum[...] = bf(f32(xsum[side(x, half)]) + f32(xgot[...]))
    to_y = remote(ysum.at[side(1 - y, quarter)], ygot, sm_s.at[2], sm_r.at[2], place.over_y)
    to_y.start()
    to_y.wait()
    zslot[z] = bf(f32(ysum[side(y, quarter)]) + f32(ygot[...]))
    zs_sends = [
        remote(zslot.at[z], zslot.at[z], zs_s.at[d - 1], zs_r.at[d - 1], place.over_z[d - 1])
        for d in range(1, place.depth)
    ]
    for copy in zs_sends:
        copy.start()

    for copy in m2_sends:
        copy.wait()
    for copy in a_sends():
        copy.start()
    for k, keep in enumerate((y, x)):
        total = bf(f32(w[k, keep]) + f32(m2[k]))
        for n in range(place.depth):
            mz[k, n] = total[n * piece : (n + 1) * piece]
    mz_sends = [
        remote(mz.at[:, (z + d) % place.depth], mzgot.at[d - 1], mz_s.at[d - 1], mz_r.at[d - 1], place.over_z[d - 1])
        for d in range(1, place.depth)
    ]
    for copy in mz_sends:
        copy.start()

    for copy in z_sends:
        copy.wait()
    total = f32(zown[...])
    for d in range(place.depth - 1):
        total += f32(zgot[d])
    zfin_ref[...] = total

    for copy in zs_sends:
        copy.wait()
    total = f32(zslot[0])
    for k in range(1, place.depth):
        total += f32(zslot[k])
    mine = pl.multiple_of(x * half + y * quarter, quarter)
    full[core, pl.ds(mine, quarter)] = bf(total)
    back_y = remote(full.at[core, pl.ds(mine, quarter)], full.at[core, pl.ds(mine, quarter)], sm_s.at[3], sm_r.at[3],
                    place.over_y)
    back_y.start()
    back_y.wait()
    back_x = remote(full.at[core, side(x, half)], full.at[core, side(x, half)], sm_s.at[4], sm_r.at[4], place.over_x)
    back_x.start()
    back_x.wait()
    back_core = remote(full.at[core], full.at[core], sm_s.at[5], sm_r.at[5], place.over_core)
    back_core.start()
    back_core.wait()
    small_ref[...] = f32(full[...])
    for copy in mz_sends:
        copy.wait()
    for k in range(2):
        total = f32(mz[k, z])
        for d in range(place.depth - 1):
            total += f32(mzgot[d, k])
        mfin_ref[k] = total
    home.wait()
    for copy in a_sends():
        copy.wait()


def closing(collective, ffn_z, mixer_c, grad, taps_grads, vectors, features, filt, net, w3, delta):
    _, depth, piece, width = ffn_z.shape
    length = grad.shape[0]
    half = depth * piece
    b16, b32, dma = jnp.bfloat16, jnp.float32, pltpu.SemaphoreType.DMA
    cols = width // 2
    vm = pl.BlockSpec(memory_space=pltpu.VMEM)
    return pl.pallas_call(
        closing_body,
        in_specs=[ANY] * 5 + [vm] * (len(vectors) + 5),
        out_specs=[vm, vm, ANY, vm],
        out_shape=[
            sds((2, piece, width), b32), sds((2, piece, cols), b32), sds((4, length // 4, width), b16),
            sds((2, SMALL, width), b32),
        ],
        scratch_shapes=[
            pltpu.VMEM((depth - 1, 2, piece, width), b16), pltpu.VMEM((2, piece, width), b16),
            pltpu.VMEM((2, 2, half, cols), b16), pltpu.VMEM((2, 2, half, cols), b16), pltpu.VMEM((2, half, cols), b16),
            pltpu.VMEM((2, depth, piece, cols), b16), pltpu.VMEM((depth - 1, 2, piece, cols), b16),
            pltpu.VMEM((2, length, width), b32),
            pltpu.VMEM((2, SMALL, width), b32), pltpu.VMEM((SMALL, width), b16), pltpu.VMEM((SMALL // 2, width), b16),
            pltpu.VMEM((SMALL, width), b16), pltpu.VMEM((SMALL // 4, width), b16), pltpu.VMEM((SMALL // 2, width), b16),
            pltpu.VMEM((depth, SMALL // 4, width), b16), pltpu.VMEM((2, SMALL, width), b16),
            pltpu.VMEM((2, SMALL, width), b16),
            dma((depth - 1,)), dma((depth - 1,)), dma((2, 2)), dma((2, 2)), dma((2,)), dma((2,)), dma((depth - 1,)),
            dma((depth - 1,)), dma((3,)), dma((3,)), dma((9,)), dma((6,)), dma((6,)), dma((depth - 1,)),
            dma((depth - 1,)),
        ],
        compiler_params=pltpu.CompilerParams(
            vmem_limit_bytes=62 * MIB, collective_id=collective, has_side_effects=True
        ),
        name="closing",
    )(ffn_z, mixer_c, grad, *taps_grads, *vectors, features, filt, net, w3, delta)


def assemble_body(
    out_in, grad_in, f0, f1, m0, m1, small, out_act, grad_x, g1, b1, w_in, short, w1, freq, w2, w3, skip, w_out, g2, b2,
    w_up, w_down,
):
    out_act[...] = f32(out_in[...])
    grad_x[...] = f32(grad_in[...])

    @pl.when(pl.program_id(0) == 0)
    def _():
        units = w2.shape[1]
        cols = m0.shape[2]
        split = w_in.shape[2]
        for layer, (f, m) in enumerate(((f0, m0), (f1, m1))):
            row = slice(layer, layer + 1)
            for k, ref in enumerate((g1, b1, g2, b2, skip)):
                ref[row, :] = small[layer, 64 + k : 65 + k, :]
            for p in range(3):
                for tap in range(3):
                    at = 69 + 3 * p + tap
                    width = small.shape[2]
                    short[layer, tap : tap + 1, p * width : (p + 1) * width] = small[layer, at : at + 1, :]
            lanes = lambda k: slice(128 * k + units * layer, 128 * k + units * (layer + 1))
            w1[layer] = jnp.concatenate([small[0, 80:104, lanes(0)], small[0, 80 : 80 + EMB - 24, lanes(1)]], axis=0)
            freq[layer] = small[0, 96:98, lanes(1)]
            w2[layer] = jnp.concatenate(
                [small[0, 80:104, lanes(2)], small[0, 80:104, lanes(3)], small[0, 80:96, lanes(4)]], axis=0
            )
            w3[layer] = small[layer, :64, :]
            w_in[layer] = jnp.concatenate([m[0], m[1][:, : split - cols]], axis=1)
            w_out[layer] = m[1][:, split - cols :]
            w_up[layer] = f[0]
            w_down[layer] = f[1].T


def assemble(out_act, grad_in, ffn, mixer, small, units):
    slots, rows, width = out_act.shape
    _, piece, cols = ffn[0].shape
    split = 3 * width // 4
    b32 = jnp.float32
    shapes = [
        (2, width), (2, width), (2, piece, split), (2, 3, 3 * width), (2, EMB, units), (2, 2, units), (2, units, units),
        (2, units, width), (2, width), (2, piece, width - split), (2, width), (2, width), (2, piece, cols),
        (2, cols, piece),
    ]
    block = pl.BlockSpec((None, rows, width), lambda j: (j, 0, 0))
    return pl.pallas_call(
        assemble_body,
        grid=(slots,),
        in_specs=[block, block] + [whole(v.shape) for v in (*ffn, *mixer, small)],
        out_specs=[block, block] + [whole(shape) for shape in shapes],
        out_shape=[sds((slots, rows, width), b32)] * 2 + [sds(shape, b32) for shape in shapes],
        compiler_params=pltpu.CompilerParams(vmem_limit_bytes=62 * MIB),
        name="assemble",
    )(out_act, grad_in, *ffn, *mixer, small)


def feature_table(length):
    bands = (EMB - 1) // 2
    step = np.arange(length, dtype=np.float64)[:, None]
    phases = 2.0 * math.pi / length * step * np.linspace(1e-4, bands - 1, bands)[None]
    parts = [step / (length - 1), np.cos(phases), -np.sin(phases), np.zeros((length, 40 - EMB))]
    return np.concatenate(parts, axis=1).astype(np.float32)


def whole_sequences(
    x_in, cotangent, counts, ln1_gain, ln1_bias, w_in, short_w, filt_w1, filt_freq, filt_w2, filt_w3, long_bias,
    w_out, ln2_gain, ln2_bias, w_up, w_down,
):
    micro_count, cap_size, tok_rows, width = x_in.shape
    slots = micro_count * cap_size
    layers = w_up.shape[0]
    toks = lax.axis_size("tok")
    length = tok_rows * toks
    me = lax.axis_index("tok")
    live = (me % cap_size < counts[me // cap_size, 0]).astype(jnp.float32).reshape(1, 1)
    table = jnp.asarray(spectral_table(length))
    features = jnp.asarray(feature_table(length))
    delta = jnp.asarray(
        np.abs(np.linspace(math.log(0.01) / 0.3, math.log(0.01) / 1.5, width, dtype=np.float64))[None].astype(np.float32)
    )
    blocks = lambda v: v.reshape(slots, tok_rows, width)
    r, filt, spectra, vecs, net = front(
        2 * layers + 1, blocks(x_in), table, features, delta, ln1_gain, ln1_bias, ln2_gain, ln2_bias, long_bias, short_w,
        filt_w1, filt_freq, filt_w2, filt_w3,
    )
    kept = []
    for layer in range(layers):
        moving = (blocks(cotangent),) if layer == 0 else ()
        hidden, normed, proj, signal, long_out, *moved = mixer_forward(
            layer, 2 * layers + 2, r, vecs, w_in, table, spectra, w_out, *moving
        )
        upstream = moved[0] if moved else upstream
        result, normed_two, raised = ffn_forward(
            layer, hidden, vecs, w_up, w_down, *((live,) if layer == layers - 1 else ())
        )
        kept.append((r, hidden, normed, proj, signal, long_out, normed_two, raised))
        r = result

    grad = upstream
    vectors, taps_grads, done = [None] * layers, [None] * layers, {}
    carried_ffn, carried_mixer = (live, r), ()
    for layer in reversed(range(layers)):
        r, hidden, normed, proj, signal, long_out, normed_two, raised = kept[layer]
        carry = layer < layers - 1
        grad, grad_g2, grad_b2, ffn_c, ffn_w, *rest = ffn_backward(
            layer, carry, 2 * layer, grad, hidden, vecs, normed_two, raised, w_up, w_down, *carried_ffn
        )
        if carry:
            done["ffn", layer + 1], *carried_mixer = rest
        else:
            out_act = rest[0]
        grad, mixer_c, ffn_z, taps_grads[layer], grad_short, grad_skip, grad_g1, grad_b1, *rest = mixer_backward(
            layer, carry, layer == 0, 2 * layer + 1, grad, r, vecs, normed, proj, signal, long_out, spectra, table, w_out,
            w_in, ffn_c, ffn_w, *carried_mixer,
        )
        if carry:
            done["mixer", layer + 1] = rest[0]
        carried_ffn = (ffn_z, mixer_c)
        vectors[layer] = (grad_g1, grad_b1, grad_g2, grad_b2, grad_skip, grad_short)
    done["ffn", 0], done["mixer", 0], grad_in, small = closing(
        2 * layers, *carried_ffn, grad, taps_grads, vectors[0] + vectors[1], features, filt, net, filt_w3, delta
    )
    pair = lambda kind: [done[kind, layer] for layer in range(layers)]
    out_act, grad_in, *grads = assemble(out_act, grad_in, pair("ffn"), pair("mixer"), small, filt_w2.shape[1])
    home = lambda v: v.reshape(micro_count, cap_size, tok_rows, width)
    return (home(out_act), home(grad_in), *grads)


def shards(*args):
    micro_count, cap_size = args[0].shape[:2]
    if lax.axis_size("tok") == 4 and micro_count * cap_size == 4:
        return whole_sequences(*args)
    return split_positions(*args)


def solution(mesh):
    return jax.shard_map(
        shards,
        mesh=mesh,
        in_specs=(
            P(None, "seq", "tok", None),
            P(None, "seq", "tok", None),
            P(None, "seq"),
            P(),
            P(),
            P(),
            P(),
            P(),
            P(),
            P(),
            P(),
            P(),
            P(),
            P(),
            P(),
            P(),
            P(),
        ),
        out_specs=(
            P(None, "seq", "tok", None),
            P(None, "seq", "tok", None),
            P(),
            P(),
            P(None, "seq", "tok"),
            P(),
            P(),
            P(),
            P(),
            P(),
            P(),
            P(None, "seq", "tok"),
            P(),
            P(),
            P(None, "seq", "tok"),
            P(None, "tok", "seq"),
        ),
        check_vma=False,
    )
```

```python
import math

import jax
import jax.numpy as jnp
import numpy as np
from jax import lax
from jax.experimental import pallas as pl
from jax.experimental.pallas import tpu as pltpu
from jax.sharding import PartitionSpec as P

EMB = 33
INNER = 64


HIGHEST = lax.Precision.HIGHEST
NORM_EPS = 1e-05
MOD_SHIFT = 0.05


def passed_along(block, axis, distance):
    devices = range(lax.axis_size(axis))
    route = [(i - distance, i) for i in devices if i - distance in devices]
    return lax.ppermute(block, axis, route)


def for_sending(value):

    def short(part):
        return part.astype(jnp.bfloat16) if part.dtype == jnp.float32 else part

    return jax.tree.map(short, value)


def position_features(length):
    band_count = (EMB - 1) // 2
    step_index = jnp.arange(length, dtype=jnp.int32).astype(jnp.float32)
    time_grid = step_index / (length - 1)
    base_angle = step_index * (2.0 * math.pi / length)
    band_freq = jnp.linspace(0.0001, band_count - 1, band_count, dtype=jnp.float32)
    phases = base_angle[:, None] * band_freq[None, :]
    return jnp.concatenate([time_grid[:, None], jnp.cos(phases), -jnp.sin(phases)], axis=1)


def decay_table(time_grid, first_chan, channels, model_width):
    fast_rate = math.log(0.01) / 0.3
    slow_rate = math.log(0.01) / 1.5
    chan_index = first_chan + jnp.arange(channels, dtype=jnp.int32).astype(jnp.float32)
    deltas = jnp.abs(fast_rate + (slow_rate - fast_rate) * chan_index / (model_width - 1))
    return jnp.exp(-time_grid * deltas[None, :]) + MOD_SHIFT


def filter_taps(features, weight_one, sine_freq, weight_two, weight_three, envelope):
    first_sine = jnp.sin(sine_freq[0] * jnp.dot(features, weight_one, precision=HIGHEST))
    second_sine = jnp.sin(sine_freq[1] * jnp.dot(first_sine, weight_two, precision=HIGHEST))
    return jnp.dot(second_sine, weight_three, precision=HIGHEST) * envelope


def layer_norm(values_in, gain_vec, bias_vec):
    mean_row = jnp.mean(values_in, axis=-1, keepdims=True)
    centred = values_in - mean_row
    variance = jnp.mean(centred * centred, axis=-1, keepdims=True)
    return centred * lax.rsqrt(variance + NORM_EPS) * gain_vec + bias_vec


def gelu_tanh(values_in):
    return jax.nn.gelu(values_in, approximate=True)


def dft_tables(outer_size, inner_size):
    padded_len = outer_size * inner_size
    outer_index = jnp.arange(outer_size, dtype=jnp.int32)
    half_index = jnp.arange(outer_size // 2, dtype=jnp.int32)
    inner_index = jnp.arange(inner_size, dtype=jnp.int32)
    angle_outer = (outer_index[:, None] * half_index[None, :] % outer_size).astype(jnp.float32) * (
        2.0 * math.pi / outer_size
    )
    angle_twist = (outer_index[:, None] * inner_index[None, :] % padded_len).astype(jnp.float32) * (
        2.0 * math.pi / padded_len
    )
    angle_inner = (inner_index[:, None] * inner_index[None, :] % inner_size).astype(jnp.float32) * (
        2.0 * math.pi / inner_size
    )
    return (
        jnp.cos(angle_outer),
        jnp.sin(angle_outer),
        jnp.cos(angle_twist)[None, :, :, None],
        jnp.sin(angle_twist)[None, :, :, None],
        jnp.cos(angle_inner),
        jnp.sin(angle_inner),
    )


def forward_dft(series, tables):
    cos_outer, sin_outer, cos_twist, sin_twist, cos_inner, sin_inner = tables
    outer_size = cos_outer.shape[0]
    inner_size = cos_inner.shape[0]
    seq_count = series.shape[0]
    channels = series.shape[2]
    token_grid = series.reshape(seq_count, outer_size // 2, inner_size, channels)
    first_re = jnp.einsum("ka,sabc->skbc", cos_outer, token_grid, precision=HIGHEST)
    first_im = -jnp.einsum("ka,sabc->skbc", sin_outer, token_grid, precision=HIGHEST)
    twist_re = first_re * cos_twist + first_im * sin_twist
    twist_im = first_im * cos_twist - first_re * sin_twist
    out_re = jnp.einsum("skbc,bj->skjc", twist_re, cos_inner, precision=HIGHEST) + jnp.einsum(
        "skbc,bj->skjc", twist_im, sin_inner, precision=HIGHEST
    )
    out_im = jnp.einsum("skbc,bj->skjc", twist_im, cos_inner, precision=HIGHEST) - jnp.einsum(
        "skbc,bj->skjc", twist_re, sin_inner, precision=HIGHEST
    )
    return (out_re, out_im)


def inverse_dft(spec_re, spec_im, tables):
    cos_outer, sin_outer, cos_twist, sin_twist, cos_inner, sin_inner = tables
    outer_size = cos_outer.shape[0]
    inner_size = cos_inner.shape[0]
    seq_count = spec_re.shape[0]
    channels = spec_re.shape[3]
    back_re = jnp.einsum("skjc,bj->skbc", spec_re, cos_inner, precision=HIGHEST) - jnp.einsum(
        "skjc,bj->skbc", spec_im, sin_inner, precision=HIGHEST
    )
    back_im = jnp.einsum("skjc,bj->skbc", spec_im, cos_inner, precision=HIGHEST) + jnp.einsum(
        "skjc,bj->skbc", spec_re, sin_inner, precision=HIGHEST
    )
    turn_re = back_re * cos_twist - back_im * sin_twist
    turn_im = back_im * cos_twist + back_re * sin_twist
    token_grid = (
        jnp.einsum("skbc,ka->sabc", turn_re, cos_outer, precision=HIGHEST)
        - jnp.einsum("skbc,ka->sabc", turn_im, sin_outer, precision=HIGHEST)
    ) / (outer_size * inner_size)
    return token_grid.reshape(seq_count, outer_size // 2 * inner_size, channels)


def complex_product(left_re, left_im, right_re, right_im):
    return (left_re * right_re - left_im * right_im, left_re * right_im + left_im * right_re)


def add_tree(running, update):
    if running is None:
        return update
    return jax.tree.map(jnp.add, running, update)


def split_positions(
    x_in,
    cotangent,
    counts,
    ln1_gain,
    ln1_bias,
    w_in,
    short_w,
    filt_w1,
    filt_freq,
    filt_w2,
    filt_w3,
    long_bias,
    w_out,
    ln2_gain,
    ln2_bias,
    w_up,
    w_down,
):
    tok_count = lax.axis_size("tok")
    micro_count, cap_size, tok_rows, model_width = x_in.shape
    channels = model_width // tok_count
    first_chan = lax.axis_index("tok") * channels
    layer_count = w_in.shape[0]
    length = tok_rows * tok_count
    tables = dft_tables(2 * length // INNER, INNER)
    features = position_features(length)
    envelope = decay_table(features[:, :1], first_chan.astype(jnp.float32), channels, model_width)
    gain_one = ln1_gain.astype(jnp.float32)
    bias_one = ln1_bias.astype(jnp.float32)
    gain_two = ln2_gain.astype(jnp.float32)
    bias_two = ln2_bias.astype(jnp.float32)
    short_taps = short_w.astype(jnp.float32)
    skip_scale = long_bias.astype(jnp.float32)
    filt_one = filt_w1.astype(jnp.float32)
    filt_sine = filt_freq.astype(jnp.float32)
    filt_two = filt_w2.astype(jnp.float32)
    filt_three = filt_w3.astype(jnp.float32)

    def taps_of(layer_index):

        def taps_fn(weight_one, sine_freq, weight_two, three_slice):
            return filter_taps(features, weight_one, sine_freq, weight_two, three_slice, envelope)

        three_slice = lax.dynamic_slice_in_dim(filt_three[layer_index], first_chan, channels, 1)
        return jax.vjp(
            taps_fn,
            filt_one[layer_index],
            filt_sine[layer_index],
            filt_two[layer_index],
            three_slice,
        )

    taps_spectra = []
    for layer_index in range(layer_count):
        filter_rows, _ = taps_of(layer_index)
        taps_spectra.append(forward_dft(filter_rows[None], tables))

    def backward_layer(grad_rows, kept, layer_index):
        (
            residual,
            normed,
            padded,
            short_out,
            carried,
            long_out,
            gated_rows,
            hidden,
            normed_two,
            raised,
            active,
            kept_signal,
        ) = kept
        down_grad = grad_rows.astype(jnp.bfloat16)
        active_grad = jnp.einsum(
            "std,fd->stf", down_grad, w_down[layer_index], preferred_element_type=jnp.float32
        )
        _, gelu_pull = jax.vjp(gelu_tanh, raised)
        raised_grad = gelu_pull(active_grad)[0].astype(jnp.bfloat16)
        normed_two_grad = jnp.einsum(
            "stf,df->std", raised_grad, w_up[layer_index], preferred_element_type=jnp.float32
        )
        _, second_pull = jax.vjp(layer_norm, hidden, gain_two[layer_index], bias_two[layer_index])
        hidden_part, grad_gain_two, grad_bias_two = second_pull(normed_two_grad)
        hidden_grad = grad_rows + hidden_part
        out_grad = hidden_grad.astype(jnp.bfloat16)
        gated_grad = jnp.einsum(
            "ste,de->std", out_grad, w_out[layer_index], preferred_element_type=jnp.float32
        )
        gate_out = short_out[:, :, :model_width]
        gate_in = short_out[:, :, model_width : 2 * model_width]
        values = short_out[:, :, 2 * model_width :]
        long_grad = gated_grad * gate_out
        gate_out_grad = gated_grad * long_out
        grad_skip = jnp.sum(carried * long_grad, axis=(0, 1))
        spec_re, spec_im = taps_spectra[layer_index]
        upstream_re, upstream_im = forward_dft(
            lax.all_to_all(
                long_grad.astype(jnp.bfloat16), "tok", split_axis=2, concat_axis=1, tiled=True
            ).astype(long_grad.dtype),
            tables,
        )
        back_re, back_im = complex_product(upstream_re, upstream_im, spec_re, -spec_im)
        back_rows = lax.all_to_all(
            for_sending(inverse_dft(back_re, back_im, tables)),
            "tok",
            split_axis=1,
            concat_axis=2,
            tiled=True,
        )
        back_rows, upstream_re, upstream_im = (back_rows, upstream_re, upstream_im)
        signal_re, signal_im = kept_signal
        cross_re = jnp.sum(signal_re * upstream_re + signal_im * upstream_im, axis=0)
        cross_im = jnp.sum(signal_re * upstream_im - signal_im * upstream_re, axis=0)
        carried_grad = back_rows + skip_scale[layer_index] * long_grad
        short_grad = jnp.concatenate(
            [gate_out_grad, carried_grad * values, carried_grad * gate_in], axis=2
        )
        next_rows = passed_along(for_sending(short_grad[:, :2, :]), "tok", -1)
        extended = jnp.concatenate([short_grad, next_rows], axis=1)
        kernel = short_taps[layer_index]
        projected_grad = (
            kernel[2] * short_grad + kernel[1] * extended[:, 1:-1] + kernel[0] * extended[:, 2:]
        ).astype(jnp.bfloat16)
        grad_short = jnp.stack(
            [
                jnp.sum(short_grad * padded[:, tap_index : tap_index + tok_rows], axis=(0, 1))
                for tap_index in range(3)
            ]
        )
        normed_grad = jnp.einsum(
            "ste,de->std", projected_grad, w_in[layer_index], preferred_element_type=jnp.float32
        )
        _, first_pull = jax.vjp(layer_norm, residual, gain_one[layer_index], bias_one[layer_index])
        residual_part, grad_gain_one, grad_bias_one = first_pull(normed_grad)
        left_all = (
            lax.all_gather(down_grad, "tok", axis=1, tiled=True),
            lax.all_gather(gated_rows, "tok", axis=1, tiled=True),
            lax.all_gather(normed_two, "tok", axis=1, tiled=True),
            lax.all_gather(normed, "tok", axis=1, tiled=True),
        )
        right_cols = (
            lax.all_to_all(active, "tok", split_axis=2, concat_axis=1, tiled=True),
            lax.all_to_all(out_grad, "tok", split_axis=2, concat_axis=1, tiled=True),
            lax.all_to_all(raised_grad, "tok", split_axis=2, concat_axis=1, tiled=True),
            lax.all_to_all(projected_grad, "tok", split_axis=2, concat_axis=1, tiled=True),
        )
        grad_down = jnp.einsum(
            "stf,std->fd", right_cols[0], left_all[0], preferred_element_type=jnp.float32
        )
        grad_out = jnp.einsum(
            "std,ste->de", left_all[1], right_cols[1], preferred_element_type=jnp.float32
        )
        grad_up = jnp.einsum(
            "std,stf->df", left_all[2], right_cols[2], preferred_element_type=jnp.float32
        )
        grad_in_proj = jnp.einsum(
            "std,ste->de", left_all[3], right_cols[3], preferred_element_type=jnp.float32
        )
        bundle = (
            (grad_in_proj, grad_out, grad_up, grad_down),
            (grad_gain_one, grad_bias_one, grad_short, grad_skip, grad_gain_two, grad_bias_two),
            (cross_re, cross_im),
        )
        return (hidden_grad + residual_part, bundle)

    def filter_grads(cross_re, cross_im, layer_index):
        taps_grad = inverse_dft(cross_re[None], cross_im[None], tables)[0]
        _, taps_pull = taps_of(layer_index)
        grad_one, grad_sine, grad_two, grad_three = taps_pull(taps_grad)
        grad_three_full = lax.dynamic_update_slice_in_dim(
            jnp.zeros_like(filt_three[layer_index]), grad_three, first_chan, 1
        )
        return (grad_one, grad_sine, grad_two, grad_three_full)

    outputs = []
    input_grads = []
    running = None
    reduced = None
    for micro_index in range(micro_count):
        live_mask = (jnp.arange(cap_size, dtype=jnp.int32) < counts[micro_index, 0]).astype(
            jnp.float32
        )[:, None, None]
        residual = x_in[micro_index].astype(jnp.float32)
        saved = []
        for layer_index in range(layer_count):
            forward_normed = layer_norm(
                residual, gain_one[layer_index], bias_one[layer_index]
            ).astype(jnp.bfloat16)
            projected = jnp.einsum(
                "std,de->ste", forward_normed, w_in[layer_index], preferred_element_type=jnp.float32
            )
            prev_rows = passed_along(projected[:, -2:, :], "tok", 1)
            forward_padded = jnp.concatenate([prev_rows, projected], axis=1)
            forward_kernel = short_taps[layer_index]
            forward_short_out = (
                forward_kernel[0] * forward_padded[:, :-2]
                + forward_kernel[1] * forward_padded[:, 1:-1]
                + forward_kernel[2] * forward_padded[:, 2:]
            )
            forward_gate_out = forward_short_out[:, :, :model_width]
            forward_gate_in = forward_short_out[:, :, model_width : 2 * model_width]
            forward_values = forward_short_out[:, :, 2 * model_width :]
            forward_carried = forward_values * forward_gate_in
            forward_spec_re, forward_spec_im = taps_spectra[layer_index]
            convolve_signal_re, convolve_signal_im = forward_dft(
                lax.all_to_all(forward_carried, "tok", split_axis=2, concat_axis=1, tiled=True),
                tables,
            )
            prod_re, prod_im = complex_product(
                convolve_signal_re, convolve_signal_im, forward_spec_re, forward_spec_im
            )
            convolve_back_rows = lax.all_to_all(
                inverse_dft(prod_re, prod_im, tables),
                "tok",
                split_axis=1,
                concat_axis=2,
                tiled=True,
            )
            results = (convolve_back_rows, convolve_signal_re, convolve_signal_im)
            forward_long_out = results[0] + skip_scale[layer_index] * forward_carried
            forward_gated_rows = (forward_long_out * forward_gate_out).astype(jnp.bfloat16)
            forward_hidden = residual + jnp.einsum(
                "std,de->ste",
                forward_gated_rows,
                w_out[layer_index],
                preferred_element_type=jnp.float32,
            )
            forward_normed_two = layer_norm(
                forward_hidden, gain_two[layer_index], bias_two[layer_index]
            ).astype(jnp.bfloat16)
            forward_raised = jnp.einsum(
                "std,df->stf",
                forward_normed_two,
                w_up[layer_index],
                preferred_element_type=jnp.float32,
            )
            forward_active = gelu_tanh(forward_raised).astype(jnp.bfloat16)
            result = forward_hidden + jnp.einsum(
                "stf,fd->std",
                forward_active,
                w_down[layer_index],
                preferred_element_type=jnp.float32,
            )
            forward_kept = (
                residual,
                forward_normed,
                forward_padded,
                forward_short_out,
                forward_carried,
                forward_long_out,
                forward_gated_rows,
                forward_hidden,
                forward_normed_two,
                forward_raised,
                forward_active,
                results[1:],
            )
            residual = result
            kept = forward_kept
            saved.append(kept)
        outputs.append(residual * live_mask)
        grad_rows = cotangent[micro_index].astype(jnp.float32) * live_mask
        layer_bundles = [None] * layer_count
        for layer_index in reversed(range(layer_count)):
            grad_rows, bundle = backward_layer(grad_rows, saved[layer_index], layer_index)
            layer_bundles[layer_index] = bundle
        input_grads.append(grad_rows)
        running = add_tree(running, layer_bundles)
    mats = [
        jnp.stack([running[layer_index][0][member] for layer_index in range(layer_count)])
        for member in range(4)
    ]
    vecs = [
        jnp.stack([running[layer_index][1][member] for layer_index in range(layer_count)])
        for member in range(6)
    ]
    filter_parts = [
        filter_grads(running[layer_index][2][0], running[layer_index][2][1], layer_index)
        for layer_index in range(layer_count)
    ]
    filt_parts = [
        jnp.stack([filter_parts[layer_index][member] for layer_index in range(layer_count)])
        for member in range(4)
    ]
    mat_done = (
        lax.psum_scatter(
            mats[0].astype(jnp.bfloat16), "seq", scatter_dimension=1, tiled=True
        ).astype(jnp.float32),
        lax.psum_scatter(
            mats[1].astype(jnp.bfloat16), "seq", scatter_dimension=1, tiled=True
        ).astype(jnp.float32),
        lax.psum_scatter(
            mats[2].astype(jnp.bfloat16), "seq", scatter_dimension=1, tiled=True
        ).astype(jnp.float32),
        lax.psum_scatter(
            mats[3].astype(jnp.bfloat16), "seq", scatter_dimension=2, tiled=True
        ).astype(jnp.float32),
    )
    small_done = lax.psum(
        (
            vecs[0],
            vecs[1],
            vecs[2],
            vecs[3],
            vecs[4],
            vecs[5],
            filt_parts[0],
            filt_parts[1],
            filt_parts[2],
            filt_parts[3],
        ),
        ("seq", "tok"),
    )
    reduced = (tuple(mat_done), tuple(small_done))
    mat_done, small_done = reduced
    return (
        jnp.stack(outputs),
        jnp.stack(input_grads),
        small_done[0],
        small_done[1],
        mat_done[0],
        small_done[2],
        small_done[6],
        small_done[7],
        small_done[8],
        small_done[9],
        small_done[3],
        mat_done[1],
        small_done[4],
        small_done[5],
        mat_done[2],
        mat_done[3],
    )


MIB = 1 << 20
MESH = pl.DeviceIdType.MESH


def mm(left, right):
    return jnp.dot(left, right, preferred_element_type=jnp.float32)


def mm_nt(left, right):
    return lax.dot_general(left, right, (((1,), (1,)), ((), ())), preferred_element_type=jnp.float32)


def mm_tn(left, right):
    return lax.dot_general(left, right, (((0,), (0,)), ((), ())), preferred_element_type=jnp.float32)


def f32(values):
    return values.astype(jnp.float32)


def bf(values):
    return values.astype(jnp.bfloat16)


def row_shift(values, distance):
    rows = values.shape[0]
    index = lax.broadcasted_iota(jnp.int32, values.shape, 0)
    rolled = pltpu.roll(values, distance % rows, 0)
    kept = index >= distance if distance > 0 else index < rows + distance
    return jnp.where(kept, rolled, 0.0)


def standardised(values):
    mean = jnp.mean(values, axis=-1, keepdims=True)
    centred = values - mean
    scale = lax.rsqrt(jnp.mean(centred * centred, axis=-1, keepdims=True) + NORM_EPS)
    return centred * scale, scale


def norm_backward(values, gain, upstream):
    xh, scale = standardised(values)
    dxh = upstream * gain
    part = scale * (
        dxh - jnp.mean(dxh, axis=-1, keepdims=True) - xh * jnp.mean(dxh * xh, axis=-1, keepdims=True)
    )
    return part, jnp.sum(upstream * xh, axis=0, keepdims=True), jnp.sum(upstream, axis=0, keepdims=True)


def gelu_parts(values):
    slope = math.sqrt(2.0 / math.pi)
    square = values * values
    bent = jnp.tanh(slope * values * (1.0 + 0.044715 * square))
    half = 0.5 * (1.0 + bent)
    inner = slope * (1.0 + (3.0 * 0.044715) * square)
    return values * half, half + 0.5 * values * (1.0 - bent * bent) * inner


def spectral_table(length):
    k = np.arange(length, dtype=np.int64)[:, None]
    t = np.arange(length, dtype=np.int64)[None, :]
    angle = ((2 * k + 1) * t % (4 * length)).astype(np.float64) * (2.0 * math.pi / (4 * length))
    return np.concatenate([np.cos(angle), -np.sin(angle)], axis=0).astype(jnp.bfloat16)


def whole(shape):
    return pl.BlockSpec(shape, lambda j: (0,) * len(shape), pipeline_mode=pl.Buffered(1))


VECS = 14


def vector(ref, layer, k):
    return ref[VECS * layer + k : VECS * layer + k + 1, :]


def short_taps(ref, layer):
    return [ref[VECS * layer + 5 + 3 * p : VECS * layer + 8 + 3 * p, :] for p in range(3)]


ANY = pl.BlockSpec(memory_space=pl.ANY)


def sds(shape, kind):
    return jax.ShapeDtypeStruct(shape, kind)


class Place:
    def __init__(self):
        s, t = lax.axis_index("seq"), lax.axis_index("tok")
        self.depth = lax.axis_size("seq") // 2
        self.z, self.core, self.y, self.x = s // 2, s % 2, t // 2, t % 2
        self.s, self.t = s, t
        self.over_core = (2 * self.z + 1 - self.core, t)
        self.over_x = (s, 2 * self.y + 1 - self.x)
        self.over_y = (s, 2 * (1 - self.y) + self.x)
        self.over_z = [(2 * ((self.z + d) % self.depth) + self.core, t) for d in range(1, self.depth)]
        self.from_z = [(2 * ((self.z + self.depth - d) % self.depth) + self.core, t) for d in range(1, self.depth)]


def greet(partners):
    barrier = pltpu.get_barrier_semaphore()
    for partner in partners:
        pl.semaphore_signal(barrier, inc=1, device_id=partner, device_id_type=MESH)


def greeted(partners):
    pl.semaphore_wait(pltpu.get_barrier_semaphore(), len(partners))


def remote(source, target, sent, landed, device):
    return pltpu.make_async_remote_copy(
        src_ref=source, dst_ref=target, send_sem=sent, recv_sem=landed, device_id=device, device_id_type=MESH
    )


def other_first(place, s, piece):
    half = place.depth * piece
    mine = (s % 2 + place.core + 1) % 2
    return pl.multiple_of(mine * half + (s // 2) * piece, 16)


def store_rows(place, target, values):
    piece = values.shape[0] // (2 * place.depth)
    for s in range(2 * place.depth):
        target[pl.ds(other_first(place, s, piece), piece), :] = values[s * piece : (s + 1) * piece]


class Transpose:
    def __init__(self, place, source, target, sent, landed, own, gathering):
        self.place, self.source, self.target, self.sent, self.landed, self.own = place, source, target, sent, landed, own
        self.gathering = gathering
        self.partners = [place.over_x, place.over_y, (place.s, 2 * (1 - place.y) + 1 - place.x)]

    def block(self, ref, k, flat):
        if not flat:
            return ref.at[k]
        rows = ref.shape[0] // 4
        return ref.at[pl.ds(pl.multiple_of(k * rows, rows), rows)]

    def copies(self):
        me = self.place.t
        flat_in, flat_out = not self.gathering, self.gathering
        target = self.block(self.target, me, flat_out)
        out = [
            remote(self.block(self.source, device[1], flat_in), target, self.sent.at[k], self.landed.at[k], device)
            for k, device in enumerate(self.partners)
        ]
        return out + [pltpu.make_async_copy(self.block(self.source, me, flat_in), target, self.own)]

    def start(self):
        for copy in self.copies():
            copy.start()

    def wait(self):
        for copy in self.copies():
            copy.wait()


TRANSPOSE_SEMS = [pltpu.SemaphoreType.DMA((3,)), pltpu.SemaphoreType.DMA((3,)), pltpu.SemaphoreType.DMA]


def sine_cosine(angle):
    turns = jnp.floor(angle * (2.0 / math.pi) + 0.5)
    rest = ((angle - turns * 1.5703125) - turns * 4.837512969970703e-4) - turns * 7.549789948768648e-8
    square = rest * rest
    sine = rest + rest * square * (
        -1.6666654611e-1 + square * (8.3321608736e-3 + square * -1.9515295891e-4)
    )
    cosine = 1.0 - 0.5 * square + square * square * (
        4.166664568298827e-2 + square * (-1.388731625493765e-3 + square * 2.443315711809948e-5)
    )
    quarter = turns - 4.0 * jnp.floor(turns * 0.25)
    odd = (quarter == 1.0) | (quarter == 3.0)
    sin_sign = jnp.where(quarter >= 2.0, -1.0, 1.0)
    cos_sign = jnp.where((quarter == 1.0) | (quarter == 2.0), -1.0, 1.0)
    return sin_sign * jnp.where(odd, cosine, sine), cos_sign * jnp.where(odd, sine, cosine)


def decay(delta, length):
    time = lax.broadcasted_iota(jnp.int32, (length, delta.shape[1]), 0).astype(jnp.float32) * (1.0 / (length - 1))
    return jnp.exp(-time * delta) + MOD_SHIFT


def front_body(
    x_in, table_in, features_ref, delta_ref, g1, b1, g2, b2, skip, short, fw1, freqs, fw2, w3_ref,
    x_out, filt_out, taps_out, vec_ref, net_ref, table_ref, filt_ref, taps_ref, table_sem, sent, landed, own,
):
    place = Place()
    layers, units, width = w3_ref.shape
    length = table_ref.shape[1]
    table_copy = pltpu.make_async_copy(table_in, table_ref, table_sem.at[0])
    table_copy.start()
    leaving = [pltpu.make_async_copy(filt_ref, filt_out, table_sem.at[1])]
    leaving += [pltpu.make_async_copy(taps_ref.at[k], taps_out.at[k], table_sem.at[2 + k]) for k in range(layers)]
    move = Transpose(place, x_in, x_out, sent, landed, own, True)
    greet(move.partners)
    vec_ref[...] = jnp.zeros_like(vec_ref)
    net_ref[...] = jnp.zeros_like(net_ref)
    for layer in range(layers):
        for k, ref in enumerate((g1, b1, g2, b2, skip)):
            vec_ref[VECS * layer + k : VECS * layer + k + 1, :] = f32(ref[...])[layer : layer + 1]
        for tap in range(3):
            row = f32(short[tap])[layer : layer + 1]
            for p in range(3):
                at = VECS * layer + 5 + 3 * p + tap
                vec_ref[at : at + 1, :] = row[:, width * p : width * (p + 1)]
        for k in range(EMB):
            net_ref[layer, k : k + 1, :] = f32(fw1[k])[layer : layer + 1]
        net_ref[layer, 40:42, :] = f32(freqs[layer])
        net_ref[layer, 48:112, :] = f32(fw2[layer])
    greeted(move.partners)
    move.start()

    def high(a, b):
        top = bf(a)
        return mm(top, bf(b)) + mm(bf(a - f32(top)), bf(b))

    wide = lambda parts: jnp.concatenate(parts, axis=1)
    freq = [wide([net_ref[layer, 40 + k : 41 + k, :] for layer in range(layers)]) for k in range(2)]
    a1 = wide([high(features_ref[...], net_ref[layer, 0:40, :]) for layer in range(layers)])
    s1, c1 = sine_cosine(freq[0] * a1)
    a2 = wide([
        high(s1[:, units * layer : units * (layer + 1)], net_ref[layer, 48:112, :]) for layer in range(layers)
    ])
    s2, c2 = sine_cosine(freq[1] * a2)
    for k, values in enumerate((s1, s2, c1 * freq[0], c1 * a1, c2 * freq[1], c2 * a2)):
        filt_ref[k] = bf(values)
    leaving[0].start()
    envelope = decay(delta_ref[...], length)
    table_copy.wait()
    for layer in range(layers):
        taps = high(s2[:, units * layer : units * (layer + 1)], w3_ref[layer]) * envelope
        taps_ref[layer] = bf(mm(table_ref[...], bf(taps)) * (1.0 / length))
        leaving[1 + layer].start()
    for copy in leaving:
        copy.wait()
    move.wait()


def front(collective, x_in, table, features, delta, *small):
    slots, rows, width = x_in.shape
    layers, units, _ = small[-1].shape
    length = slots * rows
    vm = pl.BlockSpec(memory_space=pltpu.VMEM)
    b16, b32 = jnp.bfloat16, jnp.float32
    return pl.pallas_call(
        front_body,
        in_specs=[ANY, ANY] + [vm] * (2 + len(small)),
        out_specs=[ANY, ANY, ANY, vm, vm],
        out_shape=[
            sds((length, width), b16), sds((6, length, layers * units), b16), sds((layers, 2 * length, width), b16),
            sds((-(-VECS * layers // 8) * 8, width), b32), sds((layers, 112, units), b32),
        ],
        scratch_shapes=[
            pltpu.VMEM((2 * length, length), b16), pltpu.VMEM((6, length, layers * units), b16),
            pltpu.VMEM((layers, 2 * length, width), b16), pltpu.SemaphoreType.DMA((2 + layers,)),
        ] + TRANSPOSE_SEMS,
        compiler_params=pltpu.CompilerParams(
            vmem_limit_bytes=62 * MIB, collective_id=collective, has_side_effects=True
        ),
        name="front",
    )(x_in, table, features, delta, *small)


def mixed_chunk(proj, kernel):
    return [
        kernel[p][0:1] * row_shift(proj[p], 2) + kernel[p][1:2] * row_shift(proj[p], 1) + kernel[p][2:3] * proj[p]
        for p in range(3)
    ]


def gathering_forward_body(layer, carry, *refs):
    refs = list(refs)
    take = lambda n: [refs.pop(0) for _ in range(n)]
    r_ref, vec_ref, cut_ref, w0_ref, w1_ref, w2_ref, table_ref, taps_ref, wo_ref = take(9)
    moving_in = take(1)[0] if carry else None
    hidden_ref, normed_ref, proj_ref, signal_ref, long_ref = take(5)
    if carry:
        moved_out, sent, landed, own = take(4)
        move = Transpose(Place(), moving_in, moved_out, sent, landed, own, True)
    length = r_ref.shape[0]
    j = pl.program_id(0)

    @pl.when(j == 0)
    def _():
        if carry:
            greet(move.partners)
        r = f32(r_ref[...])
        xh, _ = standardised(r)
        normed_ref[...] = bf(xh * vector(vec_ref, layer, 0) + vector(vec_ref, layer, 1))
        hidden_ref[...] = r
        if carry:
            greeted(move.partners)
            move.start()

    normed = normed_ref[...]
    proj = [mm(normed, w_ref[...]) for w_ref in (w0_ref, w1_ref, w2_ref)]
    for p in range(3):
        proj_ref[p] = bf(proj[p])
    gate_out, gate_in, vals = mixed_chunk(proj, short_taps(cut_ref, layer))
    carried = vals * gate_in
    both = mm(table_ref[...], bf(carried))
    re, im = both[:length], both[length:]
    signal_ref[...] = bf(both)
    tap_re, tap_im = f32(taps_ref[:length]), f32(taps_ref[length:])
    out = mm_tn(table_ref[:length], bf(re * tap_re - im * tap_im))
    out += mm_tn(table_ref[length:], bf(re * tap_im + im * tap_re))
    long_out = out + vector(cut_ref, layer, 4) * carried
    long_ref[...] = bf(long_out)
    hidden_ref[...] += mm(bf(long_out * gate_out), wo_ref[...])

    if carry:
        @pl.when(j == pl.num_programs(0) - 1)
        def _():
            move.wait()


def gathering_forward(layer, collective, r, vecs, w_in, table, taps, w_out, *moving):
    length, width = r.shape
    chunk = 256
    steps = width // chunk
    carry = len(moving) > 0
    third = lambda p: pl.BlockSpec((None, width, chunk), lambda j: (layer, 0, p * steps + j))
    return pl.pallas_call(
        lambda *refs: gathering_forward_body(layer, carry, *refs),
        grid=(steps,),
        in_specs=[
            whole((length, width)), whole(vecs.shape), pl.BlockSpec((vecs.shape[0], chunk), lambda j: (0, j)),
            third(0), third(1), third(2),
            whole((2 * length, length)),
            pl.BlockSpec((None, 2 * length, chunk), lambda j: (layer, 0, j)),
            pl.BlockSpec((None, chunk, width), lambda j: (layer, j, 0)),
        ] + [ANY] * len(moving),
        out_specs=[
            whole((length, width)), whole((length, width)),
            pl.BlockSpec((3, length, chunk), lambda j: (0, 0, j)),
            pl.BlockSpec((2 * length, chunk), lambda j: (0, j)),
            pl.BlockSpec((length, chunk), lambda j: (0, j)),
        ] + [ANY] * len(moving),
        out_shape=[
            sds((length, width), jnp.float32), sds((length, width), jnp.bfloat16),
            sds((3, length, width), jnp.bfloat16), sds((2 * length, width), jnp.bfloat16),
            sds((length, width), jnp.bfloat16),
        ] + ([sds((length, width), jnp.bfloat16)] if carry else []),
        scratch_shapes=TRANSPOSE_SEMS if carry else [],
        compiler_params=pltpu.CompilerParams(
            vmem_limit_bytes=60 * MIB, **(dict(collective_id=collective, has_side_effects=True) if carry else {})
        ),
        cost_estimate=pl.CostEstimate(
            flops=2 * length * width * (4 * width + 4 * length), bytes_accessed=30 * MIB, transcendentals=0
        ),
        name="gathering_forward",
    )(r, vecs, vecs, w_in, w_in, w_in, table, taps, w_out, *moving)


def mixer_forward_body(layer, order, *refs):
    refs = list(refs)
    take = lambda n: [refs.pop(0) for _ in range(n)]
    vec_ref, r_in, w_in, table_in, taps_in, wo_in = take(6)
    hidden_ref, normed_out, proj_out, signal_out, long_out = take(5)
    (r_ref, normed_ref, w_ref, table_ref, taps_ref, wo_ref, proj_ref, signal_ref, long_ref, gated_ref, first_sem, w_sem,
     taps_sem, out_sem) = take(14)
    length, width = r_ref.shape
    chunk = 256
    count = width // chunk
    span = lambda c, p=0: pl.ds(p * width + c * chunk, chunk)
    r_copy = pltpu.make_async_copy(r_in, r_ref, first_sem.at[0])
    table_copy = pltpu.make_async_copy(table_in, table_ref, first_sem.at[1])
    wo_copy = pltpu.make_async_copy(wo_in.at[layer], wo_ref, first_sem.at[2])
    w_copies = [
        [pltpu.make_async_copy(w_in.at[layer, :, span(c, p)], w_ref.at[c, :, span(p)], w_sem.at[c, p]) for p in range(3)]
        for c in range(count)
    ]
    taps_copies = [
        pltpu.make_async_copy(taps_in.at[layer, :, span(c)], taps_ref.at[c], taps_sem.at[c]) for c in range(count)
    ]
    out_copies = [
        [
            pltpu.make_async_copy(proj_ref.at[:, :, span(c)], proj_out.at[:, :, span(c)], out_sem.at[c, 0]),
            pltpu.make_async_copy(signal_ref.at[:, span(c)], signal_out.at[:, span(c)], out_sem.at[c, 1]),
            pltpu.make_async_copy(long_ref.at[:, span(c)], long_out.at[:, span(c)], out_sem.at[c, 2]),
        ]
        for c in range(count)
    ]
    normed_copy = pltpu.make_async_copy(normed_ref, normed_out, first_sem.at[3])
    r_copy.start()
    for copy in w_copies[0]:
        copy.start()
    for copy in w_copies[1] + w_copies[2] + [table_copy] + taps_copies + [wo_copy]:
        copy.start()
    r_copy.wait()
    xh, _ = standardised(f32(r_ref[...]))
    normed_ref[...] = bf(xh * vector(vec_ref, layer, 0) + vector(vec_ref, layer, 1))
    normed_copy.start()
    held = [None] * count

    def project(c):
        for copy in w_copies[c]:
            copy.wait()
        columns = slice(c * chunk, (c + 1) * chunk)
        all_three = mm(normed_ref[...], w_ref[c])
        proj = [all_three[:, p * chunk : (p + 1) * chunk] for p in range(3)]
        for p in range(3):
            proj_ref[p, :, columns] = bf(proj[p])
        out_copies[c][0].start()
        kernel = [taps[:, columns] for taps in short_taps(vec_ref, layer)]
        gate_out, gate_in, vals = mixed_chunk(proj, kernel)
        held[c] = (gate_out, vals * gate_in)

    def transform(c):
        if c == 0:
            table_copy.wait()
        taps_copies[c].wait()
        gate_out, carried = held[c]
        both = mm(table_ref[...], bf(carried))
        re, im = both[:length], both[length:]
        signal_ref[:, c * chunk : (c + 1) * chunk] = bf(both)
        out_copies[c][1].start()
        tap_re, tap_im = f32(taps_ref[c, :length]), f32(taps_ref[c, length:])
        held[c] = (gate_out, carried, bf(re * tap_re - im * tap_im), bf(re * tap_im + im * tap_re))

    def back(c):
        columns = slice(c * chunk, (c + 1) * chunk)
        gate_out, carried, prod_re, prod_im = held[c]
        out = mm_tn(table_ref[:length], prod_re) + mm_tn(table_ref[length:], prod_im)
        long = out + vector(vec_ref, layer, 4)[:, columns] * carried
        long_ref[:, columns] = bf(long)
        out_copies[c][2].start()
        gated_ref[:, columns] = bf(long * gate_out)

    for step, c in order:
        (project, transform, back)[step](c)
    wo_copy.wait()
    hidden_ref[...] = f32(r_ref[...]) + mm(gated_ref[...], wo_ref[...])
    for copies in out_copies:
        for copy in copies:
            copy.wait()
    normed_copy.wait()


ORDER = tuple((step, c) for step in range(3) for c in range(3))


def mixer_forward(layer, r, vecs, w_in, table, taps, w_out):
    length, width = r.shape
    chunk = 256
    count = width // chunk
    vm = pl.BlockSpec(memory_space=pltpu.VMEM)
    b16, b32, dma = jnp.bfloat16, jnp.float32, pltpu.SemaphoreType.DMA
    return pl.pallas_call(
        lambda *refs: mixer_forward_body(layer, ORDER, *refs),
        in_specs=[vm] + [ANY] * 5,
        out_specs=[vm] + [ANY] * 4,
        out_shape=[
            sds((length, width), b32), sds((length, width), b16), sds((3, length, width), b16),
            sds((2 * length, width), b16), sds((length, width), b16),
        ],
        scratch_shapes=[
            pltpu.VMEM((length, width), r.dtype), pltpu.VMEM((length, width), b16), pltpu.VMEM((count, width, 3 * chunk), b16),
            pltpu.VMEM((2 * length, length), b16), pltpu.VMEM((count, 2 * length, chunk), b16),
            pltpu.VMEM((width, width), b16), pltpu.VMEM((3, length, width), b16), pltpu.VMEM((2 * length, width), b16),
            pltpu.VMEM((length, width), b16), pltpu.VMEM((length, width), b16), dma((4,)), dma((count, 3)), dma((count,)),
            dma((count, 3)),
        ],
        compiler_params=pltpu.CompilerParams(vmem_limit_bytes=62 * MIB),
        cost_estimate=pl.CostEstimate(
            flops=2 * length * width * (4 * width + 4 * length), bytes_accessed=30 * MIB, transcendentals=0
        ),
        name="mixer_forward",
    )(vecs, r, w_in, table, taps, w_out)


def ffn_forward_body(layer, last, *refs):
    hidden_ref, vec_ref, up_ref, down_ref = refs[:4]
    if last:
        live_ref, out_ref, normed_ref, raised_ref, r_ref = refs[4:]
    else:
        r_ref, normed_ref, raised_ref = refs[4:]

    @pl.when(pl.program_id(0) == 0)
    def _():
        hidden = hidden_ref[...]
        xh, _ = standardised(hidden)
        normed_ref[...] = bf(xh * vector(vec_ref, layer, 2) + vector(vec_ref, layer, 3))
        r_ref[...] = hidden

    raised = mm(normed_ref[...], up_ref[...])
    raised_ref[...] = bf(raised)
    r_ref[...] += mm(bf(gelu_parts(raised)[0]), down_ref[...])

    if last:
        @pl.when(pl.program_id(0) == pl.num_programs(0) - 1)
        def _():
            out_ref[...] = bf(r_ref[...] * live_ref[0, 0])


SCALAR = pl.BlockSpec(memory_space=pltpu.SMEM)


def ffn_forward(layer, hidden, vecs, w_up, w_down, *live):
    length, width = hidden.shape
    inner = w_up.shape[2]
    chunk = inner // 4
    last = len(live) > 0
    return pl.pallas_call(
        lambda *refs: ffn_forward_body(layer, last, *refs),
        grid=(inner // chunk,),
        in_specs=[
            whole((length, width)), whole(vecs.shape),
            pl.BlockSpec((None, width, chunk), lambda j: (layer, 0, j)),
            pl.BlockSpec((None, chunk, width), lambda j: (layer, j, 0)),
        ] + [SCALAR] * len(live),
        out_specs=[
            whole((length, width)), whole((length, width)), pl.BlockSpec((length, chunk), lambda j: (0, j)),
        ],
        out_shape=[
            sds((length, width), jnp.bfloat16 if last else jnp.float32), sds((length, width), jnp.bfloat16),
            sds((length, inner), jnp.bfloat16),
        ],
        scratch_shapes=[pltpu.VMEM((length, width), jnp.float32)] if last else [],
        compiler_params=pltpu.CompilerParams(vmem_limit_bytes=60 * MIB),
        cost_estimate=pl.CostEstimate(
            flops=4 * length * width * inner, bytes_accessed=26 * MIB, transcendentals=length * inner
        ),
        name="ffn_forward",
    )(hidden, vecs, w_up, w_down, *live)


def ffn_backward_body(layer, carry, *refs):
    refs = list(refs)
    take = lambda n: [refs.pop(0) for _ in range(n)]
    g_ref, hidden_in, vec_ref, normed_ref, raised_ref, up_ref, down_ref = take(7)
    zin_ref, min_ref = take(2) if carry else (None, None)
    live_ref, moving_in = (None, None) if carry else take(2)
    upstream = lambda: g_ref[...] if carry else f32(g_ref[...]) * live_ref[0, 0]
    out_ref, gain_grad_ref, bias_grad_ref, c_out, w_out = take(5)
    zfin_ref, wmix_ref = take(2) if carry else (None, None)
    moved_out = None if carry else take(1)[0]
    g16_ref, g16t_ref, normed_t_ref, give, got, c_ref, s1, core_s, core_r, s1_s, s1_r, out_sem, hidden_ref, hidden_sem = take(14)
    hidden_copy = pltpu.make_async_copy(hidden_in, hidden_ref, hidden_sem)
    if carry:
        zgot, zown, mgot, mown, z_s, z_r, m_s, m_r, own_sem = take(9)
    move_sems = None if carry else take(3)
    j = pl.program_id(0)
    steps = pl.num_programs(0)
    width = g_ref.shape[1]
    place = Place()
    half = c_ref.shape[1]
    mcols = width // 2
    move = None if carry else Transpose(place, moving_in, moved_out, *move_sems, False)
    partners = [place.over_core, place.over_x, place.over_y]
    partners += place.over_z if carry else [(place.s, 2 * (1 - place.y) + 1 - place.x)]

    def z_sends():
        piece = [remote(zin_ref.at[:, (place.z + d) % place.depth], zgot.at[d - 1], z_s.at[d - 1], z_r.at[d - 1],
                        place.over_z[d - 1]) for d in range(1, place.depth)]
        return piece

    def m_sends():
        sends = []
        for k in range(2):
            sends.append(remote(min_ref.at[2 * k + 1 - place.x, :, pl.ds(0, mcols)], mgot.at[0, k], m_s.at[0, k],
                                m_r.at[0, k], place.over_x))
            sends.append(remote(min_ref.at[2 * (1 - place.y) + k, :, pl.ds(mcols, mcols)], mgot.at[1, k], m_s.at[1, k],
                                m_r.at[1, k], place.over_y))
        return sends

    def own_copies():
        copies = [pltpu.make_async_copy(zin_ref.at[:, place.z], zown, own_sem.at[4])]
        for k in range(2):
            copies.append(pltpu.make_async_copy(min_ref.at[2 * k + place.x, :, pl.ds(0, mcols)], mown.at[0, k],
                                                own_sem.at[k]))
            copies.append(pltpu.make_async_copy(min_ref.at[2 * place.y + k, :, pl.ds(mcols, mcols)], mown.at[1, k],
                                                own_sem.at[2 + k]))
        return copies

    def core_send(slot, side):
        columns = pl.ds(side * width, width)
        return remote(give.at[slot, :, columns], got.at[slot, :, columns], core_s.at[slot, side], core_r.at[slot, side],
                      place.over_core)

    def s1_send(side, t):
        device = place.over_x if side == 0 else place.over_y
        return remote(c_ref.at[t, :, pl.ds(side * width, width)], s1.at[side], s1_s.at[side], s1_r.at[side], device)

    def c_copy(t):
        return pltpu.make_async_copy(c_ref.at[t], c_out.at[t], out_sem.at[t])

    def finish(t, slot):
        for side in range(2):
            core_send(slot, side).wait_recv()
        c_ref[t] = bf(f32(c_ref[t]) + f32(got[slot]))
        c_copy(t).start()

    @pl.when(j == 0)
    def _():
        greet(partners)
        hidden_copy.start()
        g16 = bf(upstream())
        g16_ref[...] = g16
        store_rows(place, g16t_ref, g16.T)
        store_rows(place, normed_t_ref, normed_ref[...].T)
        out_ref[...] = jnp.zeros_like(out_ref)
        greeted(partners)
        if carry:
            for copy in z_sends() + m_sends() + own_copies():
                copy.start()
        else:
            move.start()

    slot = j % 2

    @pl.when(j == 1)
    def _():
        finish(0, 0)

        @pl.when(place.x == 1)
        def _():
            s1_send(0, 0).start()

        @pl.when(place.y == 1)
        def _():
            s1_send(1, 0).start()

    @pl.when(j == 2)
    def _():
        finish(3, 1)

        @pl.when(place.x == 0)
        def _():
            s1_send(0, 3).start()

        @pl.when(place.y == 0)
        def _():
            s1_send(1, 3).start()

    @pl.when(j == 3)
    def _():
        finish(2, 0)

    @pl.when(j >= 2)
    def _():
        for side in range(2):
            core_send(slot, side).wait_send()

    active, slope = gelu_parts(f32(raised_ref[...]))
    active = bf(active)
    raised_grad = bf(mm_nt(g16_ref[...], down_ref[...]) * slope)
    t = (steps - j) % steps
    for side, (left, right) in enumerate(((normed_t_ref, raised_grad), (g16t_ref, active))):
        product = bf(mm(left[...], right))
        give[slot, :, side * width : (side + 1) * width] = product[:half]
        c_ref[t, :, side * width : (side + 1) * width] = product[half:]
        core_send(slot, side).start()
    out_ref[...] += mm_nt(raised_grad, up_ref[...])

    @pl.when(j == steps - 1)
    def _():
        hidden_copy.wait()
        part, gain_grad, bias_grad = norm_backward(hidden_ref[...], vector(vec_ref, layer, 2), out_ref[...])
        out_ref[...] = upstream() + part
        gain_grad_ref[...] = gain_grad
        bias_grad_ref[...] = bias_grad
        finish(1, 1)
        for k in range(2):
            s1_send(k, 0).wait_recv()
        w_out[0] = bf(f32(c_ref[3 * place.x, :, :width]) + f32(s1[0]))
        w_out[1] = bf(f32(c_ref[3 * place.y, :, width:]) + f32(s1[1]))
        if carry:
            for copy in own_copies():
                copy.wait()
            for copy in z_sends() + m_sends():
                copy.wait()
            total = f32(zown[...])
            for d in range(place.depth - 1):
                total += f32(zgot[d])
            zfin_ref[...] = total
            for side in range(2):
                for k in range(2):
                    wmix_ref[side, k] = bf(f32(mown[side, k]) + f32(mgot[side, k]))
        for k in range(2):
            s1_send(k, 0).wait_send()
            for side in range(2):
                core_send(k, side).wait_send()
        for k in range(steps):
            c_copy(k).wait()
        if not carry:
            move.wait()


def ffn_backward(layer, carry, collective, g, hidden, vecs, normed, raised, w_up, w_down, *carried):
    length, width = g.shape
    inner = w_up.shape[2]
    chunk = inner // 4
    depth = lax.axis_size("seq") // 2
    piece = width // (2 * depth)
    half = depth * piece
    b16, b32, dma = jnp.bfloat16, jnp.float32, pltpu.SemaphoreType.DMA
    order = lambda j: (4 - j) % 4
    return pl.pallas_call(
        lambda *refs: ffn_backward_body(layer, carry, *refs),
        grid=(4,),
        in_specs=[
            whole((length, width)), ANY, whole(vecs.shape), whole((length, width)),
            pl.BlockSpec((length, chunk), lambda j: (0, order(j))),
            pl.BlockSpec((None, width, chunk), lambda j: (layer, 0, order(j))),
            pl.BlockSpec((None, chunk, width), lambda j: (layer, order(j), 0)),
        ] + ([ANY] * 2 if carry else [SCALAR, ANY]),
        out_specs=[whole((length, width)), whole((1, width)), whole((1, width)), ANY, whole((2, half, width))]
        + ([whole((2, piece, width)), whole((2, 2, half, width // 2))] if carry else [ANY]),
        out_shape=[
            sds((length, width), b32), sds((1, width), b32), sds((1, width), b32), sds((4, half, 2 * chunk), b16),
            sds((2, half, chunk), b16),
        ] + ([sds((2, piece, chunk), b32), sds((2, 2, half, width // 2), b16)] if carry
             else [sds((4, length // 4, width), b16)]),
        scratch_shapes=[
            pltpu.VMEM((length, width), b16), pltpu.VMEM((width, length), b16), pltpu.VMEM((width, length), b16),
            pltpu.VMEM((2, half, 2 * chunk), b16), pltpu.VMEM((2, half, 2 * chunk), b16),
            pltpu.VMEM((4, half, 2 * chunk), b16), pltpu.VMEM((2, half, chunk), b16),
            dma((2, 2)), dma((2, 2)), dma((2,)), dma((2,)), dma((4,)), pltpu.VMEM((length, width), b32), dma,
        ] + ([
            pltpu.VMEM((depth - 1, 2, piece, chunk), b16), pltpu.VMEM((2, piece, chunk), b16),
            pltpu.VMEM((2, 2, half, width // 2), b16), pltpu.VMEM((2, 2, half, width // 2), b16),
            dma((depth - 1,)), dma((depth - 1,)), dma((2, 2)), dma((2, 2)), dma((5,)),
        ] if carry else TRANSPOSE_SEMS),
        compiler_params=pltpu.CompilerParams(
            vmem_limit_bytes=62 * MIB, collective_id=collective, has_side_effects=True
        ),
        cost_estimate=pl.CostEstimate(
            flops=8 * length * width * inner, bytes_accessed=40 * MIB, transcendentals=length * inner
        ),
        name="ffn_backward",
    )(g, hidden, vecs, normed, raised, w_up, w_down, *carried)


def mixer_backward_body(layer, carry, *refs):
    refs = list(refs)
    take = lambda n: [refs.pop(0) for _ in range(n)]
    (hg_ref, vec_ref, cut_ref, proj_ref, signal_ref, long_ref, taps_ref, wo_ref, r_in, normed_in, table_in, wi_in, c_in,
     w1_in) = take(14)
    wmix_ref = take(1)[0] if carry else None
    g_ref, c_out, zout_ref, taps_grad_ref, short_grad_ref, skip_grad_ref, gain_grad_ref, bias_grad_ref = take(8)
    mfin_ref = take(1)[0] if carry else None
    (og_ref, gated_ref, pg_ref, both_ref, got, s1, wkeep, s2, core_s, core_r, s1_s, s1_r, s2_s, s2_r, own_sem,
     out_sem, r_ref, normed_ref, table_ref, wi_ref, late_sem) = take(21)
    if carry:
        mkeep, m2, mz, mzgot, m2_s, m2_r, mz_s, mz_r, m_sem = take(9)
    j = pl.program_id(0)
    steps = pl.num_programs(0)
    length, width = hg_ref.shape
    place = Place()
    half = got.shape[1]
    piece = half // place.depth
    x, y = place.x, place.y
    partners = [place.over_core, place.over_x, place.over_y] + (place.over_z if carry else [])
    table_copy = pltpu.make_async_copy(table_in, table_ref, late_sem.at[0])
    late_copies = [
        pltpu.make_async_copy(source, target, late_sem.at[1 + k])
        for k, (source, target) in enumerate(((r_in, r_ref), (normed_in, normed_ref), (wi_in.at[layer], wi_ref)))
    ]

    def s1_sends():
        return [
            remote(c_in.at[1 + x, :, pl.ds(0, width)], s1.at[0], s1_s.at[0], s1_r.at[0], place.over_x),
            remote(c_in.at[2 - y, :, pl.ds(width, width)], s1.at[1], s1_s.at[1], s1_r.at[1], place.over_y),
        ]

    def own_copies():
        return [
            pltpu.make_async_copy(w1_in.at[0], wkeep.at[0, x], own_sem.at[0]),
            pltpu.make_async_copy(w1_in.at[1], wkeep.at[1, y], own_sem.at[1]),
            pltpu.make_async_copy(c_in.at[2 - x, :, pl.ds(0, width)], wkeep.at[0, 1 - x], own_sem.at[2]),
            pltpu.make_async_copy(c_in.at[1 + y, :, pl.ds(width, width)], wkeep.at[1, 1 - y], own_sem.at[3]),
        ]

    def s2_sends():
        return [
            remote(wkeep.at[0, 1 - y], s2.at[0], s2_s.at[0], s2_r.at[0], place.over_y),
            remote(wkeep.at[1, 1 - x], s2.at[1], s2_s.at[1], s2_r.at[1], place.over_x),
        ]

    def m2_sends():
        return [
            remote(wmix_ref.at[0, 1 - y], m2.at[0], m2_s.at[0], m2_r.at[0], place.over_y),
            remote(wmix_ref.at[1, 1 - x], m2.at[1], m2_s.at[1], m2_r.at[1], place.over_x),
        ]

    def m_copies():
        return [
            pltpu.make_async_copy(wmix_ref.at[0, y], mkeep.at[0], m_sem.at[0]),
            pltpu.make_async_copy(wmix_ref.at[1, x], mkeep.at[1], m_sem.at[1]),
        ]

    def mz_sends():
        return [
            remote(mz.at[:, (place.z + d) % place.depth], mzgot.at[d - 1], mz_s.at[d - 1], mz_r.at[d - 1],
                   place.over_z[d - 1])
            for d in range(1, place.depth)
        ]

    def core_send(t):
        return remote(both_ref.at[t, pl.ds(0, half)], got.at[t], core_s.at[t], core_r.at[t], place.over_core)

    def c_copy(t):
        return pltpu.make_async_copy(both_ref.at[t, pl.ds(half, half)], c_out.at[t], out_sem.at[t])

    @pl.when(j == 0)
    def _():
        greet(partners)
        table_copy.start()
        og_ref[...] = bf(hg_ref[...])
        greeted(partners)
        if carry:
            for copy in m2_sends() + m_copies():
                copy.start()
        for copy in s1_sends() + own_copies() + late_copies:
            copy.start()
        table_copy.wait()

    @pl.when(j == 2)
    def _():
        if carry:
            for copy in m2_sends() + m_copies():
                copy.wait()
            for side in range(2):
                total = bf(f32(mkeep[side]) + f32(m2[side]))
                for k in range(place.depth):
                    mz[side, k] = total[k * piece : (k + 1) * piece]
            for copy in mz_sends():
                copy.start()
        for copy in s1_sends() + own_copies():
            copy.wait()
        wkeep[0, 1 - x] = bf(f32(wkeep[0, 1 - x]) + f32(s1[0]))
        wkeep[1, 1 - y] = bf(f32(wkeep[1, 1 - y]) + f32(s1[1]))
        for copy in s2_sends():
            copy.start()

    @pl.when(j < steps - 1)
    def _():
        chunk = long_ref.shape[1]
        proj = [f32(proj_ref[p]) for p in range(3)]
        kernel = short_taps(cut_ref, layer)
        gate_out, gate_in, vals = mixed_chunk(proj, kernel)
        carried = vals * gate_in
        long_out = f32(long_ref[...])
        skip = vector(cut_ref, layer, 4)
        gated_ref[:, pl.ds(pl.multiple_of(j * chunk, chunk), chunk)] = bf(long_out * gate_out)
        gated_grad = mm_nt(og_ref[...], wo_ref[...])
        long_grad = gated_grad * gate_out
        skip_grad_ref[...] = jnp.sum(carried * long_grad, axis=0, keepdims=True)
        both = mm(table_ref[...], bf(long_grad))
        up_re, up_im = both[:length], both[length:]
        tap_re, tap_im = f32(taps_ref[:length]), f32(taps_ref[length:])
        sig_re, sig_im = f32(signal_ref[:length]), f32(signal_ref[length:])
        left = jnp.concatenate([bf(up_re * tap_re + up_im * tap_im), bf(up_im * tap_re - up_re * tap_im)], axis=0)
        right = jnp.concatenate([bf(up_re * sig_re + up_im * sig_im), bf(up_im * sig_re - up_re * sig_im)], axis=0)
        back = mm_tn(table_ref[...], jnp.concatenate([left, right], axis=1))
        carried_grad = back[:, :chunk] + skip * long_grad
        taps_grad_ref[...] = back[:, chunk:]
        for p, part in enumerate((gated_grad * long_out, carried_grad * vals, carried_grad * gate_in)):
            one, two = row_shift(part, -1), row_shift(part, -2)
            projected_grad = bf(kernel[p][2:3] * part + kernel[p][1:2] * one + kernel[p][0:1] * two)
            for tap, moved in enumerate((two, one, part)):
                short_grad_ref[p, tap : tap + 1, :] = jnp.sum(moved * proj[p], axis=0, keepdims=True)
            pg_ref[:, pl.ds(pl.multiple_of(p * width + j * chunk, chunk), chunk)] = projected_grad

    @pl.when(j == steps - 1)
    def _():
        in_cols, out_cols = 3 * width // 4, width // 4
        for copy in late_copies:
            copy.wait()
        upstream = mm_nt(pg_ref[...], wi_ref[...])
        for t in range(4):
            rights = pg_ref[:, in_cols * t : in_cols * (t + 1)], og_ref[:, out_cols * t : out_cols * (t + 1)]
            products = [bf(mm_tn(left[...], right)) for left, right in zip((normed_ref, gated_ref), rights)]
            store_rows(place, both_ref.at[t], jnp.concatenate(products, axis=1))
            core_send(t).start()
        part, gain_grad, bias_grad = norm_backward(f32(r_ref[...]), vector(vec_ref, layer, 0), upstream)
        total = hg_ref[...] + part
        g_ref[...] = total.astype(g_ref.dtype)
        gain_grad_ref[...] = gain_grad
        bias_grad_ref[...] = bias_grad
        for t in range(4):
            core_send(t).wait()
            both_ref[t, half:] = bf(f32(both_ref[t, half:]) + f32(got[t]))
            c_copy(t).start()
        if carry:
            for copy in mz_sends():
                copy.wait()
            for side in range(2):
                total = f32(mz[side, place.z])
                for d in range(place.depth - 1):
                    total += f32(mzgot[d, side])
                mfin_ref[side] = total
        for copy in s2_sends():
            copy.wait()
        for side, keep in enumerate((y, x)):
            total = bf(f32(wkeep[side, keep]) + f32(s2[side]))
            for k in range(place.depth):
                zout_ref[side, k] = total[k * piece : (k + 1) * piece]
        for t in range(4):
            c_copy(t).wait()


def mixer_backward(
    layer, carry, last, collective, hidden_grad, r, vecs, normed, proj, signal, long_out, taps, table, w_out, w_in, ffn_c,
    ffn_w, *carried
):
    length, width = r.shape
    chunk = 256
    steps = width // chunk
    depth = lax.axis_size("seq") // 2
    piece = width // (2 * depth)
    half = depth * piece
    at = lambda j: jnp.minimum(j, steps - 1)
    b16, b32, dma = jnp.bfloat16, jnp.float32, pltpu.SemaphoreType.DMA
    return pl.pallas_call(
        lambda *refs: mixer_backward_body(layer, carry, *refs),
        grid=(steps + 1,),
        in_specs=[
            whole((length, width)), whole(vecs.shape), pl.BlockSpec((vecs.shape[0], chunk), lambda j: (0, at(j))),
            pl.BlockSpec((3, length, chunk), lambda j: (0, 0, at(j))),
            pl.BlockSpec((2 * length, chunk), lambda j: (0, at(j))),
            pl.BlockSpec((length, chunk), lambda j: (0, at(j))),
            pl.BlockSpec((None, 2 * length, chunk), lambda j: (layer, 0, at(j))),
            pl.BlockSpec((None, chunk, width), lambda j: (layer, at(j), 0)),
        ] + [ANY] * (6 + len(carried)),
        out_specs=[
            whole((length, width)), ANY, whole((2, depth, piece, width)),
            pl.BlockSpec((length, chunk), lambda j: (0, at(j))),
            pl.BlockSpec((3, 3, chunk), lambda j: (0, 0, at(j))),
            pl.BlockSpec((1, chunk), lambda j: (0, at(j))),
            whole((1, width)), whole((1, width)),
        ] + ([whole((2, piece, width // 2))] if carry else []),
        out_shape=[
            sds((length, width), b16 if last else b32), sds((4, half, width), b16),
            sds((2, depth, piece, width), b16),
            sds((length, width), b32), sds((3, 3, width), b32), sds((1, width), b32), sds((1, width), b32),
            sds((1, width), b32),
        ] + ([sds((2, piece, width // 2), b32)] if carry else []),
        scratch_shapes=[
            pltpu.VMEM((length, width), b16), pltpu.VMEM((length, width), b16), pltpu.VMEM((length, 3 * width), b16),
            pltpu.VMEM((4, width, width), b16), pltpu.VMEM((4, half, width), b16),
            pltpu.VMEM((2, half, width), b16), pltpu.VMEM((2, 2, half, width), b16), pltpu.VMEM((2, half, width), b16),
            dma((4,)), dma((4,)), dma((2,)), dma((2,)), dma((2,)), dma((2,)), dma((4,)), dma((4,)),
            pltpu.VMEM((length, width), r.dtype), pltpu.VMEM((length, width), b16), pltpu.VMEM((2 * length, length), b16),
            pltpu.VMEM((width, 3 * width), b16), dma((4,)),
        ] + ([
            pltpu.VMEM((2, half, width // 2), b16), pltpu.VMEM((2, half, width // 2), b16),
            pltpu.VMEM((2, depth, piece, width // 2), b16), pltpu.VMEM((depth - 1, 2, piece, width // 2), b16),
            dma((2,)), dma((2,)), dma((depth - 1,)), dma((depth - 1,)), dma((2,)),
        ] if carry else []) ,
        compiler_params=pltpu.CompilerParams(
            vmem_limit_bytes=63 * MIB, collective_id=collective, has_side_effects=True
        ),
        cost_estimate=pl.CostEstimate(
            flops=2 * length * width * (8 * width + 6 * length), bytes_accessed=50 * MIB, transcendentals=0
        ),
        name="mixer_backward",
    )(hidden_grad, vecs, vecs, proj, signal, long_out, taps, w_out, r, normed, table, w_in, ffn_c, ffn_w, *carried)


SMALL = 128


def closing_body(
    z_in, c_in, g_in, t0_in, t1_in, v0, v1, v2, v3, v4, v5, v6, v7, v8, v9, v10, v11, features_ref, filt_ref, net_ref,
    w3_ref, delta_ref, zfin_ref, mfin_ref, agot, small_ref,
    zgot, zown, mgot, w, m2, mz, mzgot, tgrad, pack, cgot, xgot, xsum, ygot, ysum, zslot, total16, full,
    z_s, z_r, m_s, m_r, m2_s, m2_r, mz_s, mz_r, a_s, a_r, own_sem, sm_s, sm_r, zs_s, zs_r,
):
    place = Place()
    x, y, z, core = place.x, place.y, place.z, place.core
    cols = w.shape[3]
    piece = zown.shape[1]
    rows = agot.shape[1]
    over_both = (place.s, 2 * (1 - y) + 1 - x)
    m_sends = []
    for k in range(2):
        m_sends.append(remote(c_in.at[2 * k + 1 - x, :, pl.ds(0, cols)], mgot.at[0, k], m_s.at[0, k], m_r.at[0, k],
                              place.over_x))
        m_sends.append(remote(c_in.at[2 * (1 - y) + k, :, pl.ds(cols, cols)], mgot.at[1, k], m_s.at[1, k],
                              m_r.at[1, k], place.over_y))
    z_sends = [
        remote(z_in.at[:, (z + d) % place.depth], zgot.at[d - 1], z_s.at[d - 1], z_r.at[d - 1], place.over_z[d - 1])
        for d in range(1, place.depth)
    ]
    own = [pltpu.make_async_copy(z_in.at[:, z], zown, own_sem.at[4])]
    for k in range(2):
        own.append(pltpu.make_async_copy(c_in.at[2 * k + x, :, pl.ds(0, cols)], w.at[0, k], own_sem.at[k]))
        own.append(pltpu.make_async_copy(c_in.at[2 * y + k, :, pl.ds(cols, cols)], w.at[1, k], own_sem.at[2 + k]))
    loads = [
        pltpu.make_async_copy(t0_in, tgrad.at[0], own_sem.at[5]), pltpu.make_async_copy(t1_in, tgrad.at[1], own_sem.at[6]),
    ]
    part = lambda t: g_in.at[pl.ds(pl.multiple_of(t * rows, rows), rows)]
    home = pltpu.make_async_copy(part(place.t), agot.at[place.t], own_sem.at[8])

    def a_sends():
        out = []
        for k, device in enumerate((place.over_x, place.over_y, over_both)):
            out.append(remote(part(device[1]), agot.at[place.t], a_s.at[k], a_r.at[k], device))
        return out

    for copy in loads:
        copy.start()
    partners = [place.over_core, place.over_x, place.over_y, over_both] + place.over_z
    greet(partners)
    greeted(partners)
    for copy in m_sends + z_sends + own + [home]:
        copy.start()

    units = w3_ref.shape[1]
    envelope = decay(delta_ref[...], tgrad.shape[1]) * (1.0 / tgrad.shape[1])
    pack[...] = jnp.zeros_like(pack)
    s1, s2 = filt_ref[0], filt_ref[1]
    u1, h1, u2, h2 = (f32(filt_ref[k]) for k in range(2, 6))
    wide = lambda parts: jnp.concatenate(parts, axis=1)
    for copy in loads:
        copy.wait()
    upstream = [bf(tgrad[layer] * envelope) for layer in range(2)]
    ds2 = wide([mm_nt(upstream[layer], w3_ref[layer]) for layer in range(2)])
    for layer in range(2):
        pack[layer, :64] = mm_tn(s2[:, units * layer : units * (layer + 1)], upstream[layer])
    da2 = ds2 * u2
    span = lambda v, layer: v[:, units * layer : units * (layer + 1)]
    ds1 = wide([mm_nt(bf(span(da2, layer)), bf(net_ref[layer, 48:112, :])) for layer in range(2)])
    da1 = ds1 * u1
    dw2 = wide([mm_tn(span(s1, layer), bf(span(da2, layer))) for layer in range(2)])
    dw1 = mm_tn(bf(features_ref[...]), bf(da1))
    freq = [jnp.sum(ds1 * h1, axis=0, keepdims=True), jnp.sum(ds2 * h2, axis=0, keepdims=True)]
    for k, block in enumerate((dw1[:24], jnp.concatenate([dw1[24:40], freq[0], freq[1], jnp.zeros((6, 128), jnp.float32)]),
                               dw2[:24], dw2[24:48], jnp.concatenate([dw2[48:64], jnp.zeros((8, 128), jnp.float32)]))):
        pack[0, 80:104, 128 * k : 128 * (k + 1)] = block
    vectors = ((v0, v1, v2, v3, v4, v5), (v6, v7, v8, v9, v10, v11))
    for layer in range(2):
        for k in range(5):
            pack[layer, 64 + k : 65 + k, :] = vectors[layer][k][...]
        for p in range(3):
            pack[layer, 69 + 3 * p : 72 + 3 * p, :] = vectors[layer][5][p]

    total16[0] = bf(pack[0])
    total16[1] = bf(pack[1])
    to_core = remote(total16.at[1 - core], cgot, sm_s.at[0], sm_r.at[0], place.over_core)
    to_core.start()
    to_core.wait()
    xsum[...] = bf(f32(total16[core]) + f32(cgot[...]))
    half, quarter = SMALL // 2, SMALL // 4
    side = lambda k, n: pl.ds(pl.multiple_of(k * n, n), n)
    to_x = remote(xsum.at[side(1 - x, half)], xgot, sm_s.at[1], sm_r.at[1], place.over_x)
    to_x.start()

    for copy in own + m_sends:
        copy.wait()
    for k in range(2):
        for n in range(2):
            w[k, n] = bf(f32(w[k, n]) + f32(mgot[k, n]))
    m2_sends = [
        remote(w.at[0, 1 - y], m2.at[0], m2_s.at[0], m2_r.at[0], place.over_y),
        remote(w.at[1, 1 - x], m2.at[1], m2_s.at[1], m2_r.at[1], place.over_x),
    ]
    for copy in m2_sends:
        copy.start()

    to_x.wait()
    ysum[...] = bf(f32(xsum[side(x, half)]) + f32(xgot[...]))
    to_y = remote(ysum.at[side(1 - y, quarter)], ygot, sm_s.at[2], sm_r.at[2], place.over_y)
    to_y.start()
    to_y.wait()
    zslot[z] = bf(f32(ysum[side(y, quarter)]) + f32(ygot[...]))
    zs_sends = [
        remote(zslot.at[z], zslot.at[z], zs_s.at[d - 1], zs_r.at[d - 1], place.over_z[d - 1])
        for d in range(1, place.depth)
    ]
    for copy in zs_sends:
        copy.start()

    for copy in m2_sends:
        copy.wait()
    for copy in a_sends():
        copy.start()
    for k, keep in enumerate((y, x)):
        total = bf(f32(w[k, keep]) + f32(m2[k]))
        for n in range(place.depth):
            mz[k, n] = total[n * piece : (n + 1) * piece]
    mz_sends = [
        remote(mz.at[:, (z + d) % place.depth], mzgot.at[d - 1], mz_s.at[d - 1], mz_r.at[d - 1], place.over_z[d - 1])
        for d in range(1, place.depth)
    ]
    for copy in mz_sends:
        copy.start()

    for copy in z_sends:
        copy.wait()
    total = f32(zown[...])
    for d in range(place.depth - 1):
        total += f32(zgot[d])
    zfin_ref[...] = total

    for copy in zs_sends:
        copy.wait()
    total = f32(zslot[0])
    for k in range(1, place.depth):
        total += f32(zslot[k])
    mine = pl.multiple_of(x * half + y * quarter, quarter)
    full[core, pl.ds(mine, quarter)] = bf(total)
    back_y = remote(full.at[core, pl.ds(mine, quarter)], full.at[core, pl.ds(mine, quarter)], sm_s.at[3], sm_r.at[3],
                    place.over_y)
    back_y.start()
    back_y.wait()
    back_x = remote(full.at[core, side(x, half)], full.at[core, side(x, half)], sm_s.at[4], sm_r.at[4], place.over_x)
    back_x.start()
    back_x.wait()
    back_core = remote(full.at[core], full.at[core], sm_s.at[5], sm_r.at[5], place.over_core)
    back_core.start()
    back_core.wait()
    small_ref[...] = f32(full[...])
    for copy in mz_sends:
        copy.wait()
    for k in range(2):
        total = f32(mz[k, z])
        for d in range(place.depth - 1):
            total += f32(mzgot[d, k])
        mfin_ref[k] = total
    home.wait()
    for copy in a_sends():
        copy.wait()


def closing(collective, ffn_z, mixer_c, grad, taps_grads, vectors, features, filt, net, w3, delta):
    _, depth, piece, width = ffn_z.shape
    length = grad.shape[0]
    half = depth * piece
    b16, b32, dma = jnp.bfloat16, jnp.float32, pltpu.SemaphoreType.DMA
    cols = width // 2
    vm = pl.BlockSpec(memory_space=pltpu.VMEM)
    return pl.pallas_call(
        closing_body,
        in_specs=[ANY] * 5 + [vm] * (len(vectors) + 5),
        out_specs=[vm, vm, ANY, vm],
        out_shape=[
            sds((2, piece, width), b32), sds((2, piece, cols), b32), sds((4, length // 4, width), b16),
            sds((2, SMALL, width), b32),
        ],
        scratch_shapes=[
            pltpu.VMEM((depth - 1, 2, piece, width), b16), pltpu.VMEM((2, piece, width), b16),
            pltpu.VMEM((2, 2, half, cols), b16), pltpu.VMEM((2, 2, half, cols), b16), pltpu.VMEM((2, half, cols), b16),
            pltpu.VMEM((2, depth, piece, cols), b16), pltpu.VMEM((depth - 1, 2, piece, cols), b16),
            pltpu.VMEM((2, length, width), b32),
            pltpu.VMEM((2, SMALL, width), b32), pltpu.VMEM((SMALL, width), b16), pltpu.VMEM((SMALL // 2, width), b16),
            pltpu.VMEM((SMALL, width), b16), pltpu.VMEM((SMALL // 4, width), b16), pltpu.VMEM((SMALL // 2, width), b16),
            pltpu.VMEM((depth, SMALL // 4, width), b16), pltpu.VMEM((2, SMALL, width), b16),
            pltpu.VMEM((2, SMALL, width), b16),
            dma((depth - 1,)), dma((depth - 1,)), dma((2, 2)), dma((2, 2)), dma((2,)), dma((2,)), dma((depth - 1,)),
            dma((depth - 1,)), dma((3,)), dma((3,)), dma((9,)), dma((6,)), dma((6,)), dma((depth - 1,)),
            dma((depth - 1,)),
        ],
        compiler_params=pltpu.CompilerParams(
            vmem_limit_bytes=62 * MIB, collective_id=collective, has_side_effects=True
        ),
        name="closing",
    )(ffn_z, mixer_c, grad, *taps_grads, *vectors, features, filt, net, w3, delta)


def assemble_body(
    out_in, grad_in, f0, f1, m0, m1, small, out_act, grad_x, g1, b1, w_in, short, w1, freq, w2, w3, skip, w_out, g2, b2,
    w_up, w_down,
):
    out_act[...] = f32(out_in[...])
    grad_x[...] = f32(grad_in[...])

    @pl.when(pl.program_id(0) == 0)
    def _():
        units = w2.shape[1]
        cols = m0.shape[2]
        split = w_in.shape[2]
        for layer, (f, m) in enumerate(((f0, m0), (f1, m1))):
            row = slice(layer, layer + 1)
            for k, ref in enumerate((g1, b1, g2, b2, skip)):
                ref[row, :] = small[layer, 64 + k : 65 + k, :]
            for p in range(3):
                for tap in range(3):
                    at = 69 + 3 * p + tap
                    width = small.shape[2]
                    short[tap, row, p * width : (p + 1) * width] = small[layer, at : at + 1, :]
            lanes = lambda k: slice(128 * k + units * layer, 128 * k + units * (layer + 1))
            for k in range(EMB):
                at = 80 + k % 24
                w1[k, row, :] = small[0, at : at + 1, lanes(k // 24)]
            freq[layer] = small[0, 96:98, lanes(1)]
            w2[layer] = jnp.concatenate(
                [small[0, 80:104, lanes(2)], small[0, 80:104, lanes(3)], small[0, 80:96, lanes(4)]], axis=0
            )
            w3[layer] = small[layer, :64, :]
            w_in[layer] = jnp.concatenate([m[0], m[1][:, : split - cols]], axis=1)
            w_out[layer] = m[1][:, split - cols :]
            w_up[layer] = f[0]
            w_down[layer] = f[1]


def assemble(out_act, grad_in, ffn, mixer, small, units):
    slots, rows, width = out_act.shape
    _, piece, cols = ffn[0].shape
    split = 3 * width // 4
    b32 = jnp.float32
    shapes = [
        (2, width), (2, width), (2, piece, split), (3, 2, 3 * width), (EMB, 2, units), (2, 2, units), (2, units, units),
        (2, units, width), (2, width), (2, piece, width - split), (2, width), (2, width), (2, piece, cols),
        (2, piece, cols),
    ]
    block = pl.BlockSpec((None, rows, width), lambda j: (j, 0, 0))
    return pl.pallas_call(
        assemble_body,
        grid=(slots,),
        in_specs=[block, block] + [whole(v.shape) for v in (*ffn, *mixer, small)],
        out_specs=[block, block] + [whole(shape) for shape in shapes],
        out_shape=[sds((slots, rows, width), b32)] * 2 + [sds(shape, b32) for shape in shapes],
        compiler_params=pltpu.CompilerParams(vmem_limit_bytes=62 * MIB),
        name="assemble",
    )(out_act, grad_in, *ffn, *mixer, small)


def feature_table(length):
    bands = (EMB - 1) // 2
    step = np.arange(length, dtype=np.float64)[:, None]
    phases = 2.0 * math.pi / length * step * np.linspace(1e-4, bands - 1, bands)[None]
    parts = [step / (length - 1), np.cos(phases), -np.sin(phases), np.zeros((length, 40 - EMB))]
    return np.concatenate(parts, axis=1).astype(np.float32)


def whole_sequences(
    x_in, cotangent, counts, ln1_gain, ln1_bias, w_in, short_w, filt_w1, filt_freq, filt_w2, filt_w3, long_bias,
    w_out, ln2_gain, ln2_bias, w_up, w_down,
):
    micro_count, cap_size, tok_rows, width = x_in.shape
    slots = micro_count * cap_size
    layers = w_up.shape[0]
    toks = lax.axis_size("tok")
    length = tok_rows * toks
    me = lax.axis_index("tok")
    live = (me % cap_size < counts[me // cap_size, 0]).astype(jnp.float32).reshape(1, 1)
    table = jnp.asarray(spectral_table(length))
    features = jnp.asarray(feature_table(length))
    delta = jnp.asarray(
        np.abs(np.linspace(math.log(0.01) / 0.3, math.log(0.01) / 1.5, width, dtype=np.float64))[None].astype(np.float32)
    )
    blocks = lambda v: v.reshape(slots, tok_rows, width)
    r, filt, spectra, vecs, net = front(
        2 * layers + 1, blocks(x_in), table, features, delta, ln1_gain, ln1_bias, ln2_gain, ln2_bias, long_bias,
        jnp.swapaxes(short_w, 0, 1), jnp.swapaxes(filt_w1, 0, 1), filt_freq, filt_w2, filt_w3,
    )
    kept = []
    for layer in range(layers):
        if layer == 0:
            hidden, normed, proj, signal, long_out, upstream = gathering_forward(
                layer, 2 * layers + 2, r, vecs, w_in, table, spectra, w_out, blocks(cotangent)
            )
        else:
            hidden, normed, proj, signal, long_out = mixer_forward(layer, r, vecs, w_in, table, spectra, w_out)
        result, normed_two, raised = ffn_forward(
            layer, hidden, vecs, w_up, w_down, *((live,) if layer == layers - 1 else ())
        )
        kept.append((r, hidden, normed, proj, signal, long_out, normed_two, raised))
        r = result

    grad = upstream
    vectors, taps_grads, done = [None] * layers, [None] * layers, {}
    carried_ffn, carried_mixer = (live, r), ()
    for layer in reversed(range(layers)):
        r, hidden, normed, proj, signal, long_out, normed_two, raised = kept[layer]
        carry = layer < layers - 1
        grad, grad_g2, grad_b2, ffn_c, ffn_w, *rest = ffn_backward(
            layer, carry, 2 * layer, grad, hidden, vecs, normed_two, raised, w_up, w_down, *carried_ffn
        )
        if carry:
            done["ffn", layer + 1], *carried_mixer = rest
        else:
            out_act = rest[0]
        grad, mixer_c, ffn_z, taps_grads[layer], grad_short, grad_skip, grad_g1, grad_b1, *rest = mixer_backward(
            layer, carry, layer == 0, 2 * layer + 1, grad, r, vecs, normed, proj, signal, long_out, spectra, table, w_out,
            w_in, ffn_c, ffn_w, *carried_mixer,
        )
        if carry:
            done["mixer", layer + 1] = rest[0]
        carried_ffn = (ffn_z, mixer_c)
        vectors[layer] = (grad_g1, grad_b1, grad_g2, grad_b2, grad_skip, grad_short)
    done["ffn", 0], done["mixer", 0], grad_in, small = closing(
        2 * layers, *carried_ffn, grad, taps_grads, vectors[0] + vectors[1], features, filt, net, filt_w3, delta
    )
    pair = lambda kind: [done[kind, layer] for layer in range(layers)]
    out_act, grad_in, *grads = assemble(out_act, grad_in, pair("ffn"), pair("mixer"), small, filt_w2.shape[1])
    for k, axes in ((3, (0, 1)), (4, (0, 1)), (13, (1, 2))):
        grads[k] = jnp.swapaxes(grads[k], *axes)
    home = lambda v: v.reshape(micro_count, cap_size, tok_rows, width)
    return (home(out_act), home(grad_in), *grads)


def shards(*args):
    micro_count, cap_size = args[0].shape[:2]
    if lax.axis_size("tok") == 4 and micro_count * cap_size == 4:
        return whole_sequences(*args)
    return split_positions(*args)


def solution(mesh):
    return jax.shard_map(
        shards,
        mesh=mesh,
        in_specs=(
            P(None, "seq", "tok", None),
            P(None, "seq", "tok", None),
            P(None, "seq"),
            P(),
            P(),
            P(),
            P(),
            P(),
            P(),
            P(),
            P(),
            P(),
            P(),
            P(),
            P(),
            P(),
            P(),
        ),
        out_specs=(
            P(None, "seq", "tok", None),
            P(None, "seq", "tok", None),
            P(),
            P(),
            P(None, "seq", "tok"),
            P(),
            P(),
            P(),
            P(),
            P(),
            P(),
            P(None, "seq", "tok"),
            P(),
            P(),
            P(None, "seq", "tok"),
            P(None, "tok", "seq"),
        ),
        check_vma=False,
    )
```

```python
import math

import jax
import jax.numpy as jnp
import numpy as np
from jax import lax
from jax.experimental import pallas as pl
from jax.experimental.pallas import tpu as pltpu
from jax.sharding import PartitionSpec as P

EMB = 33
INNER = 64


HIGHEST = lax.Precision.HIGHEST
NORM_EPS = 1e-05
MOD_SHIFT = 0.05


def passed_along(block, axis, distance):
    devices = range(lax.axis_size(axis))
    route = [(i - distance, i) for i in devices if i - distance in devices]
    return lax.ppermute(block, axis, route)


def for_sending(value):

    def short(part):
        return part.astype(jnp.bfloat16) if part.dtype == jnp.float32 else part

    return jax.tree.map(short, value)


def position_features(length):
    band_count = (EMB - 1) // 2
    step_index = jnp.arange(length, dtype=jnp.int32).astype(jnp.float32)
    time_grid = step_index / (length - 1)
    base_angle = step_index * (2.0 * math.pi / length)
    band_freq = jnp.linspace(0.0001, band_count - 1, band_count, dtype=jnp.float32)
    phases = base_angle[:, None] * band_freq[None, :]
    return jnp.concatenate([time_grid[:, None], jnp.cos(phases), -jnp.sin(phases)], axis=1)


def decay_table(time_grid, first_chan, channels, model_width):
    fast_rate = math.log(0.01) / 0.3
    slow_rate = math.log(0.01) / 1.5
    chan_index = first_chan + jnp.arange(channels, dtype=jnp.int32).astype(jnp.float32)
    deltas = jnp.abs(fast_rate + (slow_rate - fast_rate) * chan_index / (model_width - 1))
    return jnp.exp(-time_grid * deltas[None, :]) + MOD_SHIFT


def filter_taps(features, weight_one, sine_freq, weight_two, weight_three, envelope):
    first_sine = jnp.sin(sine_freq[0] * jnp.dot(features, weight_one, precision=HIGHEST))
    second_sine = jnp.sin(sine_freq[1] * jnp.dot(first_sine, weight_two, precision=HIGHEST))
    return jnp.dot(second_sine, weight_three, precision=HIGHEST) * envelope


def layer_norm(values_in, gain_vec, bias_vec):
    mean_row = jnp.mean(values_in, axis=-1, keepdims=True)
    centred = values_in - mean_row
    variance = jnp.mean(centred * centred, axis=-1, keepdims=True)
    return centred * lax.rsqrt(variance + NORM_EPS) * gain_vec + bias_vec


def gelu_tanh(values_in):
    return jax.nn.gelu(values_in, approximate=True)


def dft_tables(outer_size, inner_size):
    padded_len = outer_size * inner_size
    outer_index = jnp.arange(outer_size, dtype=jnp.int32)
    half_index = jnp.arange(outer_size // 2, dtype=jnp.int32)
    inner_index = jnp.arange(inner_size, dtype=jnp.int32)
    angle_outer = (outer_index[:, None] * half_index[None, :] % outer_size).astype(jnp.float32) * (
        2.0 * math.pi / outer_size
    )
    angle_twist = (outer_index[:, None] * inner_index[None, :] % padded_len).astype(jnp.float32) * (
        2.0 * math.pi / padded_len
    )
    angle_inner = (inner_index[:, None] * inner_index[None, :] % inner_size).astype(jnp.float32) * (
        2.0 * math.pi / inner_size
    )
    return (
        jnp.cos(angle_outer),
        jnp.sin(angle_outer),
        jnp.cos(angle_twist)[None, :, :, None],
        jnp.sin(angle_twist)[None, :, :, None],
        jnp.cos(angle_inner),
        jnp.sin(angle_inner),
    )


def forward_dft(series, tables):
    cos_outer, sin_outer, cos_twist, sin_twist, cos_inner, sin_inner = tables
    outer_size = cos_outer.shape[0]
    inner_size = cos_inner.shape[0]
    seq_count = series.shape[0]
    channels = series.shape[2]
    token_grid = series.reshape(seq_count, outer_size // 2, inner_size, channels)
    first_re = jnp.einsum("ka,sabc->skbc", cos_outer, token_grid, precision=HIGHEST)
    first_im = -jnp.einsum("ka,sabc->skbc", sin_outer, token_grid, precision=HIGHEST)
    twist_re = first_re * cos_twist + first_im * sin_twist
    twist_im = first_im * cos_twist - first_re * sin_twist
    out_re = jnp.einsum("skbc,bj->skjc", twist_re, cos_inner, precision=HIGHEST) + jnp.einsum(
        "skbc,bj->skjc", twist_im, sin_inner, precision=HIGHEST
    )
    out_im = jnp.einsum("skbc,bj->skjc", twist_im, cos_inner, precision=HIGHEST) - jnp.einsum(
        "skbc,bj->skjc", twist_re, sin_inner, precision=HIGHEST
    )
    return (out_re, out_im)


def inverse_dft(spec_re, spec_im, tables):
    cos_outer, sin_outer, cos_twist, sin_twist, cos_inner, sin_inner = tables
    outer_size = cos_outer.shape[0]
    inner_size = cos_inner.shape[0]
    seq_count = spec_re.shape[0]
    channels = spec_re.shape[3]
    back_re = jnp.einsum("skjc,bj->skbc", spec_re, cos_inner, precision=HIGHEST) - jnp.einsum(
        "skjc,bj->skbc", spec_im, sin_inner, precision=HIGHEST
    )
    back_im = jnp.einsum("skjc,bj->skbc", spec_im, cos_inner, precision=HIGHEST) + jnp.einsum(
        "skjc,bj->skbc", spec_re, sin_inner, precision=HIGHEST
    )
    turn_re = back_re * cos_twist - back_im * sin_twist
    turn_im = back_im * cos_twist + back_re * sin_twist
    token_grid = (
        jnp.einsum("skbc,ka->sabc", turn_re, cos_outer, precision=HIGHEST)
        - jnp.einsum("skbc,ka->sabc", turn_im, sin_outer, precision=HIGHEST)
    ) / (outer_size * inner_size)
    return token_grid.reshape(seq_count, outer_size // 2 * inner_size, channels)


def complex_product(left_re, left_im, right_re, right_im):
    return (left_re * right_re - left_im * right_im, left_re * right_im + left_im * right_re)


def add_tree(running, update):
    if running is None:
        return update
    return jax.tree.map(jnp.add, running, update)


def split_positions(
    x_in,
    cotangent,
    counts,
    ln1_gain,
    ln1_bias,
    w_in,
    short_w,
    filt_w1,
    filt_freq,
    filt_w2,
    filt_w3,
    long_bias,
    w_out,
    ln2_gain,
    ln2_bias,
    w_up,
    w_down,
):
    tok_count = lax.axis_size("tok")
    micro_count, cap_size, tok_rows, model_width = x_in.shape
    channels = model_width // tok_count
    first_chan = lax.axis_index("tok") * channels
    layer_count = w_in.shape[0]
    length = tok_rows * tok_count
    tables = dft_tables(2 * length // INNER, INNER)
    features = position_features(length)
    envelope = decay_table(features[:, :1], first_chan.astype(jnp.float32), channels, model_width)
    gain_one = ln1_gain.astype(jnp.float32)
    bias_one = ln1_bias.astype(jnp.float32)
    gain_two = ln2_gain.astype(jnp.float32)
    bias_two = ln2_bias.astype(jnp.float32)
    short_taps = short_w.astype(jnp.float32)
    skip_scale = long_bias.astype(jnp.float32)
    filt_one = filt_w1.astype(jnp.float32)
    filt_sine = filt_freq.astype(jnp.float32)
    filt_two = filt_w2.astype(jnp.float32)
    filt_three = filt_w3.astype(jnp.float32)

    def taps_of(layer_index):

        def taps_fn(weight_one, sine_freq, weight_two, three_slice):
            return filter_taps(features, weight_one, sine_freq, weight_two, three_slice, envelope)

        three_slice = lax.dynamic_slice_in_dim(filt_three[layer_index], first_chan, channels, 1)
        return jax.vjp(
            taps_fn,
            filt_one[layer_index],
            filt_sine[layer_index],
            filt_two[layer_index],
            three_slice,
        )

    taps_spectra = []
    for layer_index in range(layer_count):
        filter_rows, _ = taps_of(layer_index)
        taps_spectra.append(forward_dft(filter_rows[None], tables))

    def backward_layer(grad_rows, kept, layer_index):
        (
            residual,
            normed,
            padded,
            short_out,
            carried,
            long_out,
            gated_rows,
            hidden,
            normed_two,
            raised,
            active,
            kept_signal,
        ) = kept
        down_grad = grad_rows.astype(jnp.bfloat16)
        active_grad = jnp.einsum(
            "std,fd->stf", down_grad, w_down[layer_index], preferred_element_type=jnp.float32
        )
        _, gelu_pull = jax.vjp(gelu_tanh, raised)
        raised_grad = gelu_pull(active_grad)[0].astype(jnp.bfloat16)
        normed_two_grad = jnp.einsum(
            "stf,df->std", raised_grad, w_up[layer_index], preferred_element_type=jnp.float32
        )
        _, second_pull = jax.vjp(layer_norm, hidden, gain_two[layer_index], bias_two[layer_index])
        hidden_part, grad_gain_two, grad_bias_two = second_pull(normed_two_grad)
        hidden_grad = grad_rows + hidden_part
        out_grad = hidden_grad.astype(jnp.bfloat16)
        gated_grad = jnp.einsum(
            "ste,de->std", out_grad, w_out[layer_index], preferred_element_type=jnp.float32
        )
        gate_out = short_out[:, :, :model_width]
        gate_in = short_out[:, :, model_width : 2 * model_width]
        values = short_out[:, :, 2 * model_width :]
        long_grad = gated_grad * gate_out
        gate_out_grad = gated_grad * long_out
        grad_skip = jnp.sum(carried * long_grad, axis=(0, 1))
        spec_re, spec_im = taps_spectra[layer_index]
        upstream_re, upstream_im = forward_dft(
            lax.all_to_all(
                long_grad.astype(jnp.bfloat16), "tok", split_axis=2, concat_axis=1, tiled=True
            ).astype(long_grad.dtype),
            tables,
        )
        back_re, back_im = complex_product(upstream_re, upstream_im, spec_re, -spec_im)
        back_rows = lax.all_to_all(
            for_sending(inverse_dft(back_re, back_im, tables)),
            "tok",
            split_axis=1,
            concat_axis=2,
            tiled=True,
        )
        back_rows, upstream_re, upstream_im = (back_rows, upstream_re, upstream_im)
        signal_re, signal_im = kept_signal
        cross_re = jnp.sum(signal_re * upstream_re + signal_im * upstream_im, axis=0)
        cross_im = jnp.sum(signal_re * upstream_im - signal_im * upstream_re, axis=0)
        carried_grad = back_rows + skip_scale[layer_index] * long_grad
        short_grad = jnp.concatenate(
            [gate_out_grad, carried_grad * values, carried_grad * gate_in], axis=2
        )
        next_rows = passed_along(for_sending(short_grad[:, :2, :]), "tok", -1)
        extended = jnp.concatenate([short_grad, next_rows], axis=1)
        kernel = short_taps[layer_index]
        projected_grad = (
            kernel[2] * short_grad + kernel[1] * extended[:, 1:-1] + kernel[0] * extended[:, 2:]
        ).astype(jnp.bfloat16)
        grad_short = jnp.stack(
            [
                jnp.sum(short_grad * padded[:, tap_index : tap_index + tok_rows], axis=(0, 1))
                for tap_index in range(3)
            ]
        )
        normed_grad = jnp.einsum(
            "ste,de->std", projected_grad, w_in[layer_index], preferred_element_type=jnp.float32
        )
        _, first_pull = jax.vjp(layer_norm, residual, gain_one[layer_index], bias_one[layer_index])
        residual_part, grad_gain_one, grad_bias_one = first_pull(normed_grad)
        left_all = (
            lax.all_gather(down_grad, "tok", axis=1, tiled=True),
            lax.all_gather(gated_rows, "tok", axis=1, tiled=True),
            lax.all_gather(normed_two, "tok", axis=1, tiled=True),
            lax.all_gather(normed, "tok", axis=1, tiled=True),
        )
        right_cols = (
            lax.all_to_all(active, "tok", split_axis=2, concat_axis=1, tiled=True),
            lax.all_to_all(out_grad, "tok", split_axis=2, concat_axis=1, tiled=True),
            lax.all_to_all(raised_grad, "tok", split_axis=2, concat_axis=1, tiled=True),
            lax.all_to_all(projected_grad, "tok", split_axis=2, concat_axis=1, tiled=True),
        )
        grad_down = jnp.einsum(
            "stf,std->fd", right_cols[0], left_all[0], preferred_element_type=jnp.float32
        )
        grad_out = jnp.einsum(
            "std,ste->de", left_all[1], right_cols[1], preferred_element_type=jnp.float32
        )
        grad_up = jnp.einsum(
            "std,stf->df", left_all[2], right_cols[2], preferred_element_type=jnp.float32
        )
        grad_in_proj = jnp.einsum(
            "std,ste->de", left_all[3], right_cols[3], preferred_element_type=jnp.float32
        )
        bundle = (
            (grad_in_proj, grad_out, grad_up, grad_down),
            (grad_gain_one, grad_bias_one, grad_short, grad_skip, grad_gain_two, grad_bias_two),
            (cross_re, cross_im),
        )
        return (hidden_grad + residual_part, bundle)

    def filter_grads(cross_re, cross_im, layer_index):
        taps_grad = inverse_dft(cross_re[None], cross_im[None], tables)[0]
        _, taps_pull = taps_of(layer_index)
        grad_one, grad_sine, grad_two, grad_three = taps_pull(taps_grad)
        grad_three_full = lax.dynamic_update_slice_in_dim(
            jnp.zeros_like(filt_three[layer_index]), grad_three, first_chan, 1
        )
        return (grad_one, grad_sine, grad_two, grad_three_full)

    outputs = []
    input_grads = []
    running = None
    reduced = None
    for micro_index in range(micro_count):
        live_mask = (jnp.arange(cap_size, dtype=jnp.int32) < counts[micro_index, 0]).astype(
            jnp.float32
        )[:, None, None]
        residual = x_in[micro_index].astype(jnp.float32)
        saved = []
        for layer_index in range(layer_count):
            forward_normed = layer_norm(
                residual, gain_one[layer_index], bias_one[layer_index]
            ).astype(jnp.bfloat16)
            projected = jnp.einsum(
                "std,de->ste", forward_normed, w_in[layer_index], preferred_element_type=jnp.float32
            )
            prev_rows = passed_along(projected[:, -2:, :], "tok", 1)
            forward_padded = jnp.concatenate([prev_rows, projected], axis=1)
            forward_kernel = short_taps[layer_index]
            forward_short_out = (
                forward_kernel[0] * forward_padded[:, :-2]
                + forward_kernel[1] * forward_padded[:, 1:-1]
                + forward_kernel[2] * forward_padded[:, 2:]
            )
            forward_gate_out = forward_short_out[:, :, :model_width]
            forward_gate_in = forward_short_out[:, :, model_width : 2 * model_width]
            forward_values = forward_short_out[:, :, 2 * model_width :]
            forward_carried = forward_values * forward_gate_in
            forward_spec_re, forward_spec_im = taps_spectra[layer_index]
            convolve_signal_re, convolve_signal_im = forward_dft(
                lax.all_to_all(forward_carried, "tok", split_axis=2, concat_axis=1, tiled=True),
                tables,
            )
            prod_re, prod_im = complex_product(
                convolve_signal_re, convolve_signal_im, forward_spec_re, forward_spec_im
            )
            convolve_back_rows = lax.all_to_all(
                inverse_dft(prod_re, prod_im, tables),
                "tok",
                split_axis=1,
                concat_axis=2,
                tiled=True,
            )
            results = (convolve_back_rows, convolve_signal_re, convolve_signal_im)
            forward_long_out = results[0] + skip_scale[layer_index] * forward_carried
            forward_gated_rows = (forward_long_out * forward_gate_out).astype(jnp.bfloat16)
            forward_hidden = residual + jnp.einsum(
                "std,de->ste",
                forward_gated_rows,
                w_out[layer_index],
                preferred_element_type=jnp.float32,
            )
            forward_normed_two = layer_norm(
                forward_hidden, gain_two[layer_index], bias_two[layer_index]
            ).astype(jnp.bfloat16)
            forward_raised = jnp.einsum(
                "std,df->stf",
                forward_normed_two,
                w_up[layer_index],
                preferred_element_type=jnp.float32,
            )
            forward_active = gelu_tanh(forward_raised).astype(jnp.bfloat16)
            result = forward_hidden + jnp.einsum(
                "stf,fd->std",
                forward_active,
                w_down[layer_index],
                preferred_element_type=jnp.float32,
            )
            forward_kept = (
                residual,
                forward_normed,
                forward_padded,
                forward_short_out,
                forward_carried,
                forward_long_out,
                forward_gated_rows,
                forward_hidden,
                forward_normed_two,
                forward_raised,
                forward_active,
                results[1:],
            )
            residual = result
            kept = forward_kept
            saved.append(kept)
        outputs.append(residual * live_mask)
        grad_rows = cotangent[micro_index].astype(jnp.float32) * live_mask
        layer_bundles = [None] * layer_count
        for layer_index in reversed(range(layer_count)):
            grad_rows, bundle = backward_layer(grad_rows, saved[layer_index], layer_index)
            layer_bundles[layer_index] = bundle
        input_grads.append(grad_rows)
        running = add_tree(running, layer_bundles)
    mats = [
        jnp.stack([running[layer_index][0][member] for layer_index in range(layer_count)])
        for member in range(4)
    ]
    vecs = [
        jnp.stack([running[layer_index][1][member] for layer_index in range(layer_count)])
        for member in range(6)
    ]
    filter_parts = [
        filter_grads(running[layer_index][2][0], running[layer_index][2][1], layer_index)
        for layer_index in range(layer_count)
    ]
    filt_parts = [
        jnp.stack([filter_parts[layer_index][member] for layer_index in range(layer_count)])
        for member in range(4)
    ]
    mat_done = (
        lax.psum_scatter(
            mats[0].astype(jnp.bfloat16), "seq", scatter_dimension=1, tiled=True
        ).astype(jnp.float32),
        lax.psum_scatter(
            mats[1].astype(jnp.bfloat16), "seq", scatter_dimension=1, tiled=True
        ).astype(jnp.float32),
        lax.psum_scatter(
            mats[2].astype(jnp.bfloat16), "seq", scatter_dimension=1, tiled=True
        ).astype(jnp.float32),
        lax.psum_scatter(
            mats[3].astype(jnp.bfloat16), "seq", scatter_dimension=2, tiled=True
        ).astype(jnp.float32),
    )
    small_done = lax.psum(
        (
            vecs[0],
            vecs[1],
            vecs[2],
            vecs[3],
            vecs[4],
            vecs[5],
            filt_parts[0],
            filt_parts[1],
            filt_parts[2],
            filt_parts[3],
        ),
        ("seq", "tok"),
    )
    reduced = (tuple(mat_done), tuple(small_done))
    mat_done, small_done = reduced
    return (
        jnp.stack(outputs),
        jnp.stack(input_grads),
        small_done[0],
        small_done[1],
        mat_done[0],
        small_done[2],
        small_done[6],
        small_done[7],
        small_done[8],
        small_done[9],
        small_done[3],
        mat_done[1],
        small_done[4],
        small_done[5],
        mat_done[2],
        mat_done[3],
    )


MIB = 1 << 20
MESH = pl.DeviceIdType.MESH


def mm(left, right):
    return jnp.dot(left, right, preferred_element_type=jnp.float32)


def mm_nt(left, right):
    return lax.dot_general(left, right, (((1,), (1,)), ((), ())), preferred_element_type=jnp.float32)


def mm_tn(left, right):
    return lax.dot_general(left, right, (((0,), (0,)), ((), ())), preferred_element_type=jnp.float32)


def f32(values):
    return values.astype(jnp.float32)


def bf(values):
    return values.astype(jnp.bfloat16)


def row_shift(values, distance):
    rows = values.shape[0]
    index = lax.broadcasted_iota(jnp.int32, values.shape, 0)
    rolled = pltpu.roll(values, distance % rows, 0)
    kept = index >= distance if distance > 0 else index < rows + distance
    return jnp.where(kept, rolled, 0.0)


def standardised(values):
    mean = jnp.mean(values, axis=-1, keepdims=True)
    centred = values - mean
    scale = lax.rsqrt(jnp.mean(centred * centred, axis=-1, keepdims=True) + NORM_EPS)
    return centred * scale, scale


def norm_backward(values, gain, upstream):
    xh, scale = standardised(values)
    dxh = upstream * gain
    part = scale * (
        dxh - jnp.mean(dxh, axis=-1, keepdims=True) - xh * jnp.mean(dxh * xh, axis=-1, keepdims=True)
    )
    return part, jnp.sum(upstream * xh, axis=0, keepdims=True), jnp.sum(upstream, axis=0, keepdims=True)


def gelu_parts(values):
    slope = math.sqrt(2.0 / math.pi)
    square = values * values
    bent = jnp.tanh(slope * values * (1.0 + 0.044715 * square))
    half = 0.5 * (1.0 + bent)
    inner = slope * (1.0 + (3.0 * 0.044715) * square)
    return values * half, half + 0.5 * values * (1.0 - bent * bent) * inner


def spectral_table(length):
    k = np.arange(length, dtype=np.int64)[:, None]
    t = np.arange(length, dtype=np.int64)[None, :]
    angle = ((2 * k + 1) * t % (4 * length)).astype(np.float64) * (2.0 * math.pi / (4 * length))
    return np.concatenate([np.cos(angle), -np.sin(angle)], axis=0).astype(jnp.bfloat16)


def whole(shape):
    return pl.BlockSpec(shape, lambda j: (0,) * len(shape), pipeline_mode=pl.Buffered(1))


VECS = 14


def vector(ref, layer, k):
    return ref[VECS * layer + k : VECS * layer + k + 1, :]


def short_taps(ref, layer):
    return [ref[VECS * layer + 5 + 3 * p : VECS * layer + 8 + 3 * p, :] for p in range(3)]


ANY = pl.BlockSpec(memory_space=pl.ANY)


def sds(shape, kind):
    return jax.ShapeDtypeStruct(shape, kind)


class Place:
    def __init__(self):
        s, t = lax.axis_index("seq"), lax.axis_index("tok")
        self.depth = lax.axis_size("seq") // 2
        self.z, self.core, self.y, self.x = s // 2, s % 2, t // 2, t % 2
        self.s, self.t = s, t
        self.over_core = (2 * self.z + 1 - self.core, t)
        self.over_x = (s, 2 * self.y + 1 - self.x)
        self.over_y = (s, 2 * (1 - self.y) + self.x)
        self.over_z = [(2 * ((self.z + d) % self.depth) + self.core, t) for d in range(1, self.depth)]
        self.from_z = [(2 * ((self.z + self.depth - d) % self.depth) + self.core, t) for d in range(1, self.depth)]


def greet(partners):
    barrier = pltpu.get_barrier_semaphore()
    for partner in partners:
        pl.semaphore_signal(barrier, inc=1, device_id=partner, device_id_type=MESH)


def greeted(partners):
    pl.semaphore_wait(pltpu.get_barrier_semaphore(), len(partners))


def remote(source, target, sent, landed, device):
    return pltpu.make_async_remote_copy(
        src_ref=source, dst_ref=target, send_sem=sent, recv_sem=landed, device_id=device, device_id_type=MESH
    )


def other_first(place, s, piece):
    half = place.depth * piece
    mine = (s % 2 + place.core + 1) % 2
    return pl.multiple_of(mine * half + (s // 2) * piece, 16)


def store_rows(place, target, values):
    piece = values.shape[0] // (2 * place.depth)
    for s in range(2 * place.depth):
        target[pl.ds(other_first(place, s, piece), piece), :] = values[s * piece : (s + 1) * piece]


class Transpose:
    def __init__(self, place, source, target, sent, landed, own, gathering):
        self.place, self.source, self.target, self.sent, self.landed, self.own = place, source, target, sent, landed, own
        self.gathering = gathering
        self.partners = [place.over_x, place.over_y, (place.s, 2 * (1 - place.y) + 1 - place.x)]

    def block(self, ref, k, flat):
        if not flat:
            return ref.at[k]
        rows = ref.shape[0] // 4
        return ref.at[pl.ds(pl.multiple_of(k * rows, rows), rows)]

    def copies(self):
        me = self.place.t
        flat_in, flat_out = not self.gathering, self.gathering
        target = self.block(self.target, me, flat_out)
        out = [
            remote(self.block(self.source, device[1], flat_in), target, self.sent.at[k], self.landed.at[k], device)
            for k, device in enumerate(self.partners)
        ]
        return out + [pltpu.make_async_copy(self.block(self.source, me, flat_in), target, self.own)]

    def start(self):
        for copy in self.copies():
            copy.start()

    def wait(self):
        for copy in self.copies():
            copy.wait()


TRANSPOSE_SEMS = [pltpu.SemaphoreType.DMA((3,)), pltpu.SemaphoreType.DMA((3,)), pltpu.SemaphoreType.DMA]


def sine_cosine(angle):
    turns = jnp.floor(angle * (2.0 / math.pi) + 0.5)
    rest = ((angle - turns * 1.5703125) - turns * 4.837512969970703e-4) - turns * 7.549789948768648e-8
    square = rest * rest
    sine = rest + rest * square * (
        -1.6666654611e-1 + square * (8.3321608736e-3 + square * -1.9515295891e-4)
    )
    cosine = 1.0 - 0.5 * square + square * square * (
        4.166664568298827e-2 + square * (-1.388731625493765e-3 + square * 2.443315711809948e-5)
    )
    quarter = turns - 4.0 * jnp.floor(turns * 0.25)
    odd = (quarter == 1.0) | (quarter == 3.0)
    sin_sign = jnp.where(quarter >= 2.0, -1.0, 1.0)
    cos_sign = jnp.where((quarter == 1.0) | (quarter == 2.0), -1.0, 1.0)
    return sin_sign * jnp.where(odd, cosine, sine), cos_sign * jnp.where(odd, sine, cosine)


def decay(delta, length):
    time = lax.broadcasted_iota(jnp.int32, (length, delta.shape[1]), 0).astype(jnp.float32) * (1.0 / (length - 1))
    return jnp.exp(-time * delta) + MOD_SHIFT


def front_body(
    x_in, table_in, features_ref, delta_ref, g1, b1, g2, b2, skip, short, fw1, freqs, fw2, w3_ref,
    x_out, filt_out, taps_out, vec_ref, net_ref, table_ref, filt_ref, taps_ref, table_sem, sent, landed, own,
):
    place = Place()
    layers, units, width = w3_ref.shape
    length = table_ref.shape[1]
    table_copy = pltpu.make_async_copy(table_in, table_ref, table_sem.at[0])
    table_copy.start()
    leaving = [pltpu.make_async_copy(filt_ref, filt_out, table_sem.at[1])]
    leaving += [pltpu.make_async_copy(taps_ref.at[k], taps_out.at[k], table_sem.at[2 + k]) for k in range(layers)]
    move = Transpose(place, x_in, x_out, sent, landed, own, True)
    greet(move.partners)
    greeted(move.partners)
    move.start()
    vec_ref[...] = jnp.zeros_like(vec_ref)
    net_ref[...] = jnp.zeros_like(net_ref)
    for layer in range(layers):
        for k, ref in enumerate((g1, b1, g2, b2, skip)):
            vec_ref[VECS * layer + k : VECS * layer + k + 1, :] = f32(ref[...])[layer : layer + 1]
        for tap in range(3):
            row = f32(short[tap])[layer : layer + 1]
            for p in range(3):
                at = VECS * layer + 5 + 3 * p + tap
                vec_ref[at : at + 1, :] = row[:, width * p : width * (p + 1)]
        for k in range(EMB):
            net_ref[layer, k : k + 1, :] = f32(fw1[k])[layer : layer + 1]
        net_ref[layer, 40:42, :] = f32(freqs[layer])
        net_ref[layer, 48:112, :] = f32(fw2[layer])

    def high(a, b):
        top = bf(a)
        return mm(top, bf(b)) + mm(bf(a - f32(top)), bf(b))

    wide = lambda parts: jnp.concatenate(parts, axis=1)
    freq = [wide([net_ref[layer, 40 + k : 41 + k, :] for layer in range(layers)]) for k in range(2)]
    a1 = wide([high(features_ref[...], net_ref[layer, 0:40, :]) for layer in range(layers)])
    s1, c1 = sine_cosine(freq[0] * a1)
    a2 = wide([
        high(s1[:, units * layer : units * (layer + 1)], net_ref[layer, 48:112, :]) for layer in range(layers)
    ])
    s2, c2 = sine_cosine(freq[1] * a2)
    for k, values in enumerate((s1, s2, c1 * freq[0], c1 * a1, c2 * freq[1], c2 * a2)):
        filt_ref[k] = bf(values)
    leaving[0].start()
    envelope = decay(delta_ref[...], length)
    table_copy.wait()
    for layer in range(layers):
        taps = high(s2[:, units * layer : units * (layer + 1)], w3_ref[layer]) * envelope
        taps_ref[layer] = bf(mm(table_ref[...], bf(taps)) * (1.0 / length))
        leaving[1 + layer].start()
    for copy in leaving:
        copy.wait()
    move.wait()


def front(collective, x_in, table, features, delta, *small):
    slots, rows, width = x_in.shape
    layers, units, _ = small[-1].shape
    length = slots * rows
    vm = pl.BlockSpec(memory_space=pltpu.VMEM)
    b16, b32 = jnp.bfloat16, jnp.float32
    return pl.pallas_call(
        front_body,
        in_specs=[ANY, ANY] + [vm] * (2 + len(small)),
        out_specs=[ANY, ANY, ANY, vm, vm],
        out_shape=[
            sds((length, width), b16), sds((6, length, layers * units), b16), sds((layers, 2 * length, width), b16),
            sds((-(-VECS * layers // 8) * 8, width), b32), sds((layers, 112, units), b32),
        ],
        scratch_shapes=[
            pltpu.VMEM((2 * length, length), b16), pltpu.VMEM((6, length, layers * units), b16),
            pltpu.VMEM((layers, 2 * length, width), b16), pltpu.SemaphoreType.DMA((2 + layers,)),
        ] + TRANSPOSE_SEMS,
        compiler_params=pltpu.CompilerParams(
            vmem_limit_bytes=62 * MIB, collective_id=collective, has_side_effects=True
        ),
        name="front",
    )(x_in, table, features, delta, *small)


def mixed_chunk(proj, kernel):
    return [
        kernel[p][0:1] * row_shift(proj[p], 2) + kernel[p][1:2] * row_shift(proj[p], 1) + kernel[p][2:3] * proj[p]
        for p in range(3)
    ]


def gathering_forward_body(layer, carry, *refs):
    refs = list(refs)
    take = lambda n: [refs.pop(0) for _ in range(n)]
    r_ref, vec_ref, cut_ref, w0_ref, w1_ref, w2_ref, table_ref, taps_ref, wo_ref = take(9)
    moving_in = take(1)[0] if carry else None
    hidden_ref, normed_ref, proj_ref, signal_ref, long_ref = take(5)
    if carry:
        moved_out, sent, landed, own = take(4)
        move = Transpose(Place(), moving_in, moved_out, sent, landed, own, True)
    length = r_ref.shape[0]
    j = pl.program_id(0)

    @pl.when(j == 0)
    def _():
        if carry:
            greet(move.partners)
        r = f32(r_ref[...])
        xh, _ = standardised(r)
        normed_ref[...] = bf(xh * vector(vec_ref, layer, 0) + vector(vec_ref, layer, 1))
        hidden_ref[...] = r
        if carry:
            greeted(move.partners)
            move.start()

    normed = normed_ref[...]
    proj = [mm(normed, w_ref[...]) for w_ref in (w0_ref, w1_ref, w2_ref)]
    for p in range(3):
        proj_ref[p] = bf(proj[p])
    gate_out, gate_in, vals = mixed_chunk(proj, short_taps(cut_ref, layer))
    carried = vals * gate_in
    both = mm(table_ref[...], bf(carried))
    re, im = both[:length], both[length:]
    signal_ref[...] = bf(both)
    tap_re, tap_im = f32(taps_ref[:length]), f32(taps_ref[length:])
    out = mm_tn(table_ref[:length], bf(re * tap_re - im * tap_im))
    out += mm_tn(table_ref[length:], bf(re * tap_im + im * tap_re))
    long_out = out + vector(cut_ref, layer, 4) * carried
    long_ref[...] = bf(long_out)
    hidden_ref[...] += mm(bf(long_out * gate_out), wo_ref[...])

    if carry:
        @pl.when(j == pl.num_programs(0) - 1)
        def _():
            move.wait()


def gathering_forward(layer, collective, r, vecs, w_in, table, taps, w_out, *moving):
    length, width = r.shape
    chunk = 256
    steps = width // chunk
    carry = len(moving) > 0
    third = lambda p: pl.BlockSpec((None, width, chunk), lambda j: (layer, 0, p * steps + j))
    return pl.pallas_call(
        lambda *refs: gathering_forward_body(layer, carry, *refs),
        grid=(steps,),
        in_specs=[
            whole((length, width)), whole(vecs.shape), pl.BlockSpec((vecs.shape[0], chunk), lambda j: (0, j)),
            third(0), third(1), third(2),
            whole((2 * length, length)),
            pl.BlockSpec((None, 2 * length, chunk), lambda j: (layer, 0, j)),
            pl.BlockSpec((None, chunk, width), lambda j: (layer, j, 0)),
        ] + [ANY] * len(moving),
        out_specs=[
            whole((length, width)), whole((length, width)),
            pl.BlockSpec((3, length, chunk), lambda j: (0, 0, j)),
            pl.BlockSpec((2 * length, chunk), lambda j: (0, j)),
            pl.BlockSpec((length, chunk), lambda j: (0, j)),
        ] + [ANY] * len(moving),
        out_shape=[
            sds((length, width), jnp.float32), sds((length, width), jnp.bfloat16),
            sds((3, length, width), jnp.bfloat16), sds((2 * length, width), jnp.bfloat16),
            sds((length, width), jnp.bfloat16),
        ] + ([sds((length, width), jnp.bfloat16)] if carry else []),
        scratch_shapes=TRANSPOSE_SEMS if carry else [],
        compiler_params=pltpu.CompilerParams(
            vmem_limit_bytes=60 * MIB, **(dict(collective_id=collective, has_side_effects=True) if carry else {})
        ),
        cost_estimate=pl.CostEstimate(
            flops=2 * length * width * (4 * width + 4 * length), bytes_accessed=30 * MIB, transcendentals=0
        ),
        name="gathering_forward",
    )(r, vecs, vecs, w_in, w_in, w_in, table, taps, w_out, *moving)


def mixer_forward_body(layer, order, *refs):
    refs = list(refs)
    take = lambda n: [refs.pop(0) for _ in range(n)]
    vec_ref, r_in, w_in, table_in, taps_in, wo_in = take(6)
    hidden_ref, normed_out, proj_out, signal_out, long_out = take(5)
    (r_ref, normed_ref, w_ref, table_ref, taps_ref, wo_ref, proj_ref, signal_ref, long_ref, gated_ref, first_sem, w_sem,
     taps_sem, out_sem) = take(14)
    length, width = r_ref.shape
    chunk = 256
    count = width // chunk
    span = lambda c, p=0: pl.ds(p * width + c * chunk, chunk)
    r_copy = pltpu.make_async_copy(r_in, r_ref, first_sem.at[0])
    table_copy = pltpu.make_async_copy(table_in, table_ref, first_sem.at[1])
    wo_copy = pltpu.make_async_copy(wo_in.at[layer], wo_ref, first_sem.at[2])
    w_copies = [
        [pltpu.make_async_copy(w_in.at[layer, :, span(c, p)], w_ref.at[c, :, span(p)], w_sem.at[c, p]) for p in range(3)]
        for c in range(count)
    ]
    taps_copies = [
        pltpu.make_async_copy(taps_in.at[layer, :, span(c)], taps_ref.at[c], taps_sem.at[c]) for c in range(count)
    ]
    out_copies = [
        [
            pltpu.make_async_copy(proj_ref.at[:, :, span(c)], proj_out.at[:, :, span(c)], out_sem.at[c, 0]),
            pltpu.make_async_copy(signal_ref.at[:, span(c)], signal_out.at[:, span(c)], out_sem.at[c, 1]),
            pltpu.make_async_copy(long_ref.at[:, span(c)], long_out.at[:, span(c)], out_sem.at[c, 2]),
        ]
        for c in range(count)
    ]
    normed_copy = pltpu.make_async_copy(normed_ref, normed_out, first_sem.at[3])
    r_copy.start()
    for copy in w_copies[0]:
        copy.start()
    for copy in w_copies[1] + w_copies[2] + [table_copy] + taps_copies + [wo_copy]:
        copy.start()
    r_copy.wait()
    xh, _ = standardised(f32(r_ref[...]))
    normed_ref[...] = bf(xh * vector(vec_ref, layer, 0) + vector(vec_ref, layer, 1))
    normed_copy.start()
    held = [None] * count

    def project(c):
        for copy in w_copies[c]:
            copy.wait()
        columns = slice(c * chunk, (c + 1) * chunk)
        all_three = mm(normed_ref[...], w_ref[c])
        proj = [all_three[:, p * chunk : (p + 1) * chunk] for p in range(3)]
        for p in range(3):
            proj_ref[p, :, columns] = bf(proj[p])
        out_copies[c][0].start()
        kernel = [taps[:, columns] for taps in short_taps(vec_ref, layer)]
        gate_out, gate_in, vals = mixed_chunk(proj, kernel)
        held[c] = (gate_out, vals * gate_in)

    def transform(c):
        if c == 0:
            table_copy.wait()
        taps_copies[c].wait()
        gate_out, carried = held[c]
        both = mm(table_ref[...], bf(carried))
        re, im = both[:length], both[length:]
        signal_ref[:, c * chunk : (c + 1) * chunk] = bf(both)
        out_copies[c][1].start()
        tap_re, tap_im = f32(taps_ref[c, :length]), f32(taps_ref[c, length:])
        held[c] = (gate_out, carried, bf(re * tap_re - im * tap_im), bf(re * tap_im + im * tap_re))

    def back(c):
        columns = slice(c * chunk, (c + 1) * chunk)
        gate_out, carried, prod_re, prod_im = held[c]
        out = mm_tn(table_ref[:length], prod_re) + mm_tn(table_ref[length:], prod_im)
        long = out + vector(vec_ref, layer, 4)[:, columns] * carried
        long_ref[:, columns] = bf(long)
        out_copies[c][2].start()
        gated_ref[:, columns] = bf(long * gate_out)

    for step, c in order:
        (project, transform, back)[step](c)
    wo_copy.wait()
    hidden_ref[...] = f32(r_ref[...]) + mm(gated_ref[...], wo_ref[...])
    for copies in out_copies:
        for copy in copies:
            copy.wait()
    normed_copy.wait()


ORDER = tuple((step, c) for step in range(3) for c in range(3))


def mixer_forward(layer, r, vecs, w_in, table, taps, w_out):
    length, width = r.shape
    chunk = 256
    count = width // chunk
    vm = pl.BlockSpec(memory_space=pltpu.VMEM)
    b16, b32, dma = jnp.bfloat16, jnp.float32, pltpu.SemaphoreType.DMA
    return pl.pallas_call(
        lambda *refs: mixer_forward_body(layer, ORDER, *refs),
        in_specs=[vm] + [ANY] * 5,
        out_specs=[vm] + [ANY] * 4,
        out_shape=[
            sds((length, width), b32), sds((length, width), b16), sds((3, length, width), b16),
            sds((2 * length, width), b16), sds((length, width), b16),
        ],
        scratch_shapes=[
            pltpu.VMEM((length, width), r.dtype), pltpu.VMEM((length, width), b16), pltpu.VMEM((count, width, 3 * chunk), b16),
            pltpu.VMEM((2 * length, length), b16), pltpu.VMEM((count, 2 * length, chunk), b16),
            pltpu.VMEM((width, width), b16), pltpu.VMEM((3, length, width), b16), pltpu.VMEM((2 * length, width), b16),
            pltpu.VMEM((length, width), b16), pltpu.VMEM((length, width), b16), dma((4,)), dma((count, 3)), dma((count,)),
            dma((count, 3)),
        ],
        compiler_params=pltpu.CompilerParams(vmem_limit_bytes=62 * MIB),
        cost_estimate=pl.CostEstimate(
            flops=2 * length * width * (4 * width + 4 * length), bytes_accessed=30 * MIB, transcendentals=0
        ),
        name="mixer_forward",
    )(vecs, r, w_in, table, taps, w_out)


def ffn_forward_body(layer, last, *refs):
    hidden_ref, vec_ref, up_ref, down_ref = refs[:4]
    if last:
        live_ref, out_ref, normed_ref, raised_ref, r_ref = refs[4:]
    else:
        r_ref, normed_ref, raised_ref = refs[4:]

    @pl.when(pl.program_id(0) == 0)
    def _():
        hidden = hidden_ref[...]
        xh, _ = standardised(hidden)
        normed_ref[...] = bf(xh * vector(vec_ref, layer, 2) + vector(vec_ref, layer, 3))
        r_ref[...] = hidden

    raised = mm(normed_ref[...], up_ref[...])
    raised_ref[...] = bf(raised)
    r_ref[...] += mm(bf(gelu_parts(raised)[0]), down_ref[...])

    if last:
        @pl.when(pl.program_id(0) == pl.num_programs(0) - 1)
        def _():
            out_ref[...] = bf(r_ref[...] * live_ref[0, 0])


SCALAR = pl.BlockSpec(memory_space=pltpu.SMEM)


def ffn_forward(layer, hidden, vecs, w_up, w_down, *live):
    length, width = hidden.shape
    inner = w_up.shape[2]
    chunk = inner // 4
    last = len(live) > 0
    return pl.pallas_call(
        lambda *refs: ffn_forward_body(layer, last, *refs),
        grid=(inner // chunk,),
        in_specs=[
            whole((length, width)), whole(vecs.shape),
            pl.BlockSpec((None, width, chunk), lambda j: (layer, 0, j)),
            pl.BlockSpec((None, chunk, width), lambda j: (layer, j, 0)),
        ] + [SCALAR] * len(live),
        out_specs=[
            whole((length, width)), whole((length, width)), pl.BlockSpec((length, chunk), lambda j: (0, j)),
        ],
        out_shape=[
            sds((length, width), jnp.bfloat16 if last else jnp.float32), sds((length, width), jnp.bfloat16),
            sds((length, inner), jnp.bfloat16),
        ],
        scratch_shapes=[pltpu.VMEM((length, width), jnp.float32)] if last else [],
        compiler_params=pltpu.CompilerParams(vmem_limit_bytes=60 * MIB),
        cost_estimate=pl.CostEstimate(
            flops=4 * length * width * inner, bytes_accessed=26 * MIB, transcendentals=length * inner
        ),
        name="ffn_forward",
    )(hidden, vecs, w_up, w_down, *live)


def ffn_backward_body(layer, carry, *refs):
    refs = list(refs)
    take = lambda n: [refs.pop(0) for _ in range(n)]
    g_ref, hidden_in, vec_ref, normed_ref, raised_ref, up_ref, down_ref = take(7)
    zin_ref, min_ref = take(2) if carry else (None, None)
    live_ref, moving_in = (None, None) if carry else take(2)
    upstream = lambda: g_ref[...] if carry else f32(g_ref[...]) * live_ref[0, 0]
    out_ref, gain_grad_ref, bias_grad_ref, c_out, w_out = take(5)
    zfin_ref, wmix_ref = take(2) if carry else (None, None)
    moved_out = None if carry else take(1)[0]
    g16_ref, g16t_ref, normed_t_ref, give, got, c_ref, s1, core_s, core_r, s1_s, s1_r, out_sem, hidden_ref, hidden_sem = take(14)
    hidden_copy = pltpu.make_async_copy(hidden_in, hidden_ref, hidden_sem)
    if carry:
        zgot, zown, mgot, mown, z_s, z_r, m_s, m_r, own_sem = take(9)
    move_sems = None if carry else take(3)
    j = pl.program_id(0)
    steps = pl.num_programs(0)
    width = g_ref.shape[1]
    place = Place()
    half = c_ref.shape[1]
    mcols = width // 2
    move = None if carry else Transpose(place, moving_in, moved_out, *move_sems, False)
    partners = [place.over_core, place.over_x, place.over_y]
    partners += place.over_z if carry else [(place.s, 2 * (1 - place.y) + 1 - place.x)]

    def z_sends():
        piece = [remote(zin_ref.at[:, (place.z + d) % place.depth], zgot.at[d - 1], z_s.at[d - 1], z_r.at[d - 1],
                        place.over_z[d - 1]) for d in range(1, place.depth)]
        return piece

    def m_sends():
        sends = []
        for k in range(2):
            sends.append(remote(min_ref.at[2 * k + 1 - place.x, :, pl.ds(0, mcols)], mgot.at[0, k], m_s.at[0, k],
                                m_r.at[0, k], place.over_x))
            sends.append(remote(min_ref.at[2 * (1 - place.y) + k, :, pl.ds(mcols, mcols)], mgot.at[1, k], m_s.at[1, k],
                                m_r.at[1, k], place.over_y))
        return sends

    def own_copies():
        copies = [pltpu.make_async_copy(zin_ref.at[:, place.z], zown, own_sem.at[4])]
        for k in range(2):
            copies.append(pltpu.make_async_copy(min_ref.at[2 * k + place.x, :, pl.ds(0, mcols)], mown.at[0, k],
                                                own_sem.at[k]))
            copies.append(pltpu.make_async_copy(min_ref.at[2 * place.y + k, :, pl.ds(mcols, mcols)], mown.at[1, k],
                                                own_sem.at[2 + k]))
        return copies

    def core_send(slot, side):
        columns = pl.ds(side * width, width)
        return remote(give.at[slot, :, columns], got.at[slot, :, columns], core_s.at[slot, side], core_r.at[slot, side],
                      place.over_core)

    def s1_send(side, t):
        device = place.over_x if side == 0 else place.over_y
        return remote(c_ref.at[t, :, pl.ds(side * width, width)], s1.at[side], s1_s.at[side], s1_r.at[side], device)

    def c_copy(t):
        return pltpu.make_async_copy(c_ref.at[t], c_out.at[t], out_sem.at[t])

    def finish(t, slot):
        for side in range(2):
            core_send(slot, side).wait_recv()
        c_ref[t] = bf(f32(c_ref[t]) + f32(got[slot]))
        c_copy(t).start()

    @pl.when(j == 0)
    def _():
        greet(partners)
        hidden_copy.start()
        g16 = bf(upstream())
        g16_ref[...] = g16
        store_rows(place, g16t_ref, g16.T)
        store_rows(place, normed_t_ref, normed_ref[...].T)
        out_ref[...] = jnp.zeros_like(out_ref)
        greeted(partners)
        if carry:
            for copy in z_sends() + m_sends() + own_copies():
                copy.start()
        else:
            move.start()

    slot = j % 2

    @pl.when(j == 1)
    def _():
        finish(0, 0)

        @pl.when(place.x == 1)
        def _():
            s1_send(0, 0).start()

        @pl.when(place.y == 1)
        def _():
            s1_send(1, 0).start()

    @pl.when(j == 2)
    def _():
        finish(3, 1)

        @pl.when(place.x == 0)
        def _():
            s1_send(0, 3).start()

        @pl.when(place.y == 0)
        def _():
            s1_send(1, 3).start()

    @pl.when(j == 3)
    def _():
        finish(2, 0)

    @pl.when(j >= 2)
    def _():
        for side in range(2):
            core_send(slot, side).wait_send()

    active, slope = gelu_parts(f32(raised_ref[...]))
    active = bf(active)
    raised_grad = bf(mm_nt(g16_ref[...], down_ref[...]) * slope)
    t = (steps - j) % steps
    for side, (left, right) in enumerate(((normed_t_ref, raised_grad), (g16t_ref, active))):
        product = bf(mm(left[...], right))
        give[slot, :, side * width : (side + 1) * width] = product[:half]
        c_ref[t, :, side * width : (side + 1) * width] = product[half:]
        core_send(slot, side).start()
    out_ref[...] += mm_nt(raised_grad, up_ref[...])

    @pl.when(j == steps - 1)
    def _():
        hidden_copy.wait()
        part, gain_grad, bias_grad = norm_backward(hidden_ref[...], vector(vec_ref, layer, 2), out_ref[...])
        out_ref[...] = upstream() + part
        gain_grad_ref[...] = gain_grad
        bias_grad_ref[...] = bias_grad
        finish(1, 1)
        for k in range(2):
            s1_send(k, 0).wait_recv()
        w_out[0] = bf(f32(c_ref[3 * place.x, :, :width]) + f32(s1[0]))
        w_out[1] = bf(f32(c_ref[3 * place.y, :, width:]) + f32(s1[1]))
        if carry:
            for copy in own_copies():
                copy.wait()
            for copy in z_sends() + m_sends():
                copy.wait()
            total = f32(zown[...])
            for d in range(place.depth - 1):
                total += f32(zgot[d])
            zfin_ref[...] = total
            for side in range(2):
                for k in range(2):
                    wmix_ref[side, k] = bf(f32(mown[side, k]) + f32(mgot[side, k]))
        for k in range(2):
            s1_send(k, 0).wait_send()
            for side in range(2):
                core_send(k, side).wait_send()
        for k in range(steps):
            c_copy(k).wait()
        if not carry:
            move.wait()


def ffn_backward(layer, carry, collective, g, hidden, vecs, normed, raised, w_up, w_down, *carried):
    length, width = g.shape
    inner = w_up.shape[2]
    chunk = inner // 4
    depth = lax.axis_size("seq") // 2
    piece = width // (2 * depth)
    half = depth * piece
    b16, b32, dma = jnp.bfloat16, jnp.float32, pltpu.SemaphoreType.DMA
    order = lambda j: (4 - j) % 4
    return pl.pallas_call(
        lambda *refs: ffn_backward_body(layer, carry, *refs),
        grid=(4,),
        in_specs=[
            whole((length, width)), ANY, whole(vecs.shape), whole((length, width)),
            pl.BlockSpec((length, chunk), lambda j: (0, order(j))),
            pl.BlockSpec((None, width, chunk), lambda j: (layer, 0, order(j))),
            pl.BlockSpec((None, chunk, width), lambda j: (layer, order(j), 0)),
        ] + ([ANY] * 2 if carry else [SCALAR, ANY]),
        out_specs=[whole((length, width)), whole((1, width)), whole((1, width)), ANY, whole((2, half, width))]
        + ([whole((2, piece, width)), whole((2, 2, half, width // 2))] if carry else [ANY]),
        out_shape=[
            sds((length, width), b32), sds((1, width), b32), sds((1, width), b32), sds((4, half, 2 * chunk), b16),
            sds((2, half, chunk), b16),
        ] + ([sds((2, piece, chunk), b32), sds((2, 2, half, width // 2), b16)] if carry
             else [sds((4, length // 4, width), b16)]),
        scratch_shapes=[
            pltpu.VMEM((length, width), b16), pltpu.VMEM((width, length), b16), pltpu.VMEM((width, length), b16),
            pltpu.VMEM((2, half, 2 * chunk), b16), pltpu.VMEM((2, half, 2 * chunk), b16),
            pltpu.VMEM((4, half, 2 * chunk), b16), pltpu.VMEM((2, half, chunk), b16),
            dma((2, 2)), dma((2, 2)), dma((2,)), dma((2,)), dma((4,)), pltpu.VMEM((length, width), b32), dma,
        ] + ([
            pltpu.VMEM((depth - 1, 2, piece, chunk), b16), pltpu.VMEM((2, piece, chunk), b16),
            pltpu.VMEM((2, 2, half, width // 2), b16), pltpu.VMEM((2, 2, half, width // 2), b16),
            dma((depth - 1,)), dma((depth - 1,)), dma((2, 2)), dma((2, 2)), dma((5,)),
        ] if carry else TRANSPOSE_SEMS),
        compiler_params=pltpu.CompilerParams(
            vmem_limit_bytes=62 * MIB, collective_id=collective, has_side_effects=True
        ),
        cost_estimate=pl.CostEstimate(
            flops=8 * length * width * inner, bytes_accessed=40 * MIB, transcendentals=length * inner
        ),
        name="ffn_backward",
    )(g, hidden, vecs, normed, raised, w_up, w_down, *carried)


def mixer_backward_body(layer, carry, *refs):
    refs = list(refs)
    take = lambda n: [refs.pop(0) for _ in range(n)]
    (hg_ref, vec_ref, cut_ref, proj_ref, signal_ref, long_ref, taps_ref, wo_ref, r_in, normed_in, table_in, wi_in, c_in,
     w1_in) = take(14)
    wmix_ref = take(1)[0] if carry else None
    g_ref, c_out, zout_ref, taps_grad_ref, short_grad_ref, skip_grad_ref, gain_grad_ref, bias_grad_ref = take(8)
    mfin_ref = take(1)[0] if carry else None
    (og_ref, gated_ref, pg_ref, both_ref, got, s1, wkeep, s2, core_s, core_r, s1_s, s1_r, s2_s, s2_r, own_sem,
     out_sem, r_ref, normed_ref, table_ref, wi_ref, late_sem) = take(21)
    if carry:
        mkeep, m2, mz, mzgot, m2_s, m2_r, mz_s, mz_r, m_sem = take(9)
    j = pl.program_id(0)
    steps = pl.num_programs(0)
    length, width = hg_ref.shape
    place = Place()
    half = got.shape[1]
    piece = half // place.depth
    x, y = place.x, place.y
    partners = [place.over_core, place.over_x, place.over_y] + (place.over_z if carry else [])
    table_copy = pltpu.make_async_copy(table_in, table_ref, late_sem.at[0])
    late_copies = [
        pltpu.make_async_copy(source, target, late_sem.at[1 + k])
        for k, (source, target) in enumerate(((r_in, r_ref), (normed_in, normed_ref), (wi_in.at[layer], wi_ref)))
    ]

    def s1_sends():
        return [
            remote(c_in.at[1 + x, :, pl.ds(0, width)], s1.at[0], s1_s.at[0], s1_r.at[0], place.over_x),
            remote(c_in.at[2 - y, :, pl.ds(width, width)], s1.at[1], s1_s.at[1], s1_r.at[1], place.over_y),
        ]

    def own_copies():
        return [
            pltpu.make_async_copy(w1_in.at[0], wkeep.at[0, x], own_sem.at[0]),
            pltpu.make_async_copy(w1_in.at[1], wkeep.at[1, y], own_sem.at[1]),
            pltpu.make_async_copy(c_in.at[2 - x, :, pl.ds(0, width)], wkeep.at[0, 1 - x], own_sem.at[2]),
            pltpu.make_async_copy(c_in.at[1 + y, :, pl.ds(width, width)], wkeep.at[1, 1 - y], own_sem.at[3]),
        ]

    def s2_sends():
        return [
            remote(wkeep.at[0, 1 - y], s2.at[0], s2_s.at[0], s2_r.at[0], place.over_y),
            remote(wkeep.at[1, 1 - x], s2.at[1], s2_s.at[1], s2_r.at[1], place.over_x),
        ]

    def m2_sends():
        return [
            remote(wmix_ref.at[0, 1 - y], m2.at[0], m2_s.at[0], m2_r.at[0], place.over_y),
            remote(wmix_ref.at[1, 1 - x], m2.at[1], m2_s.at[1], m2_r.at[1], place.over_x),
        ]

    def m_copies():
        return [
            pltpu.make_async_copy(wmix_ref.at[0, y], mkeep.at[0], m_sem.at[0]),
            pltpu.make_async_copy(wmix_ref.at[1, x], mkeep.at[1], m_sem.at[1]),
        ]

    def mz_sends():
        return [
            remote(mz.at[:, (place.z + d) % place.depth], mzgot.at[d - 1], mz_s.at[d - 1], mz_r.at[d - 1],
                   place.over_z[d - 1])
            for d in range(1, place.depth)
        ]

    def core_send(t):
        return remote(both_ref.at[t, pl.ds(0, half)], got.at[t], core_s.at[t], core_r.at[t], place.over_core)

    def c_copy(t):
        return pltpu.make_async_copy(both_ref.at[t, pl.ds(half, half)], c_out.at[t], out_sem.at[t])

    @pl.when(j == 0)
    def _():
        greet(partners)
        table_copy.start()
        og_ref[...] = bf(hg_ref[...])
        greeted(partners)
        if carry:
            for copy in m2_sends() + m_copies():
                copy.start()
        for copy in s1_sends() + own_copies() + late_copies:
            copy.start()
        table_copy.wait()

    @pl.when(j == 2)
    def _():
        if carry:
            for copy in m2_sends() + m_copies():
                copy.wait()
            for side in range(2):
                total = bf(f32(mkeep[side]) + f32(m2[side]))
                for k in range(place.depth):
                    mz[side, k] = total[k * piece : (k + 1) * piece]
            for copy in mz_sends():
                copy.start()
        for copy in s1_sends() + own_copies():
            copy.wait()
        wkeep[0, 1 - x] = bf(f32(wkeep[0, 1 - x]) + f32(s1[0]))
        wkeep[1, 1 - y] = bf(f32(wkeep[1, 1 - y]) + f32(s1[1]))
        for copy in s2_sends():
            copy.start()

    @pl.when(j < steps - 1)
    def _():
        chunk = long_ref.shape[1]
        proj = [f32(proj_ref[p]) for p in range(3)]
        kernel = short_taps(cut_ref, layer)
        gate_out, gate_in, vals = mixed_chunk(proj, kernel)
        carried = vals * gate_in
        long_out = f32(long_ref[...])
        skip = vector(cut_ref, layer, 4)
        gated_ref[:, pl.ds(pl.multiple_of(j * chunk, chunk), chunk)] = bf(long_out * gate_out)
        gated_grad = mm_nt(og_ref[...], wo_ref[...])
        long_grad = gated_grad * gate_out
        skip_grad_ref[...] = jnp.sum(carried * long_grad, axis=0, keepdims=True)
        both = mm(table_ref[...], bf(long_grad))
        up_re, up_im = both[:length], both[length:]
        tap_re, tap_im = f32(taps_ref[:length]), f32(taps_ref[length:])
        sig_re, sig_im = f32(signal_ref[:length]), f32(signal_ref[length:])
        left = jnp.concatenate([bf(up_re * tap_re + up_im * tap_im), bf(up_im * tap_re - up_re * tap_im)], axis=0)
        right = jnp.concatenate([bf(up_re * sig_re + up_im * sig_im), bf(up_im * sig_re - up_re * sig_im)], axis=0)
        back = mm_tn(table_ref[...], jnp.concatenate([left, right], axis=1))
        carried_grad = back[:, :chunk] + skip * long_grad
        taps_grad_ref[...] = back[:, chunk:]
        for p, part in enumerate((gated_grad * long_out, carried_grad * vals, carried_grad * gate_in)):
            one, two = row_shift(part, -1), row_shift(part, -2)
            projected_grad = bf(kernel[p][2:3] * part + kernel[p][1:2] * one + kernel[p][0:1] * two)
            for tap, moved in enumerate((two, one, part)):
                short_grad_ref[p, tap : tap + 1, :] = jnp.sum(moved * proj[p], axis=0, keepdims=True)
            pg_ref[:, pl.ds(pl.multiple_of(p * width + j * chunk, chunk), chunk)] = projected_grad

    @pl.when(j == steps - 1)
    def _():
        in_cols, out_cols = 3 * width // 4, width // 4
        for copy in late_copies:
            copy.wait()
        upstream = mm_nt(pg_ref[...], wi_ref[...])
        for t in range(4):
            rights = pg_ref[:, in_cols * t : in_cols * (t + 1)], og_ref[:, out_cols * t : out_cols * (t + 1)]
            products = [bf(mm_tn(left[...], right)) for left, right in zip((normed_ref, gated_ref), rights)]
            store_rows(place, both_ref.at[t], jnp.concatenate(products, axis=1))
            core_send(t).start()
        part, gain_grad, bias_grad = norm_backward(f32(r_ref[...]), vector(vec_ref, layer, 0), upstream)
        total = hg_ref[...] + part
        g_ref[...] = total.astype(g_ref.dtype)
        gain_grad_ref[...] = gain_grad
        bias_grad_ref[...] = bias_grad
        for t in range(4):
            core_send(t).wait()
            both_ref[t, half:] = bf(f32(both_ref[t, half:]) + f32(got[t]))
            c_copy(t).start()
        if carry:
            for copy in mz_sends():
                copy.wait()
            for side in range(2):
                total = f32(mz[side, place.z])
                for d in range(place.depth - 1):
                    total += f32(mzgot[d, side])
                mfin_ref[side] = total
        for copy in s2_sends():
            copy.wait()
        for side, keep in enumerate((y, x)):
            total = bf(f32(wkeep[side, keep]) + f32(s2[side]))
            for k in range(place.depth):
                zout_ref[side, k] = total[k * piece : (k + 1) * piece]
        for t in range(4):
            c_copy(t).wait()


def mixer_backward(
    layer, carry, last, collective, hidden_grad, r, vecs, normed, proj, signal, long_out, taps, table, w_out, w_in, ffn_c,
    ffn_w, *carried
):
    length, width = r.shape
    chunk = 256
    steps = width // chunk
    depth = lax.axis_size("seq") // 2
    piece = width // (2 * depth)
    half = depth * piece
    at = lambda j: jnp.minimum(j, steps - 1)
    b16, b32, dma = jnp.bfloat16, jnp.float32, pltpu.SemaphoreType.DMA
    return pl.pallas_call(
        lambda *refs: mixer_backward_body(layer, carry, *refs),
        grid=(steps + 1,),
        in_specs=[
            whole((length, width)), whole(vecs.shape), pl.BlockSpec((vecs.shape[0], chunk), lambda j: (0, at(j))),
            pl.BlockSpec((3, length, chunk), lambda j: (0, 0, at(j))),
            pl.BlockSpec((2 * length, chunk), lambda j: (0, at(j))),
            pl.BlockSpec((length, chunk), lambda j: (0, at(j))),
            pl.BlockSpec((None, 2 * length, chunk), lambda j: (layer, 0, at(j))),
            pl.BlockSpec((None, chunk, width), lambda j: (layer, at(j), 0)),
        ] + [ANY] * (6 + len(carried)),
        out_specs=[
            whole((length, width)), ANY, whole((2, depth, piece, width)),
            pl.BlockSpec((length, chunk), lambda j: (0, at(j))),
            pl.BlockSpec((3, 3, chunk), lambda j: (0, 0, at(j))),
            pl.BlockSpec((1, chunk), lambda j: (0, at(j))),
            whole((1, width)), whole((1, width)),
        ] + ([whole((2, piece, width // 2))] if carry else []),
        out_shape=[
            sds((length, width), b16 if last else b32), sds((4, half, width), b16),
            sds((2, depth, piece, width), b16),
            sds((length, width), b32), sds((3, 3, width), b32), sds((1, width), b32), sds((1, width), b32),
            sds((1, width), b32),
        ] + ([sds((2, piece, width // 2), b32)] if carry else []),
        scratch_shapes=[
            pltpu.VMEM((length, width), b16), pltpu.VMEM((length, width), b16), pltpu.VMEM((length, 3 * width), b16),
            pltpu.VMEM((4, width, width), b16), pltpu.VMEM((4, half, width), b16),
            pltpu.VMEM((2, half, width), b16), pltpu.VMEM((2, 2, half, width), b16), pltpu.VMEM((2, half, width), b16),
            dma((4,)), dma((4,)), dma((2,)), dma((2,)), dma((2,)), dma((2,)), dma((4,)), dma((4,)),
            pltpu.VMEM((length, width), r.dtype), pltpu.VMEM((length, width), b16), pltpu.VMEM((2 * length, length), b16),
            pltpu.VMEM((width, 3 * width), b16), dma((4,)),
        ] + ([
            pltpu.VMEM((2, half, width // 2), b16), pltpu.VMEM((2, half, width // 2), b16),
            pltpu.VMEM((2, depth, piece, width // 2), b16), pltpu.VMEM((depth - 1, 2, piece, width // 2), b16),
            dma((2,)), dma((2,)), dma((depth - 1,)), dma((depth - 1,)), dma((2,)),
        ] if carry else []) ,
        compiler_params=pltpu.CompilerParams(
            vmem_limit_bytes=63 * MIB, collective_id=collective, has_side_effects=True
        ),
        cost_estimate=pl.CostEstimate(
            flops=2 * length * width * (8 * width + 6 * length), bytes_accessed=50 * MIB, transcendentals=0
        ),
        name="mixer_backward",
    )(hidden_grad, vecs, vecs, proj, signal, long_out, taps, w_out, r, normed, table, w_in, ffn_c, ffn_w, *carried)


SMALL = 128


def closing_body(
    z_in, c_in, g_in, t0_in, t1_in, v0, v1, v2, v3, v4, v5, v6, v7, v8, v9, v10, v11, features_ref, filt_ref, net_ref,
    w3_ref, delta_ref, zfin_ref, mfin_ref, agot, small_ref,
    zgot, zown, mgot, w, m2, mz, mzgot, tgrad, pack, cgot, xgot, xsum, ygot, ysum, zslot, total16, full,
    z_s, z_r, m_s, m_r, m2_s, m2_r, mz_s, mz_r, a_s, a_r, own_sem, sm_s, sm_r, zs_s, zs_r,
):
    place = Place()
    x, y, z, core = place.x, place.y, place.z, place.core
    cols = w.shape[3]
    piece = zown.shape[1]
    rows = agot.shape[1]
    over_both = (place.s, 2 * (1 - y) + 1 - x)
    m_sends = []
    for k in range(2):
        m_sends.append(remote(c_in.at[2 * k + 1 - x, :, pl.ds(0, cols)], mgot.at[0, k], m_s.at[0, k], m_r.at[0, k],
                              place.over_x))
        m_sends.append(remote(c_in.at[2 * (1 - y) + k, :, pl.ds(cols, cols)], mgot.at[1, k], m_s.at[1, k],
                              m_r.at[1, k], place.over_y))
    z_sends = [
        remote(z_in.at[:, (z + d) % place.depth], zgot.at[d - 1], z_s.at[d - 1], z_r.at[d - 1], place.over_z[d - 1])
        for d in range(1, place.depth)
    ]
    own = [pltpu.make_async_copy(z_in.at[:, z], zown, own_sem.at[4])]
    for k in range(2):
        own.append(pltpu.make_async_copy(c_in.at[2 * k + x, :, pl.ds(0, cols)], w.at[0, k], own_sem.at[k]))
        own.append(pltpu.make_async_copy(c_in.at[2 * y + k, :, pl.ds(cols, cols)], w.at[1, k], own_sem.at[2 + k]))
    loads = [
        pltpu.make_async_copy(t0_in, tgrad.at[0], own_sem.at[5]), pltpu.make_async_copy(t1_in, tgrad.at[1], own_sem.at[6]),
    ]
    part = lambda t: g_in.at[pl.ds(pl.multiple_of(t * rows, rows), rows)]
    home = pltpu.make_async_copy(part(place.t), agot.at[place.t], own_sem.at[8])

    def a_sends():
        out = []
        for k, device in enumerate((place.over_x, place.over_y, over_both)):
            out.append(remote(part(device[1]), agot.at[place.t], a_s.at[k], a_r.at[k], device))
        return out

    for copy in loads:
        copy.start()
    partners = [place.over_core, place.over_x, place.over_y, over_both] + place.over_z
    greet(partners)
    greeted(partners)
    for copy in m_sends + z_sends + own + [home]:
        copy.start()

    units = w3_ref.shape[1]
    envelope = decay(delta_ref[...], tgrad.shape[1]) * (1.0 / tgrad.shape[1])
    pack[...] = jnp.zeros_like(pack)
    s1, s2 = filt_ref[0], filt_ref[1]
    u1, h1, u2, h2 = (f32(filt_ref[k]) for k in range(2, 6))
    wide = lambda parts: jnp.concatenate(parts, axis=1)
    for copy in loads:
        copy.wait()
    upstream = [bf(tgrad[layer] * envelope) for layer in range(2)]
    ds2 = wide([mm_nt(upstream[layer], w3_ref[layer]) for layer in range(2)])
    for layer in range(2):
        pack[layer, :64] = mm_tn(s2[:, units * layer : units * (layer + 1)], upstream[layer])
    da2 = ds2 * u2
    span = lambda v, layer: v[:, units * layer : units * (layer + 1)]
    ds1 = wide([mm_nt(bf(span(da2, layer)), bf(net_ref[layer, 48:112, :])) for layer in range(2)])
    da1 = ds1 * u1
    dw2 = wide([mm_tn(span(s1, layer), bf(span(da2, layer))) for layer in range(2)])
    dw1 = mm_tn(bf(features_ref[...]), bf(da1))
    freq = [jnp.sum(ds1 * h1, axis=0, keepdims=True), jnp.sum(ds2 * h2, axis=0, keepdims=True)]
    for k, block in enumerate((dw1[:24], jnp.concatenate([dw1[24:40], freq[0], freq[1], jnp.zeros((6, 128), jnp.float32)]),
                               dw2[:24], dw2[24:48], jnp.concatenate([dw2[48:64], jnp.zeros((8, 128), jnp.float32)]))):
        pack[0, 80:104, 128 * k : 128 * (k + 1)] = block
    vectors = ((v0, v1, v2, v3, v4, v5), (v6, v7, v8, v9, v10, v11))
    for layer in range(2):
        for k in range(5):
            pack[layer, 64 + k : 65 + k, :] = vectors[layer][k][...]
        for p in range(3):
            pack[layer, 69 + 3 * p : 72 + 3 * p, :] = vectors[layer][5][p]

    total16[0] = bf(pack[0])
    total16[1] = bf(pack[1])
    to_core = remote(total16.at[1 - core], cgot, sm_s.at[0], sm_r.at[0], place.over_core)
    to_core.start()
    to_core.wait()
    xsum[...] = bf(f32(total16[core]) + f32(cgot[...]))
    half, quarter = SMALL // 2, SMALL // 4
    side = lambda k, n: pl.ds(pl.multiple_of(k * n, n), n)
    to_x = remote(xsum.at[side(1 - x, half)], xgot, sm_s.at[1], sm_r.at[1], place.over_x)
    to_x.start()

    for copy in own + m_sends:
        copy.wait()
    for k in range(2):
        for n in range(2):
            w[k, n] = bf(f32(w[k, n]) + f32(mgot[k, n]))
    m2_sends = [
        remote(w.at[0, 1 - y], m2.at[0], m2_s.at[0], m2_r.at[0], place.over_y),
        remote(w.at[1, 1 - x], m2.at[1], m2_s.at[1], m2_r.at[1], place.over_x),
    ]
    for copy in m2_sends:
        copy.start()

    to_x.wait()
    ysum[...] = bf(f32(xsum[side(x, half)]) + f32(xgot[...]))
    to_y = remote(ysum.at[side(1 - y, quarter)], ygot, sm_s.at[2], sm_r.at[2], place.over_y)
    to_y.start()
    to_y.wait()
    zslot[z] = bf(f32(ysum[side(y, quarter)]) + f32(ygot[...]))
    zs_sends = [
        remote(zslot.at[z], zslot.at[z], zs_s.at[d - 1], zs_r.at[d - 1], place.over_z[d - 1])
        for d in range(1, place.depth)
    ]
    for copy in zs_sends:
        copy.start()

    for copy in m2_sends:
        copy.wait()
    for copy in a_sends():
        copy.start()
    for k, keep in enumerate((y, x)):
        total = bf(f32(w[k, keep]) + f32(m2[k]))
        for n in range(place.depth):
            mz[k, n] = total[n * piece : (n + 1) * piece]
    mz_sends = [
        remote(mz.at[:, (z + d) % place.depth], mzgot.at[d - 1], mz_s.at[d - 1], mz_r.at[d - 1], place.over_z[d - 1])
        for d in range(1, place.depth)
    ]
    for copy in mz_sends:
        copy.start()

    for copy in z_sends:
        copy.wait()
    total = f32(zown[...])
    for d in range(place.depth - 1):
        total += f32(zgot[d])
    zfin_ref[...] = total

    for copy in zs_sends:
        copy.wait()
    total = f32(zslot[0])
    for k in range(1, place.depth):
        total += f32(zslot[k])
    mine = pl.multiple_of(x * half + y * quarter, quarter)
    full[core, pl.ds(mine, quarter)] = bf(total)
    back_y = remote(full.at[core, pl.ds(mine, quarter)], full.at[core, pl.ds(mine, quarter)], sm_s.at[3], sm_r.at[3],
                    place.over_y)
    back_y.start()
    back_y.wait()
    back_x = remote(full.at[core, side(x, half)], full.at[core, side(x, half)], sm_s.at[4], sm_r.at[4], place.over_x)
    back_x.start()
    back_x.wait()
    back_core = remote(full.at[core], full.at[core], sm_s.at[5], sm_r.at[5], place.over_core)
    back_core.start()
    back_core.wait()
    small_ref[...] = f32(full[...])
    for copy in mz_sends:
        copy.wait()
    for k in range(2):
        total = f32(mz[k, z])
        for d in range(place.depth - 1):
            total += f32(mzgot[d, k])
        mfin_ref[k] = total
    home.wait()
    for copy in a_sends():
        copy.wait()


def closing(collective, ffn_z, mixer_c, grad, taps_grads, vectors, features, filt, net, w3, delta):
    _, depth, piece, width = ffn_z.shape
    length = grad.shape[0]
    half = depth * piece
    b16, b32, dma = jnp.bfloat16, jnp.float32, pltpu.SemaphoreType.DMA
    cols = width // 2
    vm = pl.BlockSpec(memory_space=pltpu.VMEM)
    return pl.pallas_call(
        closing_body,
        in_specs=[ANY] * 5 + [vm] * (len(vectors) + 5),
        out_specs=[vm, vm, ANY, vm],
        out_shape=[
            sds((2, piece, width), b32), sds((2, piece, cols), b32), sds((4, length // 4, width), b16),
            sds((2, SMALL, width), b32),
        ],
        scratch_shapes=[
            pltpu.VMEM((depth - 1, 2, piece, width), b16), pltpu.VMEM((2, piece, width), b16),
            pltpu.VMEM((2, 2, half, cols), b16), pltpu.VMEM((2, 2, half, cols), b16), pltpu.VMEM((2, half, cols), b16),
            pltpu.VMEM((2, depth, piece, cols), b16), pltpu.VMEM((depth - 1, 2, piece, cols), b16),
            pltpu.VMEM((2, length, width), b32),
            pltpu.VMEM((2, SMALL, width), b32), pltpu.VMEM((SMALL, width), b16), pltpu.VMEM((SMALL // 2, width), b16),
            pltpu.VMEM((SMALL, width), b16), pltpu.VMEM((SMALL // 4, width), b16), pltpu.VMEM((SMALL // 2, width), b16),
            pltpu.VMEM((depth, SMALL // 4, width), b16), pltpu.VMEM((2, SMALL, width), b16),
            pltpu.VMEM((2, SMALL, width), b16),
            dma((depth - 1,)), dma((depth - 1,)), dma((2, 2)), dma((2, 2)), dma((2,)), dma((2,)), dma((depth - 1,)),
            dma((depth - 1,)), dma((3,)), dma((3,)), dma((9,)), dma((6,)), dma((6,)), dma((depth - 1,)),
            dma((depth - 1,)),
        ],
        compiler_params=pltpu.CompilerParams(
            vmem_limit_bytes=62 * MIB, collective_id=collective, has_side_effects=True
        ),
        name="closing",
    )(ffn_z, mixer_c, grad, *taps_grads, *vectors, features, filt, net, w3, delta)


def assemble_body(
    out_in, grad_in, f0, f1, m0, m1, small, out_act, grad_x, g1, b1, w_in, short, w1, freq, w2, w3, skip, w_out, g2, b2,
    w_up, w_down,
):
    out_act[...] = f32(out_in[...])
    grad_x[...] = f32(grad_in[...])

    @pl.when(pl.program_id(0) == 0)
    def _():
        units = w2.shape[1]
        cols = m0.shape[2]
        split = w_in.shape[2]
        for layer, (f, m) in enumerate(((f0, m0), (f1, m1))):
            row = slice(layer, layer + 1)
            for k, ref in enumerate((g1, b1, g2, b2, skip)):
                ref[row, :] = small[layer, 64 + k : 65 + k, :]
            for p in range(3):
                for tap in range(3):
                    at = 69 + 3 * p + tap
                    width = small.shape[2]
                    short[tap, row, p * width : (p + 1) * width] = small[layer, at : at + 1, :]
            lanes = lambda k: slice(128 * k + units * layer, 128 * k + units * (layer + 1))
            for k in range(EMB):
                at = 80 + k % 24
                w1[k, row, :] = small[0, at : at + 1, lanes(k // 24)]
            freq[layer] = small[0, 96:98, lanes(1)]
            w2[layer] = jnp.concatenate(
                [small[0, 80:104, lanes(2)], small[0, 80:104, lanes(3)], small[0, 80:96, lanes(4)]], axis=0
            )
            w3[layer] = small[layer, :64, :]
            w_in[layer] = jnp.concatenate([m[0], m[1][:, : split - cols]], axis=1)
            w_out[layer] = m[1][:, split - cols :]
            w_up[layer] = f[0]
            w_down[layer] = f[1]


def assemble(out_act, grad_in, ffn, mixer, small, units):
    slots, rows, width = out_act.shape
    _, piece, cols = ffn[0].shape
    split = 3 * width // 4
    b32 = jnp.float32
    shapes = [
        (2, width), (2, width), (2, piece, split), (3, 2, 3 * width), (EMB, 2, units), (2, 2, units), (2, units, units),
        (2, units, width), (2, width), (2, piece, width - split), (2, width), (2, width), (2, piece, cols),
        (2, piece, cols),
    ]
    block = pl.BlockSpec((slots // 2, rows, width), lambda j: (j, 0, 0))
    return pl.pallas_call(
        assemble_body,
        grid=(2,),
        in_specs=[block, block] + [whole(v.shape) for v in (*ffn, *mixer, small)],
        out_specs=[block, block] + [whole(shape) for shape in shapes],
        out_shape=[sds((slots, rows, width), b32)] * 2 + [sds(shape, b32) for shape in shapes],
        compiler_params=pltpu.CompilerParams(vmem_limit_bytes=62 * MIB),
        name="assemble",
    )(out_act, grad_in, *ffn, *mixer, small)


def feature_table(length):
    bands = (EMB - 1) // 2
    step = np.arange(length, dtype=np.float64)[:, None]
    phases = 2.0 * math.pi / length * step * np.linspace(1e-4, bands - 1, bands)[None]
    parts = [step / (length - 1), np.cos(phases), -np.sin(phases), np.zeros((length, 40 - EMB))]
    return np.concatenate(parts, axis=1).astype(np.float32)


def whole_sequences(
    x_in, cotangent, counts, ln1_gain, ln1_bias, w_in, short_w, filt_w1, filt_freq, filt_w2, filt_w3, long_bias,
    w_out, ln2_gain, ln2_bias, w_up, w_down,
):
    micro_count, cap_size, tok_rows, width = x_in.shape
    slots = micro_count * cap_size
    layers = w_up.shape[0]
    toks = lax.axis_size("tok")
    length = tok_rows * toks
    me = lax.axis_index("tok")
    live = (me % cap_size < counts[me // cap_size, 0]).astype(jnp.float32).reshape(1, 1)
    table = jnp.asarray(spectral_table(length))
    features = jnp.asarray(feature_table(length))
    delta = jnp.asarray(
        np.abs(np.linspace(math.log(0.01) / 0.3, math.log(0.01) / 1.5, width, dtype=np.float64))[None].astype(np.float32)
    )
    blocks = lambda v: v.reshape(slots, tok_rows, width)
    r, filt, spectra, vecs, net = front(
        2 * layers + 1, blocks(x_in), table, features, delta, ln1_gain, ln1_bias, ln2_gain, ln2_bias, long_bias,
        jnp.swapaxes(short_w, 0, 1), jnp.swapaxes(filt_w1, 0, 1), filt_freq, filt_w2, filt_w3,
    )
    kept = []
    for layer in range(layers):
        if layer == 0:
            hidden, normed, proj, signal, long_out, upstream = gathering_forward(
                layer, 2 * layers + 2, r, vecs, w_in, table, spectra, w_out, blocks(cotangent)
            )
        else:
            hidden, normed, proj, signal, long_out = mixer_forward(layer, r, vecs, w_in, table, spectra, w_out)
        result, normed_two, raised = ffn_forward(
            layer, hidden, vecs, w_up, w_down, *((live,) if layer == layers - 1 else ())
        )
        kept.append((r, hidden, normed, proj, signal, long_out, normed_two, raised))
        r = result

    grad = upstream
    vectors, taps_grads, done = [None] * layers, [None] * layers, {}
    carried_ffn, carried_mixer = (live, r), ()
    for layer in reversed(range(layers)):
        r, hidden, normed, proj, signal, long_out, normed_two, raised = kept[layer]
        carry = layer < layers - 1
        grad, grad_g2, grad_b2, ffn_c, ffn_w, *rest = ffn_backward(
            layer, carry, 2 * layer, grad, hidden, vecs, normed_two, raised, w_up, w_down, *carried_ffn
        )
        if carry:
            done["ffn", layer + 1], *carried_mixer = rest
        else:
            out_act = rest[0]
        grad, mixer_c, ffn_z, taps_grads[layer], grad_short, grad_skip, grad_g1, grad_b1, *rest = mixer_backward(
            layer, carry, layer == 0, 2 * layer + 1, grad, r, vecs, normed, proj, signal, long_out, spectra, table, w_out,
            w_in, ffn_c, ffn_w, *carried_mixer,
        )
        if carry:
            done["mixer", layer + 1] = rest[0]
        carried_ffn = (ffn_z, mixer_c)
        vectors[layer] = (grad_g1, grad_b1, grad_g2, grad_b2, grad_skip, grad_short)
    done["ffn", 0], done["mixer", 0], grad_in, small = closing(
        2 * layers, *carried_ffn, grad, taps_grads, vectors[0] + vectors[1], features, filt, net, filt_w3, delta
    )
    pair = lambda kind: [done[kind, layer] for layer in range(layers)]
    out_act, grad_in, *grads = assemble(out_act, grad_in, pair("ffn"), pair("mixer"), small, filt_w2.shape[1])
    for k, axes in ((3, (0, 1)), (4, (0, 1)), (13, (1, 2))):
        grads[k] = jnp.swapaxes(grads[k], *axes)
    home = lambda v: v.reshape(micro_count, cap_size, tok_rows, width)
    return (home(out_act), home(grad_in), *grads)


def shards(*args):
    micro_count, cap_size = args[0].shape[:2]
    if lax.axis_size("tok") == 4 and micro_count * cap_size == 4:
        return whole_sequences(*args)
    return split_positions(*args)


def solution(mesh):
    return jax.shard_map(
        shards,
        mesh=mesh,
        in_specs=(
            P(None, "seq", "tok", None),
            P(None, "seq", "tok", None),
            P(None, "seq"),
            P(),
            P(),
            P(),
            P(),
            P(),
            P(),
            P(),
            P(),
            P(),
            P(),
            P(),
            P(),
            P(),
            P(),
        ),
        out_specs=(
            P(None, "seq", "tok", None),
            P(None, "seq", "tok", None),
            P(),
            P(),
            P(None, "seq", "tok"),
            P(),
            P(),
            P(),
            P(),
            P(),
            P(),
            P(None, "seq", "tok"),
            P(),
            P(),
            P(None, "seq", "tok"),
            P(None, "tok", "seq"),
        ),
        check_vma=False,
    )
```
